32 devices in a mesh: seq: 8 (over y, x, core), head: 4 (over z).
Axes of the slice: x: 2, y: 2, z: 4, core: 2. Of those that a mesh axis runs over, the one named last changes fastest.
Arguments:
- enc_in: bfloat16 [2048, 4, 768], P(('seq', 'head')), may hold values from -6 to 6
- conv_weight: bfloat16 [5, 768, 1536], replicated, may hold values from -0.09375 to 0.09375
- norm_gain: float32 [1536], replicated, may hold values from 0.25 to 1.75
- w_qkv: bfloat16 [3, 1536, 1536], P(None, None, 'head'), may hold values from -0.63788795 to 0.63788795
- w_out: bfloat16 [1536, 1536], P('head'), may hold values from -0.15625 to 0.15625
- grad_out: bfloat16 [1024, 4, 1536], P(('seq', 'head')), may hold values from -6 to 6
Outputs:
- mixed: bfloat16 [1024, 4, 1536], P(('seq', 'head'))
- grad_input: bfloat16 [2048, 4, 768], P(('seq', 'head'))
- grad_w_qkv: float32 [3, 1536, 1536], P(None, None, 'head')
- grad_w_out: float32 [1536, 1536], P('head')
The draws below stay inside these ranges and needn't reach their ends.
All inputs are finite; a program needn't handle non-finite values.
Results may differ from the reference program's by a relative error of at most 0.024.
Values may be sent and summed in bfloat16 or wider, within the bound.
No kernel may reach another device: no remote copies, remote signals or barrier semaphores. Data moves between devices by JAX's collectives and lax.ppermute only.
A program may use at most 256 MiB of HBM per device.

```python
import jax
import jax.numpy as jnp
from jax import lax

C_IN = 768
C = 1536
HEADS = 8
DH = 192
KW = 5
SEQS = 4
L = 1024
LF = 2048
BLOCK = 128
HEADS_DEV = 2
N_SEQ = 8
N_HEAD = 4


def draw_w_qkv(key, part):
    key_base = jax.random.fold_in(key, 0)
    fan_scale = C ** (-0.5)
    drawn_draw = jax.random.truncated_normal(key_base, -4.0, 4.0, (3, C, HEADS * DH), jnp.float32) * fan_scale
    return drawn_draw.astype(jnp.bfloat16)


def level_of(key, dims, pieces, smallest, largest):
    def one(position, shards_of):
        steps = jax.random.uniform(jax.random.fold_in(jax.random.fold_in(key, 6), position), (shards_of,), jnp.float32, smallest / len(pieces), largest / len(pieces))
        return jnp.repeat(jnp.exp(steps), dims[position] // shards_of).reshape((-1,) + (1,) * (len(dims) - position - 1))

    gain = one(*pieces[0])
    for cut in pieces[1:]:
        gain = gain * one(*cut)
    return gain


def bell_draw(own_key, dims, width, reach, cuts=(), dtype=jnp.bfloat16):
    gain = level_of(own_key, dims, cuts, -0.22, 0.18) if cuts else 1.0
    values = jax.random.normal(own_key, dims, jnp.float32) * width * gain
    return jnp.minimum(jnp.maximum(values, -reach), reach).astype(dtype)


def setup_inputs(seed: int = 0) -> dict:
    key_list = jax.random.split(jax.random.key(seed), 7)
    return {
        "enc_in": bell_draw(key_list[0], (LF, SEQS, C_IN), 1.0, 6.0, ((0, 32),)),
        "conv_weight": bell_draw(key_list[1], (KW, C_IN, C), (KW * C_IN) ** -0.5, 0.09375),
        "norm_gain": jnp.clip(1.0 + 0.15 * jax.random.normal(key_list[2], (C,), jnp.float32), 0.25, 1.75),
        "w_qkv": draw_w_qkv(jax.random.fold_in(key_list[6], 71), 0),
        "w_out": bell_draw(key_list[4], (HEADS * DH, C), (HEADS * DH) ** -0.5, 0.15625, ((0, 4),)),
        "grad_out": bell_draw(key_list[5], (L, SEQS, C), 1.0, 6.0, ((0, 32),)),
    }


def rounded(value_matrix):
    return lax.optimization_barrier(value_matrix.astype(jnp.bfloat16)).astype(jnp.float32)

def broaden_heads(value_matrix):
    return value_matrix.astype(jnp.float32)

def head_forward(inputs):
    query_matrix, key_matrix, value_matrix = inputs
    logit_scale = DH ** (-0.5)
    attention_logits = jnp.einsum('ype,tpe->pyt', broaden_heads(query_matrix), broaden_heads(key_matrix), precision=lax.Precision.HIGHEST) * logit_scale
    row_peak = lax.optimization_barrier(jnp.max(attention_logits, axis=-1, keepdims=True))
    exponent = jnp.exp(attention_logits - row_peak)
    row_total = lax.optimization_barrier(jnp.sum(exponent, axis=-1, keepdims=True))
    narrow_probabilities = rounded(exponent / row_total)
    attention_output = jnp.einsum('wlc,cwy->lwy', narrow_probabilities, broaden_heads(value_matrix), precision=lax.Precision.HIGHEST)
    return (attention_output, (row_peak + jnp.log(row_total))[..., 0])

def head_back(inputs):
    query_matrix, key_matrix, value_matrix, d_out, attention_output, log_total = inputs
    logit_scale = DH ** (-0.5)
    wide_query_matrix = broaden_heads(query_matrix)
    wide_key_matrix = broaden_heads(key_matrix)
    wide_output_gradient = broaden_heads(d_out)
    attention_logits = jnp.einsum('ype,tpe->pyt', wide_query_matrix, wide_key_matrix, precision=lax.Precision.HIGHEST) * logit_scale
    soft_back = jnp.exp(attention_logits - log_total[..., None])
    probability_gradient = jnp.einsum('ype,tpe->pyt', wide_output_gradient, broaden_heads(value_matrix), precision=lax.Precision.HIGHEST)
    delta = lax.optimization_barrier(jnp.sum(wide_output_gradient * attention_output, axis=-1))
    d_scores = soft_back * (probability_gradient - jnp.transpose(delta)[..., None])
    narrow_gradient = rounded(d_scores)
    narrow_probabilities = rounded(soft_back)
    query_gradient = logit_scale * jnp.einsum('wlc,cwy->lwy', narrow_gradient, wide_key_matrix, precision=lax.Precision.HIGHEST)
    ds_blocks = narrow_gradient.reshape(SEQS, N_SEQ, BLOCK, L)
    soft_blocks = narrow_probabilities.reshape(SEQS, N_SEQ, BLOCK, L)
    query_blocks = wide_query_matrix.reshape(N_SEQ, BLOCK, SEQS, DH)
    dout_blocks = wide_output_gradient.reshape(N_SEQ, BLOCK, SEQS, DH)
    key_parts = logit_scale * jnp.einsum('bnqk,nqbd->nkbd', ds_blocks, query_blocks, precision=lax.Precision.HIGHEST)
    value_parts = jnp.einsum('bnqk,nqbd->nkbd', soft_blocks, dout_blocks, precision=lax.Precision.HIGHEST)
    d_keys = lax.optimization_barrier(jnp.sum(rounded(key_parts), axis=0))
    d_values = lax.optimization_barrier(jnp.sum(rounded(value_parts), axis=0))
    return jnp.stack([query_gradient, d_keys, d_values])

def split_heads(array):
    return jnp.transpose(array.reshape(array.shape[0], array.shape[1], HEADS, DH), (2, 0, 1, 3))

def join_heads(array):
    return jnp.transpose(array, (1, 2, 0, 3)).reshape(array.shape[1], array.shape[2], HEADS * DH)

def reference(enc_in, conv_weight, norm_gain, w_qkv, w_out, grad_out):
    padded = jnp.pad(enc_in, ((2, 2), (0, 0), (0, 0)))
    convolved = jnp.zeros((LF, SEQS, C), jnp.float32)
    for offset in range(KW):
        convolved = convolved + jnp.einsum('tbi,io->tbo', broaden_heads(padded[offset:offset + LF]), broaden_heads(conv_weight[offset]))
    activated, gelu_pull = jax.vjp(jax.nn.gelu, convolved)
    skip = lax.optimization_barrier(jnp.mean(activated.reshape(L, 2, SEQS, C), axis=1)).astype(jnp.bfloat16)
    skip_wide = broaden_heads(skip)
    inv_rms = lax.rsqrt(lax.optimization_barrier(jnp.mean(skip_wide * skip_wide, axis=-1, keepdims=True)) + 1e-06)
    normed = (skip_wide * inv_rms * norm_gain).astype(jnp.bfloat16)
    normed_wide = broaden_heads(normed)
    qkv = jnp.einsum('tbc,ice->itbe', normed_wide, broaden_heads(w_qkv)).astype(jnp.bfloat16)
    query_matrix, key_matrix, value_matrix = (split_heads(qkv[0]), split_heads(qkv[1]), split_heads(qkv[2]))
    attention_output, log_total = lax.map(head_forward, (query_matrix, key_matrix, value_matrix))
    o_narrow = join_heads(attention_output).astype(jnp.bfloat16)
    o_wide = broaden_heads(o_narrow)
    out_wide = broaden_heads(w_out)
    qkv_wide = broaden_heads(w_qkv)
    group_width = HEADS_DEV * DH
    head_sum = jnp.zeros((L, SEQS, C), jnp.float32)
    for head_group in range(N_HEAD):
        first = head_group * group_width
        term = jnp.einsum('tbe,ec->tbc', o_wide[:, :, first:first + group_width], out_wide[first:first + group_width])
        head_sum = head_sum + rounded(term)
    mixed = (skip_wide + head_sum).astype(jnp.bfloat16)
    grad_wide = broaden_heads(grad_out)
    grad_w_out = jnp.einsum('tbe,tbc->ec', o_wide, grad_wide)
    d_out = jnp.einsum('tbc,ec->tbe', grad_wide, out_wide).astype(jnp.bfloat16)
    grads = lax.map(head_back, (query_matrix, key_matrix, value_matrix, split_heads(d_out), attention_output, log_total))
    dqkv = jnp.stack([join_heads(grads[:, 0]), join_heads(grads[:, 1]), join_heads(grads[:, 2])]).astype(jnp.bfloat16)
    dqkv_wide = broaden_heads(dqkv)
    grad_w_qkv = jnp.einsum('tbc,itbe->ice', normed_wide, dqkv_wide)
    d_normed = jnp.zeros((L, SEQS, C), jnp.float32)
    for head_group in range(N_HEAD):
        first = head_group * group_width
        term = jnp.einsum('itbe,ice->tbc', dqkv_wide[:, :, :, first:first + group_width], qkv_wide[:, :, first:first + group_width])
        d_normed = d_normed + rounded(term)
    unit_rows = skip_wide * inv_rms
    scaled = d_normed * norm_gain
    d_skip = grad_wide + inv_rms * (scaled - unit_rows * lax.optimization_barrier(jnp.mean(scaled * unit_rows, axis=-1, keepdims=True)))
    d_act = jnp.repeat(d_skip, 2, axis=0) * 0.5
    d_conv = gelu_pull(d_act)[0].astype(jnp.bfloat16)
    d_pad = broaden_heads(jnp.pad(d_conv, ((2, 2), (0, 0), (0, 0))))
    grad_input = jnp.zeros((LF, SEQS, C_IN), jnp.float32)
    for offset in range(KW):
        grad_input = grad_input + jnp.einsum('tbo,io->tbi', d_pad[4 - offset:4 - offset + LF], broaden_heads(conv_weight[offset]))
    return (mixed, grad_input.astype(jnp.bfloat16), grad_w_qkv, grad_w_out)
```

```python
import functools

import jax
import jax.numpy as jnp
from jax import lax
from jax.experimental import pallas as pl
from jax.experimental.pallas import tpu as pltpu
from jax.sharding import PartitionSpec as P

DH = 192
KW = 5
VMEM_LIMIT = 56 * 1024 * 1024
BF = jnp.bfloat16
F32 = jnp.float32


def params():
    return pltpu.CompilerParams(vmem_limit_bytes=VMEM_LIMIT)


def dot(a, b, contract):
    return lax.dot_general(a, b, (contract, ((), ())), preferred_element_type=F32)


NN = ((1,), (0,))
NT = ((1,), (1,))
TN = ((0,), (0,))


def shifted(ref, parity, shift, rows):
    seqs = ref.shape[1]
    wide = ref[parity].astype(F32)[:, shift : shift + rows, :]
    return wide.reshape(seqs * rows, ref.shape[3]).astype(BF)


def conv_kernel(x_ref, w_ref, gain_ref, skip_ref, slope_ref, normed_ref, acc):
    step = pl.program_id(0)
    rows = x_ref.shape[2] - 2
    half = acc.shape[0] // 2
    for tap in range(KW):

        @pl.when(step == tap)
        def _():
            for parity in range(2):
                place = parity + tap
                lhs = shifted(x_ref, place % 2, place // 2, rows)
                term = dot(lhs, w_ref[0], NN)
                part = pl.ds(parity * half, half)
                if tap == 0:
                    acc[part, :] = term
                else:
                    acc[part, :] = acc[part, :] + term

    @pl.when(step == KW - 1)
    def _():
        root = 0.7978845608028654
        total = None
        for parity in range(2):
            x = acc[parity * half : (parity + 1) * half, :]
            square = x * x
            t = jnp.tanh(root * (x + 0.044715 * (square * x)))
            left = 0.5 * (1.0 + t)
            act = x * left
            slope_ref[parity] = left + (0.5 * root) * x * (1.0 - t * t) * (
                1.0 + (3 * 0.044715) * square
            )
            total = act if total is None else total + act
        skip = (0.5 * total).astype(BF)
        skip_ref[...] = skip
        wide = skip.astype(F32)
        inv = lax.rsqrt(jnp.mean(wide * wide, axis=-1, keepdims=True) + 1e-06)
        normed_ref[...] = (wide * inv * gain_ref[...]).astype(BF)


def encoder(padded, conv_weight, norm_gain):
    _, seqs, rows2, c_in = padded.shape
    rows = rows2 - 2
    width = conv_weight.shape[2]
    flat = seqs * rows
    return pl.pallas_call(
        conv_kernel,
        grid=(KW,),
        in_specs=[
            pl.BlockSpec(padded.shape, lambda k: (0, 0, 0, 0)),
            pl.BlockSpec((1, c_in, width), lambda k: (k, 0, 0)),
            pl.BlockSpec((1, width), lambda k: (0, 0)),
        ],
        out_specs=[
            pl.BlockSpec((flat, width), lambda k: (0, 0)),
            pl.BlockSpec((2, flat, width), lambda k: (0, 0, 0)),
            pl.BlockSpec((flat, width), lambda k: (0, 0)),
        ],
        out_shape=[
            jax.ShapeDtypeStruct((flat, width), BF),
            jax.ShapeDtypeStruct((2, flat, width), F32),
            jax.ShapeDtypeStruct((flat, width), BF),
        ],
        scratch_shapes=[pltpu.VMEM((2 * flat, width), F32)],
        compiler_params=params(),
        name="encoder_forward",
    )(padded, conv_weight, norm_gain.reshape(1, width))


def d_conv_kernel(dn_ref, skip_ref, grad_ref, gain_ref, slope_ref, out_ref):
    wide = skip_ref[...].astype(F32)
    inv = lax.rsqrt(jnp.mean(wide * wide, axis=-1, keepdims=True) + 1e-06)
    unit = wide * inv
    scaled = dn_ref[...].astype(F32) * gain_ref[...]
    d_skip = grad_ref[...].astype(F32) + inv * (
        scaled - unit * jnp.mean(scaled * unit, axis=-1, keepdims=True)
    )
    d_act = 0.5 * d_skip
    for parity in range(2):
        out_ref[parity] = (slope_ref[parity] * d_act).astype(BF)


def d_conv_call(d_normed, skip, grad, norm_gain, slope):
    return pl.pallas_call(
        d_conv_kernel,
        out_shape=jax.ShapeDtypeStruct(slope.shape, BF),
        compiler_params=params(),
        name="conv_gradient",
    )(d_normed, skip, grad, norm_gain.reshape(1, -1), slope)


def conv_back_kernel(d_ref, w_ref, out_ref, acc):
    step = pl.program_id(0)
    rows = d_ref.shape[2] - 2
    half = acc.shape[0] // 2
    for tap in range(KW):

        @pl.when(step == tap)
        def _():
            for parity in range(2):
                place = parity + KW - 1 - tap
                lhs = shifted(d_ref, place % 2, place // 2, rows)
                term = dot(lhs, w_ref[0], NT)
                part = pl.ds(parity * half, half)
                if tap == 0:
                    acc[part, :] = term
                elif tap < KW - 1:
                    acc[part, :] = acc[part, :] + term
                else:
                    out_ref[part, :] = (acc[part, :] + term).astype(BF)


def conv_back(d_pad, conv_weight):
    _, seqs, rows2, width = d_pad.shape
    c_in = conv_weight.shape[1]
    flat = 2 * seqs * (rows2 - 2)
    return pl.pallas_call(
        conv_back_kernel,
        grid=(KW,),
        in_specs=[
            pl.BlockSpec(d_pad.shape, lambda k: (0, 0, 0, 0)),
            pl.BlockSpec((1, c_in, width), lambda k: (k, 0, 0)),
        ],
        out_specs=pl.BlockSpec((flat, c_in), lambda k: (0, 0)),
        out_shape=jax.ShapeDtypeStruct((flat, c_in), BF),
        scratch_shapes=[pltpu.VMEM((flat, c_in), F32)],
        compiler_params=params(),
        name="encoder_backward",
    )(d_pad, conv_weight)


def project_kernel(x_ref, g_ref, w_ref, wo_ref, out_ref):
    groups, seqs, rows, width = x_ref.shape
    flat = groups * seqs * rows
    x = x_ref[...].reshape(flat, width)
    g = g_ref[...].reshape(flat, width)
    qkv = dot(x, w_ref[0], NN)
    d_o = dot(g, wo_ref[0], NT)
    both = jnp.concatenate([qkv, d_o], axis=1).astype(BF)
    for z in range(groups):
        for b in range(seqs):
            first = (z * seqs + b) * rows
            out_ref[b, 0, z * rows : (z + 1) * rows, :] = both[first : first + rows]


def project(x, g, w_pack, w_out):
    groups, seqs, rows, width = x.shape
    heads, _, packed = w_pack.shape
    full = packed + w_out.shape[1]
    return pl.pallas_call(
        project_kernel,
        grid=(heads,),
        in_specs=[
            pl.BlockSpec(x.shape, lambda h: (0, 0, 0, 0)),
            pl.BlockSpec(g.shape, lambda h: (0, 0, 0, 0)),
            pl.BlockSpec((1, width, packed), lambda h: (h, 0, 0)),
            pl.BlockSpec((1, w_out.shape[1], width), lambda h: (h, 0, 0)),
        ],
        out_specs=pl.BlockSpec((seqs, 1, groups * rows, full), lambda h: (0, h, 0, 0)),
        out_shape=jax.ShapeDtypeStruct((seqs, heads, groups * rows, full), BF),
        compiler_params=params(),
        name="projections",
    )(x, g, w_pack, w_out)


def attention_kernel(in_ref, out_ref, dk_acc, dv_acc, *, block):
    scale = DH ** (-0.5)
    length = in_ref.shape[0]
    k = in_ref[:, DH : 2 * DH]
    v = in_ref[:, 2 * DH : 3 * DH]
    for start in range(0, length, block):
        rows = pl.ds(start, block)
        q = in_ref[rows, 0:DH]
        d_o = in_ref[rows, 3 * DH : 4 * DH]
        s = dot(q, k, NT) * scale
        e = jnp.exp(s - jnp.max(s, axis=-1, keepdims=True))
        p = e * (1.0 / jnp.sum(e, axis=-1, keepdims=True))
        p_b = p.astype(BF)
        o = dot(p_b, v, NN)
        delta = jnp.sum(d_o.astype(F32) * o, axis=-1, keepdims=True)
        d_p = dot(d_o, v, NT)
        ds = (p * (d_p - delta)).astype(BF)
        dq = scale * dot(ds, k, NN)
        dk = dot(ds, q, TN)
        dv = dot(p_b, d_o, TN)
        if start == 0:
            dk_acc[...] = dk
            dv_acc[...] = dv
        else:
            dk_acc[...] += dk
            dv_acc[...] += dv
        out_ref[rows, 0:DH] = o.astype(BF)
        out_ref[rows, DH : 2 * DH] = dq.astype(BF)
    out_ref[:, 2 * DH : 3 * DH] = (scale * dk_acc[...]).astype(BF)
    out_ref[:, 3 * DH : 4 * DH] = dv_acc[...].astype(BF)


def attention(packed):
    length = packed.shape[0]
    return pl.pallas_call(
        functools.partial(attention_kernel, block=min(256, length)),
        out_shape=jax.ShapeDtypeStruct(packed.shape, BF),
        scratch_shapes=[pltpu.VMEM((length, DH), F32), pltpu.VMEM((length, DH), F32)],
        compiler_params=params(),
        name="attention",
    )(packed)


def ordered(ref, first, last, groups):
    seqs, _, rows, _ = ref.shape
    rows //= groups
    pieces = [
        ref[b, 0, z * rows : (z + 1) * rows, first:last]
        for z in range(groups)
        for b in range(seqs)
    ]
    return jnp.concatenate(pieces, axis=0)


def term_kernel(in_ref, w_ref, out_ref, acc, *, first, last, contract):
    groups = out_ref.shape[0]
    step = pl.program_id(0)
    term = dot(ordered(in_ref, first, last, groups), w_ref[0], contract)

    @pl.when(step == 0)
    def _():
        acc[...] = term

    @pl.when(step > 0)
    def _():
        acc[...] += term

    @pl.when(step == pl.num_programs(0) - 1)
    def _():
        out_ref[...] = acc[...].astype(BF).reshape(out_ref.shape)


def head_sum_term(units, weight, groups, first, last, contract, width, name):
    seqs, heads, rows, full = units.shape
    shape = (groups, seqs, rows // groups, width)
    return pl.pallas_call(
        functools.partial(term_kernel, first=first, last=last, contract=contract),
        grid=(heads,),
        in_specs=[
            pl.BlockSpec((seqs, 1, rows, full), lambda h: (0, h, 0, 0)),
            pl.BlockSpec((1,) + weight.shape[1:], lambda h: (h, 0, 0)),
        ],
        out_specs=pl.BlockSpec(shape, lambda h: (0, 0, 0, 0)),
        out_shape=jax.ShapeDtypeStruct(shape, BF),
        scratch_shapes=[pltpu.VMEM((seqs * rows, width), F32)],
        compiler_params=params(),
        name=name,
    )(units, weight)


def weight_kernel(in_ref, x_ref, g_ref, qkv_ref, out_ref):
    groups, seqs, rows, width = x_ref.shape
    flat = groups * seqs * rows
    x = x_ref[...].reshape(flat, width)
    g = g_ref[...].reshape(flat, width)
    both = ordered(in_ref, 0, 4 * DH, groups)
    qkv_ref[0] = dot(x, both[:, DH:], TN).astype(BF)
    out_ref[0] = dot(both[:, :DH], g, TN).astype(BF)


def weight_gradients(units, x, g):
    seqs, heads, rows, full = units.shape
    width = x.shape[-1]
    return pl.pallas_call(
        weight_kernel,
        grid=(heads,),
        in_specs=[
            pl.BlockSpec((seqs, 1, rows, full), lambda h: (0, h, 0, 0)),
            pl.BlockSpec(x.shape, lambda h: (0, 0, 0, 0)),
            pl.BlockSpec(g.shape, lambda h: (0, 0, 0, 0)),
        ],
        out_specs=[
            pl.BlockSpec((1, width, 3 * DH), lambda h: (h, 0, 0)),
            pl.BlockSpec((1, DH, width), lambda h: (h, 0, 0)),
        ],
        out_shape=[
            jax.ShapeDtypeStruct((heads, width, 3 * DH), BF),
            jax.ShapeDtypeStruct((heads, DH, width), BF),
        ],
        compiler_params=params(),
        name="weight_gradients",
    )(units, x, g)


def neighbour_edges(pairs):
    axes = ("seq", "head")
    count = lax.axis_size(axes)
    forward = [(i, i + 1) for i in range(count - 1)]
    backward = [(target, source) for source, target in forward]
    low = lax.ppermute(pairs[:, :, -1:, :], axes, forward)
    high = lax.ppermute(pairs[:, :, :1, :], axes, backward)
    return jnp.concatenate([low, pairs, high], axis=2)


def unit_body(enc_in, conv_weight, norm_gain, w_qkv, w_out, grad_out):
    rows = enc_in.shape[0] // 2
    seqs = enc_in.shape[1]
    width = conv_weight.shape[2]
    local = w_qkv.shape[2]
    heads = local // DH
    groups = lax.axis_size("head")
    blocks = lax.axis_size("seq")

    grad = jnp.transpose(grad_out, (1, 0, 2))
    grad_rows = lax.all_gather(grad, "head", axis=0, tiled=False)

    pairs = jnp.transpose(enc_in.reshape(rows, 2, seqs, enc_in.shape[2]), (1, 2, 0, 3))
    skip, slope, normed = encoder(neighbour_edges(pairs), conv_weight, norm_gain)
    normed_rows = lax.all_gather(normed.reshape(seqs, rows, width), "head", axis=0, tiled=False)

    w_pack = jnp.transpose(w_qkv.reshape(3, width, heads, DH), (2, 1, 0, 3))
    w_pack = w_pack.reshape(heads, width, 3 * DH)
    w_rows = w_out.reshape(heads, DH, width)
    mine = project(normed_rows, grad_rows, w_pack, w_rows)
    tower = groups * rows
    sent = mine.reshape(blocks, tower, 4 * DH)
    unit = lax.all_to_all(sent, "seq", split_axis=0, concat_axis=0, tiled=True)
    result = attention(unit.reshape(blocks * tower, 4 * DH))
    back = lax.all_to_all(
        result.reshape(blocks, tower, 4 * DH), "seq", split_axis=0, concat_axis=0, tiled=True
    )
    units = back.reshape(seqs, heads, tower, 4 * DH)

    d_term = head_sum_term(units, w_pack, groups, DH, 4 * DH, NT, width, "d_term")
    d_normed = lax.psum_scatter(d_term, "head", scatter_dimension=0, tiled=False)
    head_term = head_sum_term(units, w_rows, groups, 0, DH, NN, width, "head_term")
    head_sum = lax.psum_scatter(head_term, "head", scatter_dimension=0, tiled=False)
    part_qkv, part_out = weight_gradients(units, normed_rows, grad_rows)
    sum_qkv = lax.psum(part_qkv, "seq")
    sum_out = lax.psum(part_out, "seq")

    flat = seqs * rows
    d_conv = d_conv_call(
        d_normed.reshape(flat, width), skip, grad.reshape(flat, width), norm_gain, slope
    )
    d_pad = neighbour_edges(d_conv.reshape(2, seqs, rows, width))
    grad_input = conv_back(d_pad, conv_weight)
    grad_input = jnp.transpose(grad_input.reshape(2, seqs, rows, -1), (2, 0, 1, 3))

    mixed = skip.reshape(seqs, rows, width).astype(F32) + head_sum.astype(F32)
    grad_qkv = jnp.transpose(sum_qkv.reshape(heads, width, 3, DH), (2, 1, 0, 3))
    return (
        jnp.transpose(mixed.astype(BF), (1, 0, 2)),
        grad_input.reshape(enc_in.shape),
        grad_qkv.reshape(3, width, local).astype(F32),
        sum_out.reshape(local, width).astype(F32),
    )


def padded_2(block, sides, width):
    for axis, dim in sides:
        count = lax.axis_size(axis)
        forward = [(i, i + 1) for i in range(count - 1)]
        backward = [(target, source) for source, target in forward]
        low = lax.ppermute(
            lax.slice_in_dim(block, block.shape[dim] - width, None, axis=dim), axis, forward
        )
        high = lax.ppermute(lax.slice_in_dim(block, 0, width, axis=dim), axis, backward)
        block = jnp.concatenate([low, block, high], axis=dim)
    return block


def gathered_body(enc_in, conv_weight, norm_gain, w_qkv, w_out, grad_out):
    fine_rows = enc_in.shape[0]
    slab_rows = fine_rows // 2
    seq_count = enc_in.shape[1]
    out_width = conv_weight.shape[2]
    local_width = w_qkv.shape[2]
    local_heads = local_width // DH
    logit_scale = DH ** (-0.5)
    padded = padded_2(enc_in, ((("seq", "head"), 0),), 2)
    convolved = jnp.zeros((fine_rows, seq_count, out_width), jnp.float32)
    for offset in range(KW):
        convolved = convolved + jnp.einsum(
            "tbi,io->tbo",
            padded[offset : offset + fine_rows],
            conv_weight[offset],
            preferred_element_type=jnp.float32,
        )
    activated, gelu_pull = jax.vjp(jax.nn.gelu, convolved)
    skip = jnp.mean(activated.reshape(slab_rows, 2, seq_count, out_width), axis=1).astype(
        jnp.bfloat16
    )
    skip_wide = skip.astype(jnp.float32)
    inv_rms = lax.rsqrt(jnp.mean(skip_wide * skip_wide, axis=-1, keepdims=True) + 1e-06)
    normed = (skip_wide * inv_rms * norm_gain).astype(jnp.bfloat16)
    normed_rows = lax.all_gather(normed, "head", axis=0, tiled=True)
    grad_rows = lax.all_gather(grad_out, "head", axis=0, tiled=True)
    tower_rows = normed_rows.shape[0]
    qkv = jnp.einsum(
        "tbc,ice->itbe", normed_rows, w_qkv, preferred_element_type=jnp.float32
    ).astype(jnp.bfloat16)
    qkv = qkv.reshape(3, tower_rows, seq_count, local_heads, DH)
    query_matrix, key_matrix, value_matrix = (qkv[0], qkv[1], qkv[2])
    key_all, value_all = (
        lax.all_gather(key_matrix, "seq", axis=0, tiled=True),
        lax.all_gather(value_matrix, "seq", axis=0, tiled=True),
    )
    attention_logits = (
        jnp.einsum("qbhd,kbhd->bhqk", query_matrix, key_all, preferred_element_type=jnp.float32)
        * logit_scale
    )
    row_peak = jnp.max(attention_logits, axis=-1, keepdims=True)
    exponent = jnp.exp(attention_logits - row_peak)
    row_total = jnp.sum(exponent, axis=-1, keepdims=True)
    soft_weights = exponent / row_total
    narrow_probabilities = soft_weights.astype(jnp.bfloat16)
    attention_output = jnp.einsum(
        "bhqk,kbhd->qbhd", narrow_probabilities, value_all, preferred_element_type=jnp.float32
    )
    o_narrow = attention_output.reshape(tower_rows, seq_count, local_width).astype(jnp.bfloat16)
    piece = o_narrow
    head_sum = lax.psum_scatter(
        jnp.einsum("tbe,ec->tbc", piece, w_out, preferred_element_type=jnp.float32).astype(
            jnp.bfloat16
        ),
        "head",
        scatter_dimension=0,
        tiled=True,
    ).astype(jnp.float32)
    mixed = (skip_wide + head_sum).astype(jnp.bfloat16)
    part_w_out = jnp.einsum("tbe,tbc->ec", o_narrow, grad_rows, preferred_element_type=jnp.float32)
    d_out = jnp.einsum("tbc,ec->tbe", grad_rows, w_out, preferred_element_type=jnp.float32).astype(
        jnp.bfloat16
    )
    d_out = d_out.reshape(tower_rows, seq_count, local_heads, DH)
    delta = jnp.sum(d_out.astype(jnp.float32) * attention_output, axis=-1)
    probability_gradient = jnp.einsum(
        "qbhd,kbhd->bhqk", d_out, value_all, preferred_element_type=jnp.float32
    )
    d_scores = soft_weights * (probability_gradient - jnp.transpose(delta, (1, 2, 0))[..., None])
    narrow_gradient = d_scores.astype(jnp.bfloat16)
    query_gradient = logit_scale * jnp.einsum(
        "bhqk,kbhd->qbhd", narrow_gradient, key_all, preferred_element_type=jnp.float32
    )
    key_terms = logit_scale * jnp.einsum(
        "bhqk,qbhd->kbhd", narrow_gradient, query_matrix, preferred_element_type=jnp.float32
    )
    value_terms = jnp.einsum(
        "bhqk,qbhd->kbhd", narrow_probabilities, d_out, preferred_element_type=jnp.float32
    )
    d_keys, d_values = (
        lax.psum_scatter(
            key_terms.astype(jnp.bfloat16), "seq", scatter_dimension=0, tiled=True
        ).astype(jnp.float32),
        lax.psum_scatter(
            value_terms.astype(jnp.bfloat16), "seq", scatter_dimension=0, tiled=True
        ).astype(jnp.float32),
    )
    dqkv = (
        jnp.stack([query_gradient, d_keys, d_values])
        .reshape(3, tower_rows, seq_count, local_width)
        .astype(jnp.bfloat16)
    )
    part_w_qkv = jnp.einsum("tbc,itbe->ice", normed_rows, dqkv, preferred_element_type=jnp.float32)
    piece = dqkv
    d_normed = lax.psum_scatter(
        jnp.einsum("itbe,ice->tbc", piece, w_qkv, preferred_element_type=jnp.float32).astype(
            jnp.bfloat16
        ),
        "head",
        scatter_dimension=0,
        tiled=True,
    ).astype(jnp.float32)
    unit_rows = skip_wide * inv_rms
    scaled = d_normed * norm_gain
    d_skip = grad_out.astype(jnp.float32) + inv_rms * (
        scaled - unit_rows * jnp.mean(scaled * unit_rows, axis=-1, keepdims=True)
    )
    d_act = jnp.repeat(d_skip, 2, axis=0) * 0.5
    d_conv = gelu_pull(d_act)[0].astype(jnp.bfloat16)
    d_pad = padded_2(d_conv, ((("seq", "head"), 0),), 2)
    grad_input = jnp.zeros((fine_rows, seq_count, enc_in.shape[2]), jnp.float32)
    for offset in range(KW):
        grad_input = grad_input + jnp.einsum(
            "tbo,io->tbi",
            d_pad[4 - offset : 4 - offset + fine_rows],
            conv_weight[offset],
            preferred_element_type=jnp.float32,
        )
    grad_w_qkv, grad_w_out = (
        lax.psum(part_w_qkv.astype(jnp.bfloat16), "seq").astype(jnp.float32),
        lax.psum(part_w_out.astype(jnp.bfloat16), "seq").astype(jnp.float32),
    )
    return (mixed, grad_input.astype(jnp.bfloat16), grad_w_qkv, grad_w_out)


def body(enc_in, conv_weight, norm_gain, w_qkv, w_out, grad_out):
    units = enc_in.shape[1] * (w_qkv.shape[2] // DH)
    chosen = unit_body if units == lax.axis_size("seq") else gathered_body
    return chosen(enc_in, conv_weight, norm_gain, w_qkv, w_out, grad_out)


def solution(mesh):
    return jax.shard_map(
        body,
        mesh=mesh,
        in_specs=(
            P(("seq", "head"), None, None),
            P(),
            P(),
            P(None, None, "head"),
            P("head", None),
            P(("seq", "head"), None, None),
        ),
        out_specs=(
            P(("seq", "head"), None, None),
            P(("seq", "head"), None, None),
            P(None, None, "head"),
            P("head", None),
        ),
        check_vma=False,
    )
```

```python
import functools

import jax
import jax.numpy as jnp
from jax import lax
from jax.experimental import pallas as pl
from jax.experimental.pallas import tpu as pltpu
from jax.sharding import PartitionSpec as P

DH = 192
KW = 5
VMEM_LIMIT = 56 * 1024 * 1024
BF = jnp.bfloat16
F32 = jnp.float32


def params():
    return pltpu.CompilerParams(vmem_limit_bytes=VMEM_LIMIT)


def dot(a, b, contract):
    return lax.dot_general(a, b, (contract, ((), ())), preferred_element_type=F32)


NN = ((1,), (0,))
NT = ((1,), (1,))
TN = ((0,), (0,))


def whole(shape):
    return pl.BlockSpec(shape, lambda *_: (0,) * len(shape))


SCALARS = pl.BlockSpec(memory_space=pltpu.SMEM)


def wrapped(value, size):
    return jnp.where(value < 0, value + size, jnp.where(value >= size, value - size, value))


def shifted(ref, start, rows):
    seqs = ref.shape[1]
    parts = []
    for parity in range(2):
        place = parity + start
        wide = ref[place % 2].astype(F32)[:, place // 2 : place // 2 + rows, :]
        parts.append(wide.reshape(seqs * rows, ref.shape[3]))
    return jnp.concatenate(parts, axis=0).astype(BF)


def conv_kernel(at_ref, x_ref, w_ref, gain_ref, skip_ref, slope_ref, normed_ref, acc):
    step = pl.program_id(0)
    rows = x_ref.shape[2] - 2
    seqs = x_ref.shape[1]
    half = acc.shape[0] // 2
    for tap in range(KW):

        @pl.when(step == tap)
        def _():
            term = dot(shifted(x_ref, tap, rows), w_ref[0], NN)
            if tap == 0:
                acc[...] = term
            else:
                acc[...] += term

    @pl.when(step == KW - 1)
    def _():
        root = 0.7978845608028654
        total = None
        for parity in range(2):
            x = acc[parity * half : (parity + 1) * half, :]
            square = x * x
            t = jnp.tanh(root * (x + 0.044715 * (square * x)))
            left = 0.5 * (1.0 + t)
            act = x * left
            slope = left + (0.5 * root) * x * (1.0 - t * t) * (1.0 + (3 * 0.044715) * square)
            slope_ref[parity] = slope.reshape(slope_ref.shape[1:])
            total = act if total is None else total + act
        skip = (0.5 * total).astype(BF)
        skip_ref[...] = skip.reshape(skip_ref.shape)
        wide = skip.astype(F32)
        inv = lax.rsqrt(jnp.mean(wide * wide, axis=-1, keepdims=True) + 1e-06)
        normed = (wide * inv * gain_ref[...]).astype(BF)
        for b in range(seqs):
            normed_ref[wrapped(b - at_ref[0], seqs)] = normed[b * rows : (b + 1) * rows]


def encoder(at, padded, conv_weight, norm_gain):
    _, seqs, rows2, c_in = padded.shape
    rows = rows2 - 2
    width = conv_weight.shape[2]
    shape = (seqs, rows, width)
    return pl.pallas_call(
        conv_kernel,
        grid=(KW,),
        in_specs=[
            SCALARS,
            whole(padded.shape),
            pl.BlockSpec((1, c_in, width), lambda k: (k, 0, 0)),
            whole((1, width)),
        ],
        out_specs=[whole(shape), whole((2,) + shape), whole(shape)],
        out_shape=[
            jax.ShapeDtypeStruct(shape, BF),
            jax.ShapeDtypeStruct((2,) + shape, F32),
            jax.ShapeDtypeStruct(shape, BF),
        ],
        scratch_shapes=[pltpu.VMEM((2 * seqs * rows, width), F32)],
        compiler_params=params(),
        name="encoder_forward",
    )(at, padded, conv_weight, norm_gain.reshape(1, width))


def d_conv_body(seqs, at_ref, *refs):
    dn_refs = refs[:seqs]
    skip_ref, grad_ref, gain_ref, slope_ref, out_ref = refs[seqs:]
    for slot in range(seqs):
        b = wrapped(at_ref[0] + slot, seqs)
        wide = skip_ref[b].astype(F32)
        inv = lax.rsqrt(jnp.mean(wide * wide, axis=-1, keepdims=True) + 1e-06)
        unit = wide * inv
        scaled = dn_refs[slot][...].astype(F32) * gain_ref[...]
        d_skip = grad_ref[b].astype(F32) + inv * (
            scaled - unit * jnp.mean(scaled * unit, axis=-1, keepdims=True)
        )
        d_act = 0.5 * d_skip
        for parity in range(2):
            out_ref[parity, b] = (slope_ref[parity, b] * d_act).astype(BF)


def conv_gradient(at, d_normed, skip, grad, norm_gain, slope):
    seqs = len(d_normed)
    vmem = pl.BlockSpec(memory_space=pltpu.VMEM)
    return pl.pallas_call(
        functools.partial(d_conv_body, seqs),
        in_specs=[SCALARS] + [vmem] * (seqs + 4),
        out_specs=vmem,
        out_shape=jax.ShapeDtypeStruct(slope.shape, BF),
        compiler_params=params(),
        name="conv_gradient",
    )(at, *d_normed, skip, grad, norm_gain.reshape(1, -1), slope)


def mixed_body(seqs, at_ref, *refs):
    skip_ref, out_ref = refs[seqs:]
    for slot in range(seqs):
        b = wrapped(at_ref[0] + slot, seqs)
        out_ref[b] = (skip_ref[b].astype(F32) + refs[slot][...].astype(F32)).astype(BF)


def mixed_call(at, terms, skip):
    seqs = len(terms)
    vmem = pl.BlockSpec(memory_space=pltpu.VMEM)
    return pl.pallas_call(
        functools.partial(mixed_body, seqs),
        in_specs=[SCALARS] + [vmem] * (seqs + 1),
        out_specs=vmem,
        out_shape=jax.ShapeDtypeStruct(skip.shape, BF),
        compiler_params=params(),
        name="mixed_sum",
    )(at, *terms, skip)


def conv_back_kernel(d_ref, w_ref, out_ref, acc):
    step = pl.program_id(0)
    rows = d_ref.shape[2] - 2
    for tap in range(KW):

        @pl.when(step == tap)
        def _():
            term = dot(shifted(d_ref, KW - 1 - tap, rows), w_ref[0], NT)
            if tap == 0:
                acc[...] = term
            elif tap < KW - 1:
                acc[...] += term
            else:
                out_ref[...] = (acc[...] + term).astype(BF)


def conv_back(d_pad, conv_weight):
    _, seqs, rows2, width = d_pad.shape
    c_in = conv_weight.shape[1]
    flat = 2 * seqs * (rows2 - 2)
    return pl.pallas_call(
        conv_back_kernel,
        grid=(KW,),
        in_specs=[
            whole(d_pad.shape),
            pl.BlockSpec((1, c_in, width), lambda k: (k, 0, 0)),
        ],
        out_specs=whole((flat, c_in)),
        out_shape=jax.ShapeDtypeStruct((flat, c_in), BF),
        scratch_shapes=[pltpu.VMEM((flat, c_in), F32)],
        compiler_params=params(),
        name="encoder_backward",
    )(d_pad, conv_weight)


def product_kernel(head_ref, x_ref, w_ref, out_ref, *, contract):
    del head_ref
    out_ref[...] = dot(x_ref[...], w_ref[0], contract).astype(BF)


def head_product(head, x, weight, contract, name):
    columns = weight.shape[2] if contract == NN else weight.shape[1]
    rows, width = x.shape
    return pl.pallas_call(
        functools.partial(product_kernel, contract=contract),
        grid_spec=pltpu.PrefetchScalarGridSpec(
            num_scalar_prefetch=1,
            grid=(1,),
            in_specs=[
                pl.BlockSpec((rows, width), lambda i, head: (0, 0)),
                pl.BlockSpec((1,) + weight.shape[1:], lambda i, head: (head[0], 0, 0)),
            ],
            out_specs=pl.BlockSpec((rows, columns), lambda i, head: (0, 0)),
        ),
        out_shape=jax.ShapeDtypeStruct((rows, columns), BF),
        compiler_params=params(),
        name=name,
    )(head, x, weight)


def attention_kernel(qa_ref, qb_ref, da_ref, db_ref, oa_ref, ob_ref, k_all, v_all, dk_acc, dv_acc, *, block):
    scale = DH ** (-0.5)
    half = qa_ref.shape[0]
    for place, ref in enumerate((qa_ref, qb_ref)):
        rows = pl.ds(place * half, half)
        k_all[rows, :] = ref[:, DH : 2 * DH]
        v_all[rows, :] = ref[:, 2 * DH : 3 * DH]
    k = k_all[...]
    v = v_all[...]
    for place, (q_ref, d_ref, out_ref) in enumerate(
        ((qa_ref, da_ref, oa_ref), (qb_ref, db_ref, ob_ref))
    ):
        for start in range(0, half, block):
            rows = pl.ds(start, block)
            q = q_ref[rows, 0:DH]
            d_o = d_ref[rows, :]
            s = dot(q, k, NT) * scale
            e = jnp.exp(s - jnp.max(s, axis=-1, keepdims=True))
            p = e * (1.0 / jnp.sum(e, axis=-1, keepdims=True))
            p_b = p.astype(BF)
            o = dot(p_b, v, NN)
            delta = jnp.sum(d_o.astype(F32) * o, axis=-1, keepdims=True)
            d_p = dot(d_o, v, NT)
            ds = (p * (d_p - delta)).astype(BF)
            dq = scale * dot(ds, k, NN)
            dk = dot(ds, q, TN)
            dv = dot(p_b, d_o, TN)
            if place == 0 and start == 0:
                dk_acc[...] = dk
                dv_acc[...] = dv
            else:
                dk_acc[...] += dk
                dv_acc[...] += dv
            out_ref[rows, 0:DH] = o.astype(BF)
            out_ref[rows, DH : 2 * DH] = dq.astype(BF)
    for place, out_ref in enumerate((oa_ref, ob_ref)):
        rows = pl.ds(place * half, half)
        out_ref[:, 2 * DH : 3 * DH] = (scale * dk_acc[rows, :]).astype(BF)
        out_ref[:, 3 * DH : 4 * DH] = dv_acc[rows, :].astype(BF)


def attention(qkv_a, qkv_b, d_a, d_b):
    half = qkv_a.shape[0]
    shape = jax.ShapeDtypeStruct((half, 4 * DH), BF)
    return pl.pallas_call(
        functools.partial(attention_kernel, block=min(256, half)),
        out_shape=[shape, shape],
        scratch_shapes=[
            pltpu.VMEM((2 * half, DH), BF),
            pltpu.VMEM((2 * half, DH), BF),
            pltpu.VMEM((2 * half, DH), F32),
            pltpu.VMEM((2 * half, DH), F32),
        ],
        compiler_params=params(),
        name="attention",
    )(qkv_a, qkv_b, d_a, d_b)


def term_kernel(head_ref, a_ref, b_ref, w_ref, out_ref, acc, *, first, last, contract):
    step = pl.program_id(0)
    groups = out_ref.shape[0]

    @pl.when(step == 0)
    def _():
        acc[...] = dot(a_ref[:, first:last], w_ref[0], contract)

    @pl.when(step == 1)
    def _():
        total = acc[...] + dot(b_ref[:, first:last], w_ref[0], contract)
        total = total.astype(BF).reshape(out_ref.shape)
        for z in range(groups):
            out_ref[wrapped(z - head_ref[1], groups)] = total[z]


def pair_term(place, mine, got, weight, shape, first, last, contract, name):
    half, full = mine.shape
    return pl.pallas_call(
        functools.partial(term_kernel, first=first, last=last, contract=contract),
        grid_spec=pltpu.PrefetchScalarGridSpec(
            num_scalar_prefetch=1,
            grid=(2,),
            in_specs=[
                pl.BlockSpec((half, full), lambda i, at: (0, 0)),
                pl.BlockSpec((half, full), lambda i, at: (0, 0)),
                pl.BlockSpec(
                    (1,) + weight.shape[1:],
                    lambda i, at: (jnp.where(i == 0, at[0], 1 - at[0]), 0, 0),
                ),
            ],
            out_specs=pl.BlockSpec(shape, lambda i, at: (0, 0, 0, 0)),
            scratch_shapes=[pltpu.VMEM((half, shape[-1]), F32)],
        ),
        out_shape=jax.ShapeDtypeStruct(shape, BF),
        compiler_params=params(),
        name=name,
    )(place, mine, got, weight)


def place_kernel(at_ref, *refs):
    step = pl.program_id(0)
    del at_ref
    for slot, ref in enumerate(refs[:-1]):

        @pl.when(step == slot)
        def _():
            refs[-1][...] = ref[...]


def in_order(at, slots, name):
    count = len(slots)
    rows, width = slots[0].shape
    return pl.pallas_call(
        place_kernel,
        grid_spec=pltpu.PrefetchScalarGridSpec(
            num_scalar_prefetch=1,
            grid=(count,),
            in_specs=[pl.BlockSpec((rows, width), lambda q, at: (0, 0))] * count,
            out_specs=pl.BlockSpec(
                (rows, width), lambda q, at: (lax.rem(at[0] - q + count, count), 0)
            ),
        ),
        out_shape=jax.ShapeDtypeStruct((count * rows, width), slots[0].dtype),
        compiler_params=params(),
        name=name,
    )(at, *slots)


def sum_kernel(*refs):
    total = refs[0][...].astype(F32)
    for ref in refs[1:-1]:
        total = total + ref[...].astype(F32)
    refs[-1][...] = total.astype(BF)


def summed(parts, name):
    return pl.pallas_call(
        sum_kernel,
        out_shape=jax.ShapeDtypeStruct(parts[0].shape, BF),
        compiler_params=params(),
        name=name,
    )(*parts)


def weight_kernel(at_ref, xa_ref, xb_ref, ga_ref, gb_ref, ra_ref, rb_ref, out_ref):
    del at_ref
    qkv = dot(xa_ref[...], ra_ref[:, DH:], TN) + dot(xb_ref[...], rb_ref[:, DH:], TN)
    out = dot(ga_ref[...], ra_ref[:, :DH], TN) + dot(gb_ref[...], rb_ref[:, :DH], TN)
    out_ref[0, :, : 3 * DH] = qkv.astype(BF)
    out_ref[0, :, 3 * DH :] = out.astype(BF)


def weight_gradients(at, xa, xb, ga, gb, ra, rb, seqs):
    half, width = xa.shape
    chunk = width // seqs
    full = ra.shape[1]
    column = pl.BlockSpec((half, chunk), lambda r, at: (0, lax.rem(r + at[0], seqs)))
    rest = pl.BlockSpec((half, full), lambda r, at: (0, 0))
    return pl.pallas_call(
        weight_kernel,
        grid_spec=pltpu.PrefetchScalarGridSpec(
            num_scalar_prefetch=1,
            grid=(seqs,),
            in_specs=[column] * 4 + [rest] * 2,
            out_specs=pl.BlockSpec((1, chunk, full), lambda r, at: (r, 0, 0)),
        ),
        out_shape=jax.ShapeDtypeStruct((seqs, chunk, full), BF),
        compiler_params=params(),
        name="weight_gradients",
    )(at, xa, xb, ga, gb, ra, rb)


def unpack_kernel(at_ref, *refs):
    seqs = (len(refs) - 2) // 2
    qkv_ref, out_ref = refs[-2:]
    step = pl.program_id(0)
    first_head = at_ref[1] == 0
    for slot in range(seqs):

        @pl.when(step == slot)
        def _():
            mine = refs[slot][...].astype(F32)
            other = refs[seqs + slot][...].astype(F32)
            low = jnp.where(first_head, mine, other)
            high = jnp.where(first_head, other, mine)
            for i in range(3):
                columns = slice(i * DH, (i + 1) * DH)
                qkv_ref[i] = jnp.concatenate([low[:, columns], high[:, columns]], axis=1)
            out_ref[:DH, :] = low[:, 3 * DH :].T
            out_ref[DH:, :] = high[:, 3 * DH :].T


def unpack_weights(at, mine, other):
    seqs = len(mine)
    chunk, full = mine[0].shape
    width = chunk * seqs
    local = 2 * DH

    def place(r, at):
        return lax.rem(at[0] - r + seqs, seqs)

    return pl.pallas_call(
        unpack_kernel,
        grid_spec=pltpu.PrefetchScalarGridSpec(
            num_scalar_prefetch=1,
            grid=(seqs,),
            in_specs=[pl.BlockSpec((chunk, full), lambda r, at: (0, 0))] * (2 * seqs),
            out_specs=[
                pl.BlockSpec((3, chunk, local), lambda r, at: (0, place(r, at), 0)),
                pl.BlockSpec((local, chunk), lambda r, at: (0, place(r, at))),
            ],
        ),
        out_shape=[
            jax.ShapeDtypeStruct((3, width, local), F32),
            jax.ShapeDtypeStruct((local, width), F32),
        ],
        compiler_params=params(),
        name="weight_outputs",
    )(at, *mine, *other)


def neighbour_edges(pairs):
    axes = ("seq", "head")
    count = lax.axis_size(axes)
    forward = [(i, i + 1) for i in range(count - 1)]
    backward = [(target, source) for source, target in forward]
    low = lax.ppermute(pairs[:, :, -1:, :], axes, forward)
    high = lax.ppermute(pairs[:, :, :1, :], axes, backward)
    return jnp.concatenate([low, pairs, high], axis=2)


def send_chip(x, step, heads):
    count = lax.axis_size("seq")
    return lax.ppermute(x, "seq", [(s, (s + step * heads) % count) for s in range(count)])


def send_z(x, step):
    count = lax.axis_size("head")
    return lax.ppermute(x, "head", [(z, (z + step) % count) for z in range(count)])


def swap_heads(x):
    count = lax.axis_size("seq")
    return lax.ppermute(x, "seq", [(s, s + 1 - 2 * (s % 2)) for s in range(count)])


def unit_body(enc_in, conv_weight, norm_gain, w_qkv, w_out, grad_out):
    rows = enc_in.shape[0] // 2
    seqs = enc_in.shape[1]
    width = conv_weight.shape[2]
    local = w_qkv.shape[2]
    heads = local // DH
    groups = lax.axis_size("head")
    half = groups * seqs * rows
    place = lax.axis_index("seq")
    own_seq = (place // heads).astype(jnp.int32)
    own_head = (place % heads).astype(jnp.int32)
    own_z = lax.axis_index("head").astype(jnp.int32)
    zero = jnp.zeros((), jnp.int32)
    at = jnp.stack([own_seq, own_head])
    head_mine = own_head.reshape(1)
    head_other = (1 - own_head).reshape(1)

    def to_chips(slots):
        return [slots[r] if r == 0 else send_chip(slots[r], r, heads) for r in range(seqs)]

    def from_chips(slots):
        return [slots[r] if r == 0 else send_chip(slots[r], -r, heads) for r in range(seqs)]

    grad = jnp.transpose(grad_out, (1, 0, 2))
    grad_slots = [
        lax.dynamic_index_in_dim(grad, (own_seq + r) % seqs, 0, keepdims=False)
        for r in range(seqs)
    ]
    grad_slab = jnp.concatenate(to_chips(grad_slots), axis=0)
    grad_rows = in_order(
        own_z.reshape(1),
        [grad_slab if q == 0 else send_z(grad_slab, q) for q in range(groups)],
        "grad_rows",
    )

    pairs = jnp.transpose(enc_in.reshape(rows, 2, seqs, enc_in.shape[2]), (1, 2, 0, 3))
    skip, slope, normed = encoder(at, neighbour_edges(pairs), conv_weight, norm_gain)
    normed_slab = jnp.concatenate(to_chips([normed[r] for r in range(seqs)]), axis=0)
    normed_rows = lax.all_gather(normed_slab, "head", axis=0, tiled=True)

    w_pack = jnp.transpose(w_qkv.reshape(3, width, heads, DH), (2, 1, 0, 3))
    w_pack = w_pack.reshape(heads, width, 3 * DH)
    w_rows = w_out.reshape(heads, DH, width)
    d_got = swap_heads(head_product(head_other, grad_rows, w_rows, NT, "d_o_other"))
    d_mine = head_product(head_mine, grad_rows, w_rows, NT, "d_o_own")
    qkv_got = swap_heads(head_product(head_other, normed_rows, w_pack, NN, "qkv_other"))
    qkv_mine = head_product(head_mine, normed_rows, w_pack, NN, "qkv_own")
    result_mine, result_other = attention(qkv_mine, qkv_got, d_mine, d_got)
    result_got = swap_heads(result_other)

    shape = (groups, seqs, rows, width)
    plain = jnp.stack([own_head, zero])
    d_term = pair_term(
        plain, result_mine, result_got, w_pack, shape, DH, 4 * DH, NT, "d_term"
    )
    d_normed = lax.psum_scatter(d_term, "head", scatter_dimension=0, tiled=False)
    d_normed = from_chips([d_normed[r] for r in range(seqs)])

    turned = jnp.stack([own_head, own_z])
    head_term = pair_term(
        turned, result_mine, result_got, w_rows, shape, 0, DH, NN, "head_term"
    )
    head_sum = summed(
        [head_term[q] if q == 0 else send_z(head_term[q], q) for q in range(groups)], "head_sum"
    )
    head_sum = from_chips([head_sum[r] for r in range(seqs)])
    mixed = mixed_call(at, head_sum, skip)

    part = weight_gradients(
        own_seq.reshape(1),
        normed_rows,
        swap_heads(normed_rows),
        grad_rows,
        swap_heads(grad_rows),
        result_mine,
        result_other,
        seqs,
    )
    chunk = summed(to_chips([part[r] for r in range(seqs)]), "weight_sum")
    chunks = [chunk if r == 0 else send_chip(chunk, r, heads) for r in range(seqs)]
    grad_w_qkv, grad_w_out = unpack_weights(at, chunks, [swap_heads(c) for c in chunks])

    d_conv = conv_gradient(at, d_normed, skip, grad, norm_gain, slope)
    grad_input = conv_back(neighbour_edges(d_conv), conv_weight)
    grad_input = jnp.transpose(grad_input.reshape(2, seqs, rows, -1), (2, 0, 1, 3))
    return (
        jnp.transpose(mixed, (1, 0, 2)),
        grad_input.reshape(enc_in.shape),
        grad_w_qkv,
        grad_w_out,
    )


def padded_2(block, sides, width):
    for axis, dim in sides:
        count = lax.axis_size(axis)
        forward = [(i, i + 1) for i in range(count - 1)]
        backward = [(target, source) for source, target in forward]
        low = lax.ppermute(
            lax.slice_in_dim(block, block.shape[dim] - width, None, axis=dim), axis, forward
        )
        high = lax.ppermute(lax.slice_in_dim(block, 0, width, axis=dim), axis, backward)
        block = jnp.concatenate([low, block, high], axis=dim)
    return block


def gathered_body(enc_in, conv_weight, norm_gain, w_qkv, w_out, grad_out):
    fine_rows = enc_in.shape[0]
    slab_rows = fine_rows // 2
    seq_count = enc_in.shape[1]
    out_width = conv_weight.shape[2]
    local_width = w_qkv.shape[2]
    local_heads = local_width // DH
    logit_scale = DH ** (-0.5)
    padded = padded_2(enc_in, ((("seq", "head"), 0),), 2)
    convolved = jnp.zeros((fine_rows, seq_count, out_width), jnp.float32)
    for offset in range(KW):
        convolved = convolved + jnp.einsum(
            "tbi,io->tbo",
            padded[offset : offset + fine_rows],
            conv_weight[offset],
            preferred_element_type=jnp.float32,
        )
    activated, gelu_pull = jax.vjp(jax.nn.gelu, convolved)
    skip = jnp.mean(activated.reshape(slab_rows, 2, seq_count, out_width), axis=1).astype(
        jnp.bfloat16
    )
    skip_wide = skip.astype(jnp.float32)
    inv_rms = lax.rsqrt(jnp.mean(skip_wide * skip_wide, axis=-1, keepdims=True) + 1e-06)
    normed = (skip_wide * inv_rms * norm_gain).astype(jnp.bfloat16)
    normed_rows = lax.all_gather(normed, "head", axis=0, tiled=True)
    grad_rows = lax.all_gather(grad_out, "head", axis=0, tiled=True)
    tower_rows = normed_rows.shape[0]
    qkv = jnp.einsum(
        "tbc,ice->itbe", normed_rows, w_qkv, preferred_element_type=jnp.float32
    ).astype(jnp.bfloat16)
    qkv = qkv.reshape(3, tower_rows, seq_count, local_heads, DH)
    query_matrix, key_matrix, value_matrix = (qkv[0], qkv[1], qkv[2])
    key_all, value_all = (
        lax.all_gather(key_matrix, "seq", axis=0, tiled=True),
        lax.all_gather(value_matrix, "seq", axis=0, tiled=True),
    )
    attention_logits = (
        jnp.einsum("qbhd,kbhd->bhqk", query_matrix, key_all, preferred_element_type=jnp.float32)
        * logit_scale
    )
    row_peak = jnp.max(attention_logits, axis=-1, keepdims=True)
    exponent = jnp.exp(attention_logits - row_peak)
    row_total = jnp.sum(exponent, axis=-1, keepdims=True)
    soft_weights = exponent / row_total
    narrow_probabilities = soft_weights.astype(jnp.bfloat16)
    attention_output = jnp.einsum(
        "bhqk,kbhd->qbhd", narrow_probabilities, value_all, preferred_element_type=jnp.float32
    )
    o_narrow = attention_output.reshape(tower_rows, seq_count, local_width).astype(jnp.bfloat16)
    piece = o_narrow
    head_sum = lax.psum_scatter(
        jnp.einsum("tbe,ec->tbc", piece, w_out, preferred_element_type=jnp.float32).astype(
            jnp.bfloat16
        ),
        "head",
        scatter_dimension=0,
        tiled=True,
    ).astype(jnp.float32)
    mixed = (skip_wide + head_sum).astype(jnp.bfloat16)
    part_w_out = jnp.einsum("tbe,tbc->ec", o_narrow, grad_rows, preferred_element_type=jnp.float32)
    d_out = jnp.einsum("tbc,ec->tbe", grad_rows, w_out, preferred_element_type=jnp.float32).astype(
        jnp.bfloat16
    )
    d_out = d_out.reshape(tower_rows, seq_count, local_heads, DH)
    delta = jnp.sum(d_out.astype(jnp.float32) * attention_output, axis=-1)
    probability_gradient = jnp.einsum(
        "qbhd,kbhd->bhqk", d_out, value_all, preferred_element_type=jnp.float32
    )
    d_scores = soft_weights * (probability_gradient - jnp.transpose(delta, (1, 2, 0))[..., None])
    narrow_gradient = d_scores.astype(jnp.bfloat16)
    query_gradient = logit_scale * jnp.einsum(
        "bhqk,kbhd->qbhd", narrow_gradient, key_all, preferred_element_type=jnp.float32
    )
    key_terms = logit_scale * jnp.einsum(
        "bhqk,qbhd->kbhd", narrow_gradient, query_matrix, preferred_element_type=jnp.float32
    )
    value_terms = jnp.einsum(
        "bhqk,qbhd->kbhd", narrow_probabilities, d_out, preferred_element_type=jnp.float32
    )
    d_keys, d_values = (
        lax.psum_scatter(
            key_terms.astype(jnp.bfloat16), "seq", scatter_dimension=0, tiled=True
        ).astype(jnp.float32),
        lax.psum_scatter(
            value_terms.astype(jnp.bfloat16), "seq", scatter_dimension=0, tiled=True
        ).astype(jnp.float32),
    )
    dqkv = (
        jnp.stack([query_gradient, d_keys, d_values])
        .reshape(3, tower_rows, seq_count, local_width)
        .astype(jnp.bfloat16)
    )
    part_w_qkv = jnp.einsum("tbc,itbe->ice", normed_rows, dqkv, preferred_element_type=jnp.float32)
    piece = dqkv
    d_normed = lax.psum_scatter(
        jnp.einsum("itbe,ice->tbc", piece, w_qkv, preferred_element_type=jnp.float32).astype(
            jnp.bfloat16
        ),
        "head",
        scatter_dimension=0,
        tiled=True,
    ).astype(jnp.float32)
    unit_rows = skip_wide * inv_rms
    scaled = d_normed * norm_gain
    d_skip = grad_out.astype(jnp.float32) + inv_rms * (
        scaled - unit_rows * jnp.mean(scaled * unit_rows, axis=-1, keepdims=True)
    )
    d_act = jnp.repeat(d_skip, 2, axis=0) * 0.5
    d_conv = gelu_pull(d_act)[0].astype(jnp.bfloat16)
    d_pad = padded_2(d_conv, ((("seq", "head"), 0),), 2)
    grad_input = jnp.zeros((fine_rows, seq_count, enc_in.shape[2]), jnp.float32)
    for offset in range(KW):
        grad_input = grad_input + jnp.einsum(
            "tbo,io->tbi",
            d_pad[4 - offset : 4 - offset + fine_rows],
            conv_weight[offset],
            preferred_element_type=jnp.float32,
        )
    grad_w_qkv, grad_w_out = (
        lax.psum(part_w_qkv.astype(jnp.bfloat16), "seq").astype(jnp.float32),
        lax.psum(part_w_out.astype(jnp.bfloat16), "seq").astype(jnp.float32),
    )
    return (mixed, grad_input.astype(jnp.bfloat16), grad_w_qkv, grad_w_out)


def body(enc_in, conv_weight, norm_gain, w_qkv, w_out, grad_out):
    heads = w_qkv.shape[2] // DH
    fits = heads == 2 and enc_in.shape[1] * heads == lax.axis_size("seq")
    chosen = unit_body if fits else gathered_body
    return chosen(enc_in, conv_weight, norm_gain, w_qkv, w_out, grad_out)


def solution(mesh):
    return jax.shard_map(
        body,
        mesh=mesh,
        in_specs=(
            P(("seq", "head"), None, None),
            P(),
            P(),
            P(None, None, "head"),
            P("head", None),
            P(("seq", "head"), None, None),
        ),
        out_specs=(
            P(("seq", "head"), None, None),
            P(("seq", "head"), None, None),
            P(None, None, "head"),
            P("head", None),
        ),
        check_vma=False,
    )
```

```python
import functools

import jax
import jax.numpy as jnp
from jax import lax
from jax.experimental import pallas as pl
from jax.experimental.pallas import tpu as pltpu
from jax.sharding import PartitionSpec as P

DH = 192
KW = 5
VMEM_LIMIT = 56 * 1024 * 1024
BF = jnp.bfloat16
F32 = jnp.float32


def params():
    return pltpu.CompilerParams(vmem_limit_bytes=VMEM_LIMIT)


def dot(a, b, contract):
    return lax.dot_general(a, b, (contract, ((), ())), preferred_element_type=F32)


NN = ((1,), (0,))
NT = ((1,), (1,))
TN = ((0,), (0,))


def whole(shape):
    return pl.BlockSpec(shape, lambda *_: (0,) * len(shape))


SCALARS = pl.BlockSpec(memory_space=pltpu.SMEM)


def wrapped(value, size):
    return jnp.where(value < 0, value + size, jnp.where(value >= size, value - size, value))


def turned_rows(ref, low_ref, high_ref, parity, shift):
    seqs, rows, width = ref.shape[1:]
    own = ref[parity]
    if shift != 1:
        wide = own.astype(F32)
        if shift == 0:
            parts = [low_ref[parity].astype(F32), wide[:, : rows - 1]]
        else:
            parts = [wide[:, 1:], high_ref[parity].astype(F32)]
        own = jnp.concatenate(parts, axis=1).astype(BF)
    return own.reshape(seqs * rows, width)


def conv_kernel(
    at_ref, x_ref, low_ref, high_ref, w_ref, gain_ref, skip_ref, slope_ref, *rest
):
    normed_refs, (lhs, squares, whole_normed) = rest[:-3], rest[-3:]
    step = pl.program_id(0)
    seqs, rows, c_in = x_ref.shape[1:]
    half = seqs * rows
    tile = w_ref.shape[2]

    @pl.when(step == 0)
    def _():
        for parity in range(2):
            for shift in range(3):
                value = turned_rows(x_ref, low_ref, high_ref, parity, shift)
                for out in range(2):
                    tap = 2 * shift + parity - out
                    if 0 <= tap < KW:
                        lhs[out * half : (out + 1) * half, tap * c_in : (tap + 1) * c_in] = value
        squares[...] = jnp.zeros_like(squares)

    conv = dot(lhs[...], w_ref[...].reshape(KW * c_in, tile), NN)
    root = 0.7978845608028654
    total = None
    for parity in range(2):
        x = conv[parity * half : (parity + 1) * half, :]
        square = x * x
        t = jnp.tanh(root * (x + 0.044715 * (square * x)))
        left = 0.5 * (1.0 + t)
        act = x * left
        slope = left + (0.5 * root) * x * (1.0 - t * t) * (1.0 + (3 * 0.044715) * square)
        slope_ref[parity] = slope.reshape(slope_ref.shape[1:])
        total = act if total is None else total + act
    skip = (0.5 * total).astype(BF)
    columns = pl.ds(pl.multiple_of(step * tile, tile), tile)
    skip_ref[:, :, columns] = skip.reshape(seqs, rows, tile)
    wide = skip.astype(F32)
    squares[...] += jnp.sum(wide * wide, axis=-1, keepdims=True)

    @pl.when(step == pl.num_programs(0) - 1)
    def _():
        width = skip_ref.shape[2]
        inv = lax.rsqrt(squares[...] * (1.0 / width) + 1e-06)
        wide = skip_ref[...].reshape(half, width).astype(F32)
        normed = (wide * inv * gain_ref[...]).astype(BF)
        whole_normed[...] = normed.reshape(whole_normed.shape)
        for slot in range(seqs):
            normed_refs[slot][...] = whole_normed[wrapped(at_ref[0] + slot, seqs)]


def encoder(at, pairs, low, high, conv_weight, norm_gain):
    _, seqs, rows, c_in = pairs.shape
    width = conv_weight.shape[2]
    tile = 256 if width % 256 == 0 else width
    shape = (seqs, rows, width)
    outs = pl.pallas_call(
        conv_kernel,
        grid=(width // tile,),
        in_specs=[
            SCALARS,
            whole(pairs.shape),
            whole(low.shape),
            whole(high.shape),
            pl.BlockSpec((KW, c_in, tile), lambda n: (0, 0, n)),
            whole((1, width)),
        ],
        out_specs=[
            whole(shape),
            pl.BlockSpec((2, seqs, rows, tile), lambda n: (0, 0, 0, n)),
        ]
        + [whole((rows, width))] * seqs,
        out_shape=[
            jax.ShapeDtypeStruct(shape, BF),
            jax.ShapeDtypeStruct((2,) + shape, F32),
        ]
        + [jax.ShapeDtypeStruct((rows, width), BF)] * seqs,
        scratch_shapes=[
            pltpu.VMEM((2 * seqs * rows, KW * c_in), BF),
            pltpu.VMEM((seqs * rows, 1), F32),
            pltpu.VMEM(shape, BF),
        ],
        compiler_params=params(),
        name="encoder_forward",
    )(at, pairs, low, high, conv_weight, norm_gain.reshape(1, width))
    return outs[0], outs[1], list(outs[2:])


def d_conv_body(seqs, at_ref, *refs):
    dn_refs = refs[:seqs]
    skip_ref, grad_ref, gain_ref, slope_ref, out_ref, first_ref, last_ref = refs[seqs:]
    rows = out_ref.shape[2]
    for slot in range(seqs):
        b = wrapped(at_ref[0] + slot, seqs)
        wide = skip_ref[b].astype(F32)
        inv = lax.rsqrt(jnp.mean(wide * wide, axis=-1, keepdims=True) + 1e-06)
        unit = wide * inv
        scaled = dn_refs[slot][...].astype(F32) * gain_ref[...]
        d_skip = grad_ref[b].astype(F32) + inv * (
            scaled - unit * jnp.mean(scaled * unit, axis=-1, keepdims=True)
        )
        d_act = 0.5 * d_skip
        for parity in range(2):
            value = slope_ref[parity, b] * d_act
            out_ref[parity, b] = value.astype(BF)
            first_ref[parity, b] = value[:1].astype(BF)
            last_ref[parity, b] = value[rows - 1 :].astype(BF)


def conv_gradient(at, d_normed, skip, grad, norm_gain, slope):
    seqs = len(d_normed)
    vmem = pl.BlockSpec(memory_space=pltpu.VMEM)
    edge = jax.ShapeDtypeStruct(slope.shape[:2] + (1, slope.shape[3]), BF)
    return pl.pallas_call(
        functools.partial(d_conv_body, seqs),
        in_specs=[SCALARS] + [vmem] * (seqs + 4),
        out_specs=[vmem] * 3,
        out_shape=[jax.ShapeDtypeStruct(slope.shape, BF)] + [edge] * 2,
        compiler_params=params(),
        name="conv_gradient",
    )(at, *d_normed, skip, grad, norm_gain.reshape(1, -1), slope)


def mixed_body(seqs, at_ref, *refs):
    skip_ref, out_ref = refs[seqs:]
    for slot in range(seqs):
        b = wrapped(at_ref[0] + slot, seqs)
        out_ref[b] = (skip_ref[b].astype(F32) + refs[slot][...].astype(F32)).astype(BF)


def mixed_call(at, terms, skip):
    seqs = len(terms)
    vmem = pl.BlockSpec(memory_space=pltpu.VMEM)
    return pl.pallas_call(
        functools.partial(mixed_body, seqs),
        in_specs=[SCALARS] + [vmem] * (seqs + 1),
        out_specs=vmem,
        out_shape=jax.ShapeDtypeStruct(skip.shape, BF),
        compiler_params=params(),
        name="mixed_sum",
    )(at, *terms, skip)


def conv_back_kernel(d_ref, low_ref, high_ref, w_ref, out_ref, turned, acc):
    step = pl.program_id(0)

    @pl.when(step == 0)
    def _():
        for parity in range(2):
            for shift in range(3):
                turned[parity, shift] = turned_rows(d_ref, low_ref, high_ref, parity, shift)

    for tap in range(KW):

        @pl.when(step == tap)
        def _():
            places = [KW - 1 - tap, KW - tap]
            lhs = jnp.concatenate([turned[p % 2, p // 2] for p in places], axis=0)
            term = dot(lhs, w_ref[0], NT)
            if tap == 0:
                acc[...] = term
            elif tap < KW - 1:
                acc[...] += term
            else:
                out_ref[...] = (acc[...] + term).astype(BF)


def conv_back(d_conv, low, high, conv_weight):
    _, seqs, rows, width = d_conv.shape
    c_in = conv_weight.shape[1]
    flat = 2 * seqs * rows
    return pl.pallas_call(
        conv_back_kernel,
        grid=(KW,),
        in_specs=[
            whole(d_conv.shape),
            whole(low.shape),
            whole(high.shape),
            pl.BlockSpec((1, c_in, width), lambda k: (k, 0, 0)),
        ],
        out_specs=whole((flat, c_in)),
        out_shape=jax.ShapeDtypeStruct((flat, c_in), BF),
        scratch_shapes=[
            pltpu.VMEM((2, 3, seqs * rows, width), BF),
            pltpu.VMEM((flat, c_in), F32),
        ],
        compiler_params=params(),
        name="encoder_backward",
    )(d_conv, low, high, conv_weight)


def product_kernel(head_ref, x_ref, w_ref, out_ref, *, contract):
    del head_ref
    value = dot(x_ref[...], w_ref[0], contract).astype(BF)
    out_ref[:, : value.shape[1]] = value
    if value.shape[1] < out_ref.shape[1]:
        out_ref[:, value.shape[1] :] = jnp.zeros_like(out_ref[:, value.shape[1] :])


def head_product(head, x, weight, contract, name):
    columns = weight.shape[2] if contract == NN else weight.shape[1]
    columns += -columns % 128
    rows, width = x.shape
    return pl.pallas_call(
        functools.partial(product_kernel, contract=contract),
        grid_spec=pltpu.PrefetchScalarGridSpec(
            num_scalar_prefetch=1,
            grid=(1,),
            in_specs=[
                pl.BlockSpec((rows, width), lambda i, head: (0, 0)),
                pl.BlockSpec((1,) + weight.shape[1:], lambda i, head: (head[0], 0, 0)),
            ],
            out_specs=pl.BlockSpec((rows, columns), lambda i, head: (0, 0)),
        ),
        out_shape=jax.ShapeDtypeStruct((rows, columns), BF),
        compiler_params=params(),
        name=name,
    )(head, x, weight)


def attention_kernel(qa_ref, qb_ref, da_ref, db_ref, oa_ref, ob_ref, k_all, v_all, dk_acc, dv_acc, *, block):
    scale = DH ** (-0.5)
    half = qa_ref.shape[0]
    for place, ref in enumerate((qa_ref, qb_ref)):
        rows = pl.ds(place * half, half)
        k_all[rows, :] = ref[:, DH : 2 * DH]
        v_all[rows, :] = ref[:, 2 * DH : 3 * DH]
    k = k_all[...]
    v = v_all[...]
    for place, (q_ref, d_ref, out_ref) in enumerate(
        ((qa_ref, da_ref, oa_ref), (qb_ref, db_ref, ob_ref))
    ):
        for start in range(0, half, block):
            rows = pl.ds(start, block)
            q = q_ref[rows, 0:DH]
            d_o = d_ref[rows, 0:DH]
            s = dot(q, k, NT) * scale
            e = jnp.exp(s - jnp.max(s, axis=-1, keepdims=True))
            p = e * (1.0 / jnp.sum(e, axis=-1, keepdims=True))
            p_b = p.astype(BF)
            o = dot(p_b, v, NN)
            delta = jnp.sum(d_o.astype(F32) * o, axis=-1, keepdims=True)
            d_p = dot(d_o, v, NT)
            ds = (p * (d_p - delta)).astype(BF)
            dq = scale * dot(ds, k, NN)
            dk = dot(ds, q, TN)
            dv = dot(p_b, d_o, TN)
            if place == 0 and start == 0:
                dk_acc[...] = dk
                dv_acc[...] = dv
            else:
                dk_acc[...] += dk
                dv_acc[...] += dv
            out_ref[rows, 0:DH] = o.astype(BF)
            out_ref[rows, DH : 2 * DH] = dq.astype(BF)
    for place, out_ref in enumerate((oa_ref, ob_ref)):
        rows = pl.ds(place * half, half)
        out_ref[:, 2 * DH : 3 * DH] = (scale * dk_acc[rows, :]).astype(BF)
        out_ref[:, 3 * DH : 4 * DH] = dv_acc[rows, :].astype(BF)


def attention(qkv_a, qkv_b, d_a, d_b):
    half = qkv_a.shape[0]
    shape = jax.ShapeDtypeStruct((half, 4 * DH), BF)
    return pl.pallas_call(
        functools.partial(attention_kernel, block=min(256, half)),
        out_shape=[shape, shape],
        scratch_shapes=[
            pltpu.VMEM((2 * half, DH), BF),
            pltpu.VMEM((2 * half, DH), BF),
            pltpu.VMEM((2 * half, DH), F32),
            pltpu.VMEM((2 * half, DH), F32),
        ],
        compiler_params=params(),
        name="attention",
    )(qkv_a, qkv_b, d_a, d_b)


def term_kernel(head_ref, a_ref, b_ref, w_ref, *rest, first, last, contract):
    out_refs, acc = rest[:-1], rest[-1]
    step = pl.program_id(0)

    @pl.when(step == 0)
    def _():
        acc[...] = dot(a_ref[:, first:last], w_ref[0], contract)

    @pl.when(step == 1)
    def _():
        acc[...] += dot(b_ref[:, first:last], w_ref[0], contract)
        count = len(out_refs)
        if count == 1:
            out_refs[0][...] = acc[...].astype(BF)
            return
        size = out_refs[0].shape[0]
        for slot, out_ref in enumerate(out_refs):
            block = wrapped(head_ref[1] + slot, count)
            rows = pl.ds(pl.multiple_of(block * size, size), size)
            out_ref[...] = acc[rows, :].astype(BF)


def pair_term(place, mine, got, weight, width, slots, first, last, contract, name):
    half, full = mine.shape
    size = half // slots
    return pl.pallas_call(
        functools.partial(term_kernel, first=first, last=last, contract=contract),
        grid_spec=pltpu.PrefetchScalarGridSpec(
            num_scalar_prefetch=1,
            grid=(2,),
            in_specs=[
                pl.BlockSpec((half, full), lambda i, at: (0, 0)),
                pl.BlockSpec((half, full), lambda i, at: (0, 0)),
                pl.BlockSpec(
                    (1,) + weight.shape[1:],
                    lambda i, at: (jnp.where(i == 0, at[0], 1 - at[0]), 0, 0),
                ),
            ],
            out_specs=[pl.BlockSpec((size, width), lambda i, at: (0, 0))] * slots,
            scratch_shapes=[pltpu.VMEM((half, width), F32)],
        ),
        out_shape=[jax.ShapeDtypeStruct((size, width), BF)] * slots,
        compiler_params=params(),
        name=name,
    )(place, mine, got, weight)


def sum_kernel(*refs):
    total = refs[0][...].astype(F32)
    for ref in refs[1:-1]:
        total = total + ref[...].astype(F32)
    refs[-1][...] = total.astype(BF)


def summed(parts, name):
    return pl.pallas_call(
        sum_kernel,
        out_shape=jax.ShapeDtypeStruct(parts[0].shape, BF),
        compiler_params=params(),
        name=name,
    )(*parts)


def weight_kernel(at_ref, xa_ref, xb_ref, ga_ref, gb_ref, ra_ref, rb_ref, *out_refs):
    del at_ref
    qkv = dot(xa_ref[...], ra_ref[:, DH:], TN) + dot(xb_ref[...], rb_ref[:, DH:], TN)
    out = dot(ga_ref[...], ra_ref[:, :DH], TN) + dot(gb_ref[...], rb_ref[:, :DH], TN)
    for slot, out_ref in enumerate(out_refs):

        @pl.when(pl.program_id(0) == slot)
        def _():
            out_ref[:, : 3 * DH] = qkv.astype(BF)
            out_ref[:, 3 * DH :] = out.astype(BF)


def weight_gradients(at, xa, xb, ga, gb, ra, rb, seqs):
    half, width = xa.shape
    chunk = width // seqs
    full = ra.shape[1]
    column = pl.BlockSpec((half, chunk), lambda r, at: (0, lax.rem(r + at[0], seqs)))
    rest = pl.BlockSpec((half, full), lambda r, at: (0, 0))
    return pl.pallas_call(
        weight_kernel,
        grid_spec=pltpu.PrefetchScalarGridSpec(
            num_scalar_prefetch=1,
            grid=(seqs,),
            in_specs=[column] * 4 + [rest] * 2,
            out_specs=[pl.BlockSpec((chunk, full), lambda r, at: (0, 0))] * seqs,
        ),
        out_shape=[jax.ShapeDtypeStruct((chunk, full), BF)] * seqs,
        compiler_params=params(),
        name="weight_gradients",
    )(at, xa, xb, ga, gb, ra, rb)


def unpack_kernel(at_ref, *refs):
    seqs = (len(refs) - 2) // 2
    qkv_ref, out_ref = refs[-2:]
    step = pl.program_id(0)
    first_head = at_ref[1] == 0
    for slot in range(seqs):

        @pl.when(step == slot)
        def _():
            mine = refs[slot][...].astype(F32)
            other = refs[seqs + slot][...].astype(F32)
            low = jnp.where(first_head, mine, other)
            high = jnp.where(first_head, other, mine)
            for i in range(3):
                columns = slice(i * DH, (i + 1) * DH)
                qkv_ref[i] = jnp.concatenate([low[:, columns], high[:, columns]], axis=1)
            out_ref[:DH, :] = low[:, 3 * DH :].T
            out_ref[DH:, :] = high[:, 3 * DH :].T


def unpack_weights(at, mine, other):
    seqs = len(mine)
    chunk, full = mine[0].shape
    width = chunk * seqs
    local = 2 * DH

    def place(r, at):
        return lax.rem(at[0] - r + seqs, seqs)

    return pl.pallas_call(
        unpack_kernel,
        grid_spec=pltpu.PrefetchScalarGridSpec(
            num_scalar_prefetch=1,
            grid=(seqs,),
            in_specs=[pl.BlockSpec((chunk, full), lambda r, at: (0, 0))] * (2 * seqs),
            out_specs=[
                pl.BlockSpec((3, chunk, local), lambda r, at: (0, place(r, at), 0)),
                pl.BlockSpec((local, chunk), lambda r, at: (0, place(r, at))),
            ],
        ),
        out_shape=[
            jax.ShapeDtypeStruct((3, width, local), F32),
            jax.ShapeDtypeStruct((local, width), F32),
        ],
        compiler_params=params(),
        name="weight_outputs",
    )(at, *mine, *other)


def neighbour_edges(first, last):
    axes = ("seq", "head")
    count = lax.axis_size(axes)
    forward = [(i, i + 1) for i in range(count - 1)]
    backward = [(target, source) for source, target in forward]
    return lax.ppermute(last, axes, forward), lax.ppermute(first, axes, backward)


def send_chip(x, step, heads):
    count = lax.axis_size("seq")
    return lax.ppermute(x, "seq", [(s, (s + step * heads) % count) for s in range(count)])


def send_z(x, step):
    count = lax.axis_size("head")
    return lax.ppermute(x, "head", [(z, (z + step) % count) for z in range(count)])


def swap_heads(x):
    count = lax.axis_size("seq")
    return lax.ppermute(x, "seq", [(s, s + 1 - 2 * (s % 2)) for s in range(count)])


def unit_body(enc_in, conv_weight, norm_gain, w_qkv, w_out, grad_out):
    rows = enc_in.shape[0] // 2
    seqs = enc_in.shape[1]
    width = conv_weight.shape[2]
    local = w_qkv.shape[2]
    heads = local // DH
    groups = lax.axis_size("head")
    half = groups * seqs * rows
    place = lax.axis_index("seq")
    own_seq = (place // heads).astype(jnp.int32)
    own_head = (place % heads).astype(jnp.int32)
    own_z = lax.axis_index("head").astype(jnp.int32)
    zero = jnp.zeros((), jnp.int32)
    at = jnp.stack([own_seq, own_head])
    head_mine = own_head.reshape(1)
    head_other = (1 - own_head).reshape(1)

    def to_chips(slots):
        return [slots[r] if r == 0 else send_chip(slots[r], r, heads) for r in range(seqs)]

    def from_chips(slots):
        return [slots[r] if r == 0 else send_chip(slots[r], -r, heads) for r in range(seqs)]

    grad = jnp.transpose(grad_out, (1, 0, 2))
    grad_z = lax.all_gather(grad, "head", axis=0, tiled=False)
    grad_slots = [
        lax.dynamic_index_in_dim(grad_z, (own_seq + r) % seqs, 1, keepdims=False)
        for r in range(seqs)
    ]
    grad_rows = jnp.stack(to_chips(grad_slots), axis=1).reshape(half, width)

    pairs = jnp.transpose(enc_in.reshape(rows, 2, seqs, enc_in.shape[2]), (1, 2, 0, 3))
    low, high = neighbour_edges(pairs[:, :, :1, :], pairs[:, :, -1:, :])
    skip, slope, normed = encoder(at, pairs, low, high, conv_weight, norm_gain)
    normed_slab = jnp.concatenate(to_chips(normed), axis=0)
    normed_rows = lax.all_gather(normed_slab, "head", axis=0, tiled=True)

    w_pack = jnp.transpose(w_qkv.reshape(3, width, heads, DH), (2, 1, 0, 3))
    w_pack = w_pack.reshape(heads, width, 3 * DH)
    w_rows = w_out.reshape(heads, DH, width)
    d_got = swap_heads(head_product(head_other, grad_rows, w_rows, NT, "d_o_other"))
    d_mine = head_product(head_mine, grad_rows, w_rows, NT, "d_o_own")
    qkv_got = swap_heads(head_product(head_other, normed_rows, w_pack, NN, "qkv_other"))
    qkv_mine = head_product(head_mine, normed_rows, w_pack, NN, "qkv_own")
    result_mine, result_other = attention(qkv_mine, qkv_got, d_mine, d_got)
    result_got = swap_heads(result_other)

    plain = jnp.stack([own_head, zero])
    (d_term,) = pair_term(
        plain, result_mine, result_got, w_pack, width, 1, DH, 4 * DH, NT, "d_term"
    )
    d_normed = lax.psum_scatter(
        d_term.reshape(groups, seqs, rows, width), "head", scatter_dimension=0, tiled=False
    )

    turned = jnp.stack([own_head, own_z])
    head_term = pair_term(
        turned, result_mine, result_got, w_rows, width, groups, 0, DH, NN, "head_term"
    )
    head_term, d_normed = lax.optimization_barrier((head_term, d_normed))
    d_normed = from_chips([d_normed[r] for r in range(seqs)])
    head_sum = summed(
        [head_term[q] if q == 0 else send_z(head_term[q], q) for q in range(groups)], "head_sum"
    ).reshape(seqs, rows, width)
    head_sum = from_chips([head_sum[r] for r in range(seqs)])
    mixed = mixed_call(at, head_sum, skip)

    part = weight_gradients(
        own_seq.reshape(1),
        normed_rows,
        swap_heads(normed_rows),
        grad_rows,
        swap_heads(grad_rows),
        result_mine,
        result_other,
        seqs,
    )
    chunk = summed(to_chips(part), "weight_sum")
    chunks = [chunk if r == 0 else send_chip(chunk, r, heads) for r in range(seqs)]
    grad_w_qkv, grad_w_out = unpack_weights(at, chunks, [swap_heads(c) for c in chunks])

    d_conv, first, last = conv_gradient(at, d_normed, skip, grad, norm_gain, slope)
    low, high = neighbour_edges(first, last)
    grad_input = conv_back(d_conv, low, high, conv_weight)
    grad_input = jnp.transpose(grad_input.reshape(2, seqs, rows, -1), (2, 0, 1, 3))
    return (
        jnp.transpose(mixed, (1, 0, 2)),
        grad_input.reshape(enc_in.shape),
        grad_w_qkv,
        grad_w_out,
    )


def padded_2(block, sides, width):
    for axis, dim in sides:
        count = lax.axis_size(axis)
        forward = [(i, i + 1) for i in range(count - 1)]
        backward = [(target, source) for source, target in forward]
        low = lax.ppermute(
            lax.slice_in_dim(block, block.shape[dim] - width, None, axis=dim), axis, forward
        )
        high = lax.ppermute(lax.slice_in_dim(block, 0, width, axis=dim), axis, backward)
        block = jnp.concatenate([low, block, high], axis=dim)
    return block


def gathered_body(enc_in, conv_weight, norm_gain, w_qkv, w_out, grad_out):
    fine_rows = enc_in.shape[0]
    slab_rows = fine_rows // 2
    seq_count = enc_in.shape[1]
    out_width = conv_weight.shape[2]
    local_width = w_qkv.shape[2]
    local_heads = local_width // DH
    logit_scale = DH ** (-0.5)
    padded = padded_2(enc_in, ((("seq", "head"), 0),), 2)
    convolved = jnp.zeros((fine_rows, seq_count, out_width), jnp.float32)
    for offset in range(KW):
        convolved = convolved + jnp.einsum(
            "tbi,io->tbo",
            padded[offset : offset + fine_rows],
            conv_weight[offset],
            preferred_element_type=jnp.float32,
        )
    activated, gelu_pull = jax.vjp(jax.nn.gelu, convolved)
    skip = jnp.mean(activated.reshape(slab_rows, 2, seq_count, out_width), axis=1).astype(
        jnp.bfloat16
    )
    skip_wide = skip.astype(jnp.float32)
    inv_rms = lax.rsqrt(jnp.mean(skip_wide * skip_wide, axis=-1, keepdims=True) + 1e-06)
    normed = (skip_wide * inv_rms * norm_gain).astype(jnp.bfloat16)
    normed_rows = lax.all_gather(normed, "head", axis=0, tiled=True)
    grad_rows = lax.all_gather(grad_out, "head", axis=0, tiled=True)
    tower_rows = normed_rows.shape[0]
    qkv = jnp.einsum(
        "tbc,ice->itbe", normed_rows, w_qkv, preferred_element_type=jnp.float32
    ).astype(jnp.bfloat16)
    qkv = qkv.reshape(3, tower_rows, seq_count, local_heads, DH)
    query_matrix, key_matrix, value_matrix = (qkv[0], qkv[1], qkv[2])
    key_all, value_all = (
        lax.all_gather(key_matrix, "seq", axis=0, tiled=True),
        lax.all_gather(value_matrix, "seq", axis=0, tiled=True),
    )
    attention_logits = (
        jnp.einsum("qbhd,kbhd->bhqk", query_matrix, key_all, preferred_element_type=jnp.float32)
        * logit_scale
    )
    row_peak = jnp.max(attention_logits, axis=-1, keepdims=True)
    exponent = jnp.exp(attention_logits - row_peak)
    row_total = jnp.sum(exponent, axis=-1, keepdims=True)
    soft_weights = exponent / row_total
    narrow_probabilities = soft_weights.astype(jnp.bfloat16)
    attention_output = jnp.einsum(
        "bhqk,kbhd->qbhd", narrow_probabilities, value_all, preferred_element_type=jnp.float32
    )
    o_narrow = attention_output.reshape(tower_rows, seq_count, local_width).astype(jnp.bfloat16)
    piece = o_narrow
    head_sum = lax.psum_scatter(
        jnp.einsum("tbe,ec->tbc", piece, w_out, preferred_element_type=jnp.float32).astype(
            jnp.bfloat16
        ),
        "head",
        scatter_dimension=0,
        tiled=True,
    ).astype(jnp.float32)
    mixed = (skip_wide + head_sum).astype(jnp.bfloat16)
    part_w_out = jnp.einsum("tbe,tbc->ec", o_narrow, grad_rows, preferred_element_type=jnp.float32)
    d_out = jnp.einsum("tbc,ec->tbe", grad_rows, w_out, preferred_element_type=jnp.float32).astype(
        jnp.bfloat16
    )
    d_out = d_out.reshape(tower_rows, seq_count, local_heads, DH)
    delta = jnp.sum(d_out.astype(jnp.float32) * attention_output, axis=-1)
    probability_gradient = jnp.einsum(
        "qbhd,kbhd->bhqk", d_out, value_all, preferred_element_type=jnp.float32
    )
    d_scores = soft_weights * (probability_gradient - jnp.transpose(delta, (1, 2, 0))[..., None])
    narrow_gradient = d_scores.astype(jnp.bfloat16)
    query_gradient = logit_scale * jnp.einsum(
        "bhqk,kbhd->qbhd", narrow_gradient, key_all, preferred_element_type=jnp.float32
    )
    key_terms = logit_scale * jnp.einsum(
        "bhqk,qbhd->kbhd", narrow_gradient, query_matrix, preferred_element_type=jnp.float32
    )
    value_terms = jnp.einsum(
        "bhqk,qbhd->kbhd", narrow_probabilities, d_out, preferred_element_type=jnp.float32
    )
    d_keys, d_values = (
        lax.psum_scatter(
            key_terms.astype(jnp.bfloat16), "seq", scatter_dimension=0, tiled=True
        ).astype(jnp.float32),
        lax.psum_scatter(
            value_terms.astype(jnp.bfloat16), "seq", scatter_dimension=0, tiled=True
        ).astype(jnp.float32),
    )
    dqkv = (
        jnp.stack([query_gradient, d_keys, d_values])
        .reshape(3, tower_rows, seq_count, local_width)
        .astype(jnp.bfloat16)
    )
    part_w_qkv = jnp.einsum("tbc,itbe->ice", normed_rows, dqkv, preferred_element_type=jnp.float32)
    piece = dqkv
    d_normed = lax.psum_scatter(
        jnp.einsum("itbe,ice->tbc", piece, w_qkv, preferred_element_type=jnp.float32).astype(
            jnp.bfloat16
        ),
        "head",
        scatter_dimension=0,
        tiled=True,
    ).astype(jnp.float32)
    unit_rows = skip_wide * inv_rms
    scaled = d_normed * norm_gain
    d_skip = grad_out.astype(jnp.float32) + inv_rms * (
        scaled - unit_rows * jnp.mean(scaled * unit_rows, axis=-1, keepdims=True)
    )
    d_act = jnp.repeat(d_skip, 2, axis=0) * 0.5
    d_conv = gelu_pull(d_act)[0].astype(jnp.bfloat16)
    d_pad = padded_2(d_conv, ((("seq", "head"), 0),), 2)
    grad_input = jnp.zeros((fine_rows, seq_count, enc_in.shape[2]), jnp.float32)
    for offset in range(KW):
        grad_input = grad_input + jnp.einsum(
            "tbo,io->tbi",
            d_pad[4 - offset : 4 - offset + fine_rows],
            conv_weight[offset],
            preferred_element_type=jnp.float32,
        )
    grad_w_qkv, grad_w_out = (
        lax.psum(part_w_qkv.astype(jnp.bfloat16), "seq").astype(jnp.float32),
        lax.psum(part_w_out.astype(jnp.bfloat16), "seq").astype(jnp.float32),
    )
    return (mixed, grad_input.astype(jnp.bfloat16), grad_w_qkv, grad_w_out)


def body(enc_in, conv_weight, norm_gain, w_qkv, w_out, grad_out):
    heads = w_qkv.shape[2] // DH
    fits = heads == 2 and enc_in.shape[1] * heads == lax.axis_size("seq")
    chosen = unit_body if fits else gathered_body
    return chosen(enc_in, conv_weight, norm_gain, w_qkv, w_out, grad_out)


def solution(mesh):
    return jax.shard_map(
        body,
        mesh=mesh,
        in_specs=(
            P(("seq", "head"), None, None),
            P(),
            P(),
            P(None, None, "head"),
            P("head", None),
            P(("seq", "head"), None, None),
        ),
        out_specs=(
            P(("seq", "head"), None, None),
            P(("seq", "head"), None, None),
            P(None, None, "head"),
            P("head", None),
        ),
        check_vma=False,
    )
```

```python
import functools

import jax
import jax.numpy as jnp
from jax import lax
from jax.experimental import pallas as pl
from jax.experimental.pallas import tpu as pltpu
from jax.sharding import PartitionSpec as P

DH = 192
KW = 5
VMEM_LIMIT = 56 * 1024 * 1024
COST = pl.CostEstimate(flops=1000, bytes_accessed=1000, transcendentals=0)
BF = jnp.bfloat16
F32 = jnp.float32


def params():
    return pltpu.CompilerParams(vmem_limit_bytes=VMEM_LIMIT)


def dot(a, b, contract):
    return lax.dot_general(a, b, (contract, ((), ())), preferred_element_type=F32)


NN = ((1,), (0,))
NT = ((1,), (1,))
TN = ((0,), (0,))


def whole(shape):
    return pl.BlockSpec(shape, lambda *_: (0,) * len(shape))


SCALARS = pl.BlockSpec(memory_space=pltpu.SMEM)


def wrapped(value, size):
    return jnp.where(value < 0, value + size, jnp.where(value >= size, value - size, value))


def turned_rows(ref, low_ref, high_ref, parity, shift):
    seqs, rows, width = ref.shape[1:]
    own = ref[parity]
    if shift != 1:
        wide = own.astype(F32)
        if shift == 0:
            parts = [low_ref[parity].astype(F32), wide[:, : rows - 1]]
        else:
            parts = [wide[:, 1:], high_ref[parity].astype(F32)]
        own = jnp.concatenate(parts, axis=1).astype(BF)
    return own.reshape(seqs * rows, width)


def conv_kernel(
    at_ref, x_ref, low_ref, high_ref, w_ref, gain_ref, skip_ref, slope_ref, *rest
):
    normed_refs, (lhs, squares, whole_normed) = rest[:-3], rest[-3:]
    step = pl.program_id(0)
    seqs, rows, c_in = x_ref.shape[1:]
    half = seqs * rows
    tile = w_ref.shape[2]

    @pl.when(step == 0)
    def _():
        for parity in range(2):
            for shift in range(3):
                value = turned_rows(x_ref, low_ref, high_ref, parity, shift)
                for out in range(2):
                    tap = 2 * shift + parity - out
                    if 0 <= tap < KW:
                        lhs[out * half : (out + 1) * half, tap * c_in : (tap + 1) * c_in] = value
        squares[...] = jnp.zeros_like(squares)

    conv = dot(lhs[...], w_ref[...].reshape(KW * c_in, tile), NN)
    root = 0.7978845608028654
    total = None
    for parity in range(2):
        x = conv[parity * half : (parity + 1) * half, :]
        square = x * x
        t = jnp.tanh(root * (x + 0.044715 * (square * x)))
        left = 0.5 * (1.0 + t)
        act = x * left
        slope = left + (0.5 * root) * x * (1.0 - t * t) * (1.0 + (3 * 0.044715) * square)
        slope_ref[parity] = slope.reshape(slope_ref.shape[1:])
        total = act if total is None else total + act
    skip = (0.5 * total).astype(BF)
    columns = pl.ds(pl.multiple_of(step * tile, tile), tile)
    skip_ref[:, :, columns] = skip.reshape(seqs, rows, tile)
    wide = skip.astype(F32)
    squares[...] += jnp.sum(wide * wide, axis=-1, keepdims=True)

    @pl.when(step == pl.num_programs(0) - 1)
    def _():
        width = skip_ref.shape[2]
        inv = lax.rsqrt(squares[...] * (1.0 / width) + 1e-06)
        wide = skip_ref[...].reshape(half, width).astype(F32)
        normed = (wide * inv * gain_ref[...]).astype(BF)
        whole_normed[...] = normed.reshape(whole_normed.shape)
        for slot in range(seqs):
            normed_refs[slot][...] = whole_normed[wrapped(at_ref[0] + slot, seqs)]


def encoder(at, pairs, low, high, conv_weight, norm_gain):
    _, seqs, rows, c_in = pairs.shape
    width = conv_weight.shape[2]
    tile = 256 if width % 256 == 0 else width
    shape = (seqs, rows, width)
    outs = pl.pallas_call(
        conv_kernel,
        grid=(width // tile,),
        in_specs=[
            SCALARS,
            whole(pairs.shape),
            whole(low.shape),
            whole(high.shape),
            pl.BlockSpec((KW, c_in, tile), lambda n: (0, 0, n)),
            whole((1, width)),
        ],
        out_specs=[
            whole(shape),
            pl.BlockSpec((2, seqs, rows, tile), lambda n: (0, 0, 0, n)),
        ]
        + [whole((rows, width))] * seqs,
        out_shape=[
            jax.ShapeDtypeStruct(shape, BF),
            jax.ShapeDtypeStruct((2,) + shape, F32),
        ]
        + [jax.ShapeDtypeStruct((rows, width), BF)] * seqs,
        scratch_shapes=[
            pltpu.VMEM((2 * seqs * rows, KW * c_in), BF),
            pltpu.VMEM((seqs * rows, 1), F32),
            pltpu.VMEM(shape, BF),
        ],
        compiler_params=params(),
        cost_estimate=COST,
        name="encoder_forward",
    )(at, pairs, low, high, conv_weight, norm_gain.reshape(1, width))
    return outs[0], outs[1], list(outs[2:])


def d_conv_body(seqs, at_ref, *refs):
    dn_refs = refs[:seqs]
    skip_ref, grad_ref, gain_ref, slope_ref, out_ref, first_ref, last_ref = refs[seqs:]
    rows = out_ref.shape[2]
    for slot in range(seqs):
        b = wrapped(at_ref[0] + slot, seqs)
        wide = skip_ref[b].astype(F32)
        inv = lax.rsqrt(jnp.mean(wide * wide, axis=-1, keepdims=True) + 1e-06)
        unit = wide * inv
        scaled = dn_refs[slot][...].astype(F32) * gain_ref[...]
        d_skip = grad_ref[b].astype(F32) + inv * (
            scaled - unit * jnp.mean(scaled * unit, axis=-1, keepdims=True)
        )
        d_act = 0.5 * d_skip
        for parity in range(2):
            value = slope_ref[parity, b] * d_act
            out_ref[parity, b] = value.astype(BF)
            first_ref[parity, b] = value[:1].astype(BF)
            last_ref[parity, b] = value[rows - 1 :].astype(BF)


def conv_gradient(at, d_normed, skip, grad, norm_gain, slope):
    seqs = len(d_normed)
    vmem = pl.BlockSpec(memory_space=pltpu.VMEM)
    edge = jax.ShapeDtypeStruct(slope.shape[:2] + (1, slope.shape[3]), BF)
    return pl.pallas_call(
        functools.partial(d_conv_body, seqs),
        in_specs=[SCALARS] + [vmem] * (seqs + 4),
        out_specs=[vmem] * 3,
        out_shape=[jax.ShapeDtypeStruct(slope.shape, BF)] + [edge] * 2,
        compiler_params=params(),
        cost_estimate=COST,
        name="conv_gradient",
    )(at, *d_normed, skip, grad, norm_gain.reshape(1, -1), slope)


def mixed_body(seqs, at_ref, *refs):
    skip_ref, out_ref = refs[seqs:]
    for slot in range(seqs):
        b = wrapped(at_ref[0] + slot, seqs)
        out_ref[b] = (skip_ref[b].astype(F32) + refs[slot][...].astype(F32)).astype(BF)


def mixed_call(at, terms, skip):
    seqs = len(terms)
    vmem = pl.BlockSpec(memory_space=pltpu.VMEM)
    return pl.pallas_call(
        functools.partial(mixed_body, seqs),
        in_specs=[SCALARS] + [vmem] * (seqs + 1),
        out_specs=vmem,
        out_shape=jax.ShapeDtypeStruct(skip.shape, BF),
        compiler_params=params(),
        cost_estimate=COST,
        name="mixed_sum",
    )(at, *terms, skip)


def conv_back_kernel(d_ref, low_ref, high_ref, w_ref, out_ref, turned, acc):
    step = pl.program_id(0)

    @pl.when(step == 0)
    def _():
        for parity in range(2):
            for shift in range(3):
                turned[parity, shift] = turned_rows(d_ref, low_ref, high_ref, parity, shift).T

    for tap in range(KW):

        @pl.when(step == tap)
        def _():
            places = [KW - 1 - tap, KW - tap]
            rhs = jnp.concatenate([turned[p % 2, p // 2] for p in places], axis=1)
            term = dot(w_ref[0], rhs, NN)
            if tap == 0:
                acc[...] = term
            elif tap < KW - 1:
                acc[...] += term
            else:
                out_ref[...] = (acc[...] + term).T.astype(BF)


def conv_back(d_conv, low, high, conv_weight):
    _, seqs, rows, width = d_conv.shape
    c_in = conv_weight.shape[1]
    flat = 2 * seqs * rows
    return pl.pallas_call(
        conv_back_kernel,
        grid=(KW,),
        in_specs=[
            whole(d_conv.shape),
            whole(low.shape),
            whole(high.shape),
            pl.BlockSpec((1, c_in, width), lambda k: (k, 0, 0)),
        ],
        out_specs=whole((flat, c_in)),
        out_shape=jax.ShapeDtypeStruct((flat, c_in), BF),
        scratch_shapes=[
            pltpu.VMEM((2, 3, width, seqs * rows), BF),
            pltpu.VMEM((c_in, flat), F32),
        ],
        compiler_params=params(),
        cost_estimate=COST,
        name="encoder_backward",
    )(d_conv, low, high, conv_weight)


def pack_kernel(w_ref, pack_ref, turned_ref):
    for i in range(3):
        for head in range(pack_ref.shape[0]):
            part = w_ref[i, :, head * DH : (head + 1) * DH]
            columns = slice(i * DH, (i + 1) * DH)
            pack_ref[head, :, columns] = part
            turned_ref[head, columns, :] = part.T


def pack_weights(w_qkv):
    _, width, local = w_qkv.shape
    heads = local // DH
    tile = local
    return pl.pallas_call(
        pack_kernel,
        grid=(width // tile,),
        in_specs=[pl.BlockSpec((3, tile, local), lambda n: (0, n, 0))],
        out_specs=[
            pl.BlockSpec((heads, tile, 3 * DH), lambda n: (0, n, 0)),
            pl.BlockSpec((heads, 3 * DH, tile), lambda n: (0, 0, n)),
        ],
        out_shape=[
            jax.ShapeDtypeStruct((heads, width, 3 * DH), BF),
            jax.ShapeDtypeStruct((heads, 3 * DH, width), BF),
        ],
        compiler_params=params(),
        cost_estimate=COST,
        name="pack_weights",
    )(w_qkv)


def product_kernel(head_ref, x_ref, w_ref, out_ref, *, contract):
    del head_ref
    value = dot(x_ref[...], w_ref[0], contract).astype(BF)
    out_ref[:, : value.shape[1]] = value
    if value.shape[1] < out_ref.shape[1]:
        out_ref[:, value.shape[1] :] = jnp.zeros_like(out_ref[:, value.shape[1] :])


def head_product(head, x, weight, contract, name):
    columns = weight.shape[2] if contract == NN else weight.shape[1]
    columns += -columns % 128
    rows, width = x.shape
    return pl.pallas_call(
        functools.partial(product_kernel, contract=contract),
        grid_spec=pltpu.PrefetchScalarGridSpec(
            num_scalar_prefetch=1,
            grid=(1,),
            in_specs=[
                pl.BlockSpec((rows, width), lambda i, head: (0, 0)),
                pl.BlockSpec((1,) + weight.shape[1:], lambda i, head: (head[0], 0, 0)),
            ],
            out_specs=pl.BlockSpec((rows, columns), lambda i, head: (0, 0)),
        ),
        out_shape=jax.ShapeDtypeStruct((rows, columns), BF),
        compiler_params=params(),
        cost_estimate=COST,
        name=name,
    )(head, x, weight)


def attention_kernel(qa_ref, qb_ref, da_ref, db_ref, oa_ref, ob_ref, k_all, v_all, dk_acc, dv_acc, *, block):
    scale = DH ** (-0.5)
    half = qa_ref.shape[0]
    for place, ref in enumerate((qa_ref, qb_ref)):
        rows = pl.ds(place * half, half)
        k_all[rows, :] = ref[:, DH : 2 * DH]
        v_all[rows, :] = ref[:, 2 * DH : 3 * DH]
    k = k_all[...]
    v = v_all[...]
    for place, (q_ref, d_ref, out_ref) in enumerate(
        ((qa_ref, da_ref, oa_ref), (qb_ref, db_ref, ob_ref))
    ):
        for start in range(0, half, block):
            rows = pl.ds(start, block)
            q = q_ref[rows, 0:DH]
            d_o = d_ref[rows, 0:DH]
            s = dot(q, k, NT) * scale
            e = jnp.exp(s - jnp.max(s, axis=-1, keepdims=True))
            p = e * (1.0 / jnp.sum(e, axis=-1, keepdims=True))
            p_b = p.astype(BF)
            o = dot(p_b, v, NN)
            delta = jnp.sum(d_o.astype(F32) * o, axis=-1, keepdims=True)
            d_p = dot(d_o, v, NT)
            ds = (p * (d_p - delta)).astype(BF)
            dq = scale * dot(ds, k, NN)
            dk = dot(ds, q, TN)
            dv = dot(p_b, d_o, TN)
            if place == 0 and start == 0:
                dk_acc[...] = dk
                dv_acc[...] = dv
            else:
                dk_acc[...] += dk
                dv_acc[...] += dv
            out_ref[rows, 0:DH] = dq.astype(BF)
            out_ref[rows, 3 * DH : 4 * DH] = o.astype(BF)
    for place, out_ref in enumerate((oa_ref, ob_ref)):
        rows = pl.ds(place * half, half)
        out_ref[:, DH : 2 * DH] = (scale * dk_acc[rows, :]).astype(BF)
        out_ref[:, 2 * DH : 3 * DH] = dv_acc[rows, :].astype(BF)


def attention(qkv_a, qkv_b, d_a, d_b):
    half = qkv_a.shape[0]
    shape = jax.ShapeDtypeStruct((half, 4 * DH), BF)
    return pl.pallas_call(
        functools.partial(attention_kernel, block=min(256, half)),
        out_shape=[shape, shape],
        scratch_shapes=[
            pltpu.VMEM((2 * half, DH), BF),
            pltpu.VMEM((2 * half, DH), BF),
            pltpu.VMEM((2 * half, DH), F32),
            pltpu.VMEM((2 * half, DH), F32),
        ],
        compiler_params=params(),
        cost_estimate=COST,
        name="attention",
    )(qkv_a, qkv_b, d_a, d_b)


def term_kernel(head_ref, a_ref, b_ref, w_ref, *out_refs, first, last):
    head = head_ref[0]
    total = dot(a_ref[:, first:last], w_ref[head], NN)
    total += dot(b_ref[:, first:last], w_ref[1 - head], NN)
    count = len(out_refs)
    size = out_refs[0].shape[0]
    value = total.astype(BF)
    if count == 1:
        out_refs[0][...] = value
        return
    for block in range(count):
        for slot, out_ref in enumerate(out_refs):

            @pl.when(wrapped(block - head_ref[1], count) == slot)
            def _():
                out_ref[...] = value[block * size : (block + 1) * size]


def pair_term(place, mine, got, weight, slots, first, last, name):
    half, full = mine.shape
    heads, depth, width = weight.shape
    size = half // slots
    tile = 512 if width % 512 == 0 else width
    return pl.pallas_call(
        functools.partial(term_kernel, first=first, last=last),
        grid_spec=pltpu.PrefetchScalarGridSpec(
            num_scalar_prefetch=1,
            grid=(width // tile,),
            in_specs=[
                pl.BlockSpec((half, full), lambda n, at: (0, 0)),
                pl.BlockSpec((half, full), lambda n, at: (0, 0)),
                pl.BlockSpec((heads, depth, tile), lambda n, at: (0, 0, n)),
            ],
            out_specs=[pl.BlockSpec((size, tile), lambda n, at: (0, n))] * slots,
        ),
        out_shape=[jax.ShapeDtypeStruct((size, width), BF)] * slots,
        compiler_params=params(),
        cost_estimate=COST,
        name=name,
    )(place, mine, got, weight)


def sum_kernel(*refs):
    total = refs[0][...].astype(F32)
    for ref in refs[1:-1]:
        total = total + ref[...].astype(F32)
    refs[-1][...] = total.astype(BF)


def summed(parts, name):
    return pl.pallas_call(
        sum_kernel,
        out_shape=jax.ShapeDtypeStruct(parts[0].shape, BF),
        compiler_params=params(),
        cost_estimate=COST,
        name=name,
    )(*parts)


def weight_kernel(at_ref, xa_ref, xb_ref, ga_ref, gb_ref, ra_ref, rb_ref, *rest):
    del at_ref
    out_refs, turned = rest[:-1], rest[-1]
    step = pl.program_id(0)
    half = ra_ref.shape[0]
    split = 3 * DH

    @pl.when(step == 0)
    def _():
        turned[:, :half] = ra_ref[...].T
        turned[:, half:] = rb_ref[...].T

    a, b = slice(0, half), slice(half, 2 * half)
    qkv = dot(turned[:split, a], xa_ref[...], NN) + dot(turned[:split, b], xb_ref[...], NN)
    out = dot(turned[split:, a], ga_ref[...], NN) + dot(turned[split:, b], gb_ref[...], NN)
    for slot, out_ref in enumerate(out_refs):

        @pl.when(step == slot)
        def _():
            out_ref[:split, :] = qkv.astype(BF)
            out_ref[split:, :] = out.astype(BF)


def weight_gradients(at, xa, xb, ga, gb, ra, rb, seqs):
    half, width = xa.shape
    chunk = width // seqs
    full = ra.shape[1]
    column = pl.BlockSpec((half, chunk), lambda r, at: (0, lax.rem(r + at[0], seqs)))
    rest = pl.BlockSpec((half, full), lambda r, at: (0, 0))
    return pl.pallas_call(
        weight_kernel,
        grid_spec=pltpu.PrefetchScalarGridSpec(
            num_scalar_prefetch=1,
            grid=(seqs,),
            in_specs=[column] * 4 + [rest] * 2,
            out_specs=[pl.BlockSpec((full, chunk), lambda r, at: (0, 0))] * seqs,
            scratch_shapes=[pltpu.VMEM((full, 2 * half), BF)],
        ),
        out_shape=[jax.ShapeDtypeStruct((full, chunk), BF)] * seqs,
        compiler_params=params(),
        cost_estimate=COST,
        name="weight_gradients",
    )(at, xa, xb, ga, gb, ra, rb)


def weight_sum_kernel(*refs):
    out_ref = refs[-1]
    split = 3 * DH
    total = refs[0][...].astype(F32)
    for ref in refs[1:-1]:
        total = total + ref[...].astype(F32)
    out_ref[:, :split] = total[:split].T.astype(BF)
    for part in range(2):
        rows = slice(part * DH, (part + 1) * DH)
        out_ref[rows, split:] = total[split:, rows].astype(BF)


def weight_sum(parts):
    full, chunk = parts[0].shape
    return pl.pallas_call(
        weight_sum_kernel,
        out_shape=jax.ShapeDtypeStruct((chunk, full), BF),
        compiler_params=params(),
        cost_estimate=COST,
        name="weight_sum",
    )(*parts)


def unpack_kernel(at_ref, mine_ref, other_ref, qkv_ref, out_ref):
    first_head = at_ref[0] == 0
    mine = mine_ref[0].astype(F32)
    other = other_ref[0].astype(F32)
    low = jnp.where(first_head, mine, other)
    high = jnp.where(first_head, other, mine)
    split = 3 * DH
    for i in range(3):
        columns = slice(i * DH, (i + 1) * DH)
        qkv_ref[i] = jnp.concatenate([low[:, columns], high[:, columns]], axis=1)
    for head, value in enumerate((low, high)):
        halves = [value[part * DH : (part + 1) * DH, split:] for part in range(2)]
        out_ref[head * DH : (head + 1) * DH, :] = jnp.concatenate(halves, axis=1)


def unpack_weights(at, mine, other):
    seqs, chunk, full = mine.shape
    width = chunk * seqs
    local = 2 * DH
    block = pl.BlockSpec((1, chunk, full), lambda r: (r, 0, 0))
    return pl.pallas_call(
        unpack_kernel,
        grid=(seqs,),
        in_specs=[SCALARS, block, block],
        out_specs=[
            pl.BlockSpec((3, chunk, local), lambda r: (0, r, 0)),
            pl.BlockSpec((local, chunk), lambda r: (0, r)),
        ],
        out_shape=[
            jax.ShapeDtypeStruct((3, width, local), F32),
            jax.ShapeDtypeStruct((local, width), F32),
        ],
        compiler_params=params(),
        cost_estimate=COST,
        name="weight_outputs",
    )(at, mine, other)


def neighbour_edges(first, last):
    axes = ("seq", "head")
    count = lax.axis_size(axes)
    forward = [(i, i + 1) for i in range(count - 1)]
    backward = [(target, source) for source, target in forward]
    return lax.ppermute(last, axes, forward), lax.ppermute(first, axes, backward)


def after(value, *others):
    return lax.optimization_barrier((value,) + others)[0]


def send_chip(x, step, heads):
    count = lax.axis_size("seq")
    return lax.ppermute(x, "seq", [(s, (s + step * heads) % count) for s in range(count)])


def send_z(x, step):
    count = lax.axis_size("head")
    return lax.ppermute(x, "head", [(z, (z + step) % count) for z in range(count)])


def swap_heads(x):
    count = lax.axis_size("seq")
    return lax.ppermute(x, "seq", [(s, s + 1 - 2 * (s % 2)) for s in range(count)])


def unit_body(enc_in, conv_weight, norm_gain, w_qkv, w_out, grad_out):
    rows = enc_in.shape[0] // 2
    seqs = enc_in.shape[1]
    width = conv_weight.shape[2]
    local = w_qkv.shape[2]
    heads = local // DH
    groups = lax.axis_size("head")
    half = groups * seqs * rows
    place = lax.axis_index("seq")
    own_seq = (place // heads).astype(jnp.int32)
    own_head = (place % heads).astype(jnp.int32)
    own_z = lax.axis_index("head").astype(jnp.int32)
    zero = jnp.zeros((), jnp.int32)
    at = jnp.stack([own_seq, own_head])
    head_mine = own_head.reshape(1)
    head_other = (1 - own_head).reshape(1)

    def to_chips(slots):
        return [slots[r] if r == 0 else send_chip(slots[r], r, heads) for r in range(seqs)]

    def from_chips(slots):
        return [slots[r] if r == 0 else send_chip(slots[r], -r, heads) for r in range(seqs)]

    grad = jnp.transpose(grad_out, (1, 0, 2))
    grad_z = lax.all_gather(grad, "head", axis=0, tiled=False)
    pairs = jnp.transpose(enc_in.reshape(rows, 2, seqs, enc_in.shape[2]), (1, 2, 0, 3))
    low, high = neighbour_edges(pairs[:, :, :1, :], pairs[:, :, -1:, :])
    skip, slope, normed = encoder(at, pairs, low, high, conv_weight, norm_gain)
    normed_slab = jnp.concatenate(to_chips(normed), axis=0)
    normed_rows = lax.all_gather(normed_slab, "head", axis=0, tiled=True)

    grad_z = after(grad_z, normed_slab)
    grad_slots = [
        lax.dynamic_index_in_dim(grad_z, (own_seq + r) % seqs, 1, keepdims=False)
        for r in range(seqs)
    ]
    grad_rows = jnp.stack(to_chips(grad_slots), axis=1).reshape(half, width)
    w_pack, w_turned = pack_weights(after(w_qkv, normed_slab))
    w_rows = w_out.reshape(heads, DH, width)
    d_got = swap_heads(head_product(head_other, grad_rows, w_rows, NT, "d_o_other"))
    d_mine = head_product(head_mine, grad_rows, w_rows, NT, "d_o_own")
    grad_swapped = swap_heads(grad_rows)
    normed_rows = after(normed_rows, d_got, d_mine, grad_swapped, w_pack, w_turned)

    qkv_got = swap_heads(head_product(head_other, normed_rows, w_pack, NN, "qkv_other"))
    normed_swapped = swap_heads(normed_rows)
    qkv_mine = head_product(head_mine, normed_rows, w_pack, NN, "qkv_own")
    qkv_mine = after(qkv_mine, normed_swapped)
    result_mine, result_other = attention(qkv_mine, qkv_got, d_mine, d_got)
    result_got = swap_heads(result_other)

    plain = jnp.stack([own_head, zero])
    (d_term,) = pair_term(plain, result_mine, result_got, w_turned, 1, 0, 3 * DH, "d_term")
    d_normed = lax.psum_scatter(
        d_term.reshape(groups, seqs, rows, width), "head", scatter_dimension=0, tiled=False
    )
    part = weight_gradients(
        own_seq.reshape(1),
        normed_rows,
        normed_swapped,
        grad_rows,
        grad_swapped,
        result_mine,
        result_other,
        seqs,
    )
    part = to_chips(part)
    turned = jnp.stack([own_head, own_z])
    head_term = pair_term(
        turned, result_mine, result_got, w_rows, groups, 3 * DH, 4 * DH, "head_term"
    )
    head_slots = [head_term[0], send_z(head_term[1], 1)]
    head_slots += [send_z(after(head_term[q], d_normed), q) for q in range(2, groups)]
    part = [after(p, d_normed) for p in part]
    d_normed = from_chips([d_normed[r] for r in range(seqs)])
    chunk = weight_sum(part)
    same_head = [[b * heads + h for b in range(seqs)] for h in range(heads)]
    chunks = lax.all_gather(chunk, "seq", axis_index_groups=same_head)

    d_conv, first, last = conv_gradient(at, d_normed, skip, grad, norm_gain, slope)
    low, high = neighbour_edges(first, last)
    grad_input = conv_back(d_conv, low, high, conv_weight)

    head_slots = [after(h, low, high) for h in head_slots]
    head_sum = summed(head_slots, "head_sum").reshape(seqs, rows, width)
    head_sum = from_chips([head_sum[r] for r in range(seqs)])
    mixed = mixed_call(at, head_sum, skip)
    chunks = after(chunks, grad_input)
    grad_w_qkv, grad_w_out = unpack_weights(head_mine, chunks, swap_heads(chunks))
    grad_input = jnp.transpose(grad_input.reshape(2, seqs, rows, -1), (2, 0, 1, 3))
    return (
        jnp.transpose(mixed, (1, 0, 2)),
        grad_input.reshape(enc_in.shape),
        grad_w_qkv,
        grad_w_out,
    )


def padded_2(block, sides, width):
    for axis, dim in sides:
        count = lax.axis_size(axis)
        forward = [(i, i + 1) for i in range(count - 1)]
        backward = [(target, source) for source, target in forward]
        low = lax.ppermute(
            lax.slice_in_dim(block, block.shape[dim] - width, None, axis=dim), axis, forward
        )
        high = lax.ppermute(lax.slice_in_dim(block, 0, width, axis=dim), axis, backward)
        block = jnp.concatenate([low, block, high], axis=dim)
    return block


def gathered_body(enc_in, conv_weight, norm_gain, w_qkv, w_out, grad_out):
    fine_rows = enc_in.shape[0]
    slab_rows = fine_rows // 2
    seq_count = enc_in.shape[1]
    out_width = conv_weight.shape[2]
    local_width = w_qkv.shape[2]
    local_heads = local_width // DH
    logit_scale = DH ** (-0.5)
    padded = padded_2(enc_in, ((("seq", "head"), 0),), 2)
    convolved = jnp.zeros((fine_rows, seq_count, out_width), jnp.float32)
    for offset in range(KW):
        convolved = convolved + jnp.einsum(
            "tbi,io->tbo",
            padded[offset : offset + fine_rows],
            conv_weight[offset],
            preferred_element_type=jnp.float32,
        )
    activated, gelu_pull = jax.vjp(jax.nn.gelu, convolved)
    skip = jnp.mean(activated.reshape(slab_rows, 2, seq_count, out_width), axis=1).astype(
        jnp.bfloat16
    )
    skip_wide = skip.astype(jnp.float32)
    inv_rms = lax.rsqrt(jnp.mean(skip_wide * skip_wide, axis=-1, keepdims=True) + 1e-06)
    normed = (skip_wide * inv_rms * norm_gain).astype(jnp.bfloat16)
    normed_rows = lax.all_gather(normed, "head", axis=0, tiled=True)
    grad_rows = lax.all_gather(grad_out, "head", axis=0, tiled=True)
    tower_rows = normed_rows.shape[0]
    qkv = jnp.einsum(
        "tbc,ice->itbe", normed_rows, w_qkv, preferred_element_type=jnp.float32
    ).astype(jnp.bfloat16)
    qkv = qkv.reshape(3, tower_rows, seq_count, local_heads, DH)
    query_matrix, key_matrix, value_matrix = (qkv[0], qkv[1], qkv[2])
    key_all, value_all = (
        lax.all_gather(key_matrix, "seq", axis=0, tiled=True),
        lax.all_gather(value_matrix, "seq", axis=0, tiled=True),
    )
    attention_logits = (
        jnp.einsum("qbhd,kbhd->bhqk", query_matrix, key_all, preferred_element_type=jnp.float32)
        * logit_scale
    )
    row_peak = jnp.max(attention_logits, axis=-1, keepdims=True)
    exponent = jnp.exp(attention_logits - row_peak)
    row_total = jnp.sum(exponent, axis=-1, keepdims=True)
    soft_weights = exponent / row_total
    narrow_probabilities = soft_weights.astype(jnp.bfloat16)
    attention_output = jnp.einsum(
        "bhqk,kbhd->qbhd", narrow_probabilities, value_all, preferred_element_type=jnp.float32
    )
    o_narrow = attention_output.reshape(tower_rows, seq_count, local_width).astype(jnp.bfloat16)
    piece = o_narrow
    head_sum = lax.psum_scatter(
        jnp.einsum("tbe,ec->tbc", piece, w_out, preferred_element_type=jnp.float32).astype(
            jnp.bfloat16
        ),
        "head",
        scatter_dimension=0,
        tiled=True,
    ).astype(jnp.float32)
    mixed = (skip_wide + head_sum).astype(jnp.bfloat16)
    part_w_out = jnp.einsum("tbe,tbc->ec", o_narrow, grad_rows, preferred_element_type=jnp.float32)
    d_out = jnp.einsum("tbc,ec->tbe", grad_rows, w_out, preferred_element_type=jnp.float32).astype(
        jnp.bfloat16
    )
    d_out = d_out.reshape(tower_rows, seq_count, local_heads, DH)
    delta = jnp.sum(d_out.astype(jnp.float32) * attention_output, axis=-1)
    probability_gradient = jnp.einsum(
        "qbhd,kbhd->bhqk", d_out, value_all, preferred_element_type=jnp.float32
    )
    d_scores = soft_weights * (probability_gradient - jnp.transpose(delta, (1, 2, 0))[..., None])
    narrow_gradient = d_scores.astype(jnp.bfloat16)
    query_gradient = logit_scale * jnp.einsum(
        "bhqk,kbhd->qbhd", narrow_gradient, key_all, preferred_element_type=jnp.float32
    )
    key_terms = logit_scale * jnp.einsum(
        "bhqk,qbhd->kbhd", narrow_gradient, query_matrix, preferred_element_type=jnp.float32
    )
    value_terms = jnp.einsum(
        "bhqk,qbhd->kbhd", narrow_probabilities, d_out, preferred_element_type=jnp.float32
    )
    d_keys, d_values = (
        lax.psum_scatter(
            key_terms.astype(jnp.bfloat16), "seq", scatter_dimension=0, tiled=True
        ).astype(jnp.float32),
        lax.psum_scatter(
            value_terms.astype(jnp.bfloat16), "seq", scatter_dimension=0, tiled=True
        ).astype(jnp.float32),
    )
    dqkv = (
        jnp.stack([query_gradient, d_keys, d_values])
        .reshape(3, tower_rows, seq_count, local_width)
        .astype(jnp.bfloat16)
    )
    part_w_qkv = jnp.einsum("tbc,itbe->ice", normed_rows, dqkv, preferred_element_type=jnp.float32)
    piece = dqkv
    d_normed = lax.psum_scatter(
        jnp.einsum("itbe,ice->tbc", piece, w_qkv, preferred_element_type=jnp.float32).astype(
            jnp.bfloat16
        ),
        "head",
        scatter_dimension=0,
        tiled=True,
    ).astype(jnp.float32)
    unit_rows = skip_wide * inv_rms
    scaled = d_normed * norm_gain
    d_skip = grad_out.astype(jnp.float32) + inv_rms * (
        scaled - unit_rows * jnp.mean(scaled * unit_rows, axis=-1, keepdims=True)
    )
    d_act = jnp.repeat(d_skip, 2, axis=0) * 0.5
    d_conv = gelu_pull(d_act)[0].astype(jnp.bfloat16)
    d_pad = padded_2(d_conv, ((("seq", "head"), 0),), 2)
    grad_input = jnp.zeros((fine_rows, seq_count, enc_in.shape[2]), jnp.float32)
    for offset in range(KW):
        grad_input = grad_input + jnp.einsum(
            "tbo,io->tbi",
            d_pad[4 - offset : 4 - offset + fine_rows],
            conv_weight[offset],
            preferred_element_type=jnp.float32,
        )
    grad_w_qkv, grad_w_out = (
        lax.psum(part_w_qkv.astype(jnp.bfloat16), "seq").astype(jnp.float32),
        lax.psum(part_w_out.astype(jnp.bfloat16), "seq").astype(jnp.float32),
    )
    return (mixed, grad_input.astype(jnp.bfloat16), grad_w_qkv, grad_w_out)


def body(enc_in, conv_weight, norm_gain, w_qkv, w_out, grad_out):
    heads = w_qkv.shape[2] // DH
    seqs = enc_in.shape[1]
    fits = heads == 2 and seqs * heads == lax.axis_size("seq")
    fits = fits and conv_weight.shape[2] == seqs * w_qkv.shape[2]
    chosen = unit_body if fits else gathered_body
    return chosen(enc_in, conv_weight, norm_gain, w_qkv, w_out, grad_out)


def solution(mesh):
    return jax.shard_map(
        body,
        mesh=mesh,
        in_specs=(
            P(("seq", "head"), None, None),
            P(),
            P(),
            P(None, None, "head"),
            P("head", None),
            P(("seq", "head"), None, None),
        ),
        out_specs=(
            P(("seq", "head"), None, None),
            P(("seq", "head"), None, None),
            P(None, None, "head"),
            P("head", None),
        ),
        check_vma=False,
    )
```

```python
import functools

import jax
import jax.numpy as jnp
from jax import lax
from jax.experimental import pallas as pl
from jax.experimental.pallas import tpu as pltpu
from jax.sharding import PartitionSpec as P

DH = 192
KW = 5
VMEM_LIMIT = 24 * 1024 * 1024
COST = pl.CostEstimate(flops=1000, bytes_accessed=1000, transcendentals=0)
BF = jnp.bfloat16
F32 = jnp.float32


def params():
    return pltpu.CompilerParams(vmem_limit_bytes=VMEM_LIMIT)


def dot(a, b, contract):
    return lax.dot_general(a, b, (contract, ((), ())), preferred_element_type=F32)


NN = ((1,), (0,))
NT = ((1,), (1,))
TN = ((0,), (0,))


def whole(shape):
    return pl.BlockSpec(shape, lambda *_: (0,) * len(shape))


SCALARS = pl.BlockSpec(memory_space=pltpu.SMEM)


def wrapped(value, size):
    return jnp.where(value < 0, value + size, jnp.where(value >= size, value - size, value))


def turned_rows(ref, low_ref, high_ref, parity, shift):
    seqs, rows, width = ref.shape[1:]
    own = ref[parity]
    if shift != 1:
        wide = own.astype(F32)
        if shift == 0:
            parts = [low_ref[parity].astype(F32), wide[:, : rows - 1]]
        else:
            parts = [wide[:, 1:], high_ref[parity].astype(F32)]
        own = jnp.concatenate(parts, axis=1).astype(BF)
    return own.reshape(seqs * rows, width)


def conv_kernel(
    at_ref, x_ref, low_ref, high_ref, w_ref, gain_ref, skip_ref, slope_ref, *rest
):
    normed_refs, (lhs, squares, whole_normed) = rest[:-3], rest[-3:]
    step = pl.program_id(0)
    seqs, rows, c_in = x_ref.shape[1:]
    half = seqs * rows
    tile = w_ref.shape[2]

    @pl.when(step == 0)
    def _():
        for parity in range(2):
            for shift in range(3):
                value = turned_rows(x_ref, low_ref, high_ref, parity, shift)
                for out in range(2):
                    tap = 2 * shift + parity - out
                    if 0 <= tap < KW:
                        lhs[out * half : (out + 1) * half, tap * c_in : (tap + 1) * c_in] = value
        squares[...] = jnp.zeros_like(squares)

    conv = dot(lhs[...], w_ref[...].reshape(KW * c_in, tile), NN)
    root = 0.7978845608028654
    total = None
    for parity in range(2):
        x = conv[parity * half : (parity + 1) * half, :]
        square = x * x
        t = jnp.tanh(root * (x + 0.044715 * (square * x)))
        left = 0.5 * (1.0 + t)
        act = x * left
        slope = left + (0.5 * root) * x * (1.0 - t * t) * (1.0 + (3 * 0.044715) * square)
        slope_ref[parity] = slope.reshape(slope_ref.shape[1:])
        total = act if total is None else total + act
    skip = (0.5 * total).astype(BF)
    columns = pl.ds(pl.multiple_of(step * tile, tile), tile)
    skip_ref[:, :, columns] = skip.reshape(seqs, rows, tile)
    wide = skip.astype(F32)
    squares[...] += jnp.sum(wide * wide, axis=-1, keepdims=True)

    @pl.when(step == pl.num_programs(0) - 1)
    def _():
        width = skip_ref.shape[2]
        inv = lax.rsqrt(squares[...] * (1.0 / width) + 1e-06)
        wide = skip_ref[...].reshape(half, width).astype(F32)
        normed = (wide * inv * gain_ref[...]).astype(BF)
        whole_normed[...] = normed.reshape(whole_normed.shape)
        for slot in range(seqs):
            normed_refs[slot][...] = whole_normed[wrapped(at_ref[0] + slot, seqs)]


def encoder(at, pairs, low, high, conv_weight, norm_gain):
    _, seqs, rows, c_in = pairs.shape
    width = conv_weight.shape[2]
    tile = 256 if width % 256 == 0 else width
    shape = (seqs, rows, width)
    outs = pl.pallas_call(
        conv_kernel,
        grid=(width // tile,),
        in_specs=[
            SCALARS,
            whole(pairs.shape),
            whole(low.shape),
            whole(high.shape),
            pl.BlockSpec((KW, c_in, tile), lambda n: (0, 0, n)),
            whole((1, width)),
        ],
        out_specs=[
            whole(shape),
            pl.BlockSpec((2, seqs, rows, tile), lambda n: (0, 0, 0, n)),
        ]
        + [whole((rows, width))] * seqs,
        out_shape=[
            jax.ShapeDtypeStruct(shape, BF),
            jax.ShapeDtypeStruct((2,) + shape, F32),
        ]
        + [jax.ShapeDtypeStruct((rows, width), BF)] * seqs,
        scratch_shapes=[
            pltpu.VMEM((2 * seqs * rows, KW * c_in), BF),
            pltpu.VMEM((seqs * rows, 1), F32),
            pltpu.VMEM(shape, BF),
        ],
        compiler_params=params(),
        cost_estimate=COST,
        name="encoder_forward",
    )(at, pairs, low, high, conv_weight, norm_gain.reshape(1, width))
    return outs[0], outs[1], list(outs[2:])


def d_conv_body(seqs, at_ref, *refs):
    dn_refs = refs[:seqs]
    skip_ref, grad_ref, gain_ref, slope_ref, out_ref, first_ref, last_ref = refs[seqs:]
    rows = out_ref.shape[2]
    for slot in range(seqs):
        b = wrapped(at_ref[0] + slot, seqs)
        wide = skip_ref[b].astype(F32)
        inv = lax.rsqrt(jnp.mean(wide * wide, axis=-1, keepdims=True) + 1e-06)
        unit = wide * inv
        scaled = dn_refs[slot][...].astype(F32) * gain_ref[...]
        d_skip = grad_ref[b].astype(F32) + inv * (
            scaled - unit * jnp.mean(scaled * unit, axis=-1, keepdims=True)
        )
        d_act = 0.5 * d_skip
        for parity in range(2):
            value = slope_ref[parity, b] * d_act
            out_ref[parity, b] = value.astype(BF)
            first_ref[parity, b] = value[:1].astype(BF)
            last_ref[parity, b] = value[rows - 1 :].astype(BF)


def conv_gradient(at, d_normed, skip, grad, norm_gain, slope):
    seqs = len(d_normed)
    vmem = pl.BlockSpec(memory_space=pltpu.VMEM)
    edge = jax.ShapeDtypeStruct(slope.shape[:2] + (1, slope.shape[3]), BF)
    return pl.pallas_call(
        functools.partial(d_conv_body, seqs),
        in_specs=[SCALARS] + [vmem] * (seqs + 4),
        out_specs=[vmem] * 3,
        out_shape=[jax.ShapeDtypeStruct(slope.shape, BF)] + [edge] * 2,
        compiler_params=params(),
        cost_estimate=COST,
        name="conv_gradient",
    )(at, *d_normed, skip, grad, norm_gain.reshape(1, -1), slope)


def mixed_body(seqs, at_ref, *refs):
    skip_ref, out_ref = refs[seqs:]
    for slot in range(seqs):
        b = wrapped(at_ref[0] + slot, seqs)
        out_ref[b] = (skip_ref[b].astype(F32) + refs[slot][...].astype(F32)).astype(BF)


def mixed_call(at, terms, skip):
    seqs = len(terms)
    vmem = pl.BlockSpec(memory_space=pltpu.VMEM)
    return pl.pallas_call(
        functools.partial(mixed_body, seqs),
        in_specs=[SCALARS] + [vmem] * (seqs + 1),
        out_specs=vmem,
        out_shape=jax.ShapeDtypeStruct(skip.shape, BF),
        compiler_params=params(),
        cost_estimate=COST,
        name="mixed_sum",
    )(at, *terms, skip)


def conv_back_kernel(d_ref, low_ref, high_ref, w_ref, out_ref, turned, acc):
    step = pl.program_id(0)

    @pl.when(step == 0)
    def _():
        for parity in range(2):
            for shift in range(3):
                turned[parity, shift] = turned_rows(d_ref, low_ref, high_ref, parity, shift).T

    for tap in range(KW):

        @pl.when(step == tap)
        def _():
            places = [KW - 1 - tap, KW - tap]
            rhs = jnp.concatenate([turned[p % 2, p // 2] for p in places], axis=1)
            term = dot(w_ref[0], rhs, NN)
            if tap == 0:
                acc[...] = term
            elif tap < KW - 1:
                acc[...] += term
            else:
                out_ref[...] = (acc[...] + term).T.astype(BF)


def conv_back(d_conv, low, high, conv_weight):
    _, seqs, rows, width = d_conv.shape
    c_in = conv_weight.shape[1]
    flat = 2 * seqs * rows
    return pl.pallas_call(
        conv_back_kernel,
        grid=(KW,),
        in_specs=[
            whole(d_conv.shape),
            whole(low.shape),
            whole(high.shape),
            pl.BlockSpec((1, c_in, width), lambda k: (k, 0, 0)),
        ],
        out_specs=whole((flat, c_in)),
        out_shape=jax.ShapeDtypeStruct((flat, c_in), BF),
        scratch_shapes=[
            pltpu.VMEM((2, 3, width, seqs * rows), BF),
            pltpu.VMEM((c_in, flat), F32),
        ],
        compiler_params=params(),
        cost_estimate=COST,
        name="encoder_backward",
    )(d_conv, low, high, conv_weight)


def pack_kernel(w_ref, pack_ref, turned_ref):
    for i in range(3):
        for head in range(pack_ref.shape[0]):
            part = w_ref[i, :, head * DH : (head + 1) * DH]
            columns = slice(i * DH, (i + 1) * DH)
            pack_ref[head, :, columns] = part
            turned_ref[head, columns, :] = part.T


def pack_weights(w_qkv):
    _, width, local = w_qkv.shape
    heads = local // DH
    tile = local
    return pl.pallas_call(
        pack_kernel,
        grid=(width // tile,),
        in_specs=[pl.BlockSpec((3, tile, local), lambda n: (0, n, 0))],
        out_specs=[
            pl.BlockSpec((heads, tile, 3 * DH), lambda n: (0, n, 0)),
            pl.BlockSpec((heads, 3 * DH, tile), lambda n: (0, 0, n)),
        ],
        out_shape=[
            jax.ShapeDtypeStruct((heads, width, 3 * DH), BF),
            jax.ShapeDtypeStruct((heads, 3 * DH, width), BF),
        ],
        compiler_params=params(),
        cost_estimate=COST,
        name="pack_weights",
    )(w_qkv)


def product_kernel(head_ref, x_ref, w_ref, out_ref, *, contract):
    del head_ref
    value = dot(x_ref[...], w_ref[0], contract).astype(BF)
    out_ref[:, : value.shape[1]] = value
    if value.shape[1] < out_ref.shape[1]:
        out_ref[:, value.shape[1] :] = jnp.zeros_like(out_ref[:, value.shape[1] :])


def head_product(head, x, weight, contract, name):
    columns = weight.shape[2] if contract == NN else weight.shape[1]
    columns += -columns % 128
    rows, width = x.shape
    return pl.pallas_call(
        functools.partial(product_kernel, contract=contract),
        grid_spec=pltpu.PrefetchScalarGridSpec(
            num_scalar_prefetch=1,
            grid=(1,),
            in_specs=[
                pl.BlockSpec((rows, width), lambda i, head: (0, 0)),
                pl.BlockSpec((1,) + weight.shape[1:], lambda i, head: (head[0], 0, 0)),
            ],
            out_specs=pl.BlockSpec((rows, columns), lambda i, head: (0, 0)),
        ),
        out_shape=jax.ShapeDtypeStruct((rows, columns), BF),
        compiler_params=params(),
        cost_estimate=COST,
        name=name,
    )(head, x, weight)


def attention_kernel(qa_ref, qb_ref, da_ref, db_ref, oa_ref, ob_ref, k_all, v_all, dk_acc, dv_acc, *, block):
    scale = DH ** (-0.5)
    half = qa_ref.shape[0]
    for place, ref in enumerate((qa_ref, qb_ref)):
        rows = pl.ds(place * half, half)
        k_all[rows, :] = ref[:, DH : 2 * DH]
        v_all[rows, :] = ref[:, 2 * DH : 3 * DH]
    k = k_all[...]
    v = v_all[...]
    for place, (q_ref, d_ref, out_ref) in enumerate(
        ((qa_ref, da_ref, oa_ref), (qb_ref, db_ref, ob_ref))
    ):
        for start in range(0, half, block):
            rows = pl.ds(start, block)
            q = q_ref[rows, 0:DH]
            d_o = d_ref[rows, 0:DH]
            s = dot(q, k, NT) * scale
            e = jnp.exp(s - jnp.max(s, axis=-1, keepdims=True))
            p = e * (1.0 / jnp.sum(e, axis=-1, keepdims=True))
            p_b = p.astype(BF)
            o = dot(p_b, v, NN)
            delta = jnp.sum(d_o.astype(F32) * o, axis=-1, keepdims=True)
            d_p = dot(d_o, v, NT)
            ds = (p * (d_p - delta)).astype(BF)
            dq = scale * dot(ds, k, NN)
            dk = dot(ds, q, TN)
            dv = dot(p_b, d_o, TN)
            if place == 0 and start == 0:
                dk_acc[...] = dk
                dv_acc[...] = dv
            else:
                dk_acc[...] += dk
                dv_acc[...] += dv
            out_ref[rows, 0:DH] = dq.astype(BF)
            out_ref[rows, 3 * DH : 4 * DH] = o.astype(BF)
    for place, out_ref in enumerate((oa_ref, ob_ref)):
        rows = pl.ds(place * half, half)
        out_ref[:, DH : 2 * DH] = (scale * dk_acc[rows, :]).astype(BF)
        out_ref[:, 2 * DH : 3 * DH] = dv_acc[rows, :].astype(BF)


def attention(qkv_a, qkv_b, d_a, d_b):
    half = qkv_a.shape[0]
    shape = jax.ShapeDtypeStruct((half, 4 * DH), BF)
    return pl.pallas_call(
        functools.partial(attention_kernel, block=min(256, half)),
        out_shape=[shape, shape],
        scratch_shapes=[
            pltpu.VMEM((2 * half, DH), BF),
            pltpu.VMEM((2 * half, DH), BF),
            pltpu.VMEM((2 * half, DH), F32),
            pltpu.VMEM((2 * half, DH), F32),
        ],
        compiler_params=params(),
        cost_estimate=COST,
        name="attention",
    )(qkv_a, qkv_b, d_a, d_b)


def term_kernel(head_ref, a_ref, b_ref, w_ref, *out_refs, first, last):
    head = head_ref[0]
    total = dot(a_ref[:, first:last], w_ref[head], NN)
    total += dot(b_ref[:, first:last], w_ref[1 - head], NN)
    count = len(out_refs)
    size = out_refs[0].shape[0]
    value = total.astype(BF)
    if count == 1:
        out_refs[0][...] = value
        return
    for block in range(count):
        for slot, out_ref in enumerate(out_refs):

            @pl.when(wrapped(block - head_ref[1], count) == slot)
            def _():
                out_ref[...] = value[block * size : (block + 1) * size]


def pair_term(place, mine, got, weight, slots, first, last, name):
    half, full = mine.shape
    heads, depth, width = weight.shape
    size = half // slots
    tile = 512 if width % 512 == 0 else width
    return pl.pallas_call(
        functools.partial(term_kernel, first=first, last=last),
        grid_spec=pltpu.PrefetchScalarGridSpec(
            num_scalar_prefetch=1,
            grid=(width // tile,),
            in_specs=[
                pl.BlockSpec((half, full), lambda n, at: (0, 0)),
                pl.BlockSpec((half, full), lambda n, at: (0, 0)),
                pl.BlockSpec((heads, depth, tile), lambda n, at: (0, 0, n)),
            ],
            out_specs=[pl.BlockSpec((size, tile), lambda n, at: (0, n))] * slots,
        ),
        out_shape=[jax.ShapeDtypeStruct((size, width), BF)] * slots,
        compiler_params=params(),
        cost_estimate=COST,
        name=name,
    )(place, mine, got, weight)


def sum_kernel(*refs, count):
    out_refs = refs[count:]
    size = out_refs[0].shape[0]
    total = refs[0][...].astype(F32)
    for ref in refs[1:count]:
        total = total + ref[...].astype(F32)
    for slot, out_ref in enumerate(out_refs):
        out_ref[...] = total[slot * size : (slot + 1) * size].astype(BF)


def summed(parts, slots, name):
    rows, width = parts[0].shape
    return pl.pallas_call(
        functools.partial(sum_kernel, count=len(parts)),
        out_shape=[jax.ShapeDtypeStruct((rows // slots, width), BF)] * slots,
        compiler_params=params(),
        cost_estimate=COST,
        name=name,
    )(*parts)


def weight_kernel(at_ref, xa_ref, xb_ref, ga_ref, gb_ref, ra_ref, rb_ref, *rest):
    del at_ref
    out_refs, turned = rest[:-1], rest[-1]
    step = pl.program_id(0)
    half = ra_ref.shape[0]
    split = 3 * DH

    @pl.when(step == 0)
    def _():
        turned[:, :half] = ra_ref[...].T
        turned[:, half:] = rb_ref[...].T

    a, b = slice(0, half), slice(half, 2 * half)
    qkv = dot(turned[:split, a], xa_ref[...], NN) + dot(turned[:split, b], xb_ref[...], NN)
    out = dot(turned[split:, a], ga_ref[...], NN) + dot(turned[split:, b], gb_ref[...], NN)
    for slot, out_ref in enumerate(out_refs):

        @pl.when(step == slot)
        def _():
            out_ref[:split, :] = qkv.astype(BF)
            out_ref[split:, :] = out.astype(BF)


def weight_gradients(at, xa, xb, ga, gb, ra, rb, seqs):
    half, width = xa.shape
    chunk = width // seqs
    full = ra.shape[1]
    column = pl.BlockSpec((half, chunk), lambda r, at: (0, lax.rem(r + at[0], seqs)))
    rest = pl.BlockSpec((half, full), lambda r, at: (0, 0))
    return pl.pallas_call(
        weight_kernel,
        grid_spec=pltpu.PrefetchScalarGridSpec(
            num_scalar_prefetch=1,
            grid=(seqs,),
            in_specs=[column] * 4 + [rest] * 2,
            out_specs=[pl.BlockSpec((full, chunk), lambda r, at: (0, 0))] * seqs,
            scratch_shapes=[pltpu.VMEM((full, 2 * half), BF)],
        ),
        out_shape=[jax.ShapeDtypeStruct((full, chunk), BF)] * seqs,
        compiler_params=params(),
        cost_estimate=COST,
        name="weight_gradients",
    )(at, xa, xb, ga, gb, ra, rb)


def weight_sum_kernel(*refs):
    out_ref = refs[-1]
    split = 3 * DH
    total = refs[0][...].astype(F32)
    for ref in refs[1:-1]:
        total = total + ref[...].astype(F32)
    out_ref[:, :split] = total[:split].T.astype(BF)
    for part in range(2):
        rows = slice(part * DH, (part + 1) * DH)
        out_ref[rows, split:] = total[split:, rows].astype(BF)


def weight_sum(parts):
    full, chunk = parts[0].shape
    return pl.pallas_call(
        weight_sum_kernel,
        out_shape=jax.ShapeDtypeStruct((chunk, full), BF),
        compiler_params=params(),
        cost_estimate=COST,
        name="weight_sum",
    )(*parts)


def unpack_kernel(at_ref, mine_ref, other_ref, qkv_ref, out_ref):
    first_head = at_ref[0] == 0
    mine = mine_ref[0].astype(F32)
    other = other_ref[0].astype(F32)
    low = jnp.where(first_head, mine, other)
    high = jnp.where(first_head, other, mine)
    split = 3 * DH
    for i in range(3):
        columns = slice(i * DH, (i + 1) * DH)
        qkv_ref[i] = jnp.concatenate([low[:, columns], high[:, columns]], axis=1)
    for head, value in enumerate((low, high)):
        halves = [value[part * DH : (part + 1) * DH, split:] for part in range(2)]
        out_ref[head * DH : (head + 1) * DH, :] = jnp.concatenate(halves, axis=1)


def unpack_weights(at, mine, other):
    seqs, chunk, full = mine.shape
    width = chunk * seqs
    local = 2 * DH
    block = pl.BlockSpec((1, chunk, full), lambda r: (r, 0, 0))
    return pl.pallas_call(
        unpack_kernel,
        grid=(seqs,),
        in_specs=[SCALARS, block, block],
        out_specs=[
            pl.BlockSpec((3, chunk, local), lambda r: (0, r, 0)),
            pl.BlockSpec((local, chunk), lambda r: (0, r)),
        ],
        out_shape=[
            jax.ShapeDtypeStruct((3, width, local), F32),
            jax.ShapeDtypeStruct((local, width), F32),
        ],
        compiler_params=params(),
        cost_estimate=COST,
        name="weight_outputs",
    )(at, mine, other)


def neighbour_edges(first, last):
    axes = ("seq", "head")
    count = lax.axis_size(axes)
    forward = [(i, i + 1) for i in range(count - 1)]
    backward = [(target, source) for source, target in forward]
    return lax.ppermute(last, axes, forward), lax.ppermute(first, axes, backward)


def after(value, *others):
    return lax.optimization_barrier((value,) + others)[0]


def send_chip(x, step, heads):
    count = lax.axis_size("seq")
    return lax.ppermute(x, "seq", [(s, (s + step * heads) % count) for s in range(count)])


def send_z(x, step):
    count = lax.axis_size("head")
    return lax.ppermute(x, "head", [(z, (z + step) % count) for z in range(count)])


def swap_heads(x):
    count = lax.axis_size("seq")
    return lax.ppermute(x, "seq", [(s, s + 1 - 2 * (s % 2)) for s in range(count)])


def unit_body(enc_in, conv_weight, norm_gain, w_qkv, w_out, grad_out):
    rows = enc_in.shape[0] // 2
    seqs = enc_in.shape[1]
    width = conv_weight.shape[2]
    local = w_qkv.shape[2]
    heads = local // DH
    groups = lax.axis_size("head")
    half = groups * seqs * rows
    place = lax.axis_index("seq")
    own_seq = (place // heads).astype(jnp.int32)
    own_head = (place % heads).astype(jnp.int32)
    own_z = lax.axis_index("head").astype(jnp.int32)
    zero = jnp.zeros((), jnp.int32)
    at = jnp.stack([own_seq, own_head])
    head_mine = own_head.reshape(1)
    head_other = (1 - own_head).reshape(1)

    def to_chips(slots):
        return [slots[r] if r == 0 else send_chip(slots[r], r, heads) for r in range(seqs)]

    def from_chips(slots):
        return [slots[r] if r == 0 else send_chip(slots[r], -r, heads) for r in range(seqs)]

    grad_z = lax.all_gather(grad_out, "head", axis=0, tiled=False)
    pairs = jnp.transpose(enc_in.reshape(rows, 2, seqs, enc_in.shape[2]), (1, 2, 0, 3))
    low, high = neighbour_edges(pairs[:, :, :1, :], pairs[:, :, -1:, :])
    skip, slope, normed = encoder(at, pairs, low, high, conv_weight, norm_gain)
    normed_slab = jnp.concatenate(to_chips(normed), axis=0)
    normed_rows = lax.all_gather(normed_slab, "head", axis=0, tiled=True)

    grad_z = after(grad_z, normed_slab)
    grad_slots = [
        lax.dynamic_index_in_dim(grad_z, (own_seq + r) % seqs, 2, keepdims=False)
        for r in range(seqs)
    ]
    grad_rows = jnp.stack(to_chips(grad_slots), axis=1).reshape(half, width)
    w_pack, w_turned = pack_weights(after(w_qkv, normed_slab))
    w_rows = w_out.reshape(heads, DH, width)
    d_got = swap_heads(head_product(head_other, grad_rows, w_rows, NT, "d_o_other"))
    d_mine = head_product(head_mine, grad_rows, w_rows, NT, "d_o_own")
    grad_swapped = swap_heads(grad_rows)
    normed_rows = after(normed_rows, d_got, d_mine, grad_swapped, w_pack, w_turned)

    qkv_got = swap_heads(head_product(head_other, normed_rows, w_pack, NN, "qkv_other"))
    normed_swapped = swap_heads(normed_rows)
    qkv_mine = head_product(head_mine, normed_rows, w_pack, NN, "qkv_own")
    qkv_mine = after(qkv_mine, normed_swapped)
    result_mine, result_other = attention(qkv_mine, qkv_got, d_mine, d_got)
    result_got = swap_heads(result_other)

    plain = jnp.stack([own_head, zero])
    (d_term,) = pair_term(plain, result_mine, result_got, w_turned, 1, 0, 3 * DH, "d_term")
    d_normed = lax.psum_scatter(
        d_term.reshape(groups, seqs, rows, width), "head", scatter_dimension=0, tiled=False
    )
    part = weight_gradients(
        own_seq.reshape(1),
        normed_rows,
        normed_swapped,
        grad_rows,
        grad_swapped,
        result_mine,
        result_other,
        seqs,
    )
    part = to_chips(part)
    turned = jnp.stack([own_head, own_z])
    head_term = pair_term(
        turned, result_mine, result_got, w_rows, groups, 3 * DH, 4 * DH, "head_term"
    )
    head_slots = [head_term[0], send_z(head_term[1], 1)]
    part = [after(p, d_normed, head_slots[1]) for p in part]
    d_normed = from_chips([d_normed[r] for r in range(seqs)])
    chunk = weight_sum(part)
    same_head = [[b * heads + h for b in range(seqs)] for h in range(heads)]
    chunks = lax.all_gather(chunk, "seq", axis_index_groups=same_head)

    for q in range(2, groups):
        head_slots.append(send_z(after(head_term[q], head_slots[1]), q))
    grad = jnp.transpose(after(grad_out, d_term), (1, 0, 2))
    d_normed[0] = after(d_normed[0], head_slots[-1])
    d_conv, first, last = conv_gradient(at, d_normed, skip, grad, norm_gain, slope)
    low, high = neighbour_edges(first, last)
    head_sum = summed(head_slots, seqs, "head_sum")
    grad_input = conv_back(d_conv, after(low, *head_sum), high, conv_weight)
    head_sum = from_chips(head_sum)

    mixed = mixed_call(at, [after(h, low, high) for h in head_sum], skip)
    chunks = after(chunks, grad_input, mixed)
    grad_w_qkv, grad_w_out = unpack_weights(head_mine, chunks, swap_heads(chunks))
    grad_input = jnp.transpose(grad_input.reshape(2, seqs, rows, -1), (2, 0, 1, 3))
    return (
        jnp.transpose(mixed, (1, 0, 2)),
        grad_input.reshape(enc_in.shape),
        grad_w_qkv,
        grad_w_out,
    )


def padded_2(block, sides, width):
    for axis, dim in sides:
        count = lax.axis_size(axis)
        forward = [(i, i + 1) for i in range(count - 1)]
        backward = [(target, source) for source, target in forward]
        low = lax.ppermute(
            lax.slice_in_dim(block, block.shape[dim] - width, None, axis=dim), axis, forward
        )
        high = lax.ppermute(lax.slice_in_dim(block, 0, width, axis=dim), axis, backward)
        block = jnp.concatenate([low, block, high], axis=dim)
    return block


def gathered_body(enc_in, conv_weight, norm_gain, w_qkv, w_out, grad_out):
    fine_rows = enc_in.shape[0]
    slab_rows = fine_rows // 2
    seq_count = enc_in.shape[1]
    out_width = conv_weight.shape[2]
    local_width = w_qkv.shape[2]
    local_heads = local_width // DH
    logit_scale = DH ** (-0.5)
    padded = padded_2(enc_in, ((("seq", "head"), 0),), 2)
    convolved = jnp.zeros((fine_rows, seq_count, out_width), jnp.float32)
    for offset in range(KW):
        convolved = convolved + jnp.einsum(
            "tbi,io->tbo",
            padded[offset : offset + fine_rows],
            conv_weight[offset],
            preferred_element_type=jnp.float32,
        )
    activated, gelu_pull = jax.vjp(jax.nn.gelu, convolved)
    skip = jnp.mean(activated.reshape(slab_rows, 2, seq_count, out_width), axis=1).astype(
        jnp.bfloat16
    )
    skip_wide = skip.astype(jnp.float32)
    inv_rms = lax.rsqrt(jnp.mean(skip_wide * skip_wide, axis=-1, keepdims=True) + 1e-06)
    normed = (skip_wide * inv_rms * norm_gain).astype(jnp.bfloat16)
    normed_rows = lax.all_gather(normed, "head", axis=0, tiled=True)
    grad_rows = lax.all_gather(grad_out, "head", axis=0, tiled=True)
    tower_rows = normed_rows.shape[0]
    qkv = jnp.einsum(
        "tbc,ice->itbe", normed_rows, w_qkv, preferred_element_type=jnp.float32
    ).astype(jnp.bfloat16)
    qkv = qkv.reshape(3, tower_rows, seq_count, local_heads, DH)
    query_matrix, key_matrix, value_matrix = (qkv[0], qkv[1], qkv[2])
    key_all, value_all = (
        lax.all_gather(key_matrix, "seq", axis=0, tiled=True),
        lax.all_gather(value_matrix, "seq", axis=0, tiled=True),
    )
    attention_logits = (
        jnp.einsum("qbhd,kbhd->bhqk", query_matrix, key_all, preferred_element_type=jnp.float32)
        * logit_scale
    )
    row_peak = jnp.max(attention_logits, axis=-1, keepdims=True)
    exponent = jnp.exp(attention_logits - row_peak)
    row_total = jnp.sum(exponent, axis=-1, keepdims=True)
    soft_weights = exponent / row_total
    narrow_probabilities = soft_weights.astype(jnp.bfloat16)
    attention_output = jnp.einsum(
        "bhqk,kbhd->qbhd", narrow_probabilities, value_all, preferred_element_type=jnp.float32
    )
    o_narrow = attention_output.reshape(tower_rows, seq_count, local_width).astype(jnp.bfloat16)
    piece = o_narrow
    head_sum = lax.psum_scatter(
        jnp.einsum("tbe,ec->tbc", piece, w_out, preferred_element_type=jnp.float32).astype(
            jnp.bfloat16
        ),
        "head",
        scatter_dimension=0,
        tiled=True,
    ).astype(jnp.float32)
    mixed = (skip_wide + head_sum).astype(jnp.bfloat16)
    part_w_out = jnp.einsum("tbe,tbc->ec", o_narrow, grad_rows, preferred_element_type=jnp.float32)
    d_out = jnp.einsum("tbc,ec->tbe", grad_rows, w_out, preferred_element_type=jnp.float32).astype(
        jnp.bfloat16
    )
    d_out = d_out.reshape(tower_rows, seq_count, local_heads, DH)
    delta = jnp.sum(d_out.astype(jnp.float32) * attention_output, axis=-1)
    probability_gradient = jnp.einsum(
        "qbhd,kbhd->bhqk", d_out, value_all, preferred_element_type=jnp.float32
    )
    d_scores = soft_weights * (probability_gradient - jnp.transpose(delta, (1, 2, 0))[..., None])
    narrow_gradient = d_scores.astype(jnp.bfloat16)
    query_gradient = logit_scale * jnp.einsum(
        "bhqk,kbhd->qbhd", narrow_gradient, key_all, preferred_element_type=jnp.float32
    )
    key_terms = logit_scale * jnp.einsum(
        "bhqk,qbhd->kbhd", narrow_gradient, query_matrix, preferred_element_type=jnp.float32
    )
    value_terms = jnp.einsum(
        "bhqk,qbhd->kbhd", narrow_probabilities, d_out, preferred_element_type=jnp.float32
    )
    d_keys, d_values = (
        lax.psum_scatter(
            key_terms.astype(jnp.bfloat16), "seq", scatter_dimension=0, tiled=True
        ).astype(jnp.float32),
        lax.psum_scatter(
            value_terms.astype(jnp.bfloat16), "seq", scatter_dimension=0, tiled=True
        ).astype(jnp.float32),
    )
    dqkv = (
        jnp.stack([query_gradient, d_keys, d_values])
        .reshape(3, tower_rows, seq_count, local_width)
        .astype(jnp.bfloat16)
    )
    part_w_qkv = jnp.einsum("tbc,itbe->ice", normed_rows, dqkv, preferred_element_type=jnp.float32)
    piece = dqkv
    d_normed = lax.psum_scatter(
        jnp.einsum("itbe,ice->tbc", piece, w_qkv, preferred_element_type=jnp.float32).astype(
            jnp.bfloat16
        ),
        "head",
        scatter_dimension=0,
        tiled=True,
    ).astype(jnp.float32)
    unit_rows = skip_wide * inv_rms
    scaled = d_normed * norm_gain
    d_skip = grad_out.astype(jnp.float32) + inv_rms * (
        scaled - unit_rows * jnp.mean(scaled * unit_rows, axis=-1, keepdims=True)
    )
    d_act = jnp.repeat(d_skip, 2, axis=0) * 0.5
    d_conv = gelu_pull(d_act)[0].astype(jnp.bfloat16)
    d_pad = padded_2(d_conv, ((("seq", "head"), 0),), 2)
    grad_input = jnp.zeros((fine_rows, seq_count, enc_in.shape[2]), jnp.float32)
    for offset in range(KW):
        grad_input = grad_input + jnp.einsum(
            "tbo,io->tbi",
            d_pad[4 - offset : 4 - offset + fine_rows],
            conv_weight[offset],
            preferred_element_type=jnp.float32,
        )
    grad_w_qkv, grad_w_out = (
        lax.psum(part_w_qkv.astype(jnp.bfloat16), "seq").astype(jnp.float32),
        lax.psum(part_w_out.astype(jnp.bfloat16), "seq").astype(jnp.float32),
    )
    return (mixed, grad_input.astype(jnp.bfloat16), grad_w_qkv, grad_w_out)


def body(enc_in, conv_weight, norm_gain, w_qkv, w_out, grad_out):
    heads = w_qkv.shape[2] // DH
    seqs = enc_in.shape[1]
    fits = heads == 2 and seqs * heads == lax.axis_size("seq")
    fits = fits and conv_weight.shape[2] == seqs * w_qkv.shape[2]
    chosen = unit_body if fits else gathered_body
    return chosen(enc_in, conv_weight, norm_gain, w_qkv, w_out, grad_out)


def solution(mesh):
    return jax.shard_map(
        body,
        mesh=mesh,
        in_specs=(
            P(("seq", "head"), None, None),
            P(),
            P(),
            P(None, None, "head"),
            P("head", None),
            P(("seq", "head"), None, None),
        ),
        out_specs=(
            P(("seq", "head"), None, None),
            P(("seq", "head"), None, None),
            P(None, None, "head"),
            P("head", None),
        ),
        check_vma=False,
    )
```

```python
import functools

import jax
import jax.numpy as jnp
from jax import lax
from jax.experimental import pallas as pl
from jax.experimental.pallas import tpu as pltpu
from jax.sharding import PartitionSpec as P

DH = 192
KW = 5
VMEM_LIMIT = 24 * 1024 * 1024
COST = pl.CostEstimate(flops=1000, bytes_accessed=1000, transcendentals=0)
BF = jnp.bfloat16
F32 = jnp.float32


def params():
    return pltpu.CompilerParams(vmem_limit_bytes=VMEM_LIMIT)


def dot(a, b, contract):
    return lax.dot_general(a, b, (contract, ((), ())), preferred_element_type=F32)


NN = ((1,), (0,))
NT = ((1,), (1,))
TN = ((0,), (0,))


def whole(shape):
    return pl.BlockSpec(shape, lambda *_: (0,) * len(shape))


SCALARS = pl.BlockSpec(memory_space=pltpu.SMEM)


def wrapped(value, size):
    return jnp.where(value < 0, value + size, jnp.where(value >= size, value - size, value))


def turned_rows(ref, low_ref, high_ref, parity, shift):
    seqs, rows, width = ref.shape[1:]
    own = ref[parity]
    if shift != 1:
        wide = own.astype(F32)
        if shift == 0:
            parts = [low_ref[parity].astype(F32), wide[:, : rows - 1]]
        else:
            parts = [wide[:, 1:], high_ref[parity].astype(F32)]
        own = jnp.concatenate(parts, axis=1).astype(BF)
    return own.reshape(seqs * rows, width)


def conv_kernel(
    at_ref, x_ref, low_ref, high_ref, w_ref, gain_ref, skip_ref, slope_ref, *rest
):
    normed_refs, (lhs, squares, whole_normed) = rest[:-3], rest[-3:]
    step = pl.program_id(0)
    seqs, rows, c_in = x_ref.shape[1:]
    half = seqs * rows
    tile = w_ref.shape[2]

    @pl.when(step == 0)
    def _():
        for parity in range(2):
            for shift in range(3):
                value = turned_rows(x_ref, low_ref, high_ref, parity, shift)
                for out in range(2):
                    tap = 2 * shift + parity - out
                    if 0 <= tap < KW:
                        lhs[out * half : (out + 1) * half, tap * c_in : (tap + 1) * c_in] = value
        squares[...] = jnp.zeros_like(squares)

    conv = dot(lhs[...], w_ref[...].reshape(KW * c_in, tile), NN)
    root = 0.7978845608028654
    total = None
    for parity in range(2):
        x = conv[parity * half : (parity + 1) * half, :]
        square = x * x
        t = jnp.tanh(root * (x + 0.044715 * (square * x)))
        left = 0.5 * (1.0 + t)
        act = x * left
        slope = left + (0.5 * root) * x * (1.0 - t * t) * (1.0 + (3 * 0.044715) * square)
        slope_ref[parity] = slope.reshape(slope_ref.shape[1:])
        total = act if total is None else total + act
    skip = (0.5 * total).astype(BF)
    columns = pl.ds(pl.multiple_of(step * tile, tile), tile)
    skip_ref[:, :, columns] = skip.reshape(seqs, rows, tile)
    wide = skip.astype(F32)
    squares[...] += jnp.sum(wide * wide, axis=-1, keepdims=True)

    @pl.when(step == pl.num_programs(0) - 1)
    def _():
        width = skip_ref.shape[2]
        inv = lax.rsqrt(squares[...] * (1.0 / width) + 1e-06)
        wide = skip_ref[...].reshape(half, width).astype(F32)
        normed = (wide * inv * gain_ref[...]).astype(BF)
        whole_normed[...] = normed.reshape(whole_normed.shape)
        for slot in range(seqs):
            normed_refs[slot][...] = whole_normed[wrapped(at_ref[0] + slot, seqs)]


def encoder(at, pairs, low, high, conv_weight, norm_gain):
    _, seqs, rows, c_in = pairs.shape
    width = conv_weight.shape[2]
    tile = 256 if width % 256 == 0 else width
    shape = (seqs, rows, width)
    outs = pl.pallas_call(
        conv_kernel,
        grid=(width // tile,),
        in_specs=[
            SCALARS,
            whole(pairs.shape),
            whole(low.shape),
            whole(high.shape),
            pl.BlockSpec((KW, c_in, tile), lambda n: (0, 0, n)),
            whole((1, width)),
        ],
        out_specs=[
            whole(shape),
            pl.BlockSpec((2, seqs, rows, tile), lambda n: (0, 0, 0, n)),
        ]
        + [whole((rows, width))] * seqs,
        out_shape=[
            jax.ShapeDtypeStruct(shape, BF),
            jax.ShapeDtypeStruct((2,) + shape, F32),
        ]
        + [jax.ShapeDtypeStruct((rows, width), BF)] * seqs,
        scratch_shapes=[
            pltpu.VMEM((2 * seqs * rows, KW * c_in), BF),
            pltpu.VMEM((seqs * rows, 1), F32),
            pltpu.VMEM(shape, BF),
        ],
        compiler_params=params(),
        cost_estimate=COST,
        name="encoder_forward",
    )(at, pairs, low, high, conv_weight, norm_gain.reshape(1, width))
    return outs[0], outs[1], list(outs[2:])


def d_conv_body(seqs, at_ref, *refs):
    dn_refs = refs[:seqs]
    skip_ref, grad_ref, gain_ref, slope_ref, out_ref, first_ref, last_ref = refs[seqs:]
    rows = out_ref.shape[2]
    for slot in range(seqs):
        b = wrapped(at_ref[0] + slot, seqs)
        wide = skip_ref[b].astype(F32)
        inv = lax.rsqrt(jnp.mean(wide * wide, axis=-1, keepdims=True) + 1e-06)
        unit = wide * inv
        scaled = dn_refs[slot][...].astype(F32) * gain_ref[...]
        d_skip = grad_ref[b].astype(F32) + inv * (
            scaled - unit * jnp.mean(scaled * unit, axis=-1, keepdims=True)
        )
        d_act = 0.5 * d_skip
        for parity in range(2):
            value = slope_ref[parity, b] * d_act
            out_ref[parity, b] = value.astype(BF)
            first_ref[parity, b] = value[:1].astype(BF)
            last_ref[parity, b] = value[rows - 1 :].astype(BF)


def conv_gradient(at, d_normed, skip, grad, norm_gain, slope):
    seqs = len(d_normed)
    vmem = pl.BlockSpec(memory_space=pltpu.VMEM)
    edge = jax.ShapeDtypeStruct(slope.shape[:2] + (1, slope.shape[3]), BF)
    return pl.pallas_call(
        functools.partial(d_conv_body, seqs),
        in_specs=[SCALARS] + [vmem] * (seqs + 4),
        out_specs=[vmem] * 3,
        out_shape=[jax.ShapeDtypeStruct(slope.shape, BF)] + [edge] * 2,
        compiler_params=params(),
        cost_estimate=COST,
        name="conv_gradient",
    )(at, *d_normed, skip, grad, norm_gain.reshape(1, -1), slope)


def mixed_body(seqs, at_ref, *refs):
    skip_ref, out_ref = refs[seqs:]
    for slot in range(seqs):
        b = wrapped(at_ref[0] + slot, seqs)
        out_ref[b] = (skip_ref[b].astype(F32) + refs[slot][...].astype(F32)).astype(BF)


def mixed_call(at, terms, skip):
    seqs = len(terms)
    vmem = pl.BlockSpec(memory_space=pltpu.VMEM)
    return pl.pallas_call(
        functools.partial(mixed_body, seqs),
        in_specs=[SCALARS] + [vmem] * (seqs + 1),
        out_specs=vmem,
        out_shape=jax.ShapeDtypeStruct(skip.shape, BF),
        compiler_params=params(),
        cost_estimate=COST,
        name="mixed_sum",
    )(at, *terms, skip)


def conv_back_kernel(d_ref, low_ref, high_ref, w_ref, out_ref, turned, acc):
    step = pl.program_id(0)

    @pl.when(step == 0)
    def _():
        for parity in range(2):
            for shift in range(3):
                turned[parity, shift] = turned_rows(d_ref, low_ref, high_ref, parity, shift).T

    for tap in range(KW):

        @pl.when(step == tap)
        def _():
            places = [KW - 1 - tap, KW - tap]
            rhs = jnp.concatenate([turned[p % 2, p // 2] for p in places], axis=1)
            term = dot(w_ref[0], rhs, NN)
            if tap == 0:
                acc[...] = term
            elif tap < KW - 1:
                acc[...] += term
            else:
                out_ref[...] = (acc[...] + term).T.astype(BF)


def conv_back(d_conv, low, high, conv_weight):
    _, seqs, rows, width = d_conv.shape
    c_in = conv_weight.shape[1]
    flat = 2 * seqs * rows
    return pl.pallas_call(
        conv_back_kernel,
        grid=(KW,),
        in_specs=[
            whole(d_conv.shape),
            whole(low.shape),
            whole(high.shape),
            pl.BlockSpec((1, c_in, width), lambda k: (k, 0, 0)),
        ],
        out_specs=whole((flat, c_in)),
        out_shape=jax.ShapeDtypeStruct((flat, c_in), BF),
        scratch_shapes=[
            pltpu.VMEM((2, 3, width, seqs * rows), BF),
            pltpu.VMEM((c_in, flat), F32),
        ],
        compiler_params=params(),
        cost_estimate=COST,
        name="encoder_backward",
    )(d_conv, low, high, conv_weight)


def pack_kernel(w_ref, pack_ref, turned_ref):
    for i in range(3):
        for head in range(pack_ref.shape[0]):
            part = w_ref[i, :, head * DH : (head + 1) * DH]
            columns = slice(i * DH, (i + 1) * DH)
            pack_ref[head, :, columns] = part
            turned_ref[head, columns, :] = part.T


def pack_weights(w_qkv):
    _, width, local = w_qkv.shape
    heads = local // DH
    tile = local
    return pl.pallas_call(
        pack_kernel,
        grid=(width // tile,),
        in_specs=[pl.BlockSpec((3, tile, local), lambda n: (0, n, 0))],
        out_specs=[
            pl.BlockSpec((heads, tile, 3 * DH), lambda n: (0, n, 0)),
            pl.BlockSpec((heads, 3 * DH, tile), lambda n: (0, 0, n)),
        ],
        out_shape=[
            jax.ShapeDtypeStruct((heads, width, 3 * DH), BF),
            jax.ShapeDtypeStruct((heads, 3 * DH, width), BF),
        ],
        compiler_params=params(),
        cost_estimate=COST,
        name="pack_weights",
    )(w_qkv)


def product_kernel(head_ref, x_ref, w_ref, out_ref, *, contract):
    del head_ref
    value = dot(x_ref[...], w_ref[0], contract).astype(BF)
    out_ref[:, : value.shape[1]] = value
    if value.shape[1] < out_ref.shape[1]:
        out_ref[:, value.shape[1] :] = jnp.zeros_like(out_ref[:, value.shape[1] :])


def head_product(head, x, weight, contract, name):
    columns = weight.shape[2] if contract == NN else weight.shape[1]
    columns += -columns % 128
    rows, width = x.shape
    return pl.pallas_call(
        functools.partial(product_kernel, contract=contract),
        grid_spec=pltpu.PrefetchScalarGridSpec(
            num_scalar_prefetch=1,
            grid=(1,),
            in_specs=[
                pl.BlockSpec((rows, width), lambda i, head: (0, 0)),
                pl.BlockSpec((1,) + weight.shape[1:], lambda i, head: (head[0], 0, 0)),
            ],
            out_specs=pl.BlockSpec((rows, columns), lambda i, head: (0, 0)),
        ),
        out_shape=jax.ShapeDtypeStruct((rows, columns), BF),
        compiler_params=params(),
        cost_estimate=COST,
        name=name,
    )(head, x, weight)


def attention_kernel(qa_ref, qb_ref, da_ref, db_ref, oa_ref, ob_ref, k_all, v_all, dk_acc, dv_acc, *, block):
    scale = DH ** (-0.5)
    half = qa_ref.shape[0]
    for place, ref in enumerate((qa_ref, qb_ref)):
        rows = pl.ds(place * half, half)
        k_all[rows, :] = ref[:, DH : 2 * DH]
        v_all[rows, :] = ref[:, 2 * DH : 3 * DH]
    k = k_all[...]
    v = v_all[...]
    for place, (q_ref, d_ref, out_ref) in enumerate(
        ((qa_ref, da_ref, oa_ref), (qb_ref, db_ref, ob_ref))
    ):
        for start in range(0, half, block):
            rows = pl.ds(start, block)
            q = q_ref[rows, 0:DH]
            d_o = d_ref[rows, 0:DH]
            s = dot(q, k, NT) * scale
            e = jnp.exp(s - jnp.max(s, axis=-1, keepdims=True))
            p = e * (1.0 / jnp.sum(e, axis=-1, keepdims=True))
            p_b = p.astype(BF)
            o = dot(p_b, v, NN)
            delta = jnp.sum(d_o.astype(F32) * o, axis=-1, keepdims=True)
            d_p = dot(d_o, v, NT)
            ds = (p * (d_p - delta)).astype(BF)
            dq = scale * dot(ds, k, NN)
            dk = dot(ds, q, TN)
            dv = dot(p_b, d_o, TN)
            if place == 0 and start == 0:
                dk_acc[...] = dk
                dv_acc[...] = dv
            else:
                dk_acc[...] += dk
                dv_acc[...] += dv
            out_ref[rows, 0:DH] = dq.astype(BF)
            out_ref[rows, 3 * DH : 4 * DH] = o.astype(BF)
    for place, out_ref in enumerate((oa_ref, ob_ref)):
        rows = pl.ds(place * half, half)
        out_ref[:, DH : 2 * DH] = (scale * dk_acc[rows, :]).astype(BF)
        out_ref[:, 2 * DH : 3 * DH] = dv_acc[rows, :].astype(BF)


def attention(qkv_a, qkv_b, d_a, d_b):
    half = qkv_a.shape[0]
    shape = jax.ShapeDtypeStruct((half, 4 * DH), BF)
    return pl.pallas_call(
        functools.partial(attention_kernel, block=min(256, half)),
        out_shape=[shape, shape],
        scratch_shapes=[
            pltpu.VMEM((2 * half, DH), BF),
            pltpu.VMEM((2 * half, DH), BF),
            pltpu.VMEM((2 * half, DH), F32),
            pltpu.VMEM((2 * half, DH), F32),
        ],
        compiler_params=params(),
        cost_estimate=COST,
        name="attention",
    )(qkv_a, qkv_b, d_a, d_b)


def term_kernel(head_ref, a_ref, b_ref, w_ref, *out_refs, first, last):
    head = head_ref[0]
    total = dot(a_ref[:, first:last], w_ref[head], NN)
    total += dot(b_ref[:, first:last], w_ref[1 - head], NN)
    count = len(out_refs)
    size = out_refs[0].shape[0]
    value = total.astype(BF)
    if count == 1:
        out_refs[0][...] = value
        return
    for block in range(count):
        for slot, out_ref in enumerate(out_refs):

            @pl.when(wrapped(block - head_ref[1], count) == slot)
            def _():
                out_ref[...] = value[block * size : (block + 1) * size]


def pair_term(place, mine, got, weight, slots, first, last, name):
    half, full = mine.shape
    heads, depth, width = weight.shape
    size = half // slots
    tile = 512 if width % 512 == 0 else width
    return pl.pallas_call(
        functools.partial(term_kernel, first=first, last=last),
        grid_spec=pltpu.PrefetchScalarGridSpec(
            num_scalar_prefetch=1,
            grid=(width // tile,),
            in_specs=[
                pl.BlockSpec((half, full), lambda n, at: (0, 0)),
                pl.BlockSpec((half, full), lambda n, at: (0, 0)),
                pl.BlockSpec((heads, depth, tile), lambda n, at: (0, 0, n)),
            ],
            out_specs=[pl.BlockSpec((size, tile), lambda n, at: (0, n))] * slots,
        ),
        out_shape=[jax.ShapeDtypeStruct((size, width), BF)] * slots,
        compiler_params=params(),
        cost_estimate=COST,
        name=name,
    )(place, mine, got, weight)


def weight_kernel(at_ref, xa_ref, xb_ref, ga_ref, gb_ref, ra_ref, rb_ref, *rest):
    del at_ref
    out_refs, turned = rest[:-1], rest[-1]
    step = pl.program_id(0)
    half = ra_ref.shape[0]
    split = 3 * DH

    @pl.when(step == 0)
    def _():
        turned[:, :half] = ra_ref[...].T
        turned[:, half:] = rb_ref[...].T

    a, b = slice(0, half), slice(half, 2 * half)
    qkv = dot(turned[:split, a], xa_ref[...], NN) + dot(turned[:split, b], xb_ref[...], NN)
    out = dot(turned[split:, a], ga_ref[...], NN) + dot(turned[split:, b], gb_ref[...], NN)
    for slot, out_ref in enumerate(out_refs):

        @pl.when(step == slot)
        def _():
            out_ref[:split, :] = qkv.astype(BF)
            out_ref[split:, :] = out.astype(BF)


def weight_gradients(at, xa, xb, ga, gb, ra, rb, seqs):
    half, width = xa.shape
    chunk = width // seqs
    full = ra.shape[1]
    column = pl.BlockSpec((half, chunk), lambda r, at: (0, lax.rem(r + at[0], seqs)))
    rest = pl.BlockSpec((half, full), lambda r, at: (0, 0))
    return pl.pallas_call(
        weight_kernel,
        grid_spec=pltpu.PrefetchScalarGridSpec(
            num_scalar_prefetch=1,
            grid=(seqs,),
            in_specs=[column] * 4 + [rest] * 2,
            out_specs=[pl.BlockSpec((full, chunk), lambda r, at: (0, 0))] * seqs,
            scratch_shapes=[pltpu.VMEM((full, 2 * half), BF)],
        ),
        out_shape=[jax.ShapeDtypeStruct((full, chunk), BF)] * seqs,
        compiler_params=params(),
        cost_estimate=COST,
        name="weight_gradients",
    )(at, xa, xb, ga, gb, ra, rb)


def weight_sum_kernel(*refs):
    part_refs, out_refs = refs[:-2], refs[-2:]
    split = 3 * DH
    total = part_refs[0][...].astype(F32)
    for ref in part_refs[1:]:
        total = total + ref[...].astype(F32)
    turned = total[:split].T.astype(BF)
    for part, out_ref in enumerate(out_refs):
        rows = slice(part * DH, (part + 1) * DH)
        out_ref[:, :split] = turned[rows]
        out_ref[:, split:] = total[split:, rows].astype(BF)


def weight_sum(parts):
    full, chunk = parts[0].shape
    return pl.pallas_call(
        weight_sum_kernel,
        out_shape=[jax.ShapeDtypeStruct((chunk // 2, full), BF)] * 2,
        compiler_params=params(),
        cost_estimate=COST,
        name="weight_sum",
    )(*parts)


def unpack_kernel(at_ref, *refs):
    qkv_ref, out_ref = refs[-2:]
    step = pl.program_id(0)
    split = 3 * DH
    for turn in range(4):

        @pl.when(step == turn)
        def _():
            both = []
            for near_a, near_b, far_a, far_b in (refs[:4], refs[4:8]):
                first = near_a if turn < 2 else far_a
                second = near_b if turn % 2 == 0 else far_b
                both.append((first[...].astype(F32), second[...].astype(F32)))
            swapped = at_ref[1] != 0
            for part in range(2):
                mine, other = both[0][part], both[1][part]
                low = jnp.where(swapped, other, mine)
                high = jnp.where(swapped, mine, other)
                rows = slice(part * DH, (part + 1) * DH)
                for i in range(3):
                    columns = slice(i * DH, (i + 1) * DH)
                    qkv_ref[i, rows, :] = jnp.concatenate(
                        [low[:, columns], high[:, columns]], axis=1
                    )
                out_ref[:DH, rows] = low[:, split:]
                out_ref[DH:, rows] = high[:, split:]


def unpack_weights(at, mine, other):
    rows, full = mine[0].shape
    half = rows // 2
    width = 4 * rows
    local = 2 * DH
    specs = [
        pl.BlockSpec((half, full), lambda j, at: (jnp.minimum(j, 1), 0)),
        pl.BlockSpec((half, full), lambda j, at: (j // 2, 0)),
        pl.BlockSpec((half, full), lambda j, at: (jnp.maximum(j - 2, 0), 0)),
        pl.BlockSpec((half, full), lambda j, at: (j // 2, 0)),
    ]
    return pl.pallas_call(
        unpack_kernel,
        grid_spec=pltpu.PrefetchScalarGridSpec(
            num_scalar_prefetch=1,
            grid=(4,),
            in_specs=specs * 2,
            out_specs=[
                pl.BlockSpec((3, rows, local), lambda j, at: (0, at[0] ^ j, 0)),
                pl.BlockSpec((local, rows), lambda j, at: (0, at[0] ^ j)),
            ],
        ),
        out_shape=[
            jax.ShapeDtypeStruct((3, width, local), F32),
            jax.ShapeDtypeStruct((local, width), F32),
        ],
        compiler_params=params(),
        cost_estimate=COST,
        name="weight_outputs",
    )(at, *mine, *other)


def neighbour_edges(first, last):
    axes = ("seq", "head")
    count = lax.axis_size(axes)
    forward = [(i, i + 1) for i in range(count - 1)]
    backward = [(target, source) for source, target in forward]
    return lax.ppermute(last, axes, forward), lax.ppermute(first, axes, backward)


def after(value, *others):
    return lax.optimization_barrier((value,) + others)[0]


def send_chip(x, step, heads):
    count = lax.axis_size("seq")
    return lax.ppermute(x, "seq", [(s, (s + step * heads) % count) for s in range(count)])


def trade_chip(x, bit, heads):
    count = lax.axis_size("seq")
    return lax.ppermute(x, "seq", [(s, s ^ (bit * heads)) for s in range(count)])


def swap_heads(x):
    count = lax.axis_size("seq")
    return lax.ppermute(x, "seq", [(s, s + 1 - 2 * (s % 2)) for s in range(count)])


def unit_body(enc_in, conv_weight, norm_gain, w_qkv, w_out, grad_out):
    rows = enc_in.shape[0] // 2
    seqs = enc_in.shape[1]
    width = conv_weight.shape[2]
    local = w_qkv.shape[2]
    heads = local // DH
    groups = lax.axis_size("head")
    half = groups * seqs * rows
    place = lax.axis_index("seq")
    own_seq = (place // heads).astype(jnp.int32)
    own_head = (place % heads).astype(jnp.int32)
    zero = jnp.zeros((), jnp.int32)
    at = jnp.stack([own_seq, own_head])
    head_mine = own_head.reshape(1)
    head_other = (1 - own_head).reshape(1)

    def to_chips(slots):
        return [slots[r] if r == 0 else send_chip(slots[r], r, heads) for r in range(seqs)]

    def from_chips(slots):
        return [slots[r] if r == 0 else send_chip(slots[r], -r, heads) for r in range(seqs)]

    grad_z = lax.all_gather(grad_out, "head", axis=0, tiled=False)
    pairs = jnp.transpose(enc_in.reshape(rows, 2, seqs, enc_in.shape[2]), (1, 2, 0, 3))
    low, high = neighbour_edges(pairs[:, :, :1, :], pairs[:, :, -1:, :])
    skip, slope, normed = encoder(at, pairs, low, high, conv_weight, norm_gain)
    normed_slab = jnp.concatenate(to_chips(normed), axis=0)
    normed_rows = lax.all_gather(normed_slab, "head", axis=0, tiled=True)

    grad_z = after(grad_z, normed_slab)
    grad_slots = [
        lax.dynamic_index_in_dim(grad_z, (own_seq + r) % seqs, 2, keepdims=False)
        for r in range(seqs)
    ]
    grad_rows = jnp.stack(to_chips(grad_slots), axis=1).reshape(half, width)
    w_pack, w_turned = pack_weights(after(w_qkv, normed_slab))
    w_rows = w_out.reshape(heads, DH, width)
    d_got = swap_heads(head_product(head_other, grad_rows, w_rows, NT, "d_o_other"))
    d_mine = head_product(head_mine, grad_rows, w_rows, NT, "d_o_own")
    grad_swapped = swap_heads(grad_rows)
    normed_rows = after(normed_rows, d_got, d_mine, grad_swapped, w_pack, w_turned)

    qkv_got = swap_heads(head_product(head_other, normed_rows, w_pack, NN, "qkv_other"))
    normed_swapped = swap_heads(normed_rows)
    qkv_mine = head_product(head_mine, normed_rows, w_pack, NN, "qkv_own")
    qkv_mine = after(qkv_mine, normed_swapped)
    result_mine, result_other = attention(qkv_mine, qkv_got, d_mine, d_got)
    result_got = swap_heads(result_other)

    plain = jnp.stack([own_head, zero])
    (d_term,) = pair_term(plain, result_mine, result_got, w_turned, 1, 0, 3 * DH, "d_term")
    d_normed = lax.psum_scatter(
        d_term.reshape(groups, seqs, rows, width), "head", scatter_dimension=0, tiled=False
    )
    part = weight_gradients(
        own_seq.reshape(1),
        normed_rows,
        normed_swapped,
        grad_rows,
        grad_swapped,
        result_mine,
        result_other,
        seqs,
    )
    (head_term,) = pair_term(
        plain, result_mine, after(result_got, *part), w_rows, 1, 3 * DH, 4 * DH, "head_term"
    )
    head_sum = lax.psum_scatter(
        head_term.reshape(groups, seqs, rows, width), "head", scatter_dimension=0, tiled=False
    )

    half_a, half_b = weight_sum([after(p, head_term) for p in to_chips(part)])
    got_a = trade_chip(half_a, 1, heads)
    got_b = trade_chip(half_b, 2, heads)

    d_normed = from_chips([d_normed[r] for r in range(seqs)])
    grad = jnp.transpose(after(grad_out, d_term), (1, 0, 2))
    d_normed[0] = after(d_normed[0], half_a)
    d_conv, first, last = conv_gradient(at, d_normed, skip, grad, norm_gain, slope)
    low, high = neighbour_edges(first, last)
    near_a = jnp.concatenate([half_a, after(got_a, first)], axis=0)
    near_b = jnp.concatenate([half_b, after(got_b, first)], axis=0)
    far_a = trade_chip(near_a, 2, heads)
    far_b = trade_chip(near_b, 1, heads)
    grad_input = conv_back(d_conv, after(low, near_a, near_b), high, conv_weight)
    mine = [near_a, near_b, far_a, far_b]
    other = [swap_heads(after(x, high)) for x in mine[:2]]
    other += [swap_heads(after(x, grad_input)) for x in mine[2:]]
    grad_w_qkv, grad_w_out = unpack_weights(at, mine, other)

    head_sum = after(head_sum, grad_input)
    head_sum = from_chips([head_sum[r] for r in range(seqs)])
    mixed = mixed_call(at, head_sum, skip)
    grad_input = jnp.transpose(grad_input.reshape(2, seqs, rows, -1), (2, 0, 1, 3))
    return (
        jnp.transpose(mixed, (1, 0, 2)),
        grad_input.reshape(enc_in.shape),
        grad_w_qkv,
        grad_w_out,
    )


def padded_2(block, sides, width):
    for axis, dim in sides:
        count = lax.axis_size(axis)
        forward = [(i, i + 1) for i in range(count - 1)]
        backward = [(target, source) for source, target in forward]
        low = lax.ppermute(
            lax.slice_in_dim(block, block.shape[dim] - width, None, axis=dim), axis, forward
        )
        high = lax.ppermute(lax.slice_in_dim(block, 0, width, axis=dim), axis, backward)
        block = jnp.concatenate([low, block, high], axis=dim)
    return block


def gathered_body(enc_in, conv_weight, norm_gain, w_qkv, w_out, grad_out):
    fine_rows = enc_in.shape[0]
    slab_rows = fine_rows // 2
    seq_count = enc_in.shape[1]
    out_width = conv_weight.shape[2]
    local_width = w_qkv.shape[2]
    local_heads = local_width // DH
    logit_scale = DH ** (-0.5)
    padded = padded_2(enc_in, ((("seq", "head"), 0),), 2)
    convolved = jnp.zeros((fine_rows, seq_count, out_width), jnp.float32)
    for offset in range(KW):
        convolved = convolved + jnp.einsum(
            "tbi,io->tbo",
            padded[offset : offset + fine_rows],
            conv_weight[offset],
            preferred_element_type=jnp.float32,
        )
    activated, gelu_pull = jax.vjp(jax.nn.gelu, convolved)
    skip = jnp.mean(activated.reshape(slab_rows, 2, seq_count, out_width), axis=1).astype(
        jnp.bfloat16
    )
    skip_wide = skip.astype(jnp.float32)
    inv_rms = lax.rsqrt(jnp.mean(skip_wide * skip_wide, axis=-1, keepdims=True) + 1e-06)
    normed = (skip_wide * inv_rms * norm_gain).astype(jnp.bfloat16)
    normed_rows = lax.all_gather(normed, "head", axis=0, tiled=True)
    grad_rows = lax.all_gather(grad_out, "head", axis=0, tiled=True)
    tower_rows = normed_rows.shape[0]
    qkv = jnp.einsum(
        "tbc,ice->itbe", normed_rows, w_qkv, preferred_element_type=jnp.float32
    ).astype(jnp.bfloat16)
    qkv = qkv.reshape(3, tower_rows, seq_count, local_heads, DH)
    query_matrix, key_matrix, value_matrix = (qkv[0], qkv[1], qkv[2])
    key_all, value_all = (
        lax.all_gather(key_matrix, "seq", axis=0, tiled=True),
        lax.all_gather(value_matrix, "seq", axis=0, tiled=True),
    )
    attention_logits = (
        jnp.einsum("qbhd,kbhd->bhqk", query_matrix, key_all, preferred_element_type=jnp.float32)
        * logit_scale
    )
    row_peak = jnp.max(attention_logits, axis=-1, keepdims=True)
    exponent = jnp.exp(attention_logits - row_peak)
    row_total = jnp.sum(exponent, axis=-1, keepdims=True)
    soft_weights = exponent / row_total
    narrow_probabilities = soft_weights.astype(jnp.bfloat16)
    attention_output = jnp.einsum(
        "bhqk,kbhd->qbhd", narrow_probabilities, value_all, preferred_element_type=jnp.float32
    )
    o_narrow = attention_output.reshape(tower_rows, seq_count, local_width).astype(jnp.bfloat16)
    piece = o_narrow
    head_sum = lax.psum_scatter(
        jnp.einsum("tbe,ec->tbc", piece, w_out, preferred_element_type=jnp.float32).astype(
            jnp.bfloat16
        ),
        "head",
        scatter_dimension=0,
        tiled=True,
    ).astype(jnp.float32)
    mixed = (skip_wide + head_sum).astype(jnp.bfloat16)
    part_w_out = jnp.einsum("tbe,tbc->ec", o_narrow, grad_rows, preferred_element_type=jnp.float32)
    d_out = jnp.einsum("tbc,ec->tbe", grad_rows, w_out, preferred_element_type=jnp.float32).astype(
        jnp.bfloat16
    )
    d_out = d_out.reshape(tower_rows, seq_count, local_heads, DH)
    delta = jnp.sum(d_out.astype(jnp.float32) * attention_output, axis=-1)
    probability_gradient = jnp.einsum(
        "qbhd,kbhd->bhqk", d_out, value_all, preferred_element_type=jnp.float32
    )
    d_scores = soft_weights * (probability_gradient - jnp.transpose(delta, (1, 2, 0))[..., None])
    narrow_gradient = d_scores.astype(jnp.bfloat16)
    query_gradient = logit_scale * jnp.einsum(
        "bhqk,kbhd->qbhd", narrow_gradient, key_all, preferred_element_type=jnp.float32
    )
    key_terms = logit_scale * jnp.einsum(
        "bhqk,qbhd->kbhd", narrow_gradient, query_matrix, preferred_element_type=jnp.float32
    )
    value_terms = jnp.einsum(
        "bhqk,qbhd->kbhd", narrow_probabilities, d_out, preferred_element_type=jnp.float32
    )
    d_keys, d_values = (
        lax.psum_scatter(
            key_terms.astype(jnp.bfloat16), "seq", scatter_dimension=0, tiled=True
        ).astype(jnp.float32),
        lax.psum_scatter(
            value_terms.astype(jnp.bfloat16), "seq", scatter_dimension=0, tiled=True
        ).astype(jnp.float32),
    )
    dqkv = (
        jnp.stack([query_gradient, d_keys, d_values])
        .reshape(3, tower_rows, seq_count, local_width)
        .astype(jnp.bfloat16)
    )
    part_w_qkv = jnp.einsum("tbc,itbe->ice", normed_rows, dqkv, preferred_element_type=jnp.float32)
    piece = dqkv
    d_normed = lax.psum_scatter(
        jnp.einsum("itbe,ice->tbc", piece, w_qkv, preferred_element_type=jnp.float32).astype(
            jnp.bfloat16
        ),
        "head",
        scatter_dimension=0,
        tiled=True,
    ).astype(jnp.float32)
    unit_rows = skip_wide * inv_rms
    scaled = d_normed * norm_gain
    d_skip = grad_out.astype(jnp.float32) + inv_rms * (
        scaled - unit_rows * jnp.mean(scaled * unit_rows, axis=-1, keepdims=True)
    )
    d_act = jnp.repeat(d_skip, 2, axis=0) * 0.5
    d_conv = gelu_pull(d_act)[0].astype(jnp.bfloat16)
    d_pad = padded_2(d_conv, ((("seq", "head"), 0),), 2)
    grad_input = jnp.zeros((fine_rows, seq_count, enc_in.shape[2]), jnp.float32)
    for offset in range(KW):
        grad_input = grad_input + jnp.einsum(
            "tbo,io->tbi",
            d_pad[4 - offset : 4 - offset + fine_rows],
            conv_weight[offset],
            preferred_element_type=jnp.float32,
        )
    grad_w_qkv, grad_w_out = (
        lax.psum(part_w_qkv.astype(jnp.bfloat16), "seq").astype(jnp.float32),
        lax.psum(part_w_out.astype(jnp.bfloat16), "seq").astype(jnp.float32),
    )
    return (mixed, grad_input.astype(jnp.bfloat16), grad_w_qkv, grad_w_out)


def body(enc_in, conv_weight, norm_gain, w_qkv, w_out, grad_out):
    heads = w_qkv.shape[2] // DH
    seqs = enc_in.shape[1]
    fits = heads == 2 and seqs == 4 and seqs * heads == lax.axis_size("seq")
    fits = fits and conv_weight.shape[2] == seqs * w_qkv.shape[2]
    chosen = unit_body if fits else gathered_body
    return chosen(enc_in, conv_weight, norm_gain, w_qkv, w_out, grad_out)


def solution(mesh):
    return jax.shard_map(
        body,
        mesh=mesh,
        in_specs=(
            P(("seq", "head"), None, None),
            P(),
            P(),
            P(None, None, "head"),
            P("head", None),
            P(("seq", "head"), None, None),
        ),
        out_specs=(
            P(("seq", "head"), None, None),
            P(("seq", "head"), None, None),
            P(None, None, "head"),
            P("head", None),
        ),
        check_vma=False,
    )
```

```python
import functools

import jax
import jax.numpy as jnp
from jax import lax
from jax.experimental import pallas as pl
from jax.experimental.pallas import tpu as pltpu
from jax.sharding import PartitionSpec as P

DH = 192
KW = 5
VMEM_LIMIT = 24 * 1024 * 1024
COST = pl.CostEstimate(flops=1000, bytes_accessed=1000, transcendentals=0)
BF = jnp.bfloat16
F32 = jnp.float32
TOKEN = jax.ShapeDtypeStruct((8, 128), F32)


def params():
    return pltpu.CompilerParams(vmem_limit_bytes=VMEM_LIMIT)


def dot(a, b, contract):
    return lax.dot_general(a, b, (contract, ((), ())), preferred_element_type=F32)


NN = ((1,), (0,))
NT = ((1,), (1,))
TN = ((0,), (0,))


def whole(shape):
    return pl.BlockSpec(shape, lambda *_: (0,) * len(shape))


SCALARS = pl.BlockSpec(memory_space=pltpu.SMEM)


def spare(deps):
    return [pl.BlockSpec(memory_space=pl.ANY)] * len(deps)


def turned_rows(ref, low_ref, high_ref, parity, shift):
    seqs, rows, width = ref.shape[1:]
    own = ref[parity]
    if shift != 1:
        wide = own.astype(F32)
        if shift == 0:
            parts = [low_ref[parity].astype(F32), wide[:, : rows - 1]]
        else:
            parts = [wide[:, 1:], high_ref[parity].astype(F32)]
        own = jnp.concatenate(parts, axis=1).astype(BF)
    return own.reshape(seqs * rows, width)


def conv_kernel(
    at_ref, x_ref, low_ref, high_ref, w_ref, gain_ref, skip_ref, slope_ref, *rest
):
    normed_refs, (lhs, squares, whole_normed) = rest[:-3], rest[-3:]
    step = pl.program_id(0)
    seqs, rows, c_in = x_ref.shape[1:]
    half = seqs * rows
    tile = w_ref.shape[2]

    @pl.when(step == 0)
    def _():
        for parity in range(2):
            for shift in range(3):
                value = turned_rows(x_ref, low_ref, high_ref, parity, shift)
                for out in range(2):
                    tap = 2 * shift + parity - out
                    if 0 <= tap < KW:
                        lhs[out * half : (out + 1) * half, tap * c_in : (tap + 1) * c_in] = value
        squares[...] = jnp.zeros_like(squares)

    conv = dot(lhs[...], w_ref[...].reshape(KW * c_in, tile), NN)
    root = 0.7978845608028654
    total = None
    for parity in range(2):
        x = conv[parity * half : (parity + 1) * half, :]
        square = x * x
        t = jnp.tanh(root * (x + 0.044715 * (square * x)))
        left = 0.5 * (1.0 + t)
        act = x * left
        slope = left + (0.5 * root) * x * (1.0 - t * t) * (1.0 + (3 * 0.044715) * square)
        slope_ref[parity] = slope.reshape(slope_ref.shape[1:])
        total = act if total is None else total + act
    skip = (0.5 * total).astype(BF)
    columns = pl.ds(pl.multiple_of(step * tile, tile), tile)
    skip_ref[:, :, columns] = skip.reshape(seqs, rows, tile)
    wide = skip.astype(F32)
    squares[...] += jnp.sum(wide * wide, axis=-1, keepdims=True)

    @pl.when(step == pl.num_programs(0) - 1)
    def _():
        width = skip_ref.shape[2]
        inv = lax.rsqrt(squares[...] * (1.0 / width) + 1e-06)
        wide = skip_ref[...].reshape(half, width).astype(F32)
        normed = (wide * inv * gain_ref[...]).astype(BF)
        whole_normed[...] = normed.reshape(whole_normed.shape)
        for slot in range(seqs):
            normed_refs[slot][...] = whole_normed[at_ref[0] ^ slot]


def encoder(at, pairs, low, high, conv_weight, norm_gain):
    _, seqs, rows, c_in = pairs.shape
    width = conv_weight.shape[2]
    tile = 256 if width % 256 == 0 else width
    shape = (seqs, rows, width)
    outs = pl.pallas_call(
        conv_kernel,
        grid=(width // tile,),
        in_specs=[
            SCALARS,
            whole(pairs.shape),
            whole(low.shape),
            whole(high.shape),
            pl.BlockSpec((KW, c_in, tile), lambda n: (0, 0, n)),
            whole((1, width)),
        ],
        out_specs=[
            whole(shape),
            pl.BlockSpec((2, seqs, rows, tile), lambda n: (0, 0, 0, n)),
        ]
        + [whole((rows, width))] * seqs,
        out_shape=[
            jax.ShapeDtypeStruct(shape, BF),
            jax.ShapeDtypeStruct((2,) + shape, F32),
        ]
        + [jax.ShapeDtypeStruct((rows, width), BF)] * seqs,
        scratch_shapes=[
            pltpu.VMEM((2 * seqs * rows, KW * c_in), BF),
            pltpu.VMEM((seqs * rows, 1), F32),
            pltpu.VMEM(shape, BF),
        ],
        compiler_params=params(),
        cost_estimate=COST,
        name="encoder_forward",
    )(at, pairs, low, high, conv_weight, norm_gain.reshape(1, width))
    return outs[0], outs[1], list(outs[2:])


def d_conv_kernel(at_ref, own_ref, near_ref, far_ref, *refs):
    skip_ref, grad_ref, gain_ref, slope_ref, out_ref, first_ref, last_ref = refs
    rows = out_ref.shape[2]
    for slot, (ref, place) in enumerate(((own_ref, 0), (near_ref, 0), (far_ref, 0), (far_ref, 1))):
        b = at_ref[0] ^ slot
        wide = skip_ref[b].astype(F32)
        inv = lax.rsqrt(jnp.mean(wide * wide, axis=-1, keepdims=True) + 1e-06)
        unit = wide * inv
        scaled = ref[place].astype(F32) * gain_ref[...]
        d_skip = grad_ref[b].astype(F32) + inv * (
            scaled - unit * jnp.mean(scaled * unit, axis=-1, keepdims=True)
        )
        d_act = 0.5 * d_skip
        for parity in range(2):
            value = slope_ref[parity, b] * d_act
            out_ref[parity, b] = value.astype(BF)
            first_ref[parity, b] = value[:1].astype(BF)
            last_ref[parity, b] = value[rows - 1 :].astype(BF)


def conv_gradient(at, own, near, far, skip, grad, norm_gain, slope):
    vmem = pl.BlockSpec(memory_space=pltpu.VMEM)
    edge = jax.ShapeDtypeStruct(slope.shape[:2] + (1, slope.shape[3]), BF)
    return pl.pallas_call(
        d_conv_kernel,
        in_specs=[SCALARS] + [vmem] * 7,
        out_specs=[vmem] * 3,
        out_shape=[jax.ShapeDtypeStruct(slope.shape, BF)] + [edge] * 2,
        compiler_params=params(),
        cost_estimate=COST,
        name="conv_gradient",
    )(at, own, near, far, skip, grad, norm_gain.reshape(1, -1), slope)


def mixed_body(seqs, at_ref, *refs):
    skip_ref, out_ref = refs[seqs:]
    for slot in range(seqs):
        b = at_ref[0] ^ slot
        out_ref[b] = (skip_ref[b].astype(F32) + refs[slot][...].astype(F32)).astype(BF)


def mixed_call(at, terms, skip):
    seqs = len(terms)
    vmem = pl.BlockSpec(memory_space=pltpu.VMEM)
    return pl.pallas_call(
        functools.partial(mixed_body, seqs),
        in_specs=[SCALARS] + [vmem] * (seqs + 1),
        out_specs=vmem,
        out_shape=jax.ShapeDtypeStruct(skip.shape, BF),
        compiler_params=params(),
        cost_estimate=COST,
        name="mixed_sum",
    )(at, *terms, skip)


def conv_back_kernel(d_ref, low_ref, high_ref, w_ref, *rest):
    out_ref, turned, acc = rest[-3:]
    step = pl.program_id(0)

    @pl.when(step == 0)
    def _():
        for parity in range(2):
            for shift in range(3):
                turned[parity, shift] = turned_rows(d_ref, low_ref, high_ref, parity, shift).T

    for tap in range(KW):

        @pl.when(step == tap)
        def _():
            places = [KW - 1 - tap, KW - tap]
            rhs = jnp.concatenate([turned[p % 2, p // 2] for p in places], axis=1)
            term = dot(w_ref[0], rhs, NN)
            if tap == 0:
                acc[...] = term
            elif tap < KW - 1:
                acc[...] += term
            else:
                out_ref[...] = (acc[...] + term).T.astype(BF)


def conv_back(d_conv, low, high, conv_weight, *deps):
    _, seqs, rows, width = d_conv.shape
    c_in = conv_weight.shape[1]
    flat = 2 * seqs * rows
    return pl.pallas_call(
        conv_back_kernel,
        grid=(KW,),
        in_specs=[
            whole(d_conv.shape),
            whole(low.shape),
            whole(high.shape),
            pl.BlockSpec((1, c_in, width), lambda k: (k, 0, 0)),
        ]
        + spare(deps),
        out_specs=whole((flat, c_in)),
        out_shape=jax.ShapeDtypeStruct((flat, c_in), BF),
        scratch_shapes=[
            pltpu.VMEM((2, 3, width, seqs * rows), BF),
            pltpu.VMEM((c_in, flat), F32),
        ],
        compiler_params=params(),
        cost_estimate=COST,
        name="encoder_backward",
    )(d_conv, low, high, conv_weight, *deps)


def pack_kernel(w_ref, pack_ref, turned_ref, token_ref):
    token_ref[...] = jnp.zeros_like(token_ref)
    for i in range(3):
        for head in range(pack_ref.shape[0]):
            part = w_ref[i, :, head * DH : (head + 1) * DH]
            columns = slice(i * DH, (i + 1) * DH)
            pack_ref[head, :, columns] = part
            turned_ref[head, columns, :] = part.T


def pack_weights(w_qkv):
    _, width, local = w_qkv.shape
    heads = local // DH
    tile = local
    return pl.pallas_call(
        pack_kernel,
        grid=(width // tile,),
        in_specs=[pl.BlockSpec((3, tile, local), lambda n: (0, n, 0))],
        out_specs=[
            pl.BlockSpec((heads, tile, 3 * DH), lambda n: (0, n, 0)),
            pl.BlockSpec((heads, 3 * DH, tile), lambda n: (0, 0, n)),
            pl.BlockSpec(TOKEN.shape, lambda n: (0, 0)),
        ],
        out_shape=[
            jax.ShapeDtypeStruct((heads, width, 3 * DH), BF),
            jax.ShapeDtypeStruct((heads, 3 * DH, width), BF),
            TOKEN,
        ],
        compiler_params=params(),
        cost_estimate=COST,
        name="pack_weights",
    )(w_qkv)


def product_kernel(head_ref, x_ref, w_ref, *rest, contract):
    del head_ref
    out_ref, token_ref = rest[-2:]
    token_ref[...] = jnp.zeros_like(token_ref)
    value = dot(x_ref[...], w_ref[0], contract).astype(BF)
    out_ref[:, : value.shape[1]] = value
    if value.shape[1] < out_ref.shape[1]:
        out_ref[:, value.shape[1] :] = jnp.zeros_like(out_ref[:, value.shape[1] :])


def head_product(head, x, weight, contract, name, *deps):
    columns = weight.shape[2] if contract == NN else weight.shape[1]
    columns += -columns % 128
    rows, width = x.shape
    return pl.pallas_call(
        functools.partial(product_kernel, contract=contract),
        grid_spec=pltpu.PrefetchScalarGridSpec(
            num_scalar_prefetch=1,
            grid=(1,),
            in_specs=[
                pl.BlockSpec((rows, width), lambda i, head: (0, 0)),
                pl.BlockSpec((1,) + weight.shape[1:], lambda i, head: (head[0], 0, 0)),
            ]
            + spare(deps),
            out_specs=[
                pl.BlockSpec((rows, columns), lambda i, head: (0, 0)),
                pl.BlockSpec(TOKEN.shape, lambda i, head: (0, 0)),
            ],
        ),
        out_shape=[jax.ShapeDtypeStruct((rows, columns), BF), TOKEN],
        compiler_params=params(),
        cost_estimate=COST,
        name=name,
    )(head, x, weight, *deps)


def attention_kernel(qa_ref, qb_ref, da_ref, db_ref, *rest, block):
    oa_ref, ob_ref, k_all, v_all, dk_acc, dv_acc = rest[-6:]
    scale = DH ** (-0.5)
    half = qa_ref.shape[0]
    for place, ref in enumerate((qa_ref, qb_ref)):
        rows = pl.ds(place * half, half)
        k_all[rows, :] = ref[:, DH : 2 * DH]
        v_all[rows, :] = ref[:, 2 * DH : 3 * DH]
    k = k_all[...]
    v = v_all[...]
    for place, (q_ref, d_ref, out_ref) in enumerate(
        ((qa_ref, da_ref, oa_ref), (qb_ref, db_ref, ob_ref))
    ):
        for start in range(0, half, block):
            rows = pl.ds(start, block)
            q = q_ref[rows, 0:DH]
            d_o = d_ref[rows, 0:DH]
            s = dot(q, k, NT) * scale
            e = jnp.exp(s - jnp.max(s, axis=-1, keepdims=True))
            p = e * (1.0 / jnp.sum(e, axis=-1, keepdims=True))
            p_b = p.astype(BF)
            o = dot(p_b, v, NN)
            delta = jnp.sum(d_o.astype(F32) * o, axis=-1, keepdims=True)
            d_p = dot(d_o, v, NT)
            ds = (p * (d_p - delta)).astype(BF)
            dq = scale * dot(ds, k, NN)
            dk = dot(ds, q, TN)
            dv = dot(p_b, d_o, TN)
            if place == 0 and start == 0:
                dk_acc[...] = dk
                dv_acc[...] = dv
            else:
                dk_acc[...] += dk
                dv_acc[...] += dv
            out_ref[rows, 0:DH] = dq.astype(BF)
            out_ref[rows, 3 * DH : 4 * DH] = o.astype(BF)
    for place, out_ref in enumerate((oa_ref, ob_ref)):
        rows = pl.ds(place * half, half)
        out_ref[:, DH : 2 * DH] = (scale * dk_acc[rows, :]).astype(BF)
        out_ref[:, 2 * DH : 3 * DH] = dv_acc[rows, :].astype(BF)


def attention(qkv_a, qkv_b, d_a, d_b, *deps):
    half = qkv_a.shape[0]
    shape = jax.ShapeDtypeStruct((half, 4 * DH), BF)
    return pl.pallas_call(
        functools.partial(attention_kernel, block=min(256, half)),
        in_specs=[pl.BlockSpec(memory_space=pltpu.VMEM)] * 4 + spare(deps),
        out_shape=[shape, shape],
        scratch_shapes=[
            pltpu.VMEM((2 * half, DH), BF),
            pltpu.VMEM((2 * half, DH), BF),
            pltpu.VMEM((2 * half, DH), F32),
            pltpu.VMEM((2 * half, DH), F32),
        ],
        compiler_params=params(),
        cost_estimate=COST,
        name="attention",
    )(qkv_a, qkv_b, d_a, d_b, *deps)


def term_kernel(head_ref, a_ref, b_ref, w_ref, *rest, first, last):
    head = head_ref[0]
    total = dot(a_ref[:, first:last], w_ref[head], NN)
    total += dot(b_ref[:, first:last], w_ref[1 - head], NN)
    rest[-1][...] = total.astype(BF)


def pair_term(head, mine, got, weight, first, last, name, *deps):
    half, full = mine.shape
    heads, depth, width = weight.shape
    tile = 512 if width % 512 == 0 else width
    return pl.pallas_call(
        functools.partial(term_kernel, first=first, last=last),
        grid_spec=pltpu.PrefetchScalarGridSpec(
            num_scalar_prefetch=1,
            grid=(width // tile,),
            in_specs=[
                pl.BlockSpec((half, full), lambda n, at: (0, 0)),
                pl.BlockSpec((half, full), lambda n, at: (0, 0)),
                pl.BlockSpec((heads, depth, tile), lambda n, at: (0, 0, n)),
            ]
            + spare(deps),
            out_specs=pl.BlockSpec((half, tile), lambda n, at: (0, n)),
        ),
        out_shape=jax.ShapeDtypeStruct((half, width), BF),
        compiler_params=params(),
        cost_estimate=COST,
        name=name,
    )(head, mine, got, weight, *deps)


def weight_kernel(at_ref, xa_ref, xb_ref, ga_ref, gb_ref, ra_ref, rb_ref, *rest):
    del at_ref
    out_refs, turned = rest[:-1], rest[-1]
    step = pl.program_id(0)
    half = ra_ref.shape[0]
    split = 3 * DH

    @pl.when(step == 0)
    def _():
        turned[:, :half] = ra_ref[...].T
        turned[:, half:] = rb_ref[...].T

    a, b = slice(0, half), slice(half, 2 * half)
    qkv = dot(turned[:split, a], xa_ref[...], NN) + dot(turned[:split, b], xb_ref[...], NN)
    out = dot(turned[split:, a], ga_ref[...], NN) + dot(turned[split:, b], gb_ref[...], NN)
    for slot, out_ref in enumerate(out_refs):

        @pl.when(step == slot)
        def _():
            out_ref[:split, :] = qkv.astype(BF)
            out_ref[split:, :] = out.astype(BF)


def weight_gradients(at, xa, xb, ga, gb, ra, rb, seqs):
    half, width = xa.shape
    chunk = width // seqs
    full = ra.shape[1]
    column = pl.BlockSpec((half, chunk), lambda r, at: (0, r ^ at[0]))
    rest = pl.BlockSpec((half, full), lambda r, at: (0, 0))
    return pl.pallas_call(
        weight_kernel,
        grid_spec=pltpu.PrefetchScalarGridSpec(
            num_scalar_prefetch=1,
            grid=(seqs,),
            in_specs=[column] * 4 + [rest] * 2,
            out_specs=[pl.BlockSpec((full, chunk), lambda r, at: (0, 0))] * seqs,
            scratch_shapes=[pltpu.VMEM((full, 2 * half), BF)],
        ),
        out_shape=[jax.ShapeDtypeStruct((full, chunk), BF)] * seqs,
        compiler_params=params(),
        cost_estimate=COST,
        name="weight_gradients",
    )(at, xa, xb, ga, gb, ra, rb)


def weight_sum_kernel(*refs, count):
    part_refs, out_refs = refs[:count], refs[-2:]
    split = 3 * DH
    total = part_refs[0][...].astype(F32)
    for ref in part_refs[1:]:
        total = total + ref[...].astype(F32)
    turned = total[:split].T.astype(BF)
    for part, out_ref in enumerate(out_refs):
        rows = slice(part * DH, (part + 1) * DH)
        out_ref[:, :split] = turned[rows]
        out_ref[:, split:] = total[split:, rows].astype(BF)


def weight_sum(parts, *deps):
    full, chunk = parts[0].shape
    return pl.pallas_call(
        functools.partial(weight_sum_kernel, count=len(parts)),
        in_specs=[pl.BlockSpec(memory_space=pltpu.VMEM)] * len(parts) + spare(deps),
        out_shape=[jax.ShapeDtypeStruct((chunk // 2, full), BF)] * 2,
        compiler_params=params(),
        cost_estimate=COST,
        name="weight_sum",
    )(*parts, *deps)


def unpack_kernel(at_ref, *refs):
    qkv_ref, out_ref = refs[-2:]
    step = pl.program_id(0)
    split = 3 * DH
    for turn in range(4):

        @pl.when(step == turn)
        def _():
            both = []
            for near_a, near_b, far_a, far_b in (refs[:4], refs[4:8]):
                first = near_a if turn < 2 else far_a
                second = near_b if turn % 2 == 0 else far_b
                both.append((first[...].astype(F32), second[...].astype(F32)))
            swapped = at_ref[1] != 0
            for part in range(2):
                mine, other = both[0][part], both[1][part]
                low = jnp.where(swapped, other, mine)
                high = jnp.where(swapped, mine, other)
                rows = slice(part * DH, (part + 1) * DH)
                for i in range(3):
                    columns = slice(i * DH, (i + 1) * DH)
                    qkv_ref[i, rows, :] = jnp.concatenate(
                        [low[:, columns], high[:, columns]], axis=1
                    )
                out_ref[:DH, rows] = low[:, split:]
                out_ref[DH:, rows] = high[:, split:]


def unpack_weights(at, mine, other):
    rows, full = mine[0].shape
    half = rows // 2
    width = 4 * rows
    local = 2 * DH
    specs = [
        pl.BlockSpec((half, full), lambda j, at: (jnp.minimum(j, 1), 0)),
        pl.BlockSpec((half, full), lambda j, at: (j // 2, 0)),
        pl.BlockSpec((half, full), lambda j, at: (jnp.maximum(j - 2, 0), 0)),
        pl.BlockSpec((half, full), lambda j, at: (j // 2, 0)),
    ]
    return pl.pallas_call(
        unpack_kernel,
        grid_spec=pltpu.PrefetchScalarGridSpec(
            num_scalar_prefetch=1,
            grid=(4,),
            in_specs=specs * 2,
            out_specs=[
                pl.BlockSpec((3, rows, local), lambda j, at: (0, at[0] ^ j, 0)),
                pl.BlockSpec((local, rows), lambda j, at: (0, at[0] ^ j)),
            ],
        ),
        out_shape=[
            jax.ShapeDtypeStruct((3, width, local), F32),
            jax.ShapeDtypeStruct((local, width), F32),
        ],
        compiler_params=params(),
        cost_estimate=COST,
        name="weight_outputs",
    )(at, *mine, *other)


def neighbour_edges(first, last):
    axes = ("seq", "head")
    count = lax.axis_size(axes)
    forward = [(i, i + 1) for i in range(count - 1)]
    backward = [(target, source) for source, target in forward]
    return lax.ppermute(last, axes, forward), lax.ppermute(first, axes, backward)


def after(value, *others):
    return lax.optimization_barrier((value,) + others)[0]


def trade_chip(x, bit, heads):
    count = lax.axis_size("seq")
    return lax.ppermute(x, "seq", [(s, s ^ (bit * heads)) for s in range(count)])


def swap_heads(x):
    count = lax.axis_size("seq")
    return lax.ppermute(x, "seq", [(s, s + 1 - 2 * (s % 2)) for s in range(count)])


def unit_body(enc_in, conv_weight, norm_gain, w_qkv, w_out, grad_out):
    rows = enc_in.shape[0] // 2
    seqs = enc_in.shape[1]
    width = conv_weight.shape[2]
    local = w_qkv.shape[2]
    heads = local // DH
    groups = lax.axis_size("head")
    half = groups * seqs * rows
    place = lax.axis_index("seq")
    own_seq = (place // heads).astype(jnp.int32)
    own_head = (place % heads).astype(jnp.int32)
    at = jnp.stack([own_seq, own_head])
    head_mine = own_head.reshape(1)
    head_other = (1 - own_head).reshape(1)

    def to_chips(slots):
        return [x if j == 0 else trade_chip(x, j, heads) for j, x in enumerate(slots)]

    order = (0, 2, 1, 3)

    grad_z = lax.all_gather(grad_out, "head", axis=0, tiled=False)

    pairs = jnp.transpose(enc_in.reshape(rows, 2, seqs, enc_in.shape[2]), (1, 2, 0, 3))
    low, high = neighbour_edges(pairs[:, :, :1, :], pairs[:, :, -1:, :])
    skip, slope, normed = encoder(at, pairs, low, high, conv_weight, norm_gain)
    normed = to_chips(normed)
    normed_slab = jnp.concatenate([normed[j] for j in order], axis=0)
    normed_rows = lax.all_gather(normed_slab, "head", axis=0, tiled=True)

    grad_z = after(grad_z, normed_slab)
    grad_slots = to_chips(
        [lax.dynamic_index_in_dim(grad_z, own_seq ^ j, 2, keepdims=False) for j in range(seqs)]
    )
    grad_rows = jnp.stack([grad_slots[j] for j in order], axis=1).reshape(half, width)
    w_pack, w_turned, packed = pack_weights(after(w_qkv, normed_slab))
    w_rows = w_out.reshape(heads, DH, width)
    d_other, one = head_product(head_other, grad_rows, w_rows, NT, "d_o_other")
    d_got = swap_heads(d_other)
    d_mine, two = head_product(head_mine, grad_rows, w_rows, NT, "d_o_own")
    grad_swapped = swap_heads(grad_rows)
    normed_rows = after(normed_rows, packed, one, two)

    qkv_other, _ = head_product(
        head_other, normed_rows, w_pack, NN, "qkv_other", d_got, grad_swapped
    )
    qkv_got = swap_heads(qkv_other)
    normed_swapped = swap_heads(normed_rows)
    qkv_mine, _ = head_product(head_mine, normed_rows, w_pack, NN, "qkv_own")
    result_mine, result_other = attention(qkv_mine, qkv_got, d_mine, d_got, normed_swapped)
    result_got = swap_heads(result_other)

    shape = (groups, seqs, rows, width)
    d_term = pair_term(head_mine, result_mine, result_got, w_turned, 0, 3 * DH, "d_term")
    d_normed = lax.psum_scatter(d_term.reshape(shape), "head", scatter_dimension=0, tiled=False)
    part = weight_gradients(
        own_seq.reshape(1),
        normed_rows,
        normed_swapped,
        grad_rows,
        grad_swapped,
        result_mine,
        result_other,
        seqs,
    )
    part = to_chips(part)
    head_term = pair_term(
        head_mine, result_mine, result_got, w_rows, 3 * DH, 4 * DH, "head_term", part[1]
    )
    head_sum = lax.psum_scatter(head_term.reshape(shape), "head", scatter_dimension=0, tiled=False)

    near = trade_chip(d_normed[2:], 1, heads)
    far = trade_chip(jnp.stack([d_normed[1], near[1]]), 2, heads)
    grad = jnp.transpose(after(grad_out, d_term), (1, 0, 2))
    d_conv, first, last = conv_gradient(at, d_normed, near, far, skip, grad, norm_gain, slope)
    low, high = neighbour_edges(first, last)

    half_a, half_b = weight_sum(part, far)
    got_a = trade_chip(half_a, 1, heads)
    got_b = trade_chip(half_b, 2, heads)
    near_a = jnp.concatenate([half_a, after(got_a, low, high)], axis=0)
    near_b = jnp.concatenate([half_b, after(got_b, low, high)], axis=0)
    far_a = trade_chip(near_a, 2, heads)
    far_b = trade_chip(near_b, 1, heads)
    near_other = [swap_heads(near_a), swap_heads(near_b)]
    grad_input = conv_back(d_conv, low, high, conv_weight, *near_other)
    far_other = [swap_heads(after(x, grad_input)) for x in (far_a, far_b)]
    grad_w_qkv, grad_w_out = unpack_weights(
        at, [near_a, near_b, far_a, far_b], near_other + far_other
    )

    head_sum = after(head_sum, grad_input)
    head_sum = to_chips([head_sum[order.index(j)] for j in range(seqs)])
    mixed = mixed_call(at, head_sum, skip)
    grad_input = jnp.transpose(grad_input.reshape(2, seqs, rows, -1), (2, 0, 1, 3))
    return (
        jnp.transpose(mixed, (1, 0, 2)),
        grad_input.reshape(enc_in.shape),
        grad_w_qkv,
        grad_w_out,
    )


def padded_2(block, sides, width):
    for axis, dim in sides:
        count = lax.axis_size(axis)
        forward = [(i, i + 1) for i in range(count - 1)]
        backward = [(target, source) for source, target in forward]
        low = lax.ppermute(
            lax.slice_in_dim(block, block.shape[dim] - width, None, axis=dim), axis, forward
        )
        high = lax.ppermute(lax.slice_in_dim(block, 0, width, axis=dim), axis, backward)
        block = jnp.concatenate([low, block, high], axis=dim)
    return block


def gathered_body(enc_in, conv_weight, norm_gain, w_qkv, w_out, grad_out):
    fine_rows = enc_in.shape[0]
    slab_rows = fine_rows // 2
    seq_count = enc_in.shape[1]
    out_width = conv_weight.shape[2]
    local_width = w_qkv.shape[2]
    local_heads = local_width // DH
    logit_scale = DH ** (-0.5)
    padded = padded_2(enc_in, ((("seq", "head"), 0),), 2)
    convolved = jnp.zeros((fine_rows, seq_count, out_width), jnp.float32)
    for offset in range(KW):
        convolved = convolved + jnp.einsum(
            "tbi,io->tbo",
            padded[offset : offset + fine_rows],
            conv_weight[offset],
            preferred_element_type=jnp.float32,
        )
    activated, gelu_pull = jax.vjp(jax.nn.gelu, convolved)
    skip = jnp.mean(activated.reshape(slab_rows, 2, seq_count, out_width), axis=1).astype(
        jnp.bfloat16
    )
    skip_wide = skip.astype(jnp.float32)
    inv_rms = lax.rsqrt(jnp.mean(skip_wide * skip_wide, axis=-1, keepdims=True) + 1e-06)
    normed = (skip_wide * inv_rms * norm_gain).astype(jnp.bfloat16)
    normed_rows = lax.all_gather(normed, "head", axis=0, tiled=True)
    grad_rows = lax.all_gather(grad_out, "head", axis=0, tiled=True)
    tower_rows = normed_rows.shape[0]
    qkv = jnp.einsum(
        "tbc,ice->itbe", normed_rows, w_qkv, preferred_element_type=jnp.float32
    ).astype(jnp.bfloat16)
    qkv = qkv.reshape(3, tower_rows, seq_count, local_heads, DH)
    query_matrix, key_matrix, value_matrix = (qkv[0], qkv[1], qkv[2])
    key_all, value_all = (
        lax.all_gather(key_matrix, "seq", axis=0, tiled=True),
        lax.all_gather(value_matrix, "seq", axis=0, tiled=True),
    )
    attention_logits = (
        jnp.einsum("qbhd,kbhd->bhqk", query_matrix, key_all, preferred_element_type=jnp.float32)
        * logit_scale
    )
    row_peak = jnp.max(attention_logits, axis=-1, keepdims=True)
    exponent = jnp.exp(attention_logits - row_peak)
    row_total = jnp.sum(exponent, axis=-1, keepdims=True)
    soft_weights = exponent / row_total
    narrow_probabilities = soft_weights.astype(jnp.bfloat16)
    attention_output = jnp.einsum(
        "bhqk,kbhd->qbhd", narrow_probabilities, value_all, preferred_element_type=jnp.float32
    )
    o_narrow = attention_output.reshape(tower_rows, seq_count, local_width).astype(jnp.bfloat16)
    piece = o_narrow
    head_sum = lax.psum_scatter(
        jnp.einsum("tbe,ec->tbc", piece, w_out, preferred_element_type=jnp.float32).astype(
            jnp.bfloat16
        ),
        "head",
        scatter_dimension=0,
        tiled=True,
    ).astype(jnp.float32)
    mixed = (skip_wide + head_sum).astype(jnp.bfloat16)
    part_w_out = jnp.einsum("tbe,tbc->ec", o_narrow, grad_rows, preferred_element_type=jnp.float32)
    d_out = jnp.einsum("tbc,ec->tbe", grad_rows, w_out, preferred_element_type=jnp.float32).astype(
        jnp.bfloat16
    )
    d_out = d_out.reshape(tower_rows, seq_count, local_heads, DH)
    delta = jnp.sum(d_out.astype(jnp.float32) * attention_output, axis=-1)
    probability_gradient = jnp.einsum(
        "qbhd,kbhd->bhqk", d_out, value_all, preferred_element_type=jnp.float32
    )
    d_scores = soft_weights * (probability_gradient - jnp.transpose(delta, (1, 2, 0))[..., None])
    narrow_gradient = d_scores.astype(jnp.bfloat16)
    query_gradient = logit_scale * jnp.einsum(
        "bhqk,kbhd->qbhd", narrow_gradient, key_all, preferred_element_type=jnp.float32
    )
    key_terms = logit_scale * jnp.einsum(
        "bhqk,qbhd->kbhd", narrow_gradient, query_matrix, preferred_element_type=jnp.float32
    )
    value_terms = jnp.einsum(
        "bhqk,qbhd->kbhd", narrow_probabilities, d_out, preferred_element_type=jnp.float32
    )
    d_keys, d_values = (
        lax.psum_scatter(
            key_terms.astype(jnp.bfloat16), "seq", scatter_dimension=0, tiled=True
        ).astype(jnp.float32),
        lax.psum_scatter(
            value_terms.astype(jnp.bfloat16), "seq", scatter_dimension=0, tiled=True
        ).astype(jnp.float32),
    )
    dqkv = (
        jnp.stack([query_gradient, d_keys, d_values])
        .reshape(3, tower_rows, seq_count, local_width)
        .astype(jnp.bfloat16)
    )
    part_w_qkv = jnp.einsum("tbc,itbe->ice", normed_rows, dqkv, preferred_element_type=jnp.float32)
    piece = dqkv
    d_normed = lax.psum_scatter(
        jnp.einsum("itbe,ice->tbc", piece, w_qkv, preferred_element_type=jnp.float32).astype(
            jnp.bfloat16
        ),
        "head",
        scatter_dimension=0,
        tiled=True,
    ).astype(jnp.float32)
    unit_rows = skip_wide * inv_rms
    scaled = d_normed * norm_gain
    d_skip = grad_out.astype(jnp.float32) + inv_rms * (
        scaled - unit_rows * jnp.mean(scaled * unit_rows, axis=-1, keepdims=True)
    )
    d_act = jnp.repeat(d_skip, 2, axis=0) * 0.5
    d_conv = gelu_pull(d_act)[0].astype(jnp.bfloat16)
    d_pad = padded_2(d_conv, ((("seq", "head"), 0),), 2)
    grad_input = jnp.zeros((fine_rows, seq_count, enc_in.shape[2]), jnp.float32)
    for offset in range(KW):
        grad_input = grad_input + jnp.einsum(
            "tbo,io->tbi",
            d_pad[4 - offset : 4 - offset + fine_rows],
            conv_weight[offset],
            preferred_element_type=jnp.float32,
        )
    grad_w_qkv, grad_w_out = (
        lax.psum(part_w_qkv.astype(jnp.bfloat16), "seq").astype(jnp.float32),
        lax.psum(part_w_out.astype(jnp.bfloat16), "seq").astype(jnp.float32),
    )
    return (mixed, grad_input.astype(jnp.bfloat16), grad_w_qkv, grad_w_out)


def body(enc_in, conv_weight, norm_gain, w_qkv, w_out, grad_out):
    heads = w_qkv.shape[2] // DH
    seqs = enc_in.shape[1]
    fits = heads == 2 and seqs == 4 and seqs * heads == lax.axis_size("seq")
    fits = fits and conv_weight.shape[2] == seqs * w_qkv.shape[2]
    chosen = unit_body if fits else gathered_body
    return chosen(enc_in, conv_weight, norm_gain, w_qkv, w_out, grad_out)


def solution(mesh):
    return jax.shard_map(
        body,
        mesh=mesh,
        in_specs=(
            P(("seq", "head"), None, None),
            P(),
            P(),
            P(None, None, "head"),
            P("head", None),
            P(("seq", "head"), None, None),
        ),
        out_specs=(
            P(("seq", "head"), None, None),
            P(("seq", "head"), None, None),
            P(None, None, "head"),
            P("head", None),
        ),
        check_vma=False,
    )
```

```python
import functools

import jax
import jax.numpy as jnp
from jax import lax
from jax.experimental import pallas as pl
from jax.experimental.pallas import tpu as pltpu
from jax.sharding import PartitionSpec as P

DH = 192
KW = 5
VMEM_LIMIT = 24 * 1024 * 1024
COST = pl.CostEstimate(flops=1000, bytes_accessed=1000, transcendentals=0)
BF = jnp.bfloat16
F32 = jnp.float32
TOKEN = jax.ShapeDtypeStruct((8, 128), F32)


def params():
    return pltpu.CompilerParams(vmem_limit_bytes=VMEM_LIMIT)


def dot(a, b, contract):
    return lax.dot_general(a, b, (contract, ((), ())), preferred_element_type=F32)


NN = ((1,), (0,))
NT = ((1,), (1,))
TN = ((0,), (0,))


def whole(shape):
    return pl.BlockSpec(shape, lambda *_: (0,) * len(shape))


SCALARS = pl.BlockSpec(memory_space=pltpu.SMEM)


def spare(deps):
    return [pl.BlockSpec(memory_space=pl.ANY)] * len(deps)


def turned_rows(ref, low_ref, high_ref, parity, shift):
    seqs, rows, width = ref.shape[1:]
    own = ref[parity]
    if shift != 1:
        wide = own.astype(F32)
        if shift == 0:
            parts = [low_ref[parity].astype(F32), wide[:, : rows - 1]]
        else:
            parts = [wide[:, 1:], high_ref[parity].astype(F32)]
        own = jnp.concatenate(parts, axis=1).astype(BF)
    return own.reshape(seqs * rows, width)


def conv_kernel(
    at_ref, x_ref, low_ref, high_ref, w_ref, gain_ref, skip_ref, slope_ref, *rest
):
    normed_refs, (lhs, squares, whole_normed) = rest[:-3], rest[-3:]
    step = pl.program_id(0)
    seqs, rows, c_in = x_ref.shape[1:]
    half = seqs * rows
    tile = w_ref.shape[2]

    @pl.when(step == 0)
    def _():
        for parity in range(2):
            for shift in range(3):
                value = turned_rows(x_ref, low_ref, high_ref, parity, shift)
                for out in range(2):
                    tap = 2 * shift + parity - out
                    if 0 <= tap < KW:
                        lhs[out * half : (out + 1) * half, tap * c_in : (tap + 1) * c_in] = value
        squares[...] = jnp.zeros_like(squares)

    conv = dot(lhs[...], w_ref[...].reshape(KW * c_in, tile), NN)
    root = 0.7978845608028654
    total = None
    for parity in range(2):
        x = conv[parity * half : (parity + 1) * half, :]
        square = x * x
        t = jnp.tanh(root * (x + 0.044715 * (square * x)))
        left = 0.5 * (1.0 + t)
        act = x * left
        slope = left + (0.5 * root) * x * (1.0 - t * t) * (1.0 + (3 * 0.044715) * square)
        slope_ref[parity] = slope.reshape(slope_ref.shape[1:])
        total = act if total is None else total + act
    skip = (0.5 * total).astype(BF)
    columns = pl.ds(pl.multiple_of(step * tile, tile), tile)
    skip_ref[:, :, columns] = skip.reshape(seqs, rows, tile)
    wide = skip.astype(F32)
    squares[...] += jnp.sum(wide * wide, axis=-1, keepdims=True)

    @pl.when(step == pl.num_programs(0) - 1)
    def _():
        width = skip_ref.shape[2]
        inv = lax.rsqrt(squares[...] * (1.0 / width) + 1e-06)
        wide = skip_ref[...].reshape(half, width).astype(F32)
        normed = (wide * inv * gain_ref[...]).astype(BF)
        whole_normed[...] = normed.reshape(whole_normed.shape)
        for slot in range(seqs):
            normed_refs[slot][...] = whole_normed[at_ref[0] ^ slot]


def encoder(at, pairs, low, high, conv_weight, norm_gain):
    _, seqs, rows, c_in = pairs.shape
    width = conv_weight.shape[2]
    tile = 256 if width % 256 == 0 else width
    shape = (seqs, rows, width)
    outs = pl.pallas_call(
        conv_kernel,
        grid=(width // tile,),
        in_specs=[
            SCALARS,
            whole(pairs.shape),
            whole(low.shape),
            whole(high.shape),
            pl.BlockSpec((KW, c_in, tile), lambda n: (0, 0, n)),
            whole((1, width)),
        ],
        out_specs=[
            whole(shape),
            pl.BlockSpec((2, seqs, rows, tile), lambda n: (0, 0, 0, n)),
        ]
        + [whole((rows, width))] * seqs,
        out_shape=[
            jax.ShapeDtypeStruct(shape, BF),
            jax.ShapeDtypeStruct((2,) + shape, F32),
        ]
        + [jax.ShapeDtypeStruct((rows, width), BF)] * seqs,
        scratch_shapes=[
            pltpu.VMEM((2 * seqs * rows, KW * c_in), BF),
            pltpu.VMEM((seqs * rows, 1), F32),
            pltpu.VMEM(shape, BF),
        ],
        compiler_params=params(),
        cost_estimate=COST,
        name="encoder_forward",
    )(at, pairs, low, high, conv_weight, norm_gain.reshape(1, width))
    return outs[0], outs[1], list(outs[2:])


def d_conv_kernel(at_ref, own_ref, near_ref, far_ref, *refs):
    skip_ref, grad_ref, gain_ref, slope_ref, out_ref, first_ref, last_ref = refs
    rows = out_ref.shape[2]
    for slot, (ref, place) in enumerate(((own_ref, 0), (near_ref, 0), (far_ref, 0), (far_ref, 1))):
        b = at_ref[0] ^ slot
        wide = skip_ref[b].astype(F32)
        inv = lax.rsqrt(jnp.mean(wide * wide, axis=-1, keepdims=True) + 1e-06)
        unit = wide * inv
        scaled = ref[place].astype(F32) * gain_ref[...]
        d_skip = grad_ref[b].astype(F32) + inv * (
            scaled - unit * jnp.mean(scaled * unit, axis=-1, keepdims=True)
        )
        d_act = 0.5 * d_skip
        for parity in range(2):
            value = slope_ref[parity, b] * d_act
            out_ref[parity, b] = value.astype(BF)
            first_ref[parity, b] = value[:1].astype(BF)
            last_ref[parity, b] = value[rows - 1 :].astype(BF)


def conv_gradient(at, own, near, far, skip, grad, norm_gain, slope):
    vmem = pl.BlockSpec(memory_space=pltpu.VMEM)
    edge = jax.ShapeDtypeStruct(slope.shape[:2] + (1, slope.shape[3]), BF)
    return pl.pallas_call(
        d_conv_kernel,
        in_specs=[SCALARS] + [vmem] * 7,
        out_specs=[vmem] * 3,
        out_shape=[jax.ShapeDtypeStruct(slope.shape, BF)] + [edge] * 2,
        compiler_params=params(),
        cost_estimate=COST,
        name="conv_gradient",
    )(at, own, near, far, skip, grad, norm_gain.reshape(1, -1), slope)


def mixed_body(seqs, at_ref, *refs):
    skip_ref, out_ref = refs[seqs:]
    for slot in range(seqs):
        b = at_ref[0] ^ slot
        out_ref[b] = (skip_ref[b].astype(F32) + refs[slot][...].astype(F32)).astype(BF)


def mixed_call(at, terms, skip):
    seqs = len(terms)
    vmem = pl.BlockSpec(memory_space=pltpu.VMEM)
    return pl.pallas_call(
        functools.partial(mixed_body, seqs),
        in_specs=[SCALARS] + [vmem] * (seqs + 1),
        out_specs=vmem,
        out_shape=jax.ShapeDtypeStruct(skip.shape, BF),
        compiler_params=params(),
        cost_estimate=COST,
        name="mixed_sum",
    )(at, *terms, skip)


def conv_back_kernel(d_ref, low_ref, high_ref, w_ref, *rest):
    out_ref, turned, acc = rest[-3:]
    step = pl.program_id(0)

    @pl.when(step == 0)
    def _():
        for parity in range(2):
            for shift in range(3):
                turned[parity, shift] = turned_rows(d_ref, low_ref, high_ref, parity, shift).T

    for tap in range(KW):

        @pl.when(step == tap)
        def _():
            places = [KW - 1 - tap, KW - tap]
            rhs = jnp.concatenate([turned[p % 2, p // 2] for p in places], axis=1)
            term = dot(w_ref[0], rhs, NN)
            if tap == 0:
                acc[...] = term
            elif tap < KW - 1:
                acc[...] += term
            else:
                out_ref[...] = (acc[...] + term).T.astype(BF)


def conv_back(d_conv, low, high, conv_weight, *deps):
    _, seqs, rows, width = d_conv.shape
    c_in = conv_weight.shape[1]
    flat = 2 * seqs * rows
    return pl.pallas_call(
        conv_back_kernel,
        grid=(KW,),
        in_specs=[
            whole(d_conv.shape),
            whole(low.shape),
            whole(high.shape),
            pl.BlockSpec((1, c_in, width), lambda k: (k, 0, 0)),
        ]
        + spare(deps),
        out_specs=whole((flat, c_in)),
        out_shape=jax.ShapeDtypeStruct((flat, c_in), BF),
        scratch_shapes=[
            pltpu.VMEM((2, 3, width, seqs * rows), BF),
            pltpu.VMEM((c_in, flat), F32),
        ],
        compiler_params=params(),
        cost_estimate=COST,
        name="encoder_backward",
    )(d_conv, low, high, conv_weight, *deps)


def pack_kernel(w_ref, pack_ref, turned_ref, token_ref):
    token_ref[...] = jnp.zeros_like(token_ref)
    for i in range(3):
        for head in range(pack_ref.shape[0]):
            part = w_ref[i, :, head * DH : (head + 1) * DH]
            columns = slice(i * DH, (i + 1) * DH)
            pack_ref[head, :, columns] = part
            turned_ref[head, columns, :] = part.T


def pack_weights(w_qkv):
    _, width, local = w_qkv.shape
    heads = local // DH
    tile = local
    return pl.pallas_call(
        pack_kernel,
        grid=(width // tile,),
        in_specs=[pl.BlockSpec((3, tile, local), lambda n: (0, n, 0))],
        out_specs=[
            pl.BlockSpec((heads, tile, 3 * DH), lambda n: (0, n, 0)),
            pl.BlockSpec((heads, 3 * DH, tile), lambda n: (0, 0, n)),
            pl.BlockSpec(TOKEN.shape, lambda n: (0, 0)),
        ],
        out_shape=[
            jax.ShapeDtypeStruct((heads, width, 3 * DH), BF),
            jax.ShapeDtypeStruct((heads, 3 * DH, width), BF),
            TOKEN,
        ],
        compiler_params=params(),
        cost_estimate=COST,
        name="pack_weights",
    )(w_qkv)


def product_kernel(head_ref, x_ref, w_ref, *rest, contract):
    del head_ref
    out_ref, token_ref = rest[-2:]
    token_ref[...] = jnp.zeros_like(token_ref)
    value = dot(x_ref[...], w_ref[0], contract).astype(BF)
    out_ref[:, : value.shape[1]] = value
    if value.shape[1] < out_ref.shape[1]:
        out_ref[:, value.shape[1] :] = jnp.zeros_like(out_ref[:, value.shape[1] :])


def head_product(head, x, weight, contract, name, *deps):
    columns = weight.shape[2] if contract == NN else weight.shape[1]
    columns += -columns % 128
    rows, width = x.shape
    return pl.pallas_call(
        functools.partial(product_kernel, contract=contract),
        grid_spec=pltpu.PrefetchScalarGridSpec(
            num_scalar_prefetch=1,
            grid=(1,),
            in_specs=[
                pl.BlockSpec((rows, width), lambda i, head: (0, 0)),
                pl.BlockSpec((1,) + weight.shape[1:], lambda i, head: (head[0], 0, 0)),
            ]
            + spare(deps),
            out_specs=[
                pl.BlockSpec((rows, columns), lambda i, head: (0, 0)),
                pl.BlockSpec(TOKEN.shape, lambda i, head: (0, 0)),
            ],
        ),
        out_shape=[jax.ShapeDtypeStruct((rows, columns), BF), TOKEN],
        compiler_params=params(),
        cost_estimate=COST,
        name=name,
    )(head, x, weight, *deps)


def attention_kernel(qa_ref, qb_ref, da_ref, db_ref, *rest, block):
    oa_ref, ob_ref, k_all, v_all, dk_acc, dv_acc = rest[-6:]
    scale = DH ** (-0.5)
    half = qa_ref.shape[0]
    for place, ref in enumerate((qa_ref, qb_ref)):
        rows = pl.ds(place * half, half)
        k_all[rows, :] = ref[:, DH : 2 * DH]
        v_all[rows, :] = ref[:, 2 * DH : 3 * DH]
    k = k_all[...]
    v = v_all[...]
    for place, (q_ref, d_ref, out_ref) in enumerate(
        ((qa_ref, da_ref, oa_ref), (qb_ref, db_ref, ob_ref))
    ):
        for start in range(0, half, block):
            rows = pl.ds(start, block)
            q = q_ref[rows, 0:DH]
            d_o = d_ref[rows, 0:DH]
            s = dot(q, k, NT) * scale
            e = jnp.exp(s - jnp.max(s, axis=-1, keepdims=True))
            p = e * (1.0 / jnp.sum(e, axis=-1, keepdims=True))
            p_b = p.astype(BF)
            o = dot(p_b, v, NN)
            delta = jnp.sum(d_o.astype(F32) * o, axis=-1, keepdims=True)
            d_p = dot(d_o, v, NT)
            ds = (p * (d_p - delta)).astype(BF)
            dq = scale * dot(ds, k, NN)
            dk = dot(ds, q, TN)
            dv = dot(p_b, d_o, TN)
            if place == 0 and start == 0:
                dk_acc[...] = dk
                dv_acc[...] = dv
            else:
                dk_acc[...] += dk
                dv_acc[...] += dv
            out_ref[rows, 0:DH] = dq.astype(BF)
            out_ref[rows, 3 * DH : 4 * DH] = o.astype(BF)
    for place, out_ref in enumerate((oa_ref, ob_ref)):
        rows = pl.ds(place * half, half)
        out_ref[:, DH : 2 * DH] = (scale * dk_acc[rows, :]).astype(BF)
        out_ref[:, 2 * DH : 3 * DH] = dv_acc[rows, :].astype(BF)


def attention(qkv_a, qkv_b, d_a, d_b, *deps):
    half = qkv_a.shape[0]
    shape = jax.ShapeDtypeStruct((half, 4 * DH), BF)
    return pl.pallas_call(
        functools.partial(attention_kernel, block=min(256, half)),
        in_specs=[pl.BlockSpec(memory_space=pltpu.VMEM)] * 4 + spare(deps),
        out_shape=[shape, shape],
        scratch_shapes=[
            pltpu.VMEM((2 * half, DH), BF),
            pltpu.VMEM((2 * half, DH), BF),
            pltpu.VMEM((2 * half, DH), F32),
            pltpu.VMEM((2 * half, DH), F32),
        ],
        compiler_params=params(),
        cost_estimate=COST,
        name="attention",
    )(qkv_a, qkv_b, d_a, d_b, *deps)


def term_kernel(head_ref, a_ref, b_ref, w_ref, *rest, first, last):
    head = head_ref[0]
    total = dot(a_ref[:, first:last], w_ref[head], NN)
    total += dot(b_ref[:, first:last], w_ref[1 - head], NN)
    rest[-1][...] = total.astype(BF)


def pair_term(head, mine, got, weight, first, last, name, *deps):
    half, full = mine.shape
    heads, depth, width = weight.shape
    tile = 512 if width % 512 == 0 else width
    return pl.pallas_call(
        functools.partial(term_kernel, first=first, last=last),
        grid_spec=pltpu.PrefetchScalarGridSpec(
            num_scalar_prefetch=1,
            grid=(width // tile,),
            in_specs=[
                pl.BlockSpec((half, full), lambda n, at: (0, 0)),
                pl.BlockSpec((half, full), lambda n, at: (0, 0)),
                pl.BlockSpec((heads, depth, tile), lambda n, at: (0, 0, n)),
            ]
            + spare(deps),
            out_specs=pl.BlockSpec((half, tile), lambda n, at: (0, n)),
        ),
        out_shape=jax.ShapeDtypeStruct((half, width), BF),
        compiler_params=params(),
        cost_estimate=COST,
        name=name,
    )(head, mine, got, weight, *deps)


def weight_kernel(at_ref, xa_ref, xb_ref, ga_ref, gb_ref, ra_ref, rb_ref, *rest):
    del at_ref
    out_refs, turned = rest[:-1], rest[-1]
    step = pl.program_id(0)
    half = ra_ref.shape[0]
    split = 3 * DH

    @pl.when(step == 0)
    def _():
        turned[:, :half] = ra_ref[...].T
        turned[:, half:] = rb_ref[...].T

    a, b = slice(0, half), slice(half, 2 * half)
    qkv = dot(turned[:split, a], xa_ref[...], NN) + dot(turned[:split, b], xb_ref[...], NN)
    out = dot(turned[split:, a], ga_ref[...], NN) + dot(turned[split:, b], gb_ref[...], NN)
    for slot, out_ref in enumerate(out_refs):

        @pl.when(step == slot)
        def _():
            out_ref[:split, :] = qkv.astype(BF)
            out_ref[split:, :] = out.astype(BF)


def weight_gradients(at, xa, xb, ga, gb, ra, rb, seqs):
    half, width = xa.shape
    chunk = width // seqs
    full = ra.shape[1]
    column = pl.BlockSpec((half, chunk), lambda r, at: (0, r ^ at[0]))
    rest = pl.BlockSpec((half, full), lambda r, at: (0, 0))
    return pl.pallas_call(
        weight_kernel,
        grid_spec=pltpu.PrefetchScalarGridSpec(
            num_scalar_prefetch=1,
            grid=(seqs,),
            in_specs=[column] * 4 + [rest] * 2,
            out_specs=[pl.BlockSpec((full, chunk), lambda r, at: (0, 0))] * seqs,
            scratch_shapes=[pltpu.VMEM((full, 2 * half), BF)],
        ),
        out_shape=[jax.ShapeDtypeStruct((full, chunk), BF)] * seqs,
        compiler_params=params(),
        cost_estimate=COST,
        name="weight_gradients",
    )(at, xa, xb, ga, gb, ra, rb)


def weight_sum_kernel(*refs, count):
    part_refs, out_refs = refs[:count], refs[-2:]
    split = 3 * DH
    total = part_refs[0][...].astype(F32)
    for ref in part_refs[1:]:
        total = total + ref[...].astype(F32)
    turned = total[:split].T.astype(BF)
    for part, out_ref in enumerate(out_refs):
        rows = slice(part * DH, (part + 1) * DH)
        out_ref[:, :split] = turned[rows]
        out_ref[:, split:] = total[split:, rows].astype(BF)


def weight_sum(parts, *deps):
    full, chunk = parts[0].shape
    return pl.pallas_call(
        functools.partial(weight_sum_kernel, count=len(parts)),
        in_specs=[pl.BlockSpec(memory_space=pltpu.VMEM)] * len(parts) + spare(deps),
        out_shape=[jax.ShapeDtypeStruct((chunk // 2, full), BF)] * 2,
        compiler_params=params(),
        cost_estimate=COST,
        name="weight_sum",
    )(*parts, *deps)


def unpack_kernel(at_ref, *refs):
    qkv_ref, out_ref = refs[-2:]
    step = pl.program_id(0)
    split = 3 * DH
    for turn in range(4):

        @pl.when(step == turn)
        def _():
            both = []
            for near_a, near_b, far_a, far_b in (refs[:4], refs[4:8]):
                first = near_a if turn < 2 else far_a
                second = near_b if turn % 2 == 0 else far_b
                both.append((first[...].astype(F32), second[...].astype(F32)))
            swapped = at_ref[1] != 0
            for part in range(2):
                mine, other = both[0][part], both[1][part]
                low = jnp.where(swapped, other, mine)
                high = jnp.where(swapped, mine, other)
                rows = slice(part * DH, (part + 1) * DH)
                for i in range(3):
                    columns = slice(i * DH, (i + 1) * DH)
                    qkv_ref[i, rows, :] = jnp.concatenate(
                        [low[:, columns], high[:, columns]], axis=1
                    )
                out_ref[:DH, rows] = low[:, split:]
                out_ref[DH:, rows] = high[:, split:]


def unpack_weights(at, mine, other):
    rows, full = mine[0].shape
    half = rows // 2
    width = 4 * rows
    local = 2 * DH
    specs = [
        pl.BlockSpec((half, full), lambda j, at: (jnp.minimum(j, 1), 0)),
        pl.BlockSpec((half, full), lambda j, at: (j // 2, 0)),
        pl.BlockSpec((half, full), lambda j, at: (jnp.maximum(j - 2, 0), 0)),
        pl.BlockSpec((half, full), lambda j, at: (j // 2, 0)),
    ]
    return pl.pallas_call(
        unpack_kernel,
        grid_spec=pltpu.PrefetchScalarGridSpec(
            num_scalar_prefetch=1,
            grid=(4,),
            in_specs=specs * 2,
            out_specs=[
                pl.BlockSpec((3, rows, local), lambda j, at: (0, at[0] ^ j, 0)),
                pl.BlockSpec((local, rows), lambda j, at: (0, at[0] ^ j)),
            ],
        ),
        out_shape=[
            jax.ShapeDtypeStruct((3, width, local), F32),
            jax.ShapeDtypeStruct((local, width), F32),
        ],
        compiler_params=params(),
        cost_estimate=COST,
        name="weight_outputs",
    )(at, *mine, *other)


def neighbour_edges(first, last):
    axes = ("seq", "head")
    count = lax.axis_size(axes)
    forward = [(i, i + 1) for i in range(count - 1)]
    backward = [(target, source) for source, target in forward]
    return lax.ppermute(last, axes, forward), lax.ppermute(first, axes, backward)


def after(value, *others):
    return lax.optimization_barrier((value,) + others)[0]


def trade_chip(x, bit, heads):
    count = lax.axis_size("seq")
    return lax.ppermute(x, "seq", [(s, s ^ (bit * heads)) for s in range(count)])


def swap_heads(x):
    count = lax.axis_size("seq")
    return lax.ppermute(x, "seq", [(s, s + 1 - 2 * (s % 2)) for s in range(count)])


def unit_body(enc_in, conv_weight, norm_gain, w_qkv, w_out, grad_out):
    rows = enc_in.shape[0] // 2
    seqs = enc_in.shape[1]
    width = conv_weight.shape[2]
    local = w_qkv.shape[2]
    heads = local // DH
    groups = lax.axis_size("head")
    half = groups * seqs * rows
    place = lax.axis_index("seq")
    own_seq = (place // heads).astype(jnp.int32)
    own_head = (place % heads).astype(jnp.int32)
    at = jnp.stack([own_seq, own_head])
    head_mine = own_head.reshape(1)
    head_other = (1 - own_head).reshape(1)

    def to_chips(slots):
        return [x if j == 0 else trade_chip(x, j, heads) for j, x in enumerate(slots)]

    order = (0, 2, 1, 3)

    grad_z = lax.all_gather(grad_out, "head", axis=0, tiled=False)

    pairs = jnp.transpose(enc_in.reshape(rows, 2, seqs, enc_in.shape[2]), (1, 2, 0, 3))
    low, high = neighbour_edges(pairs[:, :, :1, :], pairs[:, :, -1:, :])
    skip, slope, normed = encoder(at, pairs, low, high, conv_weight, norm_gain)
    normed = to_chips(normed)
    normed_slab = jnp.concatenate([normed[j] for j in order], axis=0)
    normed_rows = lax.all_gather(normed_slab, "head", axis=0, tiled=True)

    grad_z = after(grad_z, normed_slab)
    grad_slots = to_chips(
        [lax.dynamic_index_in_dim(grad_z, own_seq ^ j, 2, keepdims=False) for j in range(seqs)]
    )
    grad_rows = jnp.stack([grad_slots[j] for j in order], axis=1).reshape(half, width)
    w_pack, w_turned, packed = pack_weights(after(w_qkv, normed_slab))
    w_rows = w_out.reshape(heads, DH, width)
    d_other, one = head_product(head_other, grad_rows, w_rows, NT, "d_o_other")
    d_got = swap_heads(d_other)
    d_mine, two = head_product(head_mine, grad_rows, w_rows, NT, "d_o_own")
    grad_swapped = swap_heads(grad_rows)
    normed_rows, *tokens = lax.optimization_barrier((normed_rows, packed, one, two))

    normed_swapped = swap_heads(normed_rows)
    qkv_other, _ = head_product(
        head_other, normed_rows, w_pack, NN, "qkv_other", d_got, grad_swapped, *tokens
    )
    qkv_got = swap_heads(qkv_other)
    qkv_mine, _ = head_product(head_mine, normed_rows, w_pack, NN, "qkv_own")
    result_mine, result_other = attention(qkv_mine, qkv_got, d_mine, d_got, normed_swapped)
    result_got = swap_heads(result_other)

    shape = (groups, seqs, rows, width)
    d_term = pair_term(head_mine, result_mine, result_got, w_turned, 0, 3 * DH, "d_term")
    d_normed = lax.psum_scatter(d_term.reshape(shape), "head", scatter_dimension=0, tiled=False)
    part = weight_gradients(
        own_seq.reshape(1),
        normed_rows,
        normed_swapped,
        grad_rows,
        grad_swapped,
        result_mine,
        result_other,
        seqs,
    )
    part = to_chips(part)
    head_term = pair_term(
        head_mine, result_mine, result_got, w_rows, 3 * DH, 4 * DH, "head_term"
    )
    head_sum = lax.psum_scatter(head_term.reshape(shape), "head", scatter_dimension=0, tiled=False)

    near = trade_chip(d_normed[2:], 1, heads)
    far = trade_chip(jnp.stack([d_normed[1], near[1]]), 2, heads)
    grad = jnp.transpose(after(grad_out, d_term), (1, 0, 2))
    d_conv, first, last = conv_gradient(at, d_normed, near, far, skip, grad, norm_gain, slope)
    low, high = neighbour_edges(first, last)

    half_a, half_b = weight_sum(part, far)
    got_a = trade_chip(half_a, 1, heads)
    got_b = trade_chip(half_b, 2, heads)
    near_a = jnp.concatenate([half_a, after(got_a, low, high)], axis=0)
    near_b = jnp.concatenate([half_b, after(got_b, low, high)], axis=0)
    far_a = trade_chip(near_a, 2, heads)
    far_b = trade_chip(near_b, 1, heads)
    near_other = [swap_heads(near_a), swap_heads(near_b)]
    grad_input = conv_back(d_conv, low, high, conv_weight, *near_other)
    far_other = [swap_heads(after(x, grad_input)) for x in (far_a, far_b)]
    grad_w_qkv, grad_w_out = unpack_weights(
        at, [near_a, near_b, far_a, far_b], near_other + far_other
    )

    head_sum = after(head_sum, grad_input)
    head_sum = to_chips([head_sum[order.index(j)] for j in range(seqs)])
    mixed = mixed_call(at, head_sum, skip)
    grad_input = jnp.transpose(grad_input.reshape(2, seqs, rows, -1), (2, 0, 1, 3))
    return (
        jnp.transpose(mixed, (1, 0, 2)),
        grad_input.reshape(enc_in.shape),
        grad_w_qkv,
        grad_w_out,
    )


def padded_2(block, sides, width):
    for axis, dim in sides:
        count = lax.axis_size(axis)
        forward = [(i, i + 1) for i in range(count - 1)]
        backward = [(target, source) for source, target in forward]
        low = lax.ppermute(
            lax.slice_in_dim(block, block.shape[dim] - width, None, axis=dim), axis, forward
        )
        high = lax.ppermute(lax.slice_in_dim(block, 0, width, axis=dim), axis, backward)
        block = jnp.concatenate([low, block, high], axis=dim)
    return block


def gathered_body(enc_in, conv_weight, norm_gain, w_qkv, w_out, grad_out):
    fine_rows = enc_in.shape[0]
    slab_rows = fine_rows // 2
    seq_count = enc_in.shape[1]
    out_width = conv_weight.shape[2]
    local_width = w_qkv.shape[2]
    local_heads = local_width // DH
    logit_scale = DH ** (-0.5)
    padded = padded_2(enc_in, ((("seq", "head"), 0),), 2)
    convolved = jnp.zeros((fine_rows, seq_count, out_width), jnp.float32)
    for offset in range(KW):
        convolved = convolved + jnp.einsum(
            "tbi,io->tbo",
            padded[offset : offset + fine_rows],
            conv_weight[offset],
            preferred_element_type=jnp.float32,
        )
    activated, gelu_pull = jax.vjp(jax.nn.gelu, convolved)
    skip = jnp.mean(activated.reshape(slab_rows, 2, seq_count, out_width), axis=1).astype(
        jnp.bfloat16
    )
    skip_wide = skip.astype(jnp.float32)
    inv_rms = lax.rsqrt(jnp.mean(skip_wide * skip_wide, axis=-1, keepdims=True) + 1e-06)
    normed = (skip_wide * inv_rms * norm_gain).astype(jnp.bfloat16)
    normed_rows = lax.all_gather(normed, "head", axis=0, tiled=True)
    grad_rows = lax.all_gather(grad_out, "head", axis=0, tiled=True)
    tower_rows = normed_rows.shape[0]
    qkv = jnp.einsum(
        "tbc,ice->itbe", normed_rows, w_qkv, preferred_element_type=jnp.float32
    ).astype(jnp.bfloat16)
    qkv = qkv.reshape(3, tower_rows, seq_count, local_heads, DH)
    query_matrix, key_matrix, value_matrix = (qkv[0], qkv[1], qkv[2])
    key_all, value_all = (
        lax.all_gather(key_matrix, "seq", axis=0, tiled=True),
        lax.all_gather(value_matrix, "seq", axis=0, tiled=True),
    )
    attention_logits = (
        jnp.einsum("qbhd,kbhd->bhqk", query_matrix, key_all, preferred_element_type=jnp.float32)
        * logit_scale
    )
    row_peak = jnp.max(attention_logits, axis=-1, keepdims=True)
    exponent = jnp.exp(attention_logits - row_peak)
    row_total = jnp.sum(exponent, axis=-1, keepdims=True)
    soft_weights = exponent / row_total
    narrow_probabilities = soft_weights.astype(jnp.bfloat16)
    attention_output = jnp.einsum(
        "bhqk,kbhd->qbhd", narrow_probabilities, value_all, preferred_element_type=jnp.float32
    )
    o_narrow = attention_output.reshape(tower_rows, seq_count, local_width).astype(jnp.bfloat16)
    piece = o_narrow
    head_sum = lax.psum_scatter(
        jnp.einsum("tbe,ec->tbc", piece, w_out, preferred_element_type=jnp.float32).astype(
            jnp.bfloat16
        ),
        "head",
        scatter_dimension=0,
        tiled=True,
    ).astype(jnp.float32)
    mixed = (skip_wide + head_sum).astype(jnp.bfloat16)
    part_w_out = jnp.einsum("tbe,tbc->ec", o_narrow, grad_rows, preferred_element_type=jnp.float32)
    d_out = jnp.einsum("tbc,ec->tbe", grad_rows, w_out, preferred_element_type=jnp.float32).astype(
        jnp.bfloat16
    )
    d_out = d_out.reshape(tower_rows, seq_count, local_heads, DH)
    delta = jnp.sum(d_out.astype(jnp.float32) * attention_output, axis=-1)
    probability_gradient = jnp.einsum(
        "qbhd,kbhd->bhqk", d_out, value_all, preferred_element_type=jnp.float32
    )
    d_scores = soft_weights * (probability_gradient - jnp.transpose(delta, (1, 2, 0))[..., None])
    narrow_gradient = d_scores.astype(jnp.bfloat16)
    query_gradient = logit_scale * jnp.einsum(
        "bhqk,kbhd->qbhd", narrow_gradient, key_all, preferred_element_type=jnp.float32
    )
    key_terms = logit_scale * jnp.einsum(
        "bhqk,qbhd->kbhd", narrow_gradient, query_matrix, preferred_element_type=jnp.float32
    )
    value_terms = jnp.einsum(
        "bhqk,qbhd->kbhd", narrow_probabilities, d_out, preferred_element_type=jnp.float32
    )
    d_keys, d_values = (
        lax.psum_scatter(
            key_terms.astype(jnp.bfloat16), "seq", scatter_dimension=0, tiled=True
        ).astype(jnp.float32),
        lax.psum_scatter(
            value_terms.astype(jnp.bfloat16), "seq", scatter_dimension=0, tiled=True
        ).astype(jnp.float32),
    )
    dqkv = (
        jnp.stack([query_gradient, d_keys, d_values])
        .reshape(3, tower_rows, seq_count, local_width)
        .astype(jnp.bfloat16)
    )
    part_w_qkv = jnp.einsum("tbc,itbe->ice", normed_rows, dqkv, preferred_element_type=jnp.float32)
    piece = dqkv
    d_normed = lax.psum_scatter(
        jnp.einsum("itbe,ice->tbc", piece, w_qkv, preferred_element_type=jnp.float32).astype(
            jnp.bfloat16
        ),
        "head",
        scatter_dimension=0,
        tiled=True,
    ).astype(jnp.float32)
    unit_rows = skip_wide * inv_rms
    scaled = d_normed * norm_gain
    d_skip = grad_out.astype(jnp.float32) + inv_rms * (
        scaled - unit_rows * jnp.mean(scaled * unit_rows, axis=-1, keepdims=True)
    )
    d_act = jnp.repeat(d_skip, 2, axis=0) * 0.5
    d_conv = gelu_pull(d_act)[0].astype(jnp.bfloat16)
    d_pad = padded_2(d_conv, ((("seq", "head"), 0),), 2)
    grad_input = jnp.zeros((fine_rows, seq_count, enc_in.shape[2]), jnp.float32)
    for offset in range(KW):
        grad_input = grad_input + jnp.einsum(
            "tbo,io->tbi",
            d_pad[4 - offset : 4 - offset + fine_rows],
            conv_weight[offset],
            preferred_element_type=jnp.float32,
        )
    grad_w_qkv, grad_w_out = (
        lax.psum(part_w_qkv.astype(jnp.bfloat16), "seq").astype(jnp.float32),
        lax.psum(part_w_out.astype(jnp.bfloat16), "seq").astype(jnp.float32),
    )
    return (mixed, grad_input.astype(jnp.bfloat16), grad_w_qkv, grad_w_out)


def body(enc_in, conv_weight, norm_gain, w_qkv, w_out, grad_out):
    heads = w_qkv.shape[2] // DH
    seqs = enc_in.shape[1]
    fits = heads == 2 and seqs == 4 and seqs * heads == lax.axis_size("seq")
    fits = fits and conv_weight.shape[2] == seqs * w_qkv.shape[2]
    chosen = unit_body if fits else gathered_body
    return chosen(enc_in, conv_weight, norm_gain, w_qkv, w_out, grad_out)


def solution(mesh):
    return jax.shard_map(
        body,
        mesh=mesh,
        in_specs=(
            P(("seq", "head"), None, None),
            P(),
            P(),
            P(None, None, "head"),
            P("head", None),
            P(("seq", "head"), None, None),
        ),
        out_specs=(
            P(("seq", "head"), None, None),
            P(("seq", "head"), None, None),
            P(None, None, "head"),
            P("head", None),
        ),
        check_vma=False,
    )
```

```python
import functools

import jax
import jax.numpy as jnp
from jax import lax
from jax.experimental import pallas as pl
from jax.experimental.pallas import tpu as pltpu
from jax.sharding import PartitionSpec as P

DH = 192
KW = 5
VMEM_LIMIT = 24 * 1024 * 1024
STREAMING_LIMIT = 56 * 1024 * 1024
COST = pl.CostEstimate(flops=1000, bytes_accessed=1000, transcendentals=0)
BF = jnp.bfloat16
F32 = jnp.float32
TOKEN = jax.ShapeDtypeStruct((8, 128), F32)


def params(limit=VMEM_LIMIT):
    return pltpu.CompilerParams(vmem_limit_bytes=limit)


def dot(a, b, contract):
    return lax.dot_general(a, b, (contract, ((), ())), preferred_element_type=F32)


NN = ((1,), (0,))
NT = ((1,), (1,))
TN = ((0,), (0,))


def whole(shape):
    return pl.BlockSpec(shape, lambda *_: (0,) * len(shape))


SCALARS = pl.BlockSpec(memory_space=pltpu.SMEM)


def spare(deps):
    return [pl.BlockSpec(memory_space=pl.ANY)] * len(deps)


def turned_rows(ref, low_ref, high_ref, parity, shift):
    seqs, rows, width = ref.shape[1:]
    own = ref[parity]
    if shift != 1:
        wide = own.astype(F32)
        if shift == 0:
            parts = [low_ref[parity].astype(F32), wide[:, : rows - 1]]
        else:
            parts = [wide[:, 1:], high_ref[parity].astype(F32)]
        own = jnp.concatenate(parts, axis=1).astype(BF)
    return own.reshape(seqs * rows, width)


def conv_kernel(
    at_ref, x_ref, low_ref, high_ref, w_ref, gain_ref, skip_ref, slope_ref, *rest
):
    normed_refs, (lhs, squares, whole_normed) = rest[:-3], rest[-3:]
    step = pl.program_id(0)
    seqs, rows, c_in = x_ref.shape[1:]
    half = seqs * rows
    tile = w_ref.shape[2]

    @pl.when(step == 0)
    def _():
        for parity in range(2):
            for shift in range(3):
                value = turned_rows(x_ref, low_ref, high_ref, parity, shift)
                for out in range(2):
                    tap = 2 * shift + parity - out
                    if 0 <= tap < KW:
                        lhs[out * half : (out + 1) * half, tap * c_in : (tap + 1) * c_in] = value
        squares[...] = jnp.zeros_like(squares)

    conv = dot(lhs[...], w_ref[...].reshape(KW * c_in, tile), NN)
    root = 0.7978845608028654
    total = None
    for parity in range(2):
        x = conv[parity * half : (parity + 1) * half, :]
        square = x * x
        t = jnp.tanh(root * (x + 0.044715 * (square * x)))
        left = 0.5 * (1.0 + t)
        act = x * left
        slope = left + (0.5 * root) * x * (1.0 - t * t) * (1.0 + (3 * 0.044715) * square)
        slope_ref[parity] = slope.reshape(slope_ref.shape[1:])
        total = act if total is None else total + act
    skip = (0.5 * total).astype(BF)
    columns = pl.ds(pl.multiple_of(step * tile, tile), tile)
    skip_ref[:, :, columns] = skip.reshape(seqs, rows, tile)
    wide = skip.astype(F32)
    squares[...] += jnp.sum(wide * wide, axis=-1, keepdims=True)

    @pl.when(step == pl.num_programs(0) - 1)
    def _():
        width = skip_ref.shape[2]
        inv = lax.rsqrt(squares[...] * (1.0 / width) + 1e-06)
        wide = skip_ref[...].reshape(half, width).astype(F32)
        normed = (wide * inv * gain_ref[...]).astype(BF)
        whole_normed[...] = normed.reshape(whole_normed.shape)
        for slot in range(seqs):
            normed_refs[slot][...] = whole_normed[at_ref[0] ^ slot]


def encoder(at, pairs, low, high, conv_weight, norm_gain):
    _, seqs, rows, c_in = pairs.shape
    width = conv_weight.shape[2]
    tile = 256 if width % 256 == 0 else width
    shape = (seqs, rows, width)
    outs = pl.pallas_call(
        conv_kernel,
        grid=(width // tile,),
        in_specs=[
            SCALARS,
            whole(pairs.shape),
            whole(low.shape),
            whole(high.shape),
            pl.BlockSpec((KW, c_in, tile), lambda n: (0, 0, n)),
            whole((1, width)),
        ],
        out_specs=[
            whole(shape),
            pl.BlockSpec((2, seqs, rows, tile), lambda n: (0, 0, 0, n)),
        ]
        + [whole((rows, width))] * seqs,
        out_shape=[
            jax.ShapeDtypeStruct(shape, BF),
            jax.ShapeDtypeStruct((2,) + shape, F32),
        ]
        + [jax.ShapeDtypeStruct((rows, width), BF)] * seqs,
        scratch_shapes=[
            pltpu.VMEM((2 * seqs * rows, KW * c_in), BF),
            pltpu.VMEM((seqs * rows, 1), F32),
            pltpu.VMEM(shape, BF),
        ],
        compiler_params=params(STREAMING_LIMIT),
        cost_estimate=COST,
        name="encoder_forward",
    )(at, pairs, low, high, conv_weight, norm_gain.reshape(1, width))
    return outs[0], outs[1], list(outs[2:])


def d_conv_kernel(at_ref, own_ref, near_ref, far_ref, *refs):
    skip_ref, grad_ref, gain_ref, slope_ref = refs[:4]
    out_ref, first_ref, last_ref = refs[-3:]
    rows = out_ref.shape[2]
    for slot, (ref, place) in enumerate(((own_ref, 0), (near_ref, 0), (far_ref, 0), (far_ref, 1))):
        b = at_ref[0] ^ slot
        wide = skip_ref[b].astype(F32)
        inv = lax.rsqrt(jnp.mean(wide * wide, axis=-1, keepdims=True) + 1e-06)
        unit = wide * inv
        scaled = ref[place].astype(F32) * gain_ref[...]
        d_skip = grad_ref[b].astype(F32) + inv * (
            scaled - unit * jnp.mean(scaled * unit, axis=-1, keepdims=True)
        )
        d_act = 0.5 * d_skip
        for parity in range(2):
            value = slope_ref[parity, b] * d_act
            out_ref[parity, b] = value.astype(BF)
            first_ref[parity, b] = value[:1].astype(BF)
            last_ref[parity, b] = value[rows - 1 :].astype(BF)


def conv_gradient(at, own, near, far, skip, grad, norm_gain, slope, *deps):
    vmem = pl.BlockSpec(memory_space=pltpu.VMEM)
    edge = jax.ShapeDtypeStruct(slope.shape[:2] + (1, slope.shape[3]), BF)
    return pl.pallas_call(
        d_conv_kernel,
        in_specs=[SCALARS] + [vmem] * 7 + spare(deps),
        out_specs=[vmem] * 3,
        out_shape=[jax.ShapeDtypeStruct(slope.shape, BF)] + [edge] * 2,
        compiler_params=params(),
        cost_estimate=COST,
        name="conv_gradient",
    )(at, own, near, far, skip, grad, norm_gain.reshape(1, -1), slope, *deps)


def mixed_body(seqs, at_ref, *refs):
    skip_ref, out_ref = refs[seqs:]
    for slot in range(seqs):
        b = at_ref[0] ^ slot
        out_ref[b] = (skip_ref[b].astype(F32) + refs[slot][...].astype(F32)).astype(BF)


def mixed_call(at, terms, skip):
    seqs = len(terms)
    vmem = pl.BlockSpec(memory_space=pltpu.VMEM)
    return pl.pallas_call(
        functools.partial(mixed_body, seqs),
        in_specs=[SCALARS] + [vmem] * (seqs + 1),
        out_specs=vmem,
        out_shape=jax.ShapeDtypeStruct(skip.shape, BF),
        compiler_params=params(),
        cost_estimate=COST,
        name="mixed_sum",
    )(at, *terms, skip)


def conv_back_kernel(d_ref, low_ref, high_ref, w_ref, *rest):
    out_ref, turned, acc = rest[-3:]
    step = pl.program_id(0)

    @pl.when(step == 0)
    def _():
        for parity in range(2):
            for shift in range(3):
                turned[parity, shift] = turned_rows(d_ref, low_ref, high_ref, parity, shift).T

    for tap in range(KW):

        @pl.when(step == tap)
        def _():
            places = [KW - 1 - tap, KW - tap]
            rhs = jnp.concatenate([turned[p % 2, p // 2] for p in places], axis=1)
            term = dot(w_ref[0], rhs, NN)
            if tap == 0:
                acc[...] = term
            elif tap < KW - 1:
                acc[...] += term
            else:
                out_ref[...] = (acc[...] + term).T.astype(BF)


def conv_back(d_conv, low, high, conv_weight, *deps):
    _, seqs, rows, width = d_conv.shape
    c_in = conv_weight.shape[1]
    flat = 2 * seqs * rows
    return pl.pallas_call(
        conv_back_kernel,
        grid=(KW,),
        in_specs=[
            whole(d_conv.shape),
            whole(low.shape),
            whole(high.shape),
            pl.BlockSpec((1, c_in, width), lambda k: (k, 0, 0)),
        ]
        + spare(deps),
        out_specs=whole((flat, c_in)),
        out_shape=jax.ShapeDtypeStruct((flat, c_in), BF),
        scratch_shapes=[
            pltpu.VMEM((2, 3, width, seqs * rows), BF),
            pltpu.VMEM((c_in, flat), F32),
        ],
        compiler_params=params(),
        cost_estimate=COST,
        name="encoder_backward",
    )(d_conv, low, high, conv_weight, *deps)


def pack_kernel(w_ref, pack_ref, turned_ref, token_ref):
    token_ref[...] = jnp.zeros_like(token_ref)
    for i in range(3):
        for head in range(pack_ref.shape[0]):
            part = w_ref[i, :, head * DH : (head + 1) * DH]
            columns = slice(i * DH, (i + 1) * DH)
            pack_ref[head, :, columns] = part
            turned_ref[head, columns, :] = part.T


def pack_weights(w_qkv):
    _, width, local = w_qkv.shape
    heads = local // DH
    tile = local
    return pl.pallas_call(
        pack_kernel,
        grid=(width // tile,),
        in_specs=[pl.BlockSpec((3, tile, local), lambda n: (0, n, 0))],
        out_specs=[
            pl.BlockSpec((heads, tile, 3 * DH), lambda n: (0, n, 0)),
            pl.BlockSpec((heads, 3 * DH, tile), lambda n: (0, 0, n)),
            pl.BlockSpec(TOKEN.shape, lambda n: (0, 0)),
        ],
        out_shape=[
            jax.ShapeDtypeStruct((heads, width, 3 * DH), BF),
            jax.ShapeDtypeStruct((heads, 3 * DH, width), BF),
            TOKEN,
        ],
        compiler_params=params(),
        cost_estimate=COST,
        name="pack_weights",
    )(w_qkv)


def product_kernel(head_ref, x_ref, w_ref, *rest, contract):
    del head_ref
    out_ref, token_ref = rest[-2:]
    token_ref[...] = jnp.zeros_like(token_ref)
    value = dot(x_ref[...], w_ref[0], contract).astype(BF)
    out_ref[:, : value.shape[1]] = value
    if value.shape[1] < out_ref.shape[1]:
        out_ref[:, value.shape[1] :] = jnp.zeros_like(out_ref[:, value.shape[1] :])


def head_product(head, x, weight, contract, name, *deps):
    columns = weight.shape[2] if contract == NN else weight.shape[1]
    columns += -columns % 128
    rows, width = x.shape
    return pl.pallas_call(
        functools.partial(product_kernel, contract=contract),
        grid_spec=pltpu.PrefetchScalarGridSpec(
            num_scalar_prefetch=1,
            grid=(1,),
            in_specs=[
                pl.BlockSpec((rows, width), lambda i, head: (0, 0)),
                pl.BlockSpec((1,) + weight.shape[1:], lambda i, head: (head[0], 0, 0)),
            ]
            + spare(deps),
            out_specs=[
                pl.BlockSpec((rows, columns), lambda i, head: (0, 0)),
                pl.BlockSpec(TOKEN.shape, lambda i, head: (0, 0)),
            ],
        ),
        out_shape=[jax.ShapeDtypeStruct((rows, columns), BF), TOKEN],
        compiler_params=params(),
        cost_estimate=COST,
        name=name,
    )(head, x, weight, *deps)


def attention_kernel(qa_ref, qb_ref, da_ref, db_ref, *rest, block):
    oa_ref, ob_ref, k_all, v_all, dk_acc, dv_acc = rest[-6:]
    scale = DH ** (-0.5)
    half = qa_ref.shape[0]
    for place, ref in enumerate((qa_ref, qb_ref)):
        rows = pl.ds(place * half, half)
        k_all[rows, :] = ref[:, DH : 2 * DH]
        v_all[rows, :] = ref[:, 2 * DH : 3 * DH]
    k = k_all[...]
    v = v_all[...]
    for place, (q_ref, d_ref, out_ref) in enumerate(
        ((qa_ref, da_ref, oa_ref), (qb_ref, db_ref, ob_ref))
    ):
        for start in range(0, half, block):
            rows = pl.ds(start, block)
            q = q_ref[rows, 0:DH]
            d_o = d_ref[rows, 0:DH]
            s = dot(q, k, NT) * scale
            e = jnp.exp(s - jnp.max(s, axis=-1, keepdims=True))
            p = e * (1.0 / jnp.sum(e, axis=-1, keepdims=True))
            p_b = p.astype(BF)
            o = dot(p_b, v, NN)
            delta = jnp.sum(d_o.astype(F32) * o, axis=-1, keepdims=True)
            d_p = dot(d_o, v, NT)
            ds = (p * (d_p - delta)).astype(BF)
            dq = scale * dot(ds, k, NN)
            dk = dot(ds, q, TN)
            dv = dot(p_b, d_o, TN)
            if place == 0 and start == 0:
                dk_acc[...] = dk
                dv_acc[...] = dv
            else:
                dk_acc[...] += dk
                dv_acc[...] += dv
            out_ref[rows, 0:DH] = dq.astype(BF)
            out_ref[rows, 3 * DH : 4 * DH] = o.astype(BF)
    for place, out_ref in enumerate((oa_ref, ob_ref)):
        rows = pl.ds(place * half, half)
        out_ref[:, DH : 2 * DH] = (scale * dk_acc[rows, :]).astype(BF)
        out_ref[:, 2 * DH : 3 * DH] = dv_acc[rows, :].astype(BF)


def attention(qkv_a, qkv_b, d_a, d_b, *deps):
    half = qkv_a.shape[0]
    shape = jax.ShapeDtypeStruct((half, 4 * DH), BF)
    return pl.pallas_call(
        functools.partial(attention_kernel, block=min(256, half)),
        in_specs=[pl.BlockSpec(memory_space=pltpu.VMEM)] * 4 + spare(deps),
        out_shape=[shape, shape],
        scratch_shapes=[
            pltpu.VMEM((2 * half, DH), BF),
            pltpu.VMEM((2 * half, DH), BF),
            pltpu.VMEM((2 * half, DH), F32),
            pltpu.VMEM((2 * half, DH), F32),
        ],
        compiler_params=params(),
        cost_estimate=COST,
        name="attention",
    )(qkv_a, qkv_b, d_a, d_b, *deps)


def term_kernel(head_ref, a_ref, b_ref, w_ref, *rest, first, last):
    head = head_ref[0]
    total = dot(a_ref[:, first:last], w_ref[head], NN)
    total += dot(b_ref[:, first:last], w_ref[1 - head], NN)
    rest[-1][...] = total.astype(BF)


def pair_term(head, mine, got, weight, first, last, name, *deps):
    half, full = mine.shape
    heads, depth, width = weight.shape
    tile = 512 if width % 512 == 0 else width
    return pl.pallas_call(
        functools.partial(term_kernel, first=first, last=last),
        grid_spec=pltpu.PrefetchScalarGridSpec(
            num_scalar_prefetch=1,
            grid=(width // tile,),
            in_specs=[
                pl.BlockSpec((half, full), lambda n, at: (0, 0)),
                pl.BlockSpec((half, full), lambda n, at: (0, 0)),
                pl.BlockSpec((heads, depth, tile), lambda n, at: (0, 0, n)),
            ]
            + spare(deps),
            out_specs=pl.BlockSpec((half, tile), lambda n, at: (0, n)),
        ),
        out_shape=jax.ShapeDtypeStruct((half, width), BF),
        compiler_params=params(),
        cost_estimate=COST,
        name=name,
    )(head, mine, got, weight, *deps)


def weight_kernel(at_ref, xa_ref, xb_ref, ga_ref, gb_ref, ra_ref, rb_ref, *rest):
    del at_ref
    out_refs, turned = rest[:-1], rest[-1]
    step = pl.program_id(0)
    half = ra_ref.shape[0]
    split = 3 * DH

    @pl.when(step == 0)
    def _():
        turned[:, :half] = ra_ref[...].T
        turned[:, half:] = rb_ref[...].T

    a, b = slice(0, half), slice(half, 2 * half)
    qkv = dot(turned[:split, a], xa_ref[...], NN) + dot(turned[:split, b], xb_ref[...], NN)
    out = dot(turned[split:, a], ga_ref[...], NN) + dot(turned[split:, b], gb_ref[...], NN)
    for slot, out_ref in enumerate(out_refs):

        @pl.when(step == slot)
        def _():
            out_ref[:split, :] = qkv.astype(BF)
            out_ref[split:, :] = out.astype(BF)


def weight_gradients(at, xa, xb, ga, gb, ra, rb, seqs):
    half, width = xa.shape
    chunk = width // seqs
    full = ra.shape[1]
    column = pl.BlockSpec((half, chunk), lambda r, at: (0, r ^ at[0]))
    rest = pl.BlockSpec((half, full), lambda r, at: (0, 0))
    return pl.pallas_call(
        weight_kernel,
        grid_spec=pltpu.PrefetchScalarGridSpec(
            num_scalar_prefetch=1,
            grid=(seqs,),
            in_specs=[column] * 4 + [rest] * 2,
            out_specs=[pl.BlockSpec((full, chunk), lambda r, at: (0, 0))] * seqs,
            scratch_shapes=[pltpu.VMEM((full, 2 * half), BF)],
        ),
        out_shape=[jax.ShapeDtypeStruct((full, chunk), BF)] * seqs,
        compiler_params=params(STREAMING_LIMIT),
        cost_estimate=COST,
        name="weight_gradients",
    )(at, xa, xb, ga, gb, ra, rb)


def weight_sum_kernel(*refs, count):
    part_refs, out_refs = refs[:count], refs[-2:]
    split = 3 * DH
    total = part_refs[0][...].astype(F32)
    for ref in part_refs[1:]:
        total = total + ref[...].astype(F32)
    turned = total[:split].T.astype(BF)
    for part, out_ref in enumerate(out_refs):
        rows = slice(part * DH, (part + 1) * DH)
        out_ref[:, :split] = turned[rows]
        out_ref[:, split:] = total[split:, rows].astype(BF)


def weight_sum(parts, *deps):
    full, chunk = parts[0].shape
    return pl.pallas_call(
        functools.partial(weight_sum_kernel, count=len(parts)),
        in_specs=[pl.BlockSpec(memory_space=pltpu.VMEM)] * len(parts) + spare(deps),
        out_shape=[jax.ShapeDtypeStruct((chunk // 2, full), BF)] * 2,
        compiler_params=params(),
        cost_estimate=COST,
        name="weight_sum",
    )(*parts, *deps)


def unpack_kernel(at_ref, *refs):
    qkv_ref, out_ref = refs[-2:]
    step = pl.program_id(0)
    split = 3 * DH
    for turn in range(4):

        @pl.when(step == turn)
        def _():
            both = []
            for near_a, near_b, far_a, far_b in (refs[:4], refs[4:8]):
                first = near_a if turn < 2 else far_a
                second = near_b if turn % 2 == 0 else far_b
                both.append((first[...].astype(F32), second[...].astype(F32)))
            swapped = at_ref[1] != 0
            for part in range(2):
                mine, other = both[0][part], both[1][part]
                low = jnp.where(swapped, other, mine)
                high = jnp.where(swapped, mine, other)
                rows = slice(part * DH, (part + 1) * DH)
                for i in range(3):
                    columns = slice(i * DH, (i + 1) * DH)
                    qkv_ref[i, rows, :] = jnp.concatenate(
                        [low[:, columns], high[:, columns]], axis=1
                    )
                out_ref[:DH, rows] = low[:, split:]
                out_ref[DH:, rows] = high[:, split:]


def unpack_weights(at, mine, other):
    rows, full = mine[0].shape
    half = rows // 2
    width = 4 * rows
    local = 2 * DH
    specs = [
        pl.BlockSpec((half, full), lambda j, at: (jnp.minimum(j, 1), 0)),
        pl.BlockSpec((half, full), lambda j, at: (j // 2, 0)),
        pl.BlockSpec((half, full), lambda j, at: (jnp.maximum(j - 2, 0), 0)),
        pl.BlockSpec((half, full), lambda j, at: (j // 2, 0)),
    ]
    return pl.pallas_call(
        unpack_kernel,
        grid_spec=pltpu.PrefetchScalarGridSpec(
            num_scalar_prefetch=1,
            grid=(4,),
            in_specs=specs * 2,
            out_specs=[
                pl.BlockSpec((3, rows, local), lambda j, at: (0, at[0] ^ j, 0)),
                pl.BlockSpec((local, rows), lambda j, at: (0, at[0] ^ j)),
            ],
        ),
        out_shape=[
            jax.ShapeDtypeStruct((3, width, local), F32),
            jax.ShapeDtypeStruct((local, width), F32),
        ],
        compiler_params=params(),
        cost_estimate=COST,
        name="weight_outputs",
    )(at, *mine, *other)


def neighbour_edges(first, last):
    axes = ("seq", "head")
    count = lax.axis_size(axes)
    forward = [(i, i + 1) for i in range(count - 1)]
    backward = [(target, source) for source, target in forward]
    return lax.ppermute(last, axes, forward), lax.ppermute(first, axes, backward)


def after(value, *others):
    return lax.optimization_barrier((value,) + others)[0]


def trade_chip(x, bit, heads):
    count = lax.axis_size("seq")
    return lax.ppermute(x, "seq", [(s, s ^ (bit * heads)) for s in range(count)])


def swap_heads(x):
    count = lax.axis_size("seq")
    return lax.ppermute(x, "seq", [(s, s + 1 - 2 * (s % 2)) for s in range(count)])


def unit_body(enc_in, conv_weight, norm_gain, w_qkv, w_out, grad_out):
    rows = enc_in.shape[0] // 2
    seqs = enc_in.shape[1]
    width = conv_weight.shape[2]
    local = w_qkv.shape[2]
    heads = local // DH
    groups = lax.axis_size("head")
    half = groups * seqs * rows
    place = lax.axis_index("seq")
    own_seq = (place // heads).astype(jnp.int32)
    own_head = (place % heads).astype(jnp.int32)
    at = jnp.stack([own_seq, own_head])
    head_mine = own_head.reshape(1)
    head_other = (1 - own_head).reshape(1)

    def to_chips(slots):
        return [x if j == 0 else trade_chip(x, j, heads) for j, x in enumerate(slots)]

    order = (0, 2, 1, 3)

    grad_z = lax.all_gather(grad_out, "head", axis=0, tiled=False)

    pairs = jnp.transpose(enc_in.reshape(rows, 2, seqs, enc_in.shape[2]), (1, 2, 0, 3))
    low, high = neighbour_edges(pairs[:, :, :1, :], pairs[:, :, -1:, :])
    skip, slope, normed = encoder(at, pairs, low, high, conv_weight, norm_gain)
    normed = to_chips(normed)
    normed_slab = jnp.concatenate([normed[j] for j in order], axis=0)
    normed_rows = lax.all_gather(normed_slab, "head", axis=0, tiled=True)

    grad_z = after(grad_z, normed_slab)
    grad_slots = to_chips(
        [lax.dynamic_index_in_dim(grad_z, own_seq ^ j, 2, keepdims=False) for j in range(seqs)]
    )
    grad_rows = jnp.stack([grad_slots[j] for j in order], axis=1).reshape(half, width)
    w_pack, w_turned, packed = pack_weights(after(w_qkv, normed_slab))
    w_rows = w_out.reshape(heads, DH, width)
    d_other, one = head_product(head_other, grad_rows, w_rows, NT, "d_o_other")
    d_got = swap_heads(d_other)
    d_mine, two = head_product(head_mine, grad_rows, w_rows, NT, "d_o_own")
    grad_swapped = swap_heads(grad_rows)
    normed_rows, d_got, d_mine, grad_swapped, w_pack, w_turned, *tokens = (
        lax.optimization_barrier(
            (normed_rows, d_got, d_mine, grad_swapped, w_pack, w_turned, packed, one, two)
        )
    )

    normed_swapped = swap_heads(normed_rows)
    qkv_other, _ = head_product(head_other, normed_rows, w_pack, NN, "qkv_other", *tokens)
    qkv_got = swap_heads(qkv_other)
    qkv_mine, _ = head_product(head_mine, normed_rows, w_pack, NN, "qkv_own")
    result_mine, result_other = attention(qkv_mine, qkv_got, d_mine, d_got, normed_swapped)
    result_got = swap_heads(result_other)

    shape = (groups, seqs, rows, width)
    d_term = pair_term(head_mine, result_mine, result_got, w_turned, 0, 3 * DH, "d_term")
    d_normed = lax.psum_scatter(d_term.reshape(shape), "head", scatter_dimension=0, tiled=False)
    part = weight_gradients(
        own_seq.reshape(1),
        normed_rows,
        normed_swapped,
        grad_rows,
        grad_swapped,
        result_mine,
        result_other,
        seqs,
    )
    part = to_chips(part)
    head_term = pair_term(
        head_mine, result_mine, result_got, w_rows, 3 * DH, 4 * DH, "head_term"
    )
    head_sum = lax.psum_scatter(head_term.reshape(shape), "head", scatter_dimension=0, tiled=False)

    leaving = d_normed[2:]
    near = trade_chip(leaving, 1, heads)
    far = trade_chip(jnp.stack([d_normed[1], near[1]]), 2, heads)
    grad = jnp.transpose(after(grad_out, d_term), (1, 0, 2))
    half_a, half_b = weight_sum(part, leaving)
    d_conv, first, last = conv_gradient(
        at, d_normed, near, far, skip, grad, norm_gain, slope, half_a
    )
    low, high = neighbour_edges(first, last)

    got_a = trade_chip(half_a, 1, heads)
    got_b = trade_chip(half_b, 2, heads)
    near_a = jnp.concatenate([half_a, after(got_a, low, high)], axis=0)
    near_b = jnp.concatenate([half_b, after(got_b, low, high)], axis=0)
    far_a = trade_chip(near_a, 2, heads)
    far_b = trade_chip(near_b, 1, heads)
    near_other = [swap_heads(near_a), swap_heads(near_b)]
    grad_input = conv_back(d_conv, low, high, conv_weight, *near_other)
    far_other = [swap_heads(after(x, grad_input)) for x in (far_a, far_b)]
    grad_w_qkv, grad_w_out = unpack_weights(
        at, [near_a, near_b, far_a, far_b], near_other + far_other
    )

    head_sum = after(head_sum, grad_input)
    head_sum = to_chips([head_sum[order.index(j)] for j in range(seqs)])
    mixed = mixed_call(at, head_sum, skip)
    grad_input = jnp.transpose(grad_input.reshape(2, seqs, rows, -1), (2, 0, 1, 3))
    return (
        jnp.transpose(mixed, (1, 0, 2)),
        grad_input.reshape(enc_in.shape),
        grad_w_qkv,
        grad_w_out,
    )


def padded_2(block, sides, width):
    for axis, dim in sides:
        count = lax.axis_size(axis)
        forward = [(i, i + 1) for i in range(count - 1)]
        backward = [(target, source) for source, target in forward]
        low = lax.ppermute(
            lax.slice_in_dim(block, block.shape[dim] - width, None, axis=dim), axis, forward
        )
        high = lax.ppermute(lax.slice_in_dim(block, 0, width, axis=dim), axis, backward)
        block = jnp.concatenate([low, block, high], axis=dim)
    return block


def gathered_body(enc_in, conv_weight, norm_gain, w_qkv, w_out, grad_out):
    fine_rows = enc_in.shape[0]
    slab_rows = fine_rows // 2
    seq_count = enc_in.shape[1]
    out_width = conv_weight.shape[2]
    local_width = w_qkv.shape[2]
    local_heads = local_width // DH
    logit_scale = DH ** (-0.5)
    padded = padded_2(enc_in, ((("seq", "head"), 0),), 2)
    convolved = jnp.zeros((fine_rows, seq_count, out_width), jnp.float32)
    for offset in range(KW):
        convolved = convolved + jnp.einsum(
            "tbi,io->tbo",
            padded[offset : offset + fine_rows],
            conv_weight[offset],
            preferred_element_type=jnp.float32,
        )
    activated, gelu_pull = jax.vjp(jax.nn.gelu, convolved)
    skip = jnp.mean(activated.reshape(slab_rows, 2, seq_count, out_width), axis=1).astype(
        jnp.bfloat16
    )
    skip_wide = skip.astype(jnp.float32)
    inv_rms = lax.rsqrt(jnp.mean(skip_wide * skip_wide, axis=-1, keepdims=True) + 1e-06)
    normed = (skip_wide * inv_rms * norm_gain).astype(jnp.bfloat16)
    normed_rows = lax.all_gather(normed, "head", axis=0, tiled=True)
    grad_rows = lax.all_gather(grad_out, "head", axis=0, tiled=True)
    tower_rows = normed_rows.shape[0]
    qkv = jnp.einsum(
        "tbc,ice->itbe", normed_rows, w_qkv, preferred_element_type=jnp.float32
    ).astype(jnp.bfloat16)
    qkv = qkv.reshape(3, tower_rows, seq_count, local_heads, DH)
    query_matrix, key_matrix, value_matrix = (qkv[0], qkv[1], qkv[2])
    key_all, value_all = (
        lax.all_gather(key_matrix, "seq", axis=0, tiled=True),
        lax.all_gather(value_matrix, "seq", axis=0, tiled=True),
    )
    attention_logits = (
        jnp.einsum("qbhd,kbhd->bhqk", query_matrix, key_all, preferred_element_type=jnp.float32)
        * logit_scale
    )
    row_peak = jnp.max(attention_logits, axis=-1, keepdims=True)
    exponent = jnp.exp(attention_logits - row_peak)
    row_total = jnp.sum(exponent, axis=-1, keepdims=True)
    soft_weights = exponent / row_total
    narrow_probabilities = soft_weights.astype(jnp.bfloat16)
    attention_output = jnp.einsum(
        "bhqk,kbhd->qbhd", narrow_probabilities, value_all, preferred_element_type=jnp.float32
    )
    o_narrow = attention_output.reshape(tower_rows, seq_count, local_width).astype(jnp.bfloat16)
    piece = o_narrow
    head_sum = lax.psum_scatter(
        jnp.einsum("tbe,ec->tbc", piece, w_out, preferred_element_type=jnp.float32).astype(
            jnp.bfloat16
        ),
        "head",
        scatter_dimension=0,
        tiled=True,
    ).astype(jnp.float32)
    mixed = (skip_wide + head_sum).astype(jnp.bfloat16)
    part_w_out = jnp.einsum("tbe,tbc->ec", o_narrow, grad_rows, preferred_element_type=jnp.float32)
    d_out = jnp.einsum("tbc,ec->tbe", grad_rows, w_out, preferred_element_type=jnp.float32).astype(
        jnp.bfloat16
    )
    d_out = d_out.reshape(tower_rows, seq_count, local_heads, DH)
    delta = jnp.sum(d_out.astype(jnp.float32) * attention_output, axis=-1)
    probability_gradient = jnp.einsum(
        "qbhd,kbhd->bhqk", d_out, value_all, preferred_element_type=jnp.float32
    )
    d_scores = soft_weights * (probability_gradient - jnp.transpose(delta, (1, 2, 0))[..., None])
    narrow_gradient = d_scores.astype(jnp.bfloat16)
    query_gradient = logit_scale * jnp.einsum(
        "bhqk,kbhd->qbhd", narrow_gradient, key_all, preferred_element_type=jnp.float32
    )
    key_terms = logit_scale * jnp.einsum(
        "bhqk,qbhd->kbhd", narrow_gradient, query_matrix, preferred_element_type=jnp.float32
    )
    value_terms = jnp.einsum(
        "bhqk,qbhd->kbhd", narrow_probabilities, d_out, preferred_element_type=jnp.float32
    )
    d_keys, d_values = (
        lax.psum_scatter(
            key_terms.astype(jnp.bfloat16), "seq", scatter_dimension=0, tiled=True
        ).astype(jnp.float32),
        lax.psum_scatter(
            value_terms.astype(jnp.bfloat16), "seq", scatter_dimension=0, tiled=True
        ).astype(jnp.float32),
    )
    dqkv = (
        jnp.stack([query_gradient, d_keys, d_values])
        .reshape(3, tower_rows, seq_count, local_width)
        .astype(jnp.bfloat16)
    )
    part_w_qkv = jnp.einsum("tbc,itbe->ice", normed_rows, dqkv, preferred_element_type=jnp.float32)
    piece = dqkv
    d_normed = lax.psum_scatter(
        jnp.einsum("itbe,ice->tbc", piece, w_qkv, preferred_element_type=jnp.float32).astype(
            jnp.bfloat16
        ),
        "head",
        scatter_dimension=0,
        tiled=True,
    ).astype(jnp.float32)
    unit_rows = skip_wide * inv_rms
    scaled = d_normed * norm_gain
    d_skip = grad_out.astype(jnp.float32) + inv_rms * (
        scaled - unit_rows * jnp.mean(scaled * unit_rows, axis=-1, keepdims=True)
    )
    d_act = jnp.repeat(d_skip, 2, axis=0) * 0.5
    d_conv = gelu_pull(d_act)[0].astype(jnp.bfloat16)
    d_pad = padded_2(d_conv, ((("seq", "head"), 0),), 2)
    grad_input = jnp.zeros((fine_rows, seq_count, enc_in.shape[2]), jnp.float32)
    for offset in range(KW):
        grad_input = grad_input + jnp.einsum(
            "tbo,io->tbi",
            d_pad[4 - offset : 4 - offset + fine_rows],
            conv_weight[offset],
            preferred_element_type=jnp.float32,
        )
    grad_w_qkv, grad_w_out = (
        lax.psum(part_w_qkv.astype(jnp.bfloat16), "seq").astype(jnp.float32),
        lax.psum(part_w_out.astype(jnp.bfloat16), "seq").astype(jnp.float32),
    )
    return (mixed, grad_input.astype(jnp.bfloat16), grad_w_qkv, grad_w_out)


def body(enc_in, conv_weight, norm_gain, w_qkv, w_out, grad_out):
    heads = w_qkv.shape[2] // DH
    seqs = enc_in.shape[1]
    fits = heads == 2 and seqs == 4 and seqs * heads == lax.axis_size("seq")
    fits = fits and conv_weight.shape[2] == seqs * w_qkv.shape[2]
    chosen = unit_body if fits else gathered_body
    return chosen(enc_in, conv_weight, norm_gain, w_qkv, w_out, grad_out)


def solution(mesh):
    return jax.shard_map(
        body,
        mesh=mesh,
        in_specs=(
            P(("seq", "head"), None, None),
            P(),
            P(),
            P(None, None, "head"),
            P("head", None),
            P(("seq", "head"), None, None),
        ),
        out_specs=(
            P(("seq", "head"), None, None),
            P(("seq", "head"), None, None),
            P(None, None, "head"),
            P("head", None),
        ),
        check_vma=False,
    )
```

```python
import functools

import jax
import jax.numpy as jnp
from jax import lax
from jax.experimental import pallas as pl
from jax.experimental.pallas import tpu as pltpu
from jax.sharding import PartitionSpec as P

DH = 192
KW = 5
VMEM_LIMIT = 24 * 1024 * 1024
STREAMING_LIMIT = 56 * 1024 * 1024
COST = pl.CostEstimate(flops=1000, bytes_accessed=1000, transcendentals=0)
BF = jnp.bfloat16
F32 = jnp.float32
TOKEN = jax.ShapeDtypeStruct((8, 128), F32)


def params(limit=VMEM_LIMIT):
    return pltpu.CompilerParams(vmem_limit_bytes=limit)


def dot(a, b, contract):
    return lax.dot_general(a, b, (contract, ((), ())), preferred_element_type=F32)


NN = ((1,), (0,))
NT = ((1,), (1,))
TN = ((0,), (0,))


def whole(shape):
    return pl.BlockSpec(shape, lambda *_: (0,) * len(shape))


SCALARS = pl.BlockSpec(memory_space=pltpu.SMEM)


def spare(deps):
    return [pl.BlockSpec(memory_space=pl.ANY)] * len(deps)


def turned_rows(ref, low_ref, high_ref, parity, shift):
    seqs, rows, width = ref.shape[1:]
    own = ref[parity]
    if shift != 1:
        wide = own.astype(F32)
        if shift == 0:
            parts = [low_ref[parity].astype(F32), wide[:, : rows - 1]]
        else:
            parts = [wide[:, 1:], high_ref[parity].astype(F32)]
        own = jnp.concatenate(parts, axis=1).astype(BF)
    return own.reshape(seqs * rows, width)


def conv_kernel(
    at_ref, x_ref, low_ref, high_ref, w_ref, gain_ref, skip_ref, slope_ref, *rest
):
    normed_refs, (lhs, squares, whole_normed) = rest[:-3], rest[-3:]
    step = pl.program_id(0)
    seqs, rows, c_in = x_ref.shape[1:]
    half = seqs * rows
    tile = w_ref.shape[2]

    @pl.when(step == 0)
    def _():
        for parity in range(2):
            for shift in range(3):
                value = turned_rows(x_ref, low_ref, high_ref, parity, shift)
                for out in range(2):
                    tap = 2 * shift + parity - out
                    if 0 <= tap < KW:
                        lhs[out * half : (out + 1) * half, tap * c_in : (tap + 1) * c_in] = value
        squares[...] = jnp.zeros_like(squares)

    conv = dot(lhs[...], w_ref[...].reshape(KW * c_in, tile), NN)
    root = 0.7978845608028654
    total = None
    for parity in range(2):
        x = conv[parity * half : (parity + 1) * half, :]
        square = x * x
        t = jnp.tanh(root * (x + 0.044715 * (square * x)))
        left = 0.5 * (1.0 + t)
        act = x * left
        slope = left + (0.5 * root) * x * (1.0 - t * t) * (1.0 + (3 * 0.044715) * square)
        slope_ref[parity] = slope.reshape(slope_ref.shape[1:])
        total = act if total is None else total + act
    skip = (0.5 * total).astype(BF)
    columns = pl.ds(pl.multiple_of(step * tile, tile), tile)
    skip_ref[:, :, columns] = skip.reshape(seqs, rows, tile)
    wide = skip.astype(F32)
    squares[...] += jnp.sum(wide * wide, axis=-1, keepdims=True)

    @pl.when(step == pl.num_programs(0) - 1)
    def _():
        width = skip_ref.shape[2]
        inv = lax.rsqrt(squares[...] * (1.0 / width) + 1e-06)
        wide = skip_ref[...].reshape(half, width).astype(F32)
        normed = (wide * inv * gain_ref[...]).astype(BF)
        whole_normed[...] = normed.reshape(whole_normed.shape)
        for slot in range(seqs):
            normed_refs[slot][...] = whole_normed[at_ref[0] ^ slot]


def encoder(at, pairs, low, high, conv_weight, norm_gain):
    _, seqs, rows, c_in = pairs.shape
    width = conv_weight.shape[2]
    tile = 256 if width % 256 == 0 else width
    shape = (seqs, rows, width)
    outs = pl.pallas_call(
        conv_kernel,
        grid=(width // tile,),
        in_specs=[
            SCALARS,
            whole(pairs.shape),
            whole(low.shape),
            whole(high.shape),
            pl.BlockSpec((KW, c_in, tile), lambda n: (0, 0, n)),
            whole((1, width)),
        ],
        out_specs=[
            whole(shape),
            pl.BlockSpec((2, seqs, rows, tile), lambda n: (0, 0, 0, n)),
        ]
        + [whole((rows, width))] * seqs,
        out_shape=[
            jax.ShapeDtypeStruct(shape, BF),
            jax.ShapeDtypeStruct((2,) + shape, F32),
        ]
        + [jax.ShapeDtypeStruct((rows, width), BF)] * seqs,
        scratch_shapes=[
            pltpu.VMEM((2 * seqs * rows, KW * c_in), BF),
            pltpu.VMEM((seqs * rows, 1), F32),
            pltpu.VMEM(shape, BF),
        ],
        compiler_params=params(STREAMING_LIMIT),
        cost_estimate=COST,
        name="encoder_forward",
    )(at, pairs, low, high, conv_weight, norm_gain.reshape(1, width))
    return outs[0], outs[1], list(outs[2:])


def d_conv_kernel(at_ref, own_ref, near_ref, far_ref, *refs):
    skip_ref, grad_ref, gain_ref, slope_ref = refs[:4]
    out_ref, first_ref, last_ref = refs[-3:]
    rows = out_ref.shape[2]
    for slot, (ref, place) in enumerate(((own_ref, 0), (near_ref, 0), (far_ref, 0), (far_ref, 1))):
        b = at_ref[0] ^ slot
        wide = skip_ref[b].astype(F32)
        inv = lax.rsqrt(jnp.mean(wide * wide, axis=-1, keepdims=True) + 1e-06)
        unit = wide * inv
        scaled = ref[place].astype(F32) * gain_ref[...]
        d_skip = grad_ref[b].astype(F32) + inv * (
            scaled - unit * jnp.mean(scaled * unit, axis=-1, keepdims=True)
        )
        d_act = 0.5 * d_skip
        for parity in range(2):
            value = slope_ref[parity, b] * d_act
            out_ref[parity, b] = value.astype(BF)
            first_ref[parity, b] = value[:1].astype(BF)
            last_ref[parity, b] = value[rows - 1 :].astype(BF)


def conv_gradient(at, own, near, far, skip, grad, norm_gain, slope, *deps):
    vmem = pl.BlockSpec(memory_space=pltpu.VMEM)
    edge = jax.ShapeDtypeStruct(slope.shape[:2] + (1, slope.shape[3]), BF)
    return pl.pallas_call(
        d_conv_kernel,
        in_specs=[SCALARS] + [vmem] * 7 + spare(deps),
        out_specs=[vmem] * 3,
        out_shape=[jax.ShapeDtypeStruct(slope.shape, BF)] + [edge] * 2,
        compiler_params=params(),
        cost_estimate=COST,
        name="conv_gradient",
    )(at, own, near, far, skip, grad, norm_gain.reshape(1, -1), slope, *deps)


def mixed_body(seqs, at_ref, *refs):
    skip_ref, out_ref = refs[seqs:]
    for slot in range(seqs):
        b = at_ref[0] ^ slot
        out_ref[b] = (skip_ref[b].astype(F32) + refs[slot][...].astype(F32)).astype(BF)


def mixed_call(at, terms, skip):
    seqs = len(terms)
    vmem = pl.BlockSpec(memory_space=pltpu.VMEM)
    return pl.pallas_call(
        functools.partial(mixed_body, seqs),
        in_specs=[SCALARS] + [vmem] * (seqs + 1),
        out_specs=vmem,
        out_shape=jax.ShapeDtypeStruct(skip.shape, BF),
        compiler_params=params(),
        cost_estimate=COST,
        name="mixed_sum",
    )(at, *terms, skip)


def conv_back_kernel(d_ref, low_ref, high_ref, w_ref, *rest):
    out_ref, turned, acc = rest[-3:]
    step = pl.program_id(0)

    @pl.when(step == 0)
    def _():
        for parity in range(2):
            for shift in range(3):
                turned[parity, shift] = turned_rows(d_ref, low_ref, high_ref, parity, shift).T

    for tap in range(KW):

        @pl.when(step == tap)
        def _():
            places = [KW - 1 - tap, KW - tap]
            rhs = jnp.concatenate([turned[p % 2, p // 2] for p in places], axis=1)
            term = dot(w_ref[0], rhs, NN)
            if tap == 0:
                acc[...] = term
            elif tap < KW - 1:
                acc[...] += term
            else:
                out_ref[...] = (acc[...] + term).T.astype(BF)


def conv_back(d_conv, low, high, conv_weight, *deps):
    _, seqs, rows, width = d_conv.shape
    c_in = conv_weight.shape[1]
    flat = 2 * seqs * rows
    return pl.pallas_call(
        conv_back_kernel,
        grid=(KW,),
        in_specs=[
            whole(d_conv.shape),
            whole(low.shape),
            whole(high.shape),
            pl.BlockSpec((1, c_in, width), lambda k: (k, 0, 0)),
        ]
        + spare(deps),
        out_specs=whole((flat, c_in)),
        out_shape=jax.ShapeDtypeStruct((flat, c_in), BF),
        scratch_shapes=[
            pltpu.VMEM((2, 3, width, seqs * rows), BF),
            pltpu.VMEM((c_in, flat), F32),
        ],
        compiler_params=params(),
        cost_estimate=COST,
        name="encoder_backward",
    )(d_conv, low, high, conv_weight, *deps)


def pack_kernel(w_ref, pack_ref, turned_ref, token_ref):
    token_ref[...] = jnp.zeros_like(token_ref)
    for i in range(3):
        for head in range(pack_ref.shape[0]):
            part = w_ref[i, :, head * DH : (head + 1) * DH]
            columns = slice(i * DH, (i + 1) * DH)
            pack_ref[head, :, columns] = part
            turned_ref[head, columns, :] = part.T


def pack_weights(w_qkv):
    _, width, local = w_qkv.shape
    heads = local // DH
    tile = local
    return pl.pallas_call(
        pack_kernel,
        grid=(width // tile,),
        in_specs=[pl.BlockSpec((3, tile, local), lambda n: (0, n, 0))],
        out_specs=[
            pl.BlockSpec((heads, tile, 3 * DH), lambda n: (0, n, 0)),
            pl.BlockSpec((heads, 3 * DH, tile), lambda n: (0, 0, n)),
            pl.BlockSpec(TOKEN.shape, lambda n: (0, 0)),
        ],
        out_shape=[
            jax.ShapeDtypeStruct((heads, width, 3 * DH), BF),
            jax.ShapeDtypeStruct((heads, 3 * DH, width), BF),
            TOKEN,
        ],
        compiler_params=params(),
        cost_estimate=COST,
        name="pack_weights",
    )(w_qkv)


def product_kernel(head_ref, x_ref, w_ref, *rest, contract):
    del head_ref
    out_ref, token_ref = rest[-2:]
    token_ref[...] = jnp.zeros_like(token_ref)
    value = dot(x_ref[...], w_ref[0], contract).astype(BF)
    out_ref[:, : value.shape[1]] = value
    if value.shape[1] < out_ref.shape[1]:
        out_ref[:, value.shape[1] :] = jnp.zeros_like(out_ref[:, value.shape[1] :])


def head_product(head, x, weight, contract, name, *deps):
    columns = weight.shape[2] if contract == NN else weight.shape[1]
    columns += -columns % 128
    rows, width = x.shape
    return pl.pallas_call(
        functools.partial(product_kernel, contract=contract),
        grid_spec=pltpu.PrefetchScalarGridSpec(
            num_scalar_prefetch=1,
            grid=(1,),
            in_specs=[
                pl.BlockSpec((rows, width), lambda i, head: (0, 0)),
                pl.BlockSpec((1,) + weight.shape[1:], lambda i, head: (head[0], 0, 0)),
            ]
            + spare(deps),
            out_specs=[
                pl.BlockSpec((rows, columns), lambda i, head: (0, 0)),
                pl.BlockSpec(TOKEN.shape, lambda i, head: (0, 0)),
            ],
        ),
        out_shape=[jax.ShapeDtypeStruct((rows, columns), BF), TOKEN],
        compiler_params=params(),
        cost_estimate=COST,
        name=name,
    )(head, x, weight, *deps)


def attention_kernel(qa_ref, qb_ref, da_ref, db_ref, *rest, block):
    oa_ref, ob_ref, k_all, v_all, dk_acc, dv_acc = rest[-6:]
    scale = DH ** (-0.5)
    half = qa_ref.shape[0]
    for place, ref in enumerate((qa_ref, qb_ref)):
        rows = pl.ds(place * half, half)
        k_all[rows, :] = ref[:, DH : 2 * DH]
        v_all[rows, :] = ref[:, 2 * DH : 3 * DH]
    k = k_all[...]
    v = v_all[...]
    for place, (q_ref, d_ref, out_ref) in enumerate(
        ((qa_ref, da_ref, oa_ref), (qb_ref, db_ref, ob_ref))
    ):
        for start in range(0, half, block):
            rows = pl.ds(start, block)
            q = q_ref[rows, 0:DH]
            d_o = d_ref[rows, 0:DH]
            s = dot(q, k, NT) * scale
            e = jnp.exp(s - jnp.max(s, axis=-1, keepdims=True))
            p = e * (1.0 / jnp.sum(e, axis=-1, keepdims=True))
            p_b = p.astype(BF)
            o = dot(p_b, v, NN)
            delta = jnp.sum(d_o.astype(F32) * o, axis=-1, keepdims=True)
            d_p = dot(d_o, v, NT)
            ds = (p * (d_p - delta)).astype(BF)
            dq = scale * dot(ds, k, NN)
            dk = dot(ds, q, TN)
            dv = dot(p_b, d_o, TN)
            if place == 0 and start == 0:
                dk_acc[...] = dk
                dv_acc[...] = dv
            else:
                dk_acc[...] += dk
                dv_acc[...] += dv
            out_ref[rows, 0:DH] = dq.astype(BF)
            out_ref[rows, 3 * DH : 4 * DH] = o.astype(BF)
    for place, out_ref in enumerate((oa_ref, ob_ref)):
        rows = pl.ds(place * half, half)
        out_ref[:, DH : 2 * DH] = (scale * dk_acc[rows, :]).astype(BF)
        out_ref[:, 2 * DH : 3 * DH] = dv_acc[rows, :].astype(BF)


def attention(qkv_a, qkv_b, d_a, d_b, *deps):
    half = qkv_a.shape[0]
    shape = jax.ShapeDtypeStruct((half, 4 * DH), BF)
    return pl.pallas_call(
        functools.partial(attention_kernel, block=min(256, half)),
        in_specs=[pl.BlockSpec(memory_space=pltpu.VMEM)] * 4 + spare(deps),
        out_shape=[shape, shape],
        scratch_shapes=[
            pltpu.VMEM((2 * half, DH), BF),
            pltpu.VMEM((2 * half, DH), BF),
            pltpu.VMEM((2 * half, DH), F32),
            pltpu.VMEM((2 * half, DH), F32),
        ],
        compiler_params=params(),
        cost_estimate=COST,
        name="attention",
    )(qkv_a, qkv_b, d_a, d_b, *deps)


def term_kernel(head_ref, a_ref, b_ref, w_ref, *rest, first, last):
    head = head_ref[0]
    total = dot(a_ref[:, first:last], w_ref[head], NN)
    total += dot(b_ref[:, first:last], w_ref[1 - head], NN)
    rest[-1][...] = total.astype(BF)


def pair_term(head, mine, got, weight, first, last, name, *deps):
    half, full = mine.shape
    heads, depth, width = weight.shape
    tile = 512 if width % 512 == 0 else width
    return pl.pallas_call(
        functools.partial(term_kernel, first=first, last=last),
        grid_spec=pltpu.PrefetchScalarGridSpec(
            num_scalar_prefetch=1,
            grid=(width // tile,),
            in_specs=[
                pl.BlockSpec((half, full), lambda n, at: (0, 0)),
                pl.BlockSpec((half, full), lambda n, at: (0, 0)),
                pl.BlockSpec((heads, depth, tile), lambda n, at: (0, 0, n)),
            ]
            + spare(deps),
            out_specs=pl.BlockSpec((half, tile), lambda n, at: (0, n)),
        ),
        out_shape=jax.ShapeDtypeStruct((half, width), BF),
        compiler_params=params(),
        cost_estimate=COST,
        name=name,
    )(head, mine, got, weight, *deps)


def weight_kernel(at_ref, xa_ref, xb_ref, ga_ref, gb_ref, ra_ref, rb_ref, *rest):
    del at_ref
    out_refs, turned = rest[:-1], rest[-1]
    step = pl.program_id(0)
    half = ra_ref.shape[0]
    split = 3 * DH

    @pl.when(step == 0)
    def _():
        turned[:, :half] = ra_ref[...].T
        turned[:, half:] = rb_ref[...].T

    a, b = slice(0, half), slice(half, 2 * half)
    qkv = dot(turned[:split, a], xa_ref[...], NN) + dot(turned[:split, b], xb_ref[...], NN)
    out = dot(turned[split:, a], ga_ref[...], NN) + dot(turned[split:, b], gb_ref[...], NN)
    for slot, out_ref in enumerate(out_refs):

        @pl.when(step == slot)
        def _():
            out_ref[:split, :] = qkv.astype(BF)
            out_ref[split:, :] = out.astype(BF)


def weight_gradients(at, xa, xb, ga, gb, ra, rb, seqs):
    half, width = xa.shape
    chunk = width // seqs
    full = ra.shape[1]
    column = pl.BlockSpec((half, chunk), lambda r, at: (0, r ^ at[0]))
    rest = pl.BlockSpec((half, full), lambda r, at: (0, 0))
    return pl.pallas_call(
        weight_kernel,
        grid_spec=pltpu.PrefetchScalarGridSpec(
            num_scalar_prefetch=1,
            grid=(seqs,),
            in_specs=[column] * 4 + [rest] * 2,
            out_specs=[pl.BlockSpec((full, chunk), lambda r, at: (0, 0))] * seqs,
            scratch_shapes=[pltpu.VMEM((full, 2 * half), BF)],
        ),
        out_shape=[jax.ShapeDtypeStruct((full, chunk), BF)] * seqs,
        compiler_params=params(STREAMING_LIMIT),
        cost_estimate=COST,
        name="weight_gradients",
    )(at, xa, xb, ga, gb, ra, rb)


def weight_sum_kernel(*refs, count):
    part_refs, out_refs = refs[:count], refs[-2:]
    split = 3 * DH
    total = part_refs[0][...].astype(F32)
    for ref in part_refs[1:]:
        total = total + ref[...].astype(F32)
    turned = total[:split].T.astype(BF)
    quarter = DH // 2
    for part, out_ref in enumerate(out_refs):
        out_ref[:, :split] = turned[part * DH : (part + 1) * DH]
        first = split + part * quarter
        piece = total[first : first + quarter].astype(BF)
        out_ref[:quarter, split:] = piece[:, :DH]
        out_ref[quarter:, split:] = piece[:, DH:]


def weight_sum(parts, *deps):
    full, chunk = parts[0].shape
    return pl.pallas_call(
        functools.partial(weight_sum_kernel, count=len(parts)),
        in_specs=[pl.BlockSpec(memory_space=pltpu.VMEM)] * len(parts) + spare(deps),
        out_shape=[jax.ShapeDtypeStruct((chunk // 2, full), BF)] * 2,
        compiler_params=params(),
        cost_estimate=COST,
        name="weight_sum",
    )(*parts, *deps)


def unpack_kernel(at_ref, *refs):
    qkv_ref, out_ref, token_ref = refs[-3:]
    step = pl.program_id(0)
    split = 3 * DH
    quarter = DH // 2
    token_ref[...] = jnp.zeros_like(token_ref)
    for half in range(2):

        @pl.when(step // 2 == half)
        def _():
            mine = refs[half][...].astype(F32)
            other = refs[2 + half][...].astype(F32)
            swapped = at_ref[1] != 0
            low = jnp.where(swapped, other, mine)
            high = jnp.where(swapped, mine, other)
            for i in range(3):
                columns = slice(i * DH, (i + 1) * DH)
                qkv_ref[i] = jnp.concatenate([low[:, columns], high[:, columns]], axis=1)
            for head, value in enumerate((low, high)):
                folded = [value[:quarter, split:], value[quarter:, split:]]
                out_ref[head, 0] = jnp.concatenate(folded, axis=1)


def unpack_weights(at, mine, other, far, before=()):
    rows, full = mine[0].shape
    half = rows // 2
    width = 4 * rows

    def chunk(t, at):
        if far:
            return at[0] ^ jnp.where(t < 2, t + 2, 2 * t - 3)
        return at[0] ^ jnp.where(t < 2, t, 2 * t - 4)

    specs = [
        pl.BlockSpec((half, full), lambda t, at: (jnp.minimum(t, 1), 0)),
        pl.BlockSpec((half, full), lambda t, at: (jnp.maximum(t - 2, 0), 0)),
    ]
    return pl.pallas_call(
        unpack_kernel,
        grid_spec=pltpu.PrefetchScalarGridSpec(
            num_scalar_prefetch=1,
            grid=(4,),
            in_specs=specs * 2 + spare(before),
            out_specs=[
                pl.BlockSpec((3, half, 2 * DH), lambda t, at: (0, 2 * chunk(t, at) + t // 2, 0)),
                pl.BlockSpec(
                    (2, 1, DH // 2, rows), lambda t, at: (0, t // 2, 0, chunk(t, at))
                ),
                pl.BlockSpec(TOKEN.shape, lambda t, at: (0, 0)),
            ],
        ),
        out_shape=[
            jax.ShapeDtypeStruct((3, width, 2 * DH), F32),
            jax.ShapeDtypeStruct((2, 2, DH // 2, width), F32),
            TOKEN,
        ],
        input_output_aliases={5 + i: i for i in range(len(before))},
        compiler_params=params(),
        cost_estimate=COST,
        name="weight_outputs_far" if far else "weight_outputs_near",
    )(at, *mine, *other, *before)


def neighbour_edges(first, last):
    axes = ("seq", "head")
    count = lax.axis_size(axes)
    forward = [(i, i + 1) for i in range(count - 1)]
    backward = [(target, source) for source, target in forward]
    return lax.ppermute(last, axes, forward), lax.ppermute(first, axes, backward)


def after(value, *others):
    return lax.optimization_barrier((value,) + others)[0]


def trade_chip(x, bit, heads):
    count = lax.axis_size("seq")
    return lax.ppermute(x, "seq", [(s, s ^ (bit * heads)) for s in range(count)])


def swap_heads(x):
    count = lax.axis_size("seq")
    return lax.ppermute(x, "seq", [(s, s + 1 - 2 * (s % 2)) for s in range(count)])


def unit_body(enc_in, conv_weight, norm_gain, w_qkv, w_out, grad_out):
    rows = enc_in.shape[0] // 2
    seqs = enc_in.shape[1]
    width = conv_weight.shape[2]
    local = w_qkv.shape[2]
    heads = local // DH
    groups = lax.axis_size("head")
    half = groups * seqs * rows
    place = lax.axis_index("seq")
    own_seq = (place // heads).astype(jnp.int32)
    own_head = (place % heads).astype(jnp.int32)
    at = jnp.stack([own_seq, own_head])
    head_mine = own_head.reshape(1)
    head_other = (1 - own_head).reshape(1)

    def to_chips(slots):
        return [x if j == 0 else trade_chip(x, j, heads) for j, x in enumerate(slots)]

    order = (0, 2, 1, 3)

    grad_z = lax.all_gather(grad_out, "head", axis=0, tiled=False)

    pairs = jnp.transpose(enc_in.reshape(rows, 2, seqs, enc_in.shape[2]), (1, 2, 0, 3))
    low, high = neighbour_edges(pairs[:, :, :1, :], pairs[:, :, -1:, :])
    skip, slope, normed = encoder(at, pairs, low, high, conv_weight, norm_gain)
    normed = to_chips(normed)
    normed_slab = jnp.concatenate([normed[j] for j in order], axis=0)
    normed_rows = lax.all_gather(normed_slab, "head", axis=0, tiled=True)

    grad_z = after(grad_z, normed_slab)
    grad_slots = to_chips(
        [lax.dynamic_index_in_dim(grad_z, own_seq ^ j, 2, keepdims=False) for j in range(seqs)]
    )
    grad_rows = jnp.stack([grad_slots[j] for j in order], axis=1).reshape(half, width)
    w_pack, w_turned, packed = pack_weights(after(w_qkv, normed_slab))
    w_rows = w_out.reshape(heads, DH, width)
    d_other, one = head_product(head_other, grad_rows, w_rows, NT, "d_o_other")
    d_got = swap_heads(d_other)
    d_mine, two = head_product(head_mine, grad_rows, w_rows, NT, "d_o_own")
    grad_swapped = swap_heads(grad_rows)
    normed_rows, d_got, d_mine, grad_swapped, w_pack, w_turned, *tokens = (
        lax.optimization_barrier(
            (normed_rows, d_got, d_mine, grad_swapped, w_pack, w_turned, packed, one, two)
        )
    )

    normed_swapped = swap_heads(normed_rows)
    qkv_other, _ = head_product(head_other, normed_rows, w_pack, NN, "qkv_other", *tokens)
    qkv_got = swap_heads(qkv_other)
    qkv_mine, _ = head_product(head_mine, normed_rows, w_pack, NN, "qkv_own")
    result_mine, result_other = attention(qkv_mine, qkv_got, d_mine, d_got, normed_swapped)
    result_got = swap_heads(result_other)

    shape = (groups, seqs, rows, width)
    d_term = pair_term(head_mine, result_mine, result_got, w_turned, 0, 3 * DH, "d_term")
    d_normed = lax.psum_scatter(d_term.reshape(shape), "head", scatter_dimension=0, tiled=False)
    part = weight_gradients(
        own_seq.reshape(1),
        normed_rows,
        normed_swapped,
        grad_rows,
        grad_swapped,
        result_mine,
        result_other,
        seqs,
    )
    part = to_chips(part)
    head_term = pair_term(
        head_mine, result_mine, result_got, w_rows, 3 * DH, 4 * DH, "head_term"
    )
    head_sum = lax.psum_scatter(head_term.reshape(shape), "head", scatter_dimension=0, tiled=False)

    leaving = d_normed[2:]
    near = trade_chip(leaving, 1, heads)
    far = trade_chip(jnp.stack([d_normed[1], near[1]]), 2, heads)
    grad = jnp.transpose(after(grad_out, d_term), (1, 0, 2))
    half_a, half_b = weight_sum(part, leaving)
    d_conv, first, last = conv_gradient(
        at, d_normed, near, far, skip, grad, norm_gain, slope, half_a
    )
    low, high = neighbour_edges(first, last)

    got_a = trade_chip(half_a, 1, heads)
    got_b = trade_chip(half_b, 2, heads)
    near_a = jnp.concatenate([half_a, after(got_a, low)], axis=0)
    near_b = jnp.concatenate([half_b, after(got_b, low)], axis=0)
    far_a = trade_chip(near_a, 2, heads)
    far_b = trade_chip(near_b, 1, heads)
    near_other = [swap_heads(near_a), swap_heads(near_b)]
    *outputs, token = unpack_weights(at, [near_a, near_b], near_other, False)
    grad_input = conv_back(d_conv, low, high, conv_weight, token)

    head_sum = after(head_sum, grad_input)
    head_sum = [head_sum[order.index(j)] for j in range(seqs)]
    far_other = [swap_heads(after(x, *head_sum)) for x in (far_a, far_b)]
    grad_w_qkv, grad_w_out, _ = unpack_weights(at, [far_a, far_b], far_other, True, outputs)
    head_sum = to_chips(head_sum)
    mixed = mixed_call(at, head_sum, skip)
    grad_input = jnp.transpose(grad_input.reshape(2, seqs, rows, -1), (2, 0, 1, 3))
    return (
        jnp.transpose(mixed, (1, 0, 2)),
        grad_input.reshape(enc_in.shape),
        grad_w_qkv,
        grad_w_out.reshape(local, width),
    )


def padded_2(block, sides, width):
    for axis, dim in sides:
        count = lax.axis_size(axis)
        forward = [(i, i + 1) for i in range(count - 1)]
        backward = [(target, source) for source, target in forward]
        low = lax.ppermute(
            lax.slice_in_dim(block, block.shape[dim] - width, None, axis=dim), axis, forward
        )
        high = lax.ppermute(lax.slice_in_dim(block, 0, width, axis=dim), axis, backward)
        block = jnp.concatenate([low, block, high], axis=dim)
    return block


def gathered_body(enc_in, conv_weight, norm_gain, w_qkv, w_out, grad_out):
    fine_rows = enc_in.shape[0]
    slab_rows = fine_rows // 2
    seq_count = enc_in.shape[1]
    out_width = conv_weight.shape[2]
    local_width = w_qkv.shape[2]
    local_heads = local_width // DH
    logit_scale = DH ** (-0.5)
    padded = padded_2(enc_in, ((("seq", "head"), 0),), 2)
    convolved = jnp.zeros((fine_rows, seq_count, out_width), jnp.float32)
    for offset in range(KW):
        convolved = convolved + jnp.einsum(
            "tbi,io->tbo",
            padded[offset : offset + fine_rows],
            conv_weight[offset],
            preferred_element_type=jnp.float32,
        )
    activated, gelu_pull = jax.vjp(jax.nn.gelu, convolved)
    skip = jnp.mean(activated.reshape(slab_rows, 2, seq_count, out_width), axis=1).astype(
        jnp.bfloat16
    )
    skip_wide = skip.astype(jnp.float32)
    inv_rms = lax.rsqrt(jnp.mean(skip_wide * skip_wide, axis=-1, keepdims=True) + 1e-06)
    normed = (skip_wide * inv_rms * norm_gain).astype(jnp.bfloat16)
    normed_rows = lax.all_gather(normed, "head", axis=0, tiled=True)
    grad_rows = lax.all_gather(grad_out, "head", axis=0, tiled=True)
    tower_rows = normed_rows.shape[0]
    qkv = jnp.einsum(
        "tbc,ice->itbe", normed_rows, w_qkv, preferred_element_type=jnp.float32
    ).astype(jnp.bfloat16)
    qkv = qkv.reshape(3, tower_rows, seq_count, local_heads, DH)
    query_matrix, key_matrix, value_matrix = (qkv[0], qkv[1], qkv[2])
    key_all, value_all = (
        lax.all_gather(key_matrix, "seq", axis=0, tiled=True),
        lax.all_gather(value_matrix, "seq", axis=0, tiled=True),
    )
    attention_logits = (
        jnp.einsum("qbhd,kbhd->bhqk", query_matrix, key_all, preferred_element_type=jnp.float32)
        * logit_scale
    )
    row_peak = jnp.max(attention_logits, axis=-1, keepdims=True)
    exponent = jnp.exp(attention_logits - row_peak)
    row_total = jnp.sum(exponent, axis=-1, keepdims=True)
    soft_weights = exponent / row_total
    narrow_probabilities = soft_weights.astype(jnp.bfloat16)
    attention_output = jnp.einsum(
        "bhqk,kbhd->qbhd", narrow_probabilities, value_all, preferred_element_type=jnp.float32
    )
    o_narrow = attention_output.reshape(tower_rows, seq_count, local_width).astype(jnp.bfloat16)
    piece = o_narrow
    head_sum = lax.psum_scatter(
        jnp.einsum("tbe,ec->tbc", piece, w_out, preferred_element_type=jnp.float32).astype(
            jnp.bfloat16
        ),
        "head",
        scatter_dimension=0,
        tiled=True,
    ).astype(jnp.float32)
    mixed = (skip_wide + head_sum).astype(jnp.bfloat16)
    part_w_out = jnp.einsum("tbe,tbc->ec", o_narrow, grad_rows, preferred_element_type=jnp.float32)
    d_out = jnp.einsum("tbc,ec->tbe", grad_rows, w_out, preferred_element_type=jnp.float32).astype(
        jnp.bfloat16
    )
    d_out = d_out.reshape(tower_rows, seq_count, local_heads, DH)
    delta = jnp.sum(d_out.astype(jnp.float32) * attention_output, axis=-1)
    probability_gradient = jnp.einsum(
        "qbhd,kbhd->bhqk", d_out, value_all, preferred_element_type=jnp.float32
    )
    d_scores = soft_weights * (probability_gradient - jnp.transpose(delta, (1, 2, 0))[..., None])
    narrow_gradient = d_scores.astype(jnp.bfloat16)
    query_gradient = logit_scale * jnp.einsum(
        "bhqk,kbhd->qbhd", narrow_gradient, key_all, preferred_element_type=jnp.float32
    )
    key_terms = logit_scale * jnp.einsum(
        "bhqk,qbhd->kbhd", narrow_gradient, query_matrix, preferred_element_type=jnp.float32
    )
    value_terms = jnp.einsum(
        "bhqk,qbhd->kbhd", narrow_probabilities, d_out, preferred_element_type=jnp.float32
    )
    d_keys, d_values = (
        lax.psum_scatter(
            key_terms.astype(jnp.bfloat16), "seq", scatter_dimension=0, tiled=True
        ).astype(jnp.float32),
        lax.psum_scatter(
            value_terms.astype(jnp.bfloat16), "seq", scatter_dimension=0, tiled=True
        ).astype(jnp.float32),
    )
    dqkv = (
        jnp.stack([query_gradient, d_keys, d_values])
        .reshape(3, tower_rows, seq_count, local_width)
        .astype(jnp.bfloat16)
    )
    part_w_qkv = jnp.einsum("tbc,itbe->ice", normed_rows, dqkv, preferred_element_type=jnp.float32)
    piece = dqkv
    d_normed = lax.psum_scatter(
        jnp.einsum("itbe,ice->tbc", piece, w_qkv, preferred_element_type=jnp.float32).astype(
            jnp.bfloat16
        ),
        "head",
        scatter_dimension=0,
        tiled=True,
    ).astype(jnp.float32)
    unit_rows = skip_wide * inv_rms
    scaled = d_normed * norm_gain
    d_skip = grad_out.astype(jnp.float32) + inv_rms * (
        scaled - unit_rows * jnp.mean(scaled * unit_rows, axis=-1, keepdims=True)
    )
    d_act = jnp.repeat(d_skip, 2, axis=0) * 0.5
    d_conv = gelu_pull(d_act)[0].astype(jnp.bfloat16)
    d_pad = padded_2(d_conv, ((("seq", "head"), 0),), 2)
    grad_input = jnp.zeros((fine_rows, seq_count, enc_in.shape[2]), jnp.float32)
    for offset in range(KW):
        grad_input = grad_input + jnp.einsum(
            "tbo,io->tbi",
            d_pad[4 - offset : 4 - offset + fine_rows],
            conv_weight[offset],
            preferred_element_type=jnp.float32,
        )
    grad_w_qkv, grad_w_out = (
        lax.psum(part_w_qkv.astype(jnp.bfloat16), "seq").astype(jnp.float32),
        lax.psum(part_w_out.astype(jnp.bfloat16), "seq").astype(jnp.float32),
    )
    return (mixed, grad_input.astype(jnp.bfloat16), grad_w_qkv, grad_w_out)


def body(enc_in, conv_weight, norm_gain, w_qkv, w_out, grad_out):
    heads = w_qkv.shape[2] // DH
    seqs = enc_in.shape[1]
    fits = heads == 2 and seqs == 4 and seqs * heads == lax.axis_size("seq")
    fits = fits and conv_weight.shape[2] == seqs * w_qkv.shape[2]
    chosen = unit_body if fits else gathered_body
    return chosen(enc_in, conv_weight, norm_gain, w_qkv, w_out, grad_out)


def solution(mesh):
    return jax.shard_map(
        body,
        mesh=mesh,
        in_specs=(
            P(("seq", "head"), None, None),
            P(),
            P(),
            P(None, None, "head"),
            P("head", None),
            P(("seq", "head"), None, None),
        ),
        out_specs=(
            P(("seq", "head"), None, None),
            P(("seq", "head"), None, None),
            P(None, None, "head"),
            P("head", None),
        ),
        check_vma=False,
    )
```

```python
import functools

import jax
import jax.numpy as jnp
from jax import lax
from jax.experimental import pallas as pl
from jax.experimental.pallas import tpu as pltpu
from jax.sharding import PartitionSpec as P

DH = 192
KW = 5
VMEM_LIMIT = 24 * 1024 * 1024
STREAMING_LIMIT = 56 * 1024 * 1024
COST = pl.CostEstimate(flops=1000, bytes_accessed=1000, transcendentals=0)
BF = jnp.bfloat16
F32 = jnp.float32
TOKEN = jax.ShapeDtypeStruct((8, 128), F32)


def params(limit=VMEM_LIMIT):
    return pltpu.CompilerParams(vmem_limit_bytes=limit)


def dot(a, b, contract):
    return lax.dot_general(a, b, (contract, ((), ())), preferred_element_type=F32)


NN = ((1,), (0,))
NT = ((1,), (1,))
TN = ((0,), (0,))


def whole(shape):
    return pl.BlockSpec(shape, lambda *_: (0,) * len(shape))


SCALARS = pl.BlockSpec(memory_space=pltpu.SMEM)


def spare(deps):
    return [pl.BlockSpec(memory_space=pl.ANY)] * len(deps)


def turned_rows(ref, low_ref, high_ref, parity, shift):
    seqs, rows, width = ref.shape[1:]
    own = ref[parity]
    if shift != 1:
        wide = own.astype(F32)
        if shift == 0:
            parts = [low_ref[parity].astype(F32), wide[:, : rows - 1]]
        else:
            parts = [wide[:, 1:], high_ref[parity].astype(F32)]
        own = jnp.concatenate(parts, axis=1).astype(BF)
    return own.reshape(seqs * rows, width)


def conv_kernel(
    at_ref, x_ref, low_ref, high_ref, w_ref, gain_ref, skip_ref, slope_ref, *rest
):
    normed_refs, (lhs, squares, whole_normed) = rest[:-3], rest[-3:]
    step = pl.program_id(0)
    seqs, rows, c_in = x_ref.shape[1:]
    half = seqs * rows
    tile = w_ref.shape[2]

    @pl.when(step == 0)
    def _():
        for parity in range(2):
            for shift in range(3):
                value = turned_rows(x_ref, low_ref, high_ref, parity, shift)
                for out in range(2):
                    tap = 2 * shift + parity - out
                    if 0 <= tap < KW:
                        lhs[out * half : (out + 1) * half, tap * c_in : (tap + 1) * c_in] = value
        squares[...] = jnp.zeros_like(squares)

    conv = dot(lhs[...], w_ref[...].reshape(KW * c_in, tile), NN)
    root = 0.7978845608028654
    total = None
    for parity in range(2):
        x = conv[parity * half : (parity + 1) * half, :]
        square = x * x
        t = jnp.tanh(root * (x + 0.044715 * (square * x)))
        left = 0.5 * (1.0 + t)
        act = x * left
        slope = left + (0.5 * root) * x * (1.0 - t * t) * (1.0 + (3 * 0.044715) * square)
        slope_ref[parity] = slope.reshape(slope_ref.shape[1:])
        total = act if total is None else total + act
    skip = (0.5 * total).astype(BF)
    columns = pl.ds(pl.multiple_of(step * tile, tile), tile)
    skip_ref[:, :, columns] = skip.reshape(seqs, rows, tile)
    wide = skip.astype(F32)
    squares[...] += jnp.sum(wide * wide, axis=-1, keepdims=True)

    @pl.when(step == pl.num_programs(0) - 1)
    def _():
        width = skip_ref.shape[2]
        inv = lax.rsqrt(squares[...] * (1.0 / width) + 1e-06)
        wide = skip_ref[...].reshape(half, width).astype(F32)
        normed = (wide * inv * gain_ref[...]).astype(BF)
        whole_normed[...] = normed.reshape(whole_normed.shape)
        for slot in range(seqs):
            normed_refs[slot][...] = whole_normed[at_ref[0] ^ slot]


def encoder(at, pairs, low, high, conv_weight, norm_gain):
    _, seqs, rows, c_in = pairs.shape
    width = conv_weight.shape[2]
    tile = 256 if width % 256 == 0 else width
    shape = (seqs, rows, width)
    outs = pl.pallas_call(
        conv_kernel,
        grid=(width // tile,),
        in_specs=[
            SCALARS,
            whole(pairs.shape),
            whole(low.shape),
            whole(high.shape),
            pl.BlockSpec((KW, c_in, tile), lambda n: (0, 0, n)),
            whole((1, width)),
        ],
        out_specs=[
            whole(shape),
            pl.BlockSpec((2, seqs, rows, tile), lambda n: (0, 0, 0, n)),
        ]
        + [whole((rows, width))] * seqs,
        out_shape=[
            jax.ShapeDtypeStruct(shape, BF),
            jax.ShapeDtypeStruct((2,) + shape, F32),
        ]
        + [jax.ShapeDtypeStruct((rows, width), BF)] * seqs,
        scratch_shapes=[
            pltpu.VMEM((2 * seqs * rows, KW * c_in), BF),
            pltpu.VMEM((seqs * rows, 1), F32),
            pltpu.VMEM(shape, BF),
        ],
        compiler_params=params(STREAMING_LIMIT),
        cost_estimate=COST,
        name="encoder_forward",
    )(at, pairs, low, high, conv_weight, norm_gain.reshape(1, width))
    return outs[0], outs[1], list(outs[2:])


def d_conv_kernel(at_ref, own_ref, near_ref, far_ref, *refs):
    skip_ref, grad_ref, gain_ref, slope_ref = refs[:4]
    out_ref, first_ref, last_ref = refs[-3:]
    rows = out_ref.shape[2]
    for slot, (ref, place) in enumerate(((own_ref, 0), (near_ref, 0), (far_ref, 0), (far_ref, 1))):
        b = at_ref[0] ^ slot
        wide = skip_ref[b].astype(F32)
        inv = lax.rsqrt(jnp.mean(wide * wide, axis=-1, keepdims=True) + 1e-06)
        unit = wide * inv
        scaled = ref[place].astype(F32) * gain_ref[...]
        d_skip = grad_ref[b].astype(F32) + inv * (
            scaled - unit * jnp.mean(scaled * unit, axis=-1, keepdims=True)
        )
        d_act = 0.5 * d_skip
        for parity in range(2):
            value = slope_ref[parity, b] * d_act
            out_ref[parity, b] = value.astype(BF)
            first_ref[parity, b] = value[:1].astype(BF)
            last_ref[parity, b] = value[rows - 1 :].astype(BF)


def conv_gradient(at, own, near, far, skip, grad, norm_gain, slope, *deps):
    vmem = pl.BlockSpec(memory_space=pltpu.VMEM)
    edge = jax.ShapeDtypeStruct(slope.shape[:2] + (1, slope.shape[3]), BF)
    return pl.pallas_call(
        d_conv_kernel,
        in_specs=[SCALARS] + [vmem] * 7 + spare(deps),
        out_specs=[vmem] * 3,
        out_shape=[jax.ShapeDtypeStruct(slope.shape, BF)] + [edge] * 2,
        compiler_params=params(),
        cost_estimate=COST,
        name="conv_gradient",
    )(at, own, near, far, skip, grad, norm_gain.reshape(1, -1), slope, *deps)


def mixed_body(seqs, at_ref, *refs):
    skip_ref, out_ref = refs[seqs:]
    for slot in range(seqs):
        b = at_ref[0] ^ slot
        out_ref[b] = (skip_ref[b].astype(F32) + refs[slot][...].astype(F32)).astype(BF)


def mixed_call(at, terms, skip):
    seqs = len(terms)
    vmem = pl.BlockSpec(memory_space=pltpu.VMEM)
    return pl.pallas_call(
        functools.partial(mixed_body, seqs),
        in_specs=[SCALARS] + [vmem] * (seqs + 1),
        out_specs=vmem,
        out_shape=jax.ShapeDtypeStruct(skip.shape, BF),
        compiler_params=params(),
        cost_estimate=COST,
        name="mixed_sum",
    )(at, *terms, skip)


def marker_kernel(*refs):
    refs[-1][...] = jnp.zeros_like(refs[-1])


def marker(*deps):
    return pl.pallas_call(
        marker_kernel,
        in_specs=spare(deps),
        out_shape=TOKEN,
        compiler_params=params(),
        cost_estimate=COST,
        name="marker",
    )(*deps)


def conv_back_kernel(d_ref, low_ref, high_ref, w_ref, *rest):
    out_ref, turned, acc = rest[-3:]
    step = pl.program_id(0)

    @pl.when(step == 0)
    def _():
        for parity in range(2):
            for shift in range(3):
                turned[parity, shift] = turned_rows(d_ref, low_ref, high_ref, parity, shift).T

    for tap in range(KW):

        @pl.when(step == tap)
        def _():
            places = [KW - 1 - tap, KW - tap]
            rhs = jnp.concatenate([turned[p % 2, p // 2] for p in places], axis=1)
            term = dot(w_ref[0], rhs, NN)
            if tap == 0:
                acc[...] = term
            elif tap < KW - 1:
                acc[...] += term
            else:
                out_ref[...] = (acc[...] + term).T.astype(BF)


def conv_back(d_conv, low, high, conv_weight, *deps):
    _, seqs, rows, width = d_conv.shape
    c_in = conv_weight.shape[1]
    flat = 2 * seqs * rows
    return pl.pallas_call(
        conv_back_kernel,
        grid=(KW,),
        in_specs=[
            whole(d_conv.shape),
            whole(low.shape),
            whole(high.shape),
            pl.BlockSpec((1, c_in, width), lambda k: (k, 0, 0)),
        ]
        + spare(deps),
        out_specs=whole((flat, c_in)),
        out_shape=jax.ShapeDtypeStruct((flat, c_in), BF),
        scratch_shapes=[
            pltpu.VMEM((2, 3, width, seqs * rows), BF),
            pltpu.VMEM((c_in, flat), F32),
        ],
        compiler_params=params(),
        cost_estimate=COST,
        name="encoder_backward",
    )(d_conv, low, high, conv_weight, *deps)


def pack_kernel(w_ref, pack_ref, turned_ref, token_ref):
    token_ref[...] = jnp.zeros_like(token_ref)
    for i in range(3):
        for head in range(pack_ref.shape[0]):
            part = w_ref[i, :, head * DH : (head + 1) * DH]
            columns = slice(i * DH, (i + 1) * DH)
            pack_ref[head, :, columns] = part
            turned_ref[head, columns, :] = part.T


def pack_weights(w_qkv):
    _, width, local = w_qkv.shape
    heads = local // DH
    tile = local
    return pl.pallas_call(
        pack_kernel,
        grid=(width // tile,),
        in_specs=[pl.BlockSpec((3, tile, local), lambda n: (0, n, 0))],
        out_specs=[
            pl.BlockSpec((heads, tile, 3 * DH), lambda n: (0, n, 0)),
            pl.BlockSpec((heads, 3 * DH, tile), lambda n: (0, 0, n)),
            pl.BlockSpec(TOKEN.shape, lambda n: (0, 0)),
        ],
        out_shape=[
            jax.ShapeDtypeStruct((heads, width, 3 * DH), BF),
            jax.ShapeDtypeStruct((heads, 3 * DH, width), BF),
            TOKEN,
        ],
        compiler_params=params(),
        cost_estimate=COST,
        name="pack_weights",
    )(w_qkv)


def product_kernel(head_ref, x_ref, w_ref, *rest, contract):
    del head_ref
    out_ref, token_ref = rest[-2:]
    token_ref[...] = jnp.zeros_like(token_ref)
    value = dot(x_ref[...], w_ref[0], contract).astype(BF)
    out_ref[:, : value.shape[1]] = value
    if value.shape[1] < out_ref.shape[1]:
        out_ref[:, value.shape[1] :] = jnp.zeros_like(out_ref[:, value.shape[1] :])


def head_product(head, x, weight, contract, name, *deps):
    columns = weight.shape[2] if contract == NN else weight.shape[1]
    columns += -columns % 128
    rows, width = x.shape
    return pl.pallas_call(
        functools.partial(product_kernel, contract=contract),
        grid_spec=pltpu.PrefetchScalarGridSpec(
            num_scalar_prefetch=1,
            grid=(1,),
            in_specs=[
                pl.BlockSpec((rows, width), lambda i, head: (0, 0)),
                pl.BlockSpec((1,) + weight.shape[1:], lambda i, head: (head[0], 0, 0)),
            ]
            + spare(deps),
            out_specs=[
                pl.BlockSpec((rows, columns), lambda i, head: (0, 0)),
                pl.BlockSpec(TOKEN.shape, lambda i, head: (0, 0)),
            ],
        ),
        out_shape=[jax.ShapeDtypeStruct((rows, columns), BF), TOKEN],
        compiler_params=params(),
        cost_estimate=COST,
        name=name,
    )(head, x, weight, *deps)


def attention_kernel(qa_ref, qb_ref, da_ref, db_ref, *rest, block):
    oa_ref, ob_ref, k_all, v_all, dk_acc, dv_acc = rest[-6:]
    scale = DH ** (-0.5)
    half = qa_ref.shape[0]
    for place, ref in enumerate((qa_ref, qb_ref)):
        rows = pl.ds(place * half, half)
        k_all[rows, :] = ref[:, DH : 2 * DH]
        v_all[rows, :] = ref[:, 2 * DH : 3 * DH]
    k = k_all[...]
    v = v_all[...]
    for place, (q_ref, d_ref, out_ref) in enumerate(
        ((qa_ref, da_ref, oa_ref), (qb_ref, db_ref, ob_ref))
    ):
        for start in range(0, half, block):
            rows = pl.ds(start, block)
            q = q_ref[rows, 0:DH]
            d_o = d_ref[rows, 0:DH]
            s = dot(q, k, NT) * scale
            e = jnp.exp(s - jnp.max(s, axis=-1, keepdims=True))
            p = e * (1.0 / jnp.sum(e, axis=-1, keepdims=True))
            p_b = p.astype(BF)
            o = dot(p_b, v, NN)
            delta = jnp.sum(d_o.astype(F32) * o, axis=-1, keepdims=True)
            d_p = dot(d_o, v, NT)
            ds = (p * (d_p - delta)).astype(BF)
            dq = scale * dot(ds, k, NN)
            dk = dot(ds, q, TN)
            dv = dot(p_b, d_o, TN)
            if place == 0 and start == 0:
                dk_acc[...] = dk
                dv_acc[...] = dv
            else:
                dk_acc[...] += dk
                dv_acc[...] += dv
            out_ref[rows, 0:DH] = dq.astype(BF)
            out_ref[rows, 3 * DH : 4 * DH] = o.astype(BF)
    for place, out_ref in enumerate((oa_ref, ob_ref)):
        rows = pl.ds(place * half, half)
        out_ref[:, DH : 2 * DH] = (scale * dk_acc[rows, :]).astype(BF)
        out_ref[:, 2 * DH : 3 * DH] = dv_acc[rows, :].astype(BF)


def attention(qkv_a, qkv_b, d_a, d_b, *deps):
    half = qkv_a.shape[0]
    shape = jax.ShapeDtypeStruct((half, 4 * DH), BF)
    return pl.pallas_call(
        functools.partial(attention_kernel, block=min(256, half)),
        in_specs=[pl.BlockSpec(memory_space=pltpu.VMEM)] * 4 + spare(deps),
        out_shape=[shape, shape],
        scratch_shapes=[
            pltpu.VMEM((2 * half, DH), BF),
            pltpu.VMEM((2 * half, DH), BF),
            pltpu.VMEM((2 * half, DH), F32),
            pltpu.VMEM((2 * half, DH), F32),
        ],
        compiler_params=params(),
        cost_estimate=COST,
        name="attention",
    )(qkv_a, qkv_b, d_a, d_b, *deps)


def term_kernel(head_ref, a_ref, b_ref, w_ref, *rest, first, last):
    head = head_ref[0]
    total = dot(a_ref[:, first:last], w_ref[head], NN)
    total += dot(b_ref[:, first:last], w_ref[1 - head], NN)
    rest[-1][...] = total.astype(BF)


def pair_term(head, mine, got, weight, first, last, name, *deps):
    half, full = mine.shape
    heads, depth, width = weight.shape
    tile = 512 if width % 512 == 0 else width
    return pl.pallas_call(
        functools.partial(term_kernel, first=first, last=last),
        grid_spec=pltpu.PrefetchScalarGridSpec(
            num_scalar_prefetch=1,
            grid=(width // tile,),
            in_specs=[
                pl.BlockSpec((half, full), lambda n, at: (0, 0)),
                pl.BlockSpec((half, full), lambda n, at: (0, 0)),
                pl.BlockSpec((heads, depth, tile), lambda n, at: (0, 0, n)),
            ]
            + spare(deps),
            out_specs=pl.BlockSpec((half, tile), lambda n, at: (0, n)),
        ),
        out_shape=jax.ShapeDtypeStruct((half, width), BF),
        compiler_params=params(),
        cost_estimate=COST,
        name=name,
    )(head, mine, got, weight, *deps)


def weight_kernel(at_ref, xa_ref, xb_ref, ga_ref, gb_ref, ra_ref, rb_ref, *rest):
    del at_ref
    out_refs, turned = rest[:-1], rest[-1]
    step = pl.program_id(0)
    half = ra_ref.shape[0]
    split = 3 * DH

    @pl.when(step == 0)
    def _():
        turned[:, :half] = ra_ref[...].T
        turned[:, half:] = rb_ref[...].T

    a, b = slice(0, half), slice(half, 2 * half)
    qkv = dot(turned[:split, a], xa_ref[...], NN) + dot(turned[:split, b], xb_ref[...], NN)
    out = dot(turned[split:, a], ga_ref[...], NN) + dot(turned[split:, b], gb_ref[...], NN)
    for slot, out_ref in enumerate(out_refs):

        @pl.when(step == slot)
        def _():
            out_ref[:split, :] = qkv.astype(BF)
            out_ref[split:, :] = out.astype(BF)


def weight_gradients(at, xa, xb, ga, gb, ra, rb, seqs):
    half, width = xa.shape
    chunk = width // seqs
    full = ra.shape[1]
    column = pl.BlockSpec((half, chunk), lambda r, at: (0, r ^ at[0]))
    rest = pl.BlockSpec((half, full), lambda r, at: (0, 0))
    return pl.pallas_call(
        weight_kernel,
        grid_spec=pltpu.PrefetchScalarGridSpec(
            num_scalar_prefetch=1,
            grid=(seqs,),
            in_specs=[column] * 4 + [rest] * 2,
            out_specs=[pl.BlockSpec((full, chunk), lambda r, at: (0, 0))] * seqs,
            scratch_shapes=[pltpu.VMEM((full, 2 * half), BF)],
        ),
        out_shape=[jax.ShapeDtypeStruct((full, chunk), BF)] * seqs,
        compiler_params=params(STREAMING_LIMIT),
        cost_estimate=COST,
        name="weight_gradients",
    )(at, xa, xb, ga, gb, ra, rb)


def weight_sum_kernel(*refs, count):
    part_refs, out_refs = refs[:count], refs[-2:]
    split = 3 * DH
    total = part_refs[0][...].astype(F32)
    for ref in part_refs[1:]:
        total = total + ref[...].astype(F32)
    turned = total[:split].T.astype(BF)
    quarter = DH // 2
    for part, out_ref in enumerate(out_refs):
        out_ref[:, :split] = turned[part * DH : (part + 1) * DH]
        first = split + part * quarter
        piece = total[first : first + quarter].astype(BF)
        out_ref[:quarter, split:] = piece[:, :DH]
        out_ref[quarter:, split:] = piece[:, DH:]


def weight_sum(parts, *deps):
    full, chunk = parts[0].shape
    return pl.pallas_call(
        functools.partial(weight_sum_kernel, count=len(parts)),
        in_specs=[pl.BlockSpec(memory_space=pltpu.VMEM)] * len(parts) + spare(deps),
        out_shape=[jax.ShapeDtypeStruct((chunk // 2, full), BF)] * 2,
        compiler_params=params(),
        cost_estimate=COST,
        name="weight_sum",
    )(*parts, *deps)


def unpack_kernel(at_ref, *refs):
    qkv_ref, out_ref, token_ref = refs[-3:]
    step = pl.program_id(0)
    split = 3 * DH
    quarter = DH // 2
    token_ref[...] = jnp.zeros_like(token_ref)
    for half in range(2):

        @pl.when(step // 2 == half)
        def _():
            mine = refs[half][...].astype(F32)
            other = refs[2 + half][...].astype(F32)
            swapped = at_ref[1] != 0
            low = jnp.where(swapped, other, mine)
            high = jnp.where(swapped, mine, other)
            for i in range(3):
                columns = slice(i * DH, (i + 1) * DH)
                qkv_ref[i] = jnp.concatenate([low[:, columns], high[:, columns]], axis=1)
            for head, value in enumerate((low, high)):
                folded = [value[:quarter, split:], value[quarter:, split:]]
                out_ref[head, 0] = jnp.concatenate(folded, axis=1)


def unpack_weights(at, mine, other, far, before=()):
    rows, full = mine[0].shape
    half = rows // 2
    width = 4 * rows

    def chunk(t, at):
        if far:
            return at[0] ^ jnp.where(t < 2, t + 2, 2 * t - 3)
        return at[0] ^ jnp.where(t < 2, t, 2 * t - 4)

    specs = [
        pl.BlockSpec((half, full), lambda t, at: (jnp.minimum(t, 1), 0)),
        pl.BlockSpec((half, full), lambda t, at: (jnp.maximum(t - 2, 0), 0)),
    ]
    return pl.pallas_call(
        unpack_kernel,
        grid_spec=pltpu.PrefetchScalarGridSpec(
            num_scalar_prefetch=1,
            grid=(4,),
            in_specs=specs * 2 + spare(before),
            out_specs=[
                pl.BlockSpec((3, half, 2 * DH), lambda t, at: (0, 2 * chunk(t, at) + t // 2, 0)),
                pl.BlockSpec(
                    (2, 1, DH // 2, rows), lambda t, at: (0, t // 2, 0, chunk(t, at))
                ),
                pl.BlockSpec(TOKEN.shape, lambda t, at: (0, 0)),
            ],
        ),
        out_shape=[
            jax.ShapeDtypeStruct((3, width, 2 * DH), F32),
            jax.ShapeDtypeStruct((2, 2, DH // 2, width), F32),
            TOKEN,
        ],
        input_output_aliases={5 + i: i for i in range(len(before))},
        compiler_params=params(),
        cost_estimate=COST,
        name="weight_outputs_far" if far else "weight_outputs_near",
    )(at, *mine, *other, *before)


def neighbour_edges(first, last):
    axes = ("seq", "head")
    count = lax.axis_size(axes)
    forward = [(i, i + 1) for i in range(count - 1)]
    backward = [(target, source) for source, target in forward]
    return lax.ppermute(last, axes, forward), lax.ppermute(first, axes, backward)


def after(value, *others):
    return lax.optimization_barrier((value,) + others)[0]


def trade_chip(x, bit, heads):
    count = lax.axis_size("seq")
    return lax.ppermute(x, "seq", [(s, s ^ (bit * heads)) for s in range(count)])


def swap_heads(x):
    count = lax.axis_size("seq")
    return lax.ppermute(x, "seq", [(s, s + 1 - 2 * (s % 2)) for s in range(count)])


def unit_body(enc_in, conv_weight, norm_gain, w_qkv, w_out, grad_out):
    rows = enc_in.shape[0] // 2
    seqs = enc_in.shape[1]
    width = conv_weight.shape[2]
    local = w_qkv.shape[2]
    heads = local // DH
    groups = lax.axis_size("head")
    half = groups * seqs * rows
    place = lax.axis_index("seq")
    own_seq = (place // heads).astype(jnp.int32)
    own_head = (place % heads).astype(jnp.int32)
    at = jnp.stack([own_seq, own_head])
    head_mine = own_head.reshape(1)
    head_other = (1 - own_head).reshape(1)

    def to_chips(slots):
        return [x if j == 0 else trade_chip(x, j, heads) for j, x in enumerate(slots)]

    order = (0, 2, 1, 3)

    grad_z = lax.all_gather(grad_out, "head", axis=0, tiled=False)

    pairs = jnp.transpose(enc_in.reshape(rows, 2, seqs, enc_in.shape[2]), (1, 2, 0, 3))
    low, high = neighbour_edges(pairs[:, :, :1, :], pairs[:, :, -1:, :])
    skip, slope, normed = encoder(at, pairs, low, high, conv_weight, norm_gain)
    normed = to_chips(normed)
    normed_slab = jnp.concatenate([normed[j] for j in order], axis=0)
    normed_rows = lax.all_gather(normed_slab, "head", axis=0, tiled=True)

    grad_z = after(grad_z, normed_slab)
    grad_slots = to_chips(
        [lax.dynamic_index_in_dim(grad_z, own_seq ^ j, 2, keepdims=False) for j in range(seqs)]
    )
    grad_rows = jnp.stack([grad_slots[j] for j in order], axis=1).reshape(half, width)
    w_pack, w_turned, packed = pack_weights(after(w_qkv, normed_slab))
    w_rows = w_out.reshape(heads, DH, width)
    d_other, one = head_product(head_other, grad_rows, w_rows, NT, "d_o_other")
    d_got = swap_heads(d_other)
    d_mine, two = head_product(head_mine, grad_rows, w_rows, NT, "d_o_own")
    grad_swapped = swap_heads(grad_rows)
    normed_rows, d_got, d_mine, grad_swapped, w_pack, w_turned, *tokens = (
        lax.optimization_barrier(
            (normed_rows, d_got, d_mine, grad_swapped, w_pack, w_turned, packed, one, two)
        )
    )

    normed_swapped = swap_heads(normed_rows)
    qkv_other, _ = head_product(head_other, normed_rows, w_pack, NN, "qkv_other", *tokens)
    qkv_got = swap_heads(qkv_other)
    qkv_mine, _ = head_product(head_mine, normed_rows, w_pack, NN, "qkv_own")
    result_mine, result_other = attention(qkv_mine, qkv_got, d_mine, d_got, normed_swapped)
    result_got = swap_heads(result_other)

    shape = (groups, seqs, rows, width)
    d_term = pair_term(head_mine, result_mine, result_got, w_turned, 0, 3 * DH, "d_term")
    d_normed = lax.psum_scatter(d_term.reshape(shape), "head", scatter_dimension=0, tiled=False)
    part = weight_gradients(
        own_seq.reshape(1),
        normed_rows,
        normed_swapped,
        grad_rows,
        grad_swapped,
        result_mine,
        result_other,
        seqs,
    )
    part = to_chips(part)
    head_term = pair_term(
        head_mine, result_mine, result_got, w_rows, 3 * DH, 4 * DH, "head_term"
    )
    head_sum = lax.psum_scatter(head_term.reshape(shape), "head", scatter_dimension=0, tiled=False)

    leaving = d_normed[2:]
    near = trade_chip(leaving, 1, heads)
    far = trade_chip(jnp.stack([d_normed[1], near[1]]), 2, heads)
    grad = jnp.transpose(after(grad_out, d_term), (1, 0, 2))
    half_a, half_b = weight_sum(part, leaving)
    d_conv, first, last = conv_gradient(
        at, d_normed, near, far, skip, grad, norm_gain, slope, half_a
    )
    low, high = neighbour_edges(first, last)
    low, high, at_hand = lax.optimization_barrier((low, high, marker(conv_weight, first)))

    got_a = trade_chip(half_a, 1, heads)
    got_b = trade_chip(half_b, 2, heads)
    near_a = jnp.concatenate([half_a, after(got_a, low, high)], axis=0)
    near_b = jnp.concatenate([half_b, after(got_b, low, high)], axis=0)
    far_a = trade_chip(near_a, 2, heads)
    far_b = trade_chip(near_b, 1, heads)
    near_other = [swap_heads(near_a), swap_heads(near_b)]
    *outputs, token = unpack_weights(at, [near_a, near_b], near_other, False)
    grad_input = conv_back(d_conv, low, high, conv_weight, token, at_hand)

    head_sum = after(head_sum, grad_input)
    head_sum = [head_sum[order.index(j)] for j in range(seqs)]
    far_other = [swap_heads(after(x, *head_sum)) for x in (far_a, far_b)]
    grad_w_qkv, grad_w_out, _ = unpack_weights(at, [far_a, far_b], far_other, True, outputs)
    head_sum = to_chips(head_sum)
    mixed = mixed_call(at, head_sum, skip)
    grad_input = jnp.transpose(grad_input.reshape(2, seqs, rows, -1), (2, 0, 1, 3))
    return (
        jnp.transpose(mixed, (1, 0, 2)),
        grad_input.reshape(enc_in.shape),
        grad_w_qkv,
        grad_w_out.reshape(local, width),
    )


def padded_2(block, sides, width):
    for axis, dim in sides:
        count = lax.axis_size(axis)
        forward = [(i, i + 1) for i in range(count - 1)]
        backward = [(target, source) for source, target in forward]
        low = lax.ppermute(
            lax.slice_in_dim(block, block.shape[dim] - width, None, axis=dim), axis, forward
        )
        high = lax.ppermute(lax.slice_in_dim(block, 0, width, axis=dim), axis, backward)
        block = jnp.concatenate([low, block, high], axis=dim)
    return block


def gathered_body(enc_in, conv_weight, norm_gain, w_qkv, w_out, grad_out):
    fine_rows = enc_in.shape[0]
    slab_rows = fine_rows // 2
    seq_count = enc_in.shape[1]
    out_width = conv_weight.shape[2]
    local_width = w_qkv.shape[2]
    local_heads = local_width // DH
    logit_scale = DH ** (-0.5)
    padded = padded_2(enc_in, ((("seq", "head"), 0),), 2)
    convolved = jnp.zeros((fine_rows, seq_count, out_width), jnp.float32)
    for offset in range(KW):
        convolved = convolved + jnp.einsum(
            "tbi,io->tbo",
            padded[offset : offset + fine_rows],
            conv_weight[offset],
            preferred_element_type=jnp.float32,
        )
    activated, gelu_pull = jax.vjp(jax.nn.gelu, convolved)
    skip = jnp.mean(activated.reshape(slab_rows, 2, seq_count, out_width), axis=1).astype(
        jnp.bfloat16
    )
    skip_wide = skip.astype(jnp.float32)
    inv_rms = lax.rsqrt(jnp.mean(skip_wide * skip_wide, axis=-1, keepdims=True) + 1e-06)
    normed = (skip_wide * inv_rms * norm_gain).astype(jnp.bfloat16)
    normed_rows = lax.all_gather(normed, "head", axis=0, tiled=True)
    grad_rows = lax.all_gather(grad_out, "head", axis=0, tiled=True)
    tower_rows = normed_rows.shape[0]
    qkv = jnp.einsum(
        "tbc,ice->itbe", normed_rows, w_qkv, preferred_element_type=jnp.float32
    ).astype(jnp.bfloat16)
    qkv = qkv.reshape(3, tower_rows, seq_count, local_heads, DH)
    query_matrix, key_matrix, value_matrix = (qkv[0], qkv[1], qkv[2])
    key_all, value_all = (
        lax.all_gather(key_matrix, "seq", axis=0, tiled=True),
        lax.all_gather(value_matrix, "seq", axis=0, tiled=True),
    )
    attention_logits = (
        jnp.einsum("qbhd,kbhd->bhqk", query_matrix, key_all, preferred_element_type=jnp.float32)
        * logit_scale
    )
    row_peak = jnp.max(attention_logits, axis=-1, keepdims=True)
    exponent = jnp.exp(attention_logits - row_peak)
    row_total = jnp.sum(exponent, axis=-1, keepdims=True)
    soft_weights = exponent / row_total
    narrow_probabilities = soft_weights.astype(jnp.bfloat16)
    attention_output = jnp.einsum(
        "bhqk,kbhd->qbhd", narrow_probabilities, value_all, preferred_element_type=jnp.float32
    )
    o_narrow = attention_output.reshape(tower_rows, seq_count, local_width).astype(jnp.bfloat16)
    piece = o_narrow
    head_sum = lax.psum_scatter(
        jnp.einsum("tbe,ec->tbc", piece, w_out, preferred_element_type=jnp.float32).astype(
            jnp.bfloat16
        ),
        "head",
        scatter_dimension=0,
        tiled=True,
    ).astype(jnp.float32)
    mixed = (skip_wide + head_sum).astype(jnp.bfloat16)
    part_w_out = jnp.einsum("tbe,tbc->ec", o_narrow, grad_rows, preferred_element_type=jnp.float32)
    d_out = jnp.einsum("tbc,ec->tbe", grad_rows, w_out, preferred_element_type=jnp.float32).astype(
        jnp.bfloat16
    )
    d_out = d_out.reshape(tower_rows, seq_count, local_heads, DH)
    delta = jnp.sum(d_out.astype(jnp.float32) * attention_output, axis=-1)
    probability_gradient = jnp.einsum(
        "qbhd,kbhd->bhqk", d_out, value_all, preferred_element_type=jnp.float32
    )
    d_scores = soft_weights * (probability_gradient - jnp.transpose(delta, (1, 2, 0))[..., None])
    narrow_gradient = d_scores.astype(jnp.bfloat16)
    query_gradient = logit_scale * jnp.einsum(
        "bhqk,kbhd->qbhd", narrow_gradient, key_all, preferred_element_type=jnp.float32
    )
    key_terms = logit_scale * jnp.einsum(
        "bhqk,qbhd->kbhd", narrow_gradient, query_matrix, preferred_element_type=jnp.float32
    )
    value_terms = jnp.einsum(
        "bhqk,qbhd->kbhd", narrow_probabilities, d_out, preferred_element_type=jnp.float32
    )
    d_keys, d_values = (
        lax.psum_scatter(
            key_terms.astype(jnp.bfloat16), "seq", scatter_dimension=0, tiled=True
        ).astype(jnp.float32),
        lax.psum_scatter(
            value_terms.astype(jnp.bfloat16), "seq", scatter_dimension=0, tiled=True
        ).astype(jnp.float32),
    )
    dqkv = (
        jnp.stack([query_gradient, d_keys, d_values])
        .reshape(3, tower_rows, seq_count, local_width)
        .astype(jnp.bfloat16)
    )
    part_w_qkv = jnp.einsum("tbc,itbe->ice", normed_rows, dqkv, preferred_element_type=jnp.float32)
    piece = dqkv
    d_normed = lax.psum_scatter(
        jnp.einsum("itbe,ice->tbc", piece, w_qkv, preferred_element_type=jnp.float32).astype(
            jnp.bfloat16
        ),
        "head",
        scatter_dimension=0,
        tiled=True,
    ).astype(jnp.float32)
    unit_rows = skip_wide * inv_rms
    scaled = d_normed * norm_gain
    d_skip = grad_out.astype(jnp.float32) + inv_rms * (
        scaled - unit_rows * jnp.mean(scaled * unit_rows, axis=-1, keepdims=True)
    )
    d_act = jnp.repeat(d_skip, 2, axis=0) * 0.5
    d_conv = gelu_pull(d_act)[0].astype(jnp.bfloat16)
    d_pad = padded_2(d_conv, ((("seq", "head"), 0),), 2)
    grad_input = jnp.zeros((fine_rows, seq_count, enc_in.shape[2]), jnp.float32)
    for offset in range(KW):
        grad_input = grad_input + jnp.einsum(
            "tbo,io->tbi",
            d_pad[4 - offset : 4 - offset + fine_rows],
            conv_weight[offset],
            preferred_element_type=jnp.float32,
        )
    grad_w_qkv, grad_w_out = (
        lax.psum(part_w_qkv.astype(jnp.bfloat16), "seq").astype(jnp.float32),
        lax.psum(part_w_out.astype(jnp.bfloat16), "seq").astype(jnp.float32),
    )
    return (mixed, grad_input.astype(jnp.bfloat16), grad_w_qkv, grad_w_out)


def body(enc_in, conv_weight, norm_gain, w_qkv, w_out, grad_out):
    heads = w_qkv.shape[2] // DH
    seqs = enc_in.shape[1]
    fits = heads == 2 and seqs == 4 and seqs * heads == lax.axis_size("seq")
    fits = fits and conv_weight.shape[2] == seqs * w_qkv.shape[2]
    chosen = unit_body if fits else gathered_body
    return chosen(enc_in, conv_weight, norm_gain, w_qkv, w_out, grad_out)


def solution(mesh):
    return jax.shard_map(
        body,
        mesh=mesh,
        in_specs=(
            P(("seq", "head"), None, None),
            P(),
            P(),
            P(None, None, "head"),
            P("head", None),
            P(("seq", "head"), None, None),
        ),
        out_specs=(
            P(("seq", "head"), None, None),
            P(("seq", "head"), None, None),
            P(None, None, "head"),
            P("head", None),
        ),
        check_vma=False,
    )
```

```python
import functools

import jax
import jax.numpy as jnp
from jax import lax
from jax.experimental import pallas as pl
from jax.experimental.pallas import tpu as pltpu
from jax.sharding import PartitionSpec as P

DH = 192
KW = 5
VMEM_LIMIT = 24 * 1024 * 1024
SMALL_LIMIT = 16 * 1024 * 1024
STREAMING_LIMIT = 56 * 1024 * 1024
COST = pl.CostEstimate(flops=1000, bytes_accessed=1000, transcendentals=0)
BF = jnp.bfloat16
F32 = jnp.float32
TOKEN = jax.ShapeDtypeStruct((8, 128), F32)


def params(limit=VMEM_LIMIT):
    return pltpu.CompilerParams(vmem_limit_bytes=limit)


def dot(a, b, contract):
    return lax.dot_general(a, b, (contract, ((), ())), preferred_element_type=F32)


NN = ((1,), (0,))
NT = ((1,), (1,))
TN = ((0,), (0,))


def whole(shape):
    return pl.BlockSpec(shape, lambda *_: (0,) * len(shape))


SCALARS = pl.BlockSpec(memory_space=pltpu.SMEM)


def spare(deps):
    return [pl.BlockSpec(memory_space=pl.ANY)] * len(deps)


def turned_rows(ref, low_ref, high_ref, parity, shift):
    seqs, rows, width = ref.shape[1:]
    own = ref[parity]
    if shift != 1:
        wide = own.astype(F32)
        if shift == 0:
            parts = [low_ref[parity].astype(F32), wide[:, : rows - 1]]
        else:
            parts = [wide[:, 1:], high_ref[parity].astype(F32)]
        own = jnp.concatenate(parts, axis=1).astype(BF)
    return own.reshape(seqs * rows, width)


def conv_kernel(
    at_ref, x_ref, low_ref, high_ref, w_ref, gain_ref, skip_ref, slope_ref, *rest
):
    normed_refs, (lhs, squares, whole_normed) = rest[:-3], rest[-3:]
    step = pl.program_id(0)
    seqs, rows, c_in = x_ref.shape[1:]
    half = seqs * rows
    tile = w_ref.shape[2]

    @pl.when(step == 0)
    def _():
        for parity in range(2):
            for shift in range(3):
                value = turned_rows(x_ref, low_ref, high_ref, parity, shift)
                for out in range(2):
                    tap = 2 * shift + parity - out
                    if 0 <= tap < KW:
                        lhs[out * half : (out + 1) * half, tap * c_in : (tap + 1) * c_in] = value
        squares[...] = jnp.zeros_like(squares)

    conv = dot(lhs[...], w_ref[...].reshape(KW * c_in, tile), NN)
    root = 0.7978845608028654
    total = None
    for parity in range(2):
        x = conv[parity * half : (parity + 1) * half, :]
        square = x * x
        t = jnp.tanh(root * (x + 0.044715 * (square * x)))
        left = 0.5 * (1.0 + t)
        act = x * left
        slope = left + (0.5 * root) * x * (1.0 - t * t) * (1.0 + (3 * 0.044715) * square)
        slope_ref[parity] = slope.reshape(slope_ref.shape[1:])
        total = act if total is None else total + act
    skip = (0.5 * total).astype(BF)
    columns = pl.ds(pl.multiple_of(step * tile, tile), tile)
    skip_ref[:, :, columns] = skip.reshape(seqs, rows, tile)
    wide = skip.astype(F32)
    squares[...] += jnp.sum(wide * wide, axis=-1, keepdims=True)

    @pl.when(step == pl.num_programs(0) - 1)
    def _():
        width = skip_ref.shape[2]
        inv = lax.rsqrt(squares[...] * (1.0 / width) + 1e-06)
        wide = skip_ref[...].reshape(half, width).astype(F32)
        normed = (wide * inv * gain_ref[...]).astype(BF)
        whole_normed[...] = normed.reshape(whole_normed.shape)
        for slot in range(seqs):
            normed_refs[slot][...] = whole_normed[at_ref[0] ^ slot]


def encoder(at, pairs, low, high, conv_weight, norm_gain):
    _, seqs, rows, c_in = pairs.shape
    width = conv_weight.shape[2]
    tile = 256 if width % 256 == 0 else width
    shape = (seqs, rows, width)
    outs = pl.pallas_call(
        conv_kernel,
        grid=(width // tile,),
        in_specs=[
            SCALARS,
            whole(pairs.shape),
            whole(low.shape),
            whole(high.shape),
            pl.BlockSpec((KW, c_in, tile), lambda n: (0, 0, n)),
            whole((1, width)),
        ],
        out_specs=[
            whole(shape),
            pl.BlockSpec((2, seqs, rows, tile), lambda n: (0, 0, 0, n)),
        ]
        + [whole((rows, width))] * seqs,
        out_shape=[
            jax.ShapeDtypeStruct(shape, BF),
            jax.ShapeDtypeStruct((2,) + shape, F32),
        ]
        + [jax.ShapeDtypeStruct((rows, width), BF)] * seqs,
        scratch_shapes=[
            pltpu.VMEM((2 * seqs * rows, KW * c_in), BF),
            pltpu.VMEM((seqs * rows, 1), F32),
            pltpu.VMEM(shape, BF),
        ],
        compiler_params=params(STREAMING_LIMIT),
        cost_estimate=COST,
        name="encoder_forward",
    )(at, pairs, low, high, conv_weight, norm_gain.reshape(1, width))
    return outs[0], outs[1], list(outs[2:])


def d_conv_kernel(at_ref, own_ref, near_ref, far_ref, *refs):
    skip_ref, grad_ref, gain_ref, slope_ref = refs[:4]
    out_ref, first_ref, last_ref = refs[-3:]
    rows = out_ref.shape[2]
    for slot, (ref, place) in enumerate(((own_ref, 0), (near_ref, 0), (far_ref, 0), (far_ref, 1))):
        b = at_ref[0] ^ slot
        wide = skip_ref[b].astype(F32)
        inv = lax.rsqrt(jnp.mean(wide * wide, axis=-1, keepdims=True) + 1e-06)
        unit = wide * inv
        scaled = ref[place].astype(F32) * gain_ref[...]
        d_skip = grad_ref[b].astype(F32) + inv * (
            scaled - unit * jnp.mean(scaled * unit, axis=-1, keepdims=True)
        )
        d_act = 0.5 * d_skip
        for parity in range(2):
            value = slope_ref[parity, b] * d_act
            out_ref[parity, b] = value.astype(BF)
            first_ref[parity, b] = value[:1].astype(BF)
            last_ref[parity, b] = value[rows - 1 :].astype(BF)


def conv_gradient(at, own, near, far, skip, grad, norm_gain, slope, *deps):
    vmem = pl.BlockSpec(memory_space=pltpu.VMEM)
    edge = jax.ShapeDtypeStruct(slope.shape[:2] + (1, slope.shape[3]), BF)
    return pl.pallas_call(
        d_conv_kernel,
        in_specs=[SCALARS] + [vmem] * 7 + spare(deps),
        out_specs=[vmem] * 3,
        out_shape=[jax.ShapeDtypeStruct(slope.shape, BF)] + [edge] * 2,
        compiler_params=params(SMALL_LIMIT),
        cost_estimate=COST,
        name="conv_gradient",
    )(at, own, near, far, skip, grad, norm_gain.reshape(1, -1), slope, *deps)


def mixed_body(seqs, at_ref, *refs):
    skip_ref, out_ref = refs[seqs], refs[-1]
    for slot in range(seqs):
        b = at_ref[0] ^ slot
        out_ref[b] = (skip_ref[b].astype(F32) + refs[slot][...].astype(F32)).astype(BF)


def mixed_call(at, terms, skip, *deps):
    seqs = len(terms)
    vmem = pl.BlockSpec(memory_space=pltpu.VMEM)
    return pl.pallas_call(
        functools.partial(mixed_body, seqs),
        in_specs=[SCALARS] + [vmem] * (seqs + 1) + spare(deps),
        out_specs=vmem,
        out_shape=jax.ShapeDtypeStruct(skip.shape, BF),
        compiler_params=params(SMALL_LIMIT),
        cost_estimate=COST,
        name="mixed_sum",
    )(at, *terms, skip, *deps)


def marker_kernel(*refs):
    refs[-1][...] = jnp.zeros_like(refs[-1])


def marker(*deps):
    return pl.pallas_call(
        marker_kernel,
        in_specs=spare(deps),
        out_shape=TOKEN,
        compiler_params=params(SMALL_LIMIT),
        cost_estimate=COST,
        name="marker",
    )(*deps)


def conv_back_kernel(d_ref, low_ref, high_ref, w_ref, *rest):
    out_ref, turned, acc = rest[-3:]
    step = pl.program_id(0)

    @pl.when(step == 0)
    def _():
        for parity in range(2):
            for shift in range(3):
                turned[parity, shift] = turned_rows(d_ref, low_ref, high_ref, parity, shift).T

    for tap in range(KW):

        @pl.when(step == tap)
        def _():
            places = [KW - 1 - tap, KW - tap]
            rhs = jnp.concatenate([turned[p % 2, p // 2] for p in places], axis=1)
            term = dot(w_ref[0], rhs, NN)
            if tap == 0:
                acc[...] = term
            elif tap < KW - 1:
                acc[...] += term
            else:
                out_ref[...] = (acc[...] + term).T.astype(BF)


def conv_back(d_conv, low, high, conv_weight, *deps):
    _, seqs, rows, width = d_conv.shape
    c_in = conv_weight.shape[1]
    flat = 2 * seqs * rows
    return pl.pallas_call(
        conv_back_kernel,
        grid=(KW,),
        in_specs=[
            whole(d_conv.shape),
            whole(low.shape),
            whole(high.shape),
            pl.BlockSpec((1, c_in, width), lambda k: (k, 0, 0)),
        ]
        + spare(deps),
        out_specs=whole((flat, c_in)),
        out_shape=jax.ShapeDtypeStruct((flat, c_in), BF),
        scratch_shapes=[
            pltpu.VMEM((2, 3, width, seqs * rows), BF),
            pltpu.VMEM((c_in, flat), F32),
        ],
        compiler_params=params(),
        cost_estimate=COST,
        name="encoder_backward",
    )(d_conv, low, high, conv_weight, *deps)


def pack_kernel(w_ref, pack_ref, turned_ref, token_ref):
    token_ref[...] = jnp.zeros_like(token_ref)
    for i in range(3):
        for head in range(pack_ref.shape[0]):
            part = w_ref[i, :, head * DH : (head + 1) * DH]
            columns = slice(i * DH, (i + 1) * DH)
            pack_ref[head, :, columns] = part
            turned_ref[head, columns, :] = part.T


def pack_weights(w_qkv):
    _, width, local = w_qkv.shape
    heads = local // DH
    tile = local
    return pl.pallas_call(
        pack_kernel,
        grid=(width // tile,),
        in_specs=[pl.BlockSpec((3, tile, local), lambda n: (0, n, 0))],
        out_specs=[
            pl.BlockSpec((heads, tile, 3 * DH), lambda n: (0, n, 0)),
            pl.BlockSpec((heads, 3 * DH, tile), lambda n: (0, 0, n)),
            pl.BlockSpec(TOKEN.shape, lambda n: (0, 0)),
        ],
        out_shape=[
            jax.ShapeDtypeStruct((heads, width, 3 * DH), BF),
            jax.ShapeDtypeStruct((heads, 3 * DH, width), BF),
            TOKEN,
        ],
        compiler_params=params(),
        cost_estimate=COST,
        name="pack_weights",
    )(w_qkv)


def product_kernel(head_ref, x_ref, w_ref, *rest, contract):
    del head_ref
    out_ref, token_ref = rest[-2:]
    token_ref[...] = jnp.zeros_like(token_ref)
    value = dot(x_ref[...], w_ref[0], contract).astype(BF)
    out_ref[:, : value.shape[1]] = value
    if value.shape[1] < out_ref.shape[1]:
        out_ref[:, value.shape[1] :] = jnp.zeros_like(out_ref[:, value.shape[1] :])


def head_product(head, x, weight, contract, name, *deps):
    columns = weight.shape[2] if contract == NN else weight.shape[1]
    columns += -columns % 128
    rows, width = x.shape
    return pl.pallas_call(
        functools.partial(product_kernel, contract=contract),
        grid_spec=pltpu.PrefetchScalarGridSpec(
            num_scalar_prefetch=1,
            grid=(1,),
            in_specs=[
                pl.BlockSpec((rows, width), lambda i, head: (0, 0)),
                pl.BlockSpec((1,) + weight.shape[1:], lambda i, head: (head[0], 0, 0)),
            ]
            + spare(deps),
            out_specs=[
                pl.BlockSpec((rows, columns), lambda i, head: (0, 0)),
                pl.BlockSpec(TOKEN.shape, lambda i, head: (0, 0)),
            ],
        ),
        out_shape=[jax.ShapeDtypeStruct((rows, columns), BF), TOKEN],
        compiler_params=params(),
        cost_estimate=COST,
        name=name,
    )(head, x, weight, *deps)


def attention_kernel(qa_ref, qb_ref, da_ref, db_ref, *rest, block):
    oa_ref, ob_ref, k_all, v_all, dk_acc, dv_acc = rest[-6:]
    scale = DH ** (-0.5)
    half = qa_ref.shape[0]
    for place, ref in enumerate((qa_ref, qb_ref)):
        rows = pl.ds(place * half, half)
        k_all[rows, :] = ref[:, DH : 2 * DH]
        v_all[rows, :] = ref[:, 2 * DH : 3 * DH]
    k = k_all[...]
    v = v_all[...]
    for place, (q_ref, d_ref, out_ref) in enumerate(
        ((qa_ref, da_ref, oa_ref), (qb_ref, db_ref, ob_ref))
    ):
        for start in range(0, half, block):
            rows = pl.ds(start, block)
            q = q_ref[rows, 0:DH]
            d_o = d_ref[rows, 0:DH]
            s = dot(q, k, NT) * scale
            e = jnp.exp(s - jnp.max(s, axis=-1, keepdims=True))
            p = e * (1.0 / jnp.sum(e, axis=-1, keepdims=True))
            p_b = p.astype(BF)
            o = dot(p_b, v, NN)
            delta = jnp.sum(d_o.astype(F32) * o, axis=-1, keepdims=True)
            d_p = dot(d_o, v, NT)
            ds = (p * (d_p - delta)).astype(BF)
            dq = scale * dot(ds, k, NN)
            dk = dot(ds, q, TN)
            dv = dot(p_b, d_o, TN)
            if place == 0 and start == 0:
                dk_acc[...] = dk
                dv_acc[...] = dv
            else:
                dk_acc[...] += dk
                dv_acc[...] += dv
            out_ref[rows, 0:DH] = dq.astype(BF)
            out_ref[rows, 3 * DH : 4 * DH] = o.astype(BF)
    for place, out_ref in enumerate((oa_ref, ob_ref)):
        rows = pl.ds(place * half, half)
        out_ref[:, DH : 2 * DH] = (scale * dk_acc[rows, :]).astype(BF)
        out_ref[:, 2 * DH : 3 * DH] = dv_acc[rows, :].astype(BF)


def attention(qkv_a, qkv_b, d_a, d_b, *deps):
    half = qkv_a.shape[0]
    shape = jax.ShapeDtypeStruct((half, 4 * DH), BF)
    return pl.pallas_call(
        functools.partial(attention_kernel, block=min(256, half)),
        in_specs=[pl.BlockSpec(memory_space=pltpu.VMEM)] * 4 + spare(deps),
        out_shape=[shape, shape],
        scratch_shapes=[
            pltpu.VMEM((2 * half, DH), BF),
            pltpu.VMEM((2 * half, DH), BF),
            pltpu.VMEM((2 * half, DH), F32),
            pltpu.VMEM((2 * half, DH), F32),
        ],
        compiler_params=params(),
        cost_estimate=COST,
        name="attention",
    )(qkv_a, qkv_b, d_a, d_b, *deps)


def term_kernel(head_ref, a_ref, b_ref, w_ref, *rest, first, last):
    head = head_ref[0]
    total = dot(a_ref[:, first:last], w_ref[head], NN)
    total += dot(b_ref[:, first:last], w_ref[1 - head], NN)
    rest[-1][...] = total.astype(BF)


def pair_term(head, mine, got, weight, first, last, name, *deps):
    half, full = mine.shape
    heads, depth, width = weight.shape
    tile = 512 if width % 512 == 0 else width
    return pl.pallas_call(
        functools.partial(term_kernel, first=first, last=last),
        grid_spec=pltpu.PrefetchScalarGridSpec(
            num_scalar_prefetch=1,
            grid=(width // tile,),
            in_specs=[
                pl.BlockSpec((half, full), lambda n, at: (0, 0)),
                pl.BlockSpec((half, full), lambda n, at: (0, 0)),
                pl.BlockSpec((heads, depth, tile), lambda n, at: (0, 0, n)),
            ]
            + spare(deps),
            out_specs=pl.BlockSpec((half, tile), lambda n, at: (0, n)),
        ),
        out_shape=jax.ShapeDtypeStruct((half, width), BF),
        compiler_params=params(),
        cost_estimate=COST,
        name=name,
    )(head, mine, got, weight, *deps)


def weight_kernel(at_ref, xa_ref, xb_ref, ga_ref, gb_ref, ra_ref, rb_ref, *rest):
    del at_ref
    out_refs, turned = rest[:-1], rest[-1]
    step = pl.program_id(0)
    half = ra_ref.shape[0]
    split = 3 * DH

    @pl.when(step == 0)
    def _():
        turned[:, :half] = ra_ref[...].T
        turned[:, half:] = rb_ref[...].T

    a, b = slice(0, half), slice(half, 2 * half)
    qkv = dot(turned[:split, a], xa_ref[...], NN) + dot(turned[:split, b], xb_ref[...], NN)
    out = dot(turned[split:, a], ga_ref[...], NN) + dot(turned[split:, b], gb_ref[...], NN)
    for slot, out_ref in enumerate(out_refs):

        @pl.when(step == slot)
        def _():
            out_ref[:split, :] = qkv.astype(BF)
            out_ref[split:, :] = out.astype(BF)


def weight_gradients(at, xa, xb, ga, gb, ra, rb, seqs):
    half, width = xa.shape
    chunk = width // seqs
    full = ra.shape[1]
    column = pl.BlockSpec((half, chunk), lambda r, at: (0, r ^ at[0]))
    rest = pl.BlockSpec((half, full), lambda r, at: (0, 0))
    return pl.pallas_call(
        weight_kernel,
        grid_spec=pltpu.PrefetchScalarGridSpec(
            num_scalar_prefetch=1,
            grid=(seqs,),
            in_specs=[column] * 4 + [rest] * 2,
            out_specs=[pl.BlockSpec((full, chunk), lambda r, at: (0, 0))] * seqs,
            scratch_shapes=[pltpu.VMEM((full, 2 * half), BF)],
        ),
        out_shape=[jax.ShapeDtypeStruct((full, chunk), BF)] * seqs,
        compiler_params=params(STREAMING_LIMIT),
        cost_estimate=COST,
        name="weight_gradients",
    )(at, xa, xb, ga, gb, ra, rb)


def weight_sum_kernel(*refs, count):
    part_refs, out_refs = refs[:count], refs[-2:]
    split = 3 * DH
    total = part_refs[0][...].astype(F32)
    for ref in part_refs[1:]:
        total = total + ref[...].astype(F32)
    turned = total[:split].T.astype(BF)
    quarter = DH // 2
    for part, out_ref in enumerate(out_refs):
        out_ref[:, :split] = turned[part * DH : (part + 1) * DH]
        first = split + part * quarter
        piece = total[first : first + quarter].astype(BF)
        out_ref[:quarter, split:] = piece[:, :DH]
        out_ref[quarter:, split:] = piece[:, DH:]


def weight_sum(parts, *deps):
    full, chunk = parts[0].shape
    return pl.pallas_call(
        functools.partial(weight_sum_kernel, count=len(parts)),
        in_specs=[pl.BlockSpec(memory_space=pltpu.VMEM)] * len(parts) + spare(deps),
        out_shape=[jax.ShapeDtypeStruct((chunk // 2, full), BF)] * 2,
        compiler_params=params(SMALL_LIMIT),
        cost_estimate=COST,
        name="weight_sum",
    )(*parts, *deps)


def unpack_kernel(at_ref, *refs):
    qkv_ref, out_ref, token_ref = refs[-3:]
    step = pl.program_id(0)
    split = 3 * DH
    quarter = DH // 2
    token_ref[...] = jnp.zeros_like(token_ref)
    for half in range(2):

        @pl.when(step // 2 == half)
        def _():
            mine = refs[half][...].astype(F32)
            other = refs[2 + half][...].astype(F32)
            swapped = at_ref[1] != 0
            low = jnp.where(swapped, other, mine)
            high = jnp.where(swapped, mine, other)
            for i in range(3):
                columns = slice(i * DH, (i + 1) * DH)
                qkv_ref[i] = jnp.concatenate([low[:, columns], high[:, columns]], axis=1)
            for head, value in enumerate((low, high)):
                folded = [value[:quarter, split:], value[quarter:, split:]]
                out_ref[head, 0] = jnp.concatenate(folded, axis=1)


def unpack_weights(at, mine, other, far, before=()):
    rows, full = mine[0].shape
    half = rows // 2
    width = 4 * rows

    def chunk(t, at):
        if far:
            return at[0] ^ jnp.where(t < 2, t + 2, 2 * t - 3)
        return at[0] ^ jnp.where(t < 2, t, 2 * t - 4)

    specs = [
        pl.BlockSpec((half, full), lambda t, at: (jnp.minimum(t, 1), 0)),
        pl.BlockSpec((half, full), lambda t, at: (jnp.maximum(t - 2, 0), 0)),
    ]
    return pl.pallas_call(
        unpack_kernel,
        grid_spec=pltpu.PrefetchScalarGridSpec(
            num_scalar_prefetch=1,
            grid=(4,),
            in_specs=specs * 2 + spare(before),
            out_specs=[
                pl.BlockSpec((3, half, 2 * DH), lambda t, at: (0, 2 * chunk(t, at) + t // 2, 0)),
                pl.BlockSpec(
                    (2, 1, DH // 2, rows), lambda t, at: (0, t // 2, 0, chunk(t, at))
                ),
                pl.BlockSpec(TOKEN.shape, lambda t, at: (0, 0)),
            ],
        ),
        out_shape=[
            jax.ShapeDtypeStruct((3, width, 2 * DH), F32),
            jax.ShapeDtypeStruct((2, 2, DH // 2, width), F32),
            TOKEN,
        ],
        input_output_aliases={5 + i: i for i in range(len(before))},
        compiler_params=params(SMALL_LIMIT),
        cost_estimate=COST,
        name="weight_outputs_far" if far else "weight_outputs_near",
    )(at, *mine, *other, *before)


def neighbour_edges(first, last):
    axes = ("seq", "head")
    count = lax.axis_size(axes)
    forward = [(i, i + 1) for i in range(count - 1)]
    backward = [(target, source) for source, target in forward]
    return lax.ppermute(last, axes, forward), lax.ppermute(first, axes, backward)


def after(value, *others):
    return lax.optimization_barrier((value,) + others)[0]


def trade_chip(x, bit, heads):
    count = lax.axis_size("seq")
    return lax.ppermute(x, "seq", [(s, s ^ (bit * heads)) for s in range(count)])


def swap_heads(x):
    count = lax.axis_size("seq")
    return lax.ppermute(x, "seq", [(s, s + 1 - 2 * (s % 2)) for s in range(count)])


def unit_body(enc_in, conv_weight, norm_gain, w_qkv, w_out, grad_out):
    rows = enc_in.shape[0] // 2
    seqs = enc_in.shape[1]
    width = conv_weight.shape[2]
    local = w_qkv.shape[2]
    heads = local // DH
    groups = lax.axis_size("head")
    half = groups * seqs * rows
    place = lax.axis_index("seq")
    own_seq = (place // heads).astype(jnp.int32)
    own_head = (place % heads).astype(jnp.int32)
    at = jnp.stack([own_seq, own_head])
    head_mine = own_head.reshape(1)
    head_other = (1 - own_head).reshape(1)

    def to_chips(slots):
        return [x if j == 0 else trade_chip(x, j, heads) for j, x in enumerate(slots)]

    order = (0, 2, 1, 3)

    grad_z = lax.all_gather(grad_out, "head", axis=0, tiled=False)

    pairs = jnp.transpose(enc_in.reshape(rows, 2, seqs, enc_in.shape[2]), (1, 2, 0, 3))
    low, high = neighbour_edges(pairs[:, :, :1, :], pairs[:, :, -1:, :])
    skip, slope, normed = encoder(at, pairs, low, high, conv_weight, norm_gain)
    normed = to_chips(normed)
    normed_slab = jnp.concatenate([normed[j] for j in order], axis=0)
    normed_rows = lax.all_gather(normed_slab, "head", axis=0, tiled=True)

    grad_z = after(grad_z, normed_slab)
    grad_slots = to_chips(
        [lax.dynamic_index_in_dim(grad_z, own_seq ^ j, 2, keepdims=False) for j in range(seqs)]
    )
    grad_rows = jnp.stack([grad_slots[j] for j in order], axis=1).reshape(half, width)
    w_pack, w_turned, packed = pack_weights(after(w_qkv, normed_slab))
    w_rows = w_out.reshape(heads, DH, width)
    d_other, one = head_product(head_other, grad_rows, w_rows, NT, "d_o_other")
    d_got = swap_heads(d_other)
    d_mine, two = head_product(head_mine, grad_rows, w_rows, NT, "d_o_own")
    grad_swapped = swap_heads(grad_rows)
    normed_rows, d_got, d_mine, grad_swapped, w_pack, w_turned, *tokens = (
        lax.optimization_barrier(
            (normed_rows, d_got, d_mine, grad_swapped, w_pack, w_turned, packed, one, two)
        )
    )

    normed_swapped = swap_heads(normed_rows)
    qkv_other, _ = head_product(head_other, normed_rows, w_pack, NN, "qkv_other", *tokens)
    qkv_got = swap_heads(qkv_other)
    qkv_mine, _ = head_product(head_mine, normed_rows, w_pack, NN, "qkv_own")
    result_mine, result_other = attention(qkv_mine, qkv_got, d_mine, d_got, normed_swapped)
    result_got = swap_heads(result_other)

    shape = (groups, seqs, rows, width)
    d_term = pair_term(head_mine, result_mine, result_got, w_turned, 0, 3 * DH, "d_term")
    d_normed = lax.psum_scatter(d_term.reshape(shape), "head", scatter_dimension=0, tiled=False)
    part = weight_gradients(
        own_seq.reshape(1),
        normed_rows,
        normed_swapped,
        grad_rows,
        grad_swapped,
        result_mine,
        result_other,
        seqs,
    )
    part = to_chips(part)
    head_term = pair_term(
        head_mine, result_mine, result_got, w_rows, 3 * DH, 4 * DH, "head_term"
    )
    head_sum = lax.psum_scatter(head_term.reshape(shape), "head", scatter_dimension=0, tiled=False)

    leaving = d_normed[2:]
    near = trade_chip(leaving, 1, heads)
    far = trade_chip(jnp.stack([d_normed[1], near[1]]), 2, heads)
    grad = jnp.transpose(after(grad_out, d_term), (1, 0, 2))
    half_a, half_b = weight_sum(part, leaving)
    d_conv, first, last = conv_gradient(
        at, d_normed, near, far, skip, grad, norm_gain, slope, half_a
    )
    low, high = neighbour_edges(first, last)
    low, high, at_hand = lax.optimization_barrier((low, high, marker(conv_weight, first)))

    got_a = trade_chip(half_a, 1, heads)
    got_b = trade_chip(half_b, 2, heads)
    near_a = jnp.concatenate([half_a, after(got_a, low, high)], axis=0)
    near_b = jnp.concatenate([half_b, after(got_b, low, high)], axis=0)
    far_a = trade_chip(near_a, 2, heads)
    far_b = trade_chip(near_b, 1, heads)
    near_other = [swap_heads(near_a), swap_heads(near_b)]
    *outputs, token = unpack_weights(at, [near_a, near_b], near_other, False)
    grad_input = conv_back(d_conv, low, high, conv_weight, at_hand, *near_other)

    head_sum = after(head_sum, grad_input)
    head_sum = [head_sum[order.index(j)] for j in range(seqs)]
    far_other = [swap_heads(after(x, *head_sum)) for x in (far_a, far_b)]
    grad_w_qkv, grad_w_out, _ = unpack_weights(at, [far_a, far_b], far_other, True, outputs)
    head_sum = to_chips(head_sum)
    mixed = mixed_call(at, head_sum, skip, token)
    grad_input = jnp.transpose(grad_input.reshape(2, seqs, rows, -1), (2, 0, 1, 3))
    return (
        jnp.transpose(mixed, (1, 0, 2)),
        grad_input.reshape(enc_in.shape),
        grad_w_qkv,
        grad_w_out.reshape(local, width),
    )


def padded_2(block, sides, width):
    for axis, dim in sides:
        count = lax.axis_size(axis)
        forward = [(i, i + 1) for i in range(count - 1)]
        backward = [(target, source) for source, target in forward]
        low = lax.ppermute(
            lax.slice_in_dim(block, block.shape[dim] - width, None, axis=dim), axis, forward
        )
        high = lax.ppermute(lax.slice_in_dim(block, 0, width, axis=dim), axis, backward)
        block = jnp.concatenate([low, block, high], axis=dim)
    return block


def gathered_body(enc_in, conv_weight, norm_gain, w_qkv, w_out, grad_out):
    fine_rows = enc_in.shape[0]
    slab_rows = fine_rows // 2
    seq_count = enc_in.shape[1]
    out_width = conv_weight.shape[2]
    local_width = w_qkv.shape[2]
    local_heads = local_width // DH
    logit_scale = DH ** (-0.5)
    padded = padded_2(enc_in, ((("seq", "head"), 0),), 2)
    convolved = jnp.zeros((fine_rows, seq_count, out_width), jnp.float32)
    for offset in range(KW):
        convolved = convolved + jnp.einsum(
            "tbi,io->tbo",
            padded[offset : offset + fine_rows],
            conv_weight[offset],
            preferred_element_type=jnp.float32,
        )
    activated, gelu_pull = jax.vjp(jax.nn.gelu, convolved)
    skip = jnp.mean(activated.reshape(slab_rows, 2, seq_count, out_width), axis=1).astype(
        jnp.bfloat16
    )
    skip_wide = skip.astype(jnp.float32)
    inv_rms = lax.rsqrt(jnp.mean(skip_wide * skip_wide, axis=-1, keepdims=True) + 1e-06)
    normed = (skip_wide * inv_rms * norm_gain).astype(jnp.bfloat16)
    normed_rows = lax.all_gather(normed, "head", axis=0, tiled=True)
    grad_rows = lax.all_gather(grad_out, "head", axis=0, tiled=True)
    tower_rows = normed_rows.shape[0]
    qkv = jnp.einsum(
        "tbc,ice->itbe", normed_rows, w_qkv, preferred_element_type=jnp.float32
    ).astype(jnp.bfloat16)
    qkv = qkv.reshape(3, tower_rows, seq_count, local_heads, DH)
    query_matrix, key_matrix, value_matrix = (qkv[0], qkv[1], qkv[2])
    key_all, value_all = (
        lax.all_gather(key_matrix, "seq", axis=0, tiled=True),
        lax.all_gather(value_matrix, "seq", axis=0, tiled=True),
    )
    attention_logits = (
        jnp.einsum("qbhd,kbhd->bhqk", query_matrix, key_all, preferred_element_type=jnp.float32)
        * logit_scale
    )
    row_peak = jnp.max(attention_logits, axis=-1, keepdims=True)
    exponent = jnp.exp(attention_logits - row_peak)
    row_total = jnp.sum(exponent, axis=-1, keepdims=True)
    soft_weights = exponent / row_total
    narrow_probabilities = soft_weights.astype(jnp.bfloat16)
    attention_output = jnp.einsum(
        "bhqk,kbhd->qbhd", narrow_probabilities, value_all, preferred_element_type=jnp.float32
    )
    o_narrow = attention_output.reshape(tower_rows, seq_count, local_width).astype(jnp.bfloat16)
    piece = o_narrow
    head_sum = lax.psum_scatter(
        jnp.einsum("tbe,ec->tbc", piece, w_out, preferred_element_type=jnp.float32).astype(
            jnp.bfloat16
        ),
        "head",
        scatter_dimension=0,
        tiled=True,
    ).astype(jnp.float32)
    mixed = (skip_wide + head_sum).astype(jnp.bfloat16)
    part_w_out = jnp.einsum("tbe,tbc->ec", o_narrow, grad_rows, preferred_element_type=jnp.float32)
    d_out = jnp.einsum("tbc,ec->tbe", grad_rows, w_out, preferred_element_type=jnp.float32).astype(
        jnp.bfloat16
    )
    d_out = d_out.reshape(tower_rows, seq_count, local_heads, DH)
    delta = jnp.sum(d_out.astype(jnp.float32) * attention_output, axis=-1)
    probability_gradient = jnp.einsum(
        "qbhd,kbhd->bhqk", d_out, value_all, preferred_element_type=jnp.float32
    )
    d_scores = soft_weights * (probability_gradient - jnp.transpose(delta, (1, 2, 0))[..., None])
    narrow_gradient = d_scores.astype(jnp.bfloat16)
    query_gradient = logit_scale * jnp.einsum(
        "bhqk,kbhd->qbhd", narrow_gradient, key_all, preferred_element_type=jnp.float32
    )
    key_terms = logit_scale * jnp.einsum(
        "bhqk,qbhd->kbhd", narrow_gradient, query_matrix, preferred_element_type=jnp.float32
    )
    value_terms = jnp.einsum(
        "bhqk,qbhd->kbhd", narrow_probabilities, d_out, preferred_element_type=jnp.float32
    )
    d_keys, d_values = (
        lax.psum_scatter(
            key_terms.astype(jnp.bfloat16), "seq", scatter_dimension=0, tiled=True
        ).astype(jnp.float32),
        lax.psum_scatter(
            value_terms.astype(jnp.bfloat16), "seq", scatter_dimension=0, tiled=True
        ).astype(jnp.float32),
    )
    dqkv = (
        jnp.stack([query_gradient, d_keys, d_values])
        .reshape(3, tower_rows, seq_count, local_width)
        .astype(jnp.bfloat16)
    )
    part_w_qkv = jnp.einsum("tbc,itbe->ice", normed_rows, dqkv, preferred_element_type=jnp.float32)
    piece = dqkv
    d_normed = lax.psum_scatter(
        jnp.einsum("itbe,ice->tbc", piece, w_qkv, preferred_element_type=jnp.float32).astype(
            jnp.bfloat16
        ),
        "head",
        scatter_dimension=0,
        tiled=True,
    ).astype(jnp.float32)
    unit_rows = skip_wide * inv_rms
    scaled = d_normed * norm_gain
    d_skip = grad_out.astype(jnp.float32) + inv_rms * (
        scaled - unit_rows * jnp.mean(scaled * unit_rows, axis=-1, keepdims=True)
    )
    d_act = jnp.repeat(d_skip, 2, axis=0) * 0.5
    d_conv = gelu_pull(d_act)[0].astype(jnp.bfloat16)
    d_pad = padded_2(d_conv, ((("seq", "head"), 0),), 2)
    grad_input = jnp.zeros((fine_rows, seq_count, enc_in.shape[2]), jnp.float32)
    for offset in range(KW):
        grad_input = grad_input + jnp.einsum(
            "tbo,io->tbi",
            d_pad[4 - offset : 4 - offset + fine_rows],
            conv_weight[offset],
            preferred_element_type=jnp.float32,
        )
    grad_w_qkv, grad_w_out = (
        lax.psum(part_w_qkv.astype(jnp.bfloat16), "seq").astype(jnp.float32),
        lax.psum(part_w_out.astype(jnp.bfloat16), "seq").astype(jnp.float32),
    )
    return (mixed, grad_input.astype(jnp.bfloat16), grad_w_qkv, grad_w_out)


def body(enc_in, conv_weight, norm_gain, w_qkv, w_out, grad_out):
    heads = w_qkv.shape[2] // DH
    seqs = enc_in.shape[1]
    fits = heads == 2 and seqs == 4 and seqs * heads == lax.axis_size("seq")
    fits = fits and conv_weight.shape[2] == seqs * w_qkv.shape[2]
    chosen = unit_body if fits else gathered_body
    return chosen(enc_in, conv_weight, norm_gain, w_qkv, w_out, grad_out)


def solution(mesh):
    return jax.shard_map(
        body,
        mesh=mesh,
        in_specs=(
            P(("seq", "head"), None, None),
            P(),
            P(),
            P(None, None, "head"),
            P("head", None),
            P(("seq", "head"), None, None),
        ),
        out_specs=(
            P(("seq", "head"), None, None),
            P(("seq", "head"), None, None),
            P(None, None, "head"),
            P("head", None),
        ),
        check_vma=False,
    )
```

```python
import functools

import jax
import jax.numpy as jnp
from jax import lax
from jax.experimental import pallas as pl
from jax.experimental.pallas import tpu as pltpu
from jax.sharding import PartitionSpec as P

DH = 192
KW = 5
VMEM_LIMIT = 24 * 1024 * 1024
STREAMING_LIMIT = 56 * 1024 * 1024
COST = pl.CostEstimate(flops=1000, bytes_accessed=1000, transcendentals=0)
BF = jnp.bfloat16
F32 = jnp.float32
TOKEN = jax.ShapeDtypeStruct((8, 128), F32)


def params(limit=VMEM_LIMIT):
    return pltpu.CompilerParams(vmem_limit_bytes=limit)


def dot(a, b, contract):
    return lax.dot_general(a, b, (contract, ((), ())), preferred_element_type=F32)


NN = ((1,), (0,))
NT = ((1,), (1,))
TN = ((0,), (0,))


def whole(shape):
    return pl.BlockSpec(shape, lambda *_: (0,) * len(shape))


SCALARS = pl.BlockSpec(memory_space=pltpu.SMEM)


def spare(deps):
    return [pl.BlockSpec(memory_space=pl.ANY)] * len(deps)


def turned_rows(ref, low_ref, high_ref, parity, shift):
    seqs, rows, width = ref.shape[1:]
    own = ref[parity]
    if shift != 1:
        wide = own.astype(F32)
        if shift == 0:
            parts = [low_ref[parity].astype(F32), wide[:, : rows - 1]]
        else:
            parts = [wide[:, 1:], high_ref[parity].astype(F32)]
        own = jnp.concatenate(parts, axis=1).astype(BF)
    return own.reshape(seqs * rows, width)


def conv_kernel(
    at_ref, x_ref, low_ref, high_ref, w_ref, gain_ref, skip_ref, slope_ref, *rest
):
    normed_refs, (lhs, squares, whole_normed) = rest[:-3], rest[-3:]
    step = pl.program_id(0)
    seqs, rows, c_in = x_ref.shape[1:]
    half = seqs * rows
    tile = w_ref.shape[2]

    @pl.when(step == 0)
    def _():
        for parity in range(2):
            for shift in range(3):
                value = turned_rows(x_ref, low_ref, high_ref, parity, shift)
                for out in range(2):
                    tap = 2 * shift + parity - out
                    if 0 <= tap < KW:
                        lhs[out * half : (out + 1) * half, tap * c_in : (tap + 1) * c_in] = value
        squares[...] = jnp.zeros_like(squares)

    conv = dot(lhs[...], w_ref[...].reshape(KW * c_in, tile), NN)
    root = 0.7978845608028654
    total = None
    for parity in range(2):
        x = conv[parity * half : (parity + 1) * half, :]
        square = x * x
        t = jnp.tanh(root * (x + 0.044715 * (square * x)))
        left = 0.5 * (1.0 + t)
        act = x * left
        slope = left + (0.5 * root) * x * (1.0 - t * t) * (1.0 + (3 * 0.044715) * square)
        slope_ref[parity] = slope.reshape(slope_ref.shape[1:])
        total = act if total is None else total + act
    skip = (0.5 * total).astype(BF)
    columns = pl.ds(pl.multiple_of(step * tile, tile), tile)
    skip_ref[:, :, columns] = skip.reshape(seqs, rows, tile)
    wide = skip.astype(F32)
    squares[...] += jnp.sum(wide * wide, axis=-1, keepdims=True)

    @pl.when(step == pl.num_programs(0) - 1)
    def _():
        width = skip_ref.shape[2]
        inv = lax.rsqrt(squares[...] * (1.0 / width) + 1e-06)
        wide = skip_ref[...].reshape(half, width).astype(F32)
        normed = (wide * inv * gain_ref[...]).astype(BF)
        whole_normed[...] = normed.reshape(whole_normed.shape)
        for slot in range(seqs):
            normed_refs[slot][...] = whole_normed[at_ref[0] ^ slot]


def encoder(at, pairs, low, high, conv_weight, norm_gain):
    _, seqs, rows, c_in = pairs.shape
    width = conv_weight.shape[2]
    tile = 256 if width % 256 == 0 else width
    shape = (seqs, rows, width)
    outs = pl.pallas_call(
        conv_kernel,
        grid=(width // tile,),
        in_specs=[
            SCALARS,
            whole(pairs.shape),
            whole(low.shape),
            whole(high.shape),
            pl.BlockSpec((KW, c_in, tile), lambda n: (0, 0, n)),
            whole((1, width)),
        ],
        out_specs=[
            whole(shape),
            pl.BlockSpec((2, seqs, rows, tile), lambda n: (0, 0, 0, n)),
        ]
        + [whole((rows, width))] * seqs,
        out_shape=[
            jax.ShapeDtypeStruct(shape, BF),
            jax.ShapeDtypeStruct((2,) + shape, F32),
        ]
        + [jax.ShapeDtypeStruct((rows, width), BF)] * seqs,
        scratch_shapes=[
            pltpu.VMEM((2 * seqs * rows, KW * c_in), BF),
            pltpu.VMEM((seqs * rows, 1), F32),
            pltpu.VMEM(shape, BF),
        ],
        compiler_params=params(STREAMING_LIMIT),
        cost_estimate=COST,
        name="encoder_forward",
    )(at, pairs, low, high, conv_weight, norm_gain.reshape(1, width))
    return outs[0], outs[1], list(outs[2:])


def d_conv_kernel(at_ref, own_ref, near_ref, far_ref, *refs):
    skip_ref, grad_ref, gain_ref, slope_ref = refs[:4]
    out_ref, first_ref, last_ref = refs[-3:]
    rows = out_ref.shape[2]
    for slot, (ref, place) in enumerate(((own_ref, 0), (near_ref, 0), (far_ref, 0), (far_ref, 1))):
        b = at_ref[0] ^ slot
        wide = skip_ref[b].astype(F32)
        inv = lax.rsqrt(jnp.mean(wide * wide, axis=-1, keepdims=True) + 1e-06)
        unit = wide * inv
        scaled = ref[place].astype(F32) * gain_ref[...]
        d_skip = grad_ref[b].astype(F32) + inv * (
            scaled - unit * jnp.mean(scaled * unit, axis=-1, keepdims=True)
        )
        d_act = 0.5 * d_skip
        for parity in range(2):
            value = slope_ref[parity, b] * d_act
            out_ref[parity, b] = value.astype(BF)
            first_ref[parity, b] = value[:1].astype(BF)
            last_ref[parity, b] = value[rows - 1 :].astype(BF)


def conv_gradient(at, own, near, far, skip, grad, norm_gain, slope, *deps):
    vmem = pl.BlockSpec(memory_space=pltpu.VMEM)
    edge = jax.ShapeDtypeStruct(slope.shape[:2] + (1, slope.shape[3]), BF)
    return pl.pallas_call(
        d_conv_kernel,
        in_specs=[SCALARS] + [vmem] * 7 + spare(deps),
        out_specs=[vmem] * 3,
        out_shape=[jax.ShapeDtypeStruct(slope.shape, BF)] + [edge] * 2,
        compiler_params=params(),
        cost_estimate=COST,
        name="conv_gradient",
    )(at, own, near, far, skip, grad, norm_gain.reshape(1, -1), slope, *deps)


def mixed_body(seqs, at_ref, *refs):
    skip_ref, out_ref = refs[seqs:]
    for slot in range(seqs):
        b = at_ref[0] ^ slot
        out_ref[b] = (skip_ref[b].astype(F32) + refs[slot][...].astype(F32)).astype(BF)


def mixed_call(at, terms, skip):
    seqs = len(terms)
    vmem = pl.BlockSpec(memory_space=pltpu.VMEM)
    return pl.pallas_call(
        functools.partial(mixed_body, seqs),
        in_specs=[SCALARS] + [vmem] * (seqs + 1),
        out_specs=vmem,
        out_shape=jax.ShapeDtypeStruct(skip.shape, BF),
        compiler_params=params(),
        cost_estimate=COST,
        name="mixed_sum",
    )(at, *terms, skip)


def conv_back_kernel(d_ref, low_ref, high_ref, w_ref, *rest):
    out_ref, turned, acc = rest[-3:]
    step = pl.program_id(0)

    @pl.when(step == 0)
    def _():
        for parity in range(2):
            for shift in range(3):
                turned[parity, shift] = turned_rows(d_ref, low_ref, high_ref, parity, shift).T

    for tap in range(KW):

        @pl.when(step == tap)
        def _():
            places = [KW - 1 - tap, KW - tap]
            rhs = jnp.concatenate([turned[p % 2, p // 2] for p in places], axis=1)
            term = dot(w_ref[0], rhs, NN)
            if tap == 0:
                acc[...] = term
            elif tap < KW - 1:
                acc[...] += term
            else:
                out_ref[...] = (acc[...] + term).T.astype(BF)


def conv_back(d_conv, low, high, conv_weight, *deps):
    _, seqs, rows, width = d_conv.shape
    c_in = conv_weight.shape[1]
    flat = 2 * seqs * rows
    return pl.pallas_call(
        conv_back_kernel,
        grid=(KW,),
        in_specs=[
            whole(d_conv.shape),
            whole(low.shape),
            whole(high.shape),
            pl.BlockSpec((1, c_in, width), lambda k: (k, 0, 0)),
        ]
        + spare(deps),
        out_specs=whole((flat, c_in)),
        out_shape=jax.ShapeDtypeStruct((flat, c_in), BF),
        scratch_shapes=[
            pltpu.VMEM((2, 3, width, seqs * rows), BF),
            pltpu.VMEM((c_in, flat), F32),
        ],
        compiler_params=params(),
        cost_estimate=COST,
        name="encoder_backward",
    )(d_conv, low, high, conv_weight, *deps)


def pack_kernel(w_ref, pack_ref, turned_ref, token_ref):
    token_ref[...] = jnp.zeros_like(token_ref)
    for i in range(3):
        for head in range(pack_ref.shape[0]):
            part = w_ref[i, :, head * DH : (head + 1) * DH]
            columns = slice(i * DH, (i + 1) * DH)
            pack_ref[head, :, columns] = part
            turned_ref[head, columns, :] = part.T


def pack_weights(w_qkv):
    _, width, local = w_qkv.shape
    heads = local // DH
    tile = local
    return pl.pallas_call(
        pack_kernel,
        grid=(width // tile,),
        in_specs=[pl.BlockSpec((3, tile, local), lambda n: (0, n, 0))],
        out_specs=[
            pl.BlockSpec((heads, tile, 3 * DH), lambda n: (0, n, 0)),
            pl.BlockSpec((heads, 3 * DH, tile), lambda n: (0, 0, n)),
            pl.BlockSpec(TOKEN.shape, lambda n: (0, 0)),
        ],
        out_shape=[
            jax.ShapeDtypeStruct((heads, width, 3 * DH), BF),
            jax.ShapeDtypeStruct((heads, 3 * DH, width), BF),
            TOKEN,
        ],
        compiler_params=params(),
        cost_estimate=COST,
        name="pack_weights",
    )(w_qkv)


def product_kernel(head_ref, x_ref, w_ref, *rest, contract):
    del head_ref
    out_ref, token_ref = rest[-2:]
    token_ref[...] = jnp.zeros_like(token_ref)
    value = dot(x_ref[...], w_ref[0], contract).astype(BF)
    out_ref[:, : value.shape[1]] = value
    if value.shape[1] < out_ref.shape[1]:
        out_ref[:, value.shape[1] :] = jnp.zeros_like(out_ref[:, value.shape[1] :])


def head_product(head, x, weight, contract, name, *deps):
    columns = weight.shape[2] if contract == NN else weight.shape[1]
    columns += -columns % 128
    rows, width = x.shape
    return pl.pallas_call(
        functools.partial(product_kernel, contract=contract),
        grid_spec=pltpu.PrefetchScalarGridSpec(
            num_scalar_prefetch=1,
            grid=(1,),
            in_specs=[
                pl.BlockSpec((rows, width), lambda i, head: (0, 0)),
                pl.BlockSpec((1,) + weight.shape[1:], lambda i, head: (head[0], 0, 0)),
            ]
            + spare(deps),
            out_specs=[
                pl.BlockSpec((rows, columns), lambda i, head: (0, 0)),
                pl.BlockSpec(TOKEN.shape, lambda i, head: (0, 0)),
            ],
        ),
        out_shape=[jax.ShapeDtypeStruct((rows, columns), BF), TOKEN],
        compiler_params=params(),
        cost_estimate=COST,
        name=name,
    )(head, x, weight, *deps)


def attention_kernel(qa_ref, qb_ref, da_ref, db_ref, *rest, block):
    oa_ref, ob_ref, k_all, v_all, dk_acc, dv_acc = rest[-6:]
    scale = DH ** (-0.5)
    half = qa_ref.shape[0]
    for place, ref in enumerate((qa_ref, qb_ref)):
        rows = pl.ds(place * half, half)
        k_all[rows, :] = ref[:, DH : 2 * DH]
        v_all[rows, :] = ref[:, 2 * DH : 3 * DH]
    k = k_all[...]
    v = v_all[...]
    for place, (q_ref, d_ref, out_ref) in enumerate(
        ((qa_ref, da_ref, oa_ref), (qb_ref, db_ref, ob_ref))
    ):
        for start in range(0, half, block):
            rows = pl.ds(start, block)
            q = q_ref[rows, 0:DH]
            d_o = d_ref[rows, 0:DH]
            s = dot(q, k, NT) * scale
            e = jnp.exp(s - jnp.max(s, axis=-1, keepdims=True))
            p = e * (1.0 / jnp.sum(e, axis=-1, keepdims=True))
            p_b = p.astype(BF)
            o = dot(p_b, v, NN)
            delta = jnp.sum(d_o.astype(F32) * o, axis=-1, keepdims=True)
            d_p = dot(d_o, v, NT)
            ds = (p * (d_p - delta)).astype(BF)
            dq = scale * dot(ds, k, NN)
            dk = dot(ds, q, TN)
            dv = dot(p_b, d_o, TN)
            if place == 0 and start == 0:
                dk_acc[...] = dk
                dv_acc[...] = dv
            else:
                dk_acc[...] += dk
                dv_acc[...] += dv
            out_ref[rows, 0:DH] = dq.astype(BF)
            out_ref[rows, 3 * DH : 4 * DH] = o.astype(BF)
    for place, out_ref in enumerate((oa_ref, ob_ref)):
        rows = pl.ds(place * half, half)
        out_ref[:, DH : 2 * DH] = (scale * dk_acc[rows, :]).astype(BF)
        out_ref[:, 2 * DH : 3 * DH] = dv_acc[rows, :].astype(BF)


def attention(qkv_a, qkv_b, d_a, d_b, *deps):
    half = qkv_a.shape[0]
    shape = jax.ShapeDtypeStruct((half, 4 * DH), BF)
    return pl.pallas_call(
        functools.partial(attention_kernel, block=min(256, half)),
        in_specs=[pl.BlockSpec(memory_space=pltpu.VMEM)] * 4 + spare(deps),
        out_shape=[shape, shape],
        scratch_shapes=[
            pltpu.VMEM((2 * half, DH), BF),
            pltpu.VMEM((2 * half, DH), BF),
            pltpu.VMEM((2 * half, DH), F32),
            pltpu.VMEM((2 * half, DH), F32),
        ],
        compiler_params=params(),
        cost_estimate=COST,
        name="attention",
    )(qkv_a, qkv_b, d_a, d_b, *deps)


def term_kernel(head_ref, a_ref, b_ref, w_ref, *rest, first, last):
    head = head_ref[0]
    total = dot(a_ref[:, first:last], w_ref[head], NN)
    total += dot(b_ref[:, first:last], w_ref[1 - head], NN)
    rest[-1][...] = total.astype(BF)


def pair_term(head, mine, got, weight, first, last, name, *deps):
    half, full = mine.shape
    heads, depth, width = weight.shape
    tile = 512 if width % 512 == 0 else width
    return pl.pallas_call(
        functools.partial(term_kernel, first=first, last=last),
        grid_spec=pltpu.PrefetchScalarGridSpec(
            num_scalar_prefetch=1,
            grid=(width // tile,),
            in_specs=[
                pl.BlockSpec((half, full), lambda n, at: (0, 0)),
                pl.BlockSpec((half, full), lambda n, at: (0, 0)),
                pl.BlockSpec((heads, depth, tile), lambda n, at: (0, 0, n)),
            ]
            + spare(deps),
            out_specs=pl.BlockSpec((half, tile), lambda n, at: (0, n)),
        ),
        out_shape=jax.ShapeDtypeStruct((half, width), BF),
        compiler_params=params(),
        cost_estimate=COST,
        name=name,
    )(head, mine, got, weight, *deps)


def part_kernel(head_ref, x_ref, w_ref, *rest, last):
    del head_ref
    total = dot(x_ref[:, :last], w_ref[0], NN)
    if len(rest) > 1:
        total += rest[0][...]
    rest[-1][...] = total.astype(rest[-1].dtype)


def term_part(head, x, weight, last, name, *before):
    half, full = x.shape
    _, depth, width = weight.shape
    tile = 512 if width % 512 == 0 else width
    column = pl.BlockSpec((half, tile), lambda n, at: (0, n))
    return pl.pallas_call(
        functools.partial(part_kernel, last=last),
        grid_spec=pltpu.PrefetchScalarGridSpec(
            num_scalar_prefetch=1,
            grid=(width // tile,),
            in_specs=[
                pl.BlockSpec((half, full), lambda n, at: (0, 0)),
                pl.BlockSpec((1, depth, tile), lambda n, at: (at[0], 0, n)),
            ]
            + [column] * len(before),
            out_specs=column,
        ),
        out_shape=jax.ShapeDtypeStruct((half, width), BF if before else F32),
        compiler_params=params(),
        cost_estimate=COST,
        name=name,
    )(head, x, weight, *before)


def weight_kernel(at_ref, xa_ref, xb_ref, ga_ref, gb_ref, ra_ref, rb_ref, *rest):
    del at_ref
    out_refs, turned = rest[:-1], rest[-1]
    step = pl.program_id(0)
    half = ra_ref.shape[0]
    split = 3 * DH

    @pl.when(step == 0)
    def _():
        turned[:, :half] = ra_ref[...].T
        turned[:, half:] = rb_ref[...].T

    a, b = slice(0, half), slice(half, 2 * half)
    qkv = dot(turned[:split, a], xa_ref[...], NN) + dot(turned[:split, b], xb_ref[...], NN)
    out = dot(turned[split:, a], ga_ref[...], NN) + dot(turned[split:, b], gb_ref[...], NN)
    keep_a, send_a, keep_b, send_b = out_refs
    rows = keep_a.shape[1]
    for slot in range(4):

        @pl.when(step == slot)
        def _():
            first = keep_a if slot % 2 == 0 else send_a
            second = keep_b if slot < 2 else send_b
            first[slot // 2] = qkv[:rows].astype(BF)
            second[slot % 2, : split - rows] = qkv[rows:].astype(BF)
            second[slot % 2, split - rows :] = out.astype(BF)


def weight_gradients(at, xa, xb, ga, gb, ra, rb, seqs):
    half, width = xa.shape
    chunk = width // seqs
    full = ra.shape[1]
    column = pl.BlockSpec((half, chunk), lambda r, at: (0, r ^ at[0]))
    rest = pl.BlockSpec((half, full), lambda r, at: (0, 0))
    return pl.pallas_call(
        weight_kernel,
        grid_spec=pltpu.PrefetchScalarGridSpec(
            num_scalar_prefetch=1,
            grid=(seqs,),
            in_specs=[column] * 4 + [rest] * 2,
            out_specs=[pl.BlockSpec((2, full // 2, chunk), lambda r, at: (0, 0, 0))] * 4,
            scratch_shapes=[pltpu.VMEM((full, 2 * half), BF)],
        ),
        out_shape=[jax.ShapeDtypeStruct((2, full // 2, chunk), BF)] * 4,
        compiler_params=params(STREAMING_LIMIT),
        cost_estimate=COST,
        name="weight_gradients",
    )(at, xa, xb, ga, gb, ra, rb)


def turn_kernel(keep_a, got_a, keep_b, got_b, out_a, out_b):
    for keep, got, out in ((keep_a, got_a, out_a), (keep_b, got_b, out_b)):
        out[...] = (keep[1].astype(F32) + got[1].astype(F32)).astype(BF)


def weight_turn(keep_a, got_a, keep_b, got_b):
    shape = jax.ShapeDtypeStruct(keep_a.shape[1:], BF)
    return pl.pallas_call(
        turn_kernel,
        out_shape=[shape, shape],
        compiler_params=params(),
        cost_estimate=COST,
        name="weight_turn",
    )(keep_a, got_a, keep_b, got_b)


def weight_sum_kernel(keep_a, got_a, last_a, keep_b, got_b, last_b, *out_refs):
    split = 3 * DH
    parts = [
        keep[0].astype(F32) + got[0].astype(F32) + last[...].astype(F32)
        for keep, got, last in ((keep_a, got_a, last_a), (keep_b, got_b, last_b))
    ]
    total = jnp.concatenate(parts, axis=0)
    turned = total[:split].T.astype(BF)
    quarter = DH // 2
    for part, out_ref in enumerate(out_refs):
        out_ref[:, :split] = turned[part * DH : (part + 1) * DH]
        first = split + part * quarter
        piece = total[first : first + quarter].astype(BF)
        out_ref[:quarter, split:] = piece[:, :DH]
        out_ref[quarter:, split:] = piece[:, DH:]


def weight_sum(*parts):
    _, rows, chunk = parts[0].shape
    return pl.pallas_call(
        weight_sum_kernel,
        out_shape=[jax.ShapeDtypeStruct((chunk // 2, 2 * rows), BF)] * 2,
        compiler_params=params(),
        cost_estimate=COST,
        name="weight_sum",
    )(*parts)


def unpack_kernel(at_ref, *refs):
    qkv_ref, out_ref, token_ref = refs[-3:]
    step = pl.program_id(0)
    split = 3 * DH
    quarter = DH // 2
    token_ref[...] = jnp.zeros_like(token_ref)
    for half in range(2):

        @pl.when(step // 2 == half)
        def _():
            mine = refs[half][...].astype(F32)
            other = refs[2 + half][...].astype(F32)
            swapped = at_ref[1] != 0
            low = jnp.where(swapped, other, mine)
            high = jnp.where(swapped, mine, other)
            for i in range(3):
                columns = slice(i * DH, (i + 1) * DH)
                qkv_ref[i] = jnp.concatenate([low[:, columns], high[:, columns]], axis=1)
            for head, value in enumerate((low, high)):
                folded = [value[:quarter, split:], value[quarter:, split:]]
                out_ref[head, 0] = jnp.concatenate(folded, axis=1)


def unpack_weights(at, mine, other, far, before=()):
    rows, full = mine[0].shape
    half = rows // 2
    width = 4 * rows

    def chunk(t, at):
        if far:
            return at[0] ^ jnp.where(t < 2, t + 2, 2 * t - 3)
        return at[0] ^ jnp.where(t < 2, t, 2 * t - 4)

    specs = [
        pl.BlockSpec((half, full), lambda t, at: (jnp.minimum(t, 1), 0)),
        pl.BlockSpec((half, full), lambda t, at: (jnp.maximum(t - 2, 0), 0)),
    ]
    return pl.pallas_call(
        unpack_kernel,
        grid_spec=pltpu.PrefetchScalarGridSpec(
            num_scalar_prefetch=1,
            grid=(4,),
            in_specs=specs * 2 + spare(before),
            out_specs=[
                pl.BlockSpec((3, half, 2 * DH), lambda t, at: (0, 2 * chunk(t, at) + t // 2, 0)),
                pl.BlockSpec(
                    (2, 1, DH // 2, rows), lambda t, at: (0, t // 2, 0, chunk(t, at))
                ),
                pl.BlockSpec(TOKEN.shape, lambda t, at: (0, 0)),
            ],
        ),
        out_shape=[
            jax.ShapeDtypeStruct((3, width, 2 * DH), F32),
            jax.ShapeDtypeStruct((2, 2, DH // 2, width), F32),
            TOKEN,
        ],
        input_output_aliases={5 + i: i for i in range(len(before))},
        compiler_params=params(),
        cost_estimate=COST,
        name="weight_outputs_far" if far else "weight_outputs_near",
    )(at, *mine, *other, *before)


def neighbour_edges(first, last):
    axes = ("seq", "head")
    count = lax.axis_size(axes)
    forward = [(i, i + 1) for i in range(count - 1)]
    backward = [(target, source) for source, target in forward]
    return lax.ppermute(last, axes, forward), lax.ppermute(first, axes, backward)


def after(value, *others):
    return lax.optimization_barrier((value,) + others)[0]


def trade_chip(x, bit, heads):
    count = lax.axis_size("seq")
    return lax.ppermute(x, "seq", [(s, s ^ (bit * heads)) for s in range(count)])


def swap_heads(x):
    count = lax.axis_size("seq")
    return lax.ppermute(x, "seq", [(s, s + 1 - 2 * (s % 2)) for s in range(count)])


def unit_body(enc_in, conv_weight, norm_gain, w_qkv, w_out, grad_out):
    rows = enc_in.shape[0] // 2
    seqs = enc_in.shape[1]
    width = conv_weight.shape[2]
    local = w_qkv.shape[2]
    heads = local // DH
    groups = lax.axis_size("head")
    half = groups * seqs * rows
    place = lax.axis_index("seq")
    own_seq = (place // heads).astype(jnp.int32)
    own_head = (place % heads).astype(jnp.int32)
    at = jnp.stack([own_seq, own_head])
    head_mine = own_head.reshape(1)
    head_other = (1 - own_head).reshape(1)

    def to_chips(slots):
        return [x if j == 0 else trade_chip(x, j, heads) for j, x in enumerate(slots)]

    order = (0, 2, 1, 3)

    grad_z = lax.all_gather(grad_out, "head", axis=0, tiled=False)

    pairs = jnp.transpose(enc_in.reshape(rows, 2, seqs, enc_in.shape[2]), (1, 2, 0, 3))
    low, high = neighbour_edges(pairs[:, :, :1, :], pairs[:, :, -1:, :])
    skip, slope, normed = encoder(at, pairs, low, high, conv_weight, norm_gain)
    normed = to_chips(normed)
    normed_slab = jnp.concatenate([normed[j] for j in order], axis=0)
    normed_rows = lax.all_gather(normed_slab, "head", axis=0, tiled=True)

    grad_z = after(grad_z, normed_slab)
    grad_slots = to_chips(
        [lax.dynamic_index_in_dim(grad_z, own_seq ^ j, 2, keepdims=False) for j in range(seqs)]
    )
    grad_rows = jnp.stack([grad_slots[j] for j in order], axis=1).reshape(half, width)
    w_pack, w_turned, packed = pack_weights(after(w_qkv, normed_slab))
    w_rows = w_out.reshape(heads, DH, width)
    d_other, one = head_product(head_other, grad_rows, w_rows, NT, "d_o_other")
    d_got = swap_heads(d_other)
    d_mine, two = head_product(head_mine, grad_rows, w_rows, NT, "d_o_own")
    grad_swapped = swap_heads(grad_rows)
    normed_rows, d_got, d_mine, grad_swapped, w_pack, w_turned, *tokens = (
        lax.optimization_barrier(
            (normed_rows, d_got, d_mine, grad_swapped, w_pack, w_turned, packed, one, two)
        )
    )

    normed_swapped = swap_heads(normed_rows)
    qkv_other, _ = head_product(head_other, normed_rows, w_pack, NN, "qkv_other", *tokens)
    qkv_got = swap_heads(qkv_other)
    qkv_mine, _ = head_product(head_mine, normed_rows, w_pack, NN, "qkv_own")
    result_mine, result_other = attention(qkv_mine, qkv_got, d_mine, d_got, normed_swapped)
    result_got = swap_heads(result_other)

    shape = (groups, seqs, rows, width)
    d_own = term_part(head_mine, result_mine, w_turned, 3 * DH, "d_term_own")
    d_term = term_part(head_other, result_got, w_turned, 3 * DH, "d_term", d_own)
    d_normed = lax.psum_scatter(d_term.reshape(shape), "head", scatter_dimension=0, tiled=False)
    keep_a, send_a, keep_b, send_b = weight_gradients(
        own_seq.reshape(1),
        normed_rows,
        normed_swapped,
        grad_rows,
        grad_swapped,
        result_mine,
        result_other,
        seqs,
    )
    got_a, got_b = trade_chip(send_a, 1, heads), trade_chip(send_b, 2, heads)
    turn_a, turn_b = weight_turn(keep_a, got_a, keep_b, got_b)
    last_a, last_b = trade_chip(turn_a, 2, heads), trade_chip(turn_b, 1, heads)
    half_a, half_b = weight_sum(keep_a, got_a, last_a, keep_b, got_b, last_b)
    head_term = pair_term(
        head_mine, result_mine, result_got, w_rows, 3 * DH, 4 * DH, "head_term"
    )
    head_sum = lax.psum_scatter(head_term.reshape(shape), "head", scatter_dimension=0, tiled=False)

    d_normed = after(d_normed, last_a, last_b)
    leaving = d_normed[2:]
    got_a, got_b = trade_chip(half_a, 1, heads), trade_chip(half_b, 2, heads)
    near_a = jnp.concatenate([half_a, after(got_a, leaving)], axis=0)
    near_b = jnp.concatenate([half_b, after(got_b, leaving)], axis=0)
    far_a = trade_chip(near_a, 2, heads)
    far_b = trade_chip(near_b, 1, heads)
    near_other = [swap_heads(near_a), swap_heads(near_b)]

    near = trade_chip(leaving, 1, heads)
    far = trade_chip(jnp.stack([d_normed[1], near[1]]), 2, heads)
    grad = jnp.transpose(after(grad_out, d_term), (1, 0, 2))
    d_conv, first, last = conv_gradient(
        at, d_normed, near, far, skip, grad, norm_gain, slope, near_a, near_b
    )
    low, high = neighbour_edges(first, last)
    *outputs, token = unpack_weights(at, [near_a, near_b], near_other, False)
    low, high, token = lax.optimization_barrier((low, high, token))
    grad_input = conv_back(d_conv, low, high, conv_weight, token)

    head_sum = after(head_sum, grad_input)
    head_sum = [head_sum[order.index(j)] for j in range(seqs)]
    far_other = [swap_heads(after(x, *head_sum)) for x in (far_a, far_b)]
    grad_w_qkv, grad_w_out, _ = unpack_weights(at, [far_a, far_b], far_other, True, outputs)
    head_sum = to_chips(head_sum)
    mixed = mixed_call(at, head_sum, skip)
    grad_input = jnp.transpose(grad_input.reshape(2, seqs, rows, -1), (2, 0, 1, 3))
    return (
        jnp.transpose(mixed, (1, 0, 2)),
        grad_input.reshape(enc_in.shape),
        grad_w_qkv,
        grad_w_out.reshape(local, width),
    )


def padded_2(block, sides, width):
    for axis, dim in sides:
        count = lax.axis_size(axis)
        forward = [(i, i + 1) for i in range(count - 1)]
        backward = [(target, source) for source, target in forward]
        low = lax.ppermute(
            lax.slice_in_dim(block, block.shape[dim] - width, None, axis=dim), axis, forward
        )
        high = lax.ppermute(lax.slice_in_dim(block, 0, width, axis=dim), axis, backward)
        block = jnp.concatenate([low, block, high], axis=dim)
    return block


def gathered_body(enc_in, conv_weight, norm_gain, w_qkv, w_out, grad_out):
    fine_rows = enc_in.shape[0]
    slab_rows = fine_rows // 2
    seq_count = enc_in.shape[1]
    out_width = conv_weight.shape[2]
    local_width = w_qkv.shape[2]
    local_heads = local_width // DH
    logit_scale = DH ** (-0.5)
    padded = padded_2(enc_in, ((("seq", "head"), 0),), 2)
    convolved = jnp.zeros((fine_rows, seq_count, out_width), jnp.float32)
    for offset in range(KW):
        convolved = convolved + jnp.einsum(
            "tbi,io->tbo",
            padded[offset : offset + fine_rows],
            conv_weight[offset],
            preferred_element_type=jnp.float32,
        )
    activated, gelu_pull = jax.vjp(jax.nn.gelu, convolved)
    skip = jnp.mean(activated.reshape(slab_rows, 2, seq_count, out_width), axis=1).astype(
        jnp.bfloat16
    )
    skip_wide = skip.astype(jnp.float32)
    inv_rms = lax.rsqrt(jnp.mean(skip_wide * skip_wide, axis=-1, keepdims=True) + 1e-06)
    normed = (skip_wide * inv_rms * norm_gain).astype(jnp.bfloat16)
    normed_rows = lax.all_gather(normed, "head", axis=0, tiled=True)
    grad_rows = lax.all_gather(grad_out, "head", axis=0, tiled=True)
    tower_rows = normed_rows.shape[0]
    qkv = jnp.einsum(
        "tbc,ice->itbe", normed_rows, w_qkv, preferred_element_type=jnp.float32
    ).astype(jnp.bfloat16)
    qkv = qkv.reshape(3, tower_rows, seq_count, local_heads, DH)
    query_matrix, key_matrix, value_matrix = (qkv[0], qkv[1], qkv[2])
    key_all, value_all = (
        lax.all_gather(key_matrix, "seq", axis=0, tiled=True),
        lax.all_gather(value_matrix, "seq", axis=0, tiled=True),
    )
    attention_logits = (
        jnp.einsum("qbhd,kbhd->bhqk", query_matrix, key_all, preferred_element_type=jnp.float32)
        * logit_scale
    )
    row_peak = jnp.max(attention_logits, axis=-1, keepdims=True)
    exponent = jnp.exp(attention_logits - row_peak)
    row_total = jnp.sum(exponent, axis=-1, keepdims=True)
    soft_weights = exponent / row_total
    narrow_probabilities = soft_weights.astype(jnp.bfloat16)
    attention_output = jnp.einsum(
        "bhqk,kbhd->qbhd", narrow_probabilities, value_all, preferred_element_type=jnp.float32
    )
    o_narrow = attention_output.reshape(tower_rows, seq_count, local_width).astype(jnp.bfloat16)
    piece = o_narrow
    head_sum = lax.psum_scatter(
        jnp.einsum("tbe,ec->tbc", piece, w_out, preferred_element_type=jnp.float32).astype(
            jnp.bfloat16
        ),
        "head",
        scatter_dimension=0,
        tiled=True,
    ).astype(jnp.float32)
    mixed = (skip_wide + head_sum).astype(jnp.bfloat16)
    part_w_out = jnp.einsum("tbe,tbc->ec", o_narrow, grad_rows, preferred_element_type=jnp.float32)
    d_out = jnp.einsum("tbc,ec->tbe", grad_rows, w_out, preferred_element_type=jnp.float32).astype(
        jnp.bfloat16
    )
    d_out = d_out.reshape(tower_rows, seq_count, local_heads, DH)
    delta = jnp.sum(d_out.astype(jnp.float32) * attention_output, axis=-1)
    probability_gradient = jnp.einsum(
        "qbhd,kbhd->bhqk", d_out, value_all, preferred_element_type=jnp.float32
    )
    d_scores = soft_weights * (probability_gradient - jnp.transpose(delta, (1, 2, 0))[..., None])
    narrow_gradient = d_scores.astype(jnp.bfloat16)
    query_gradient = logit_scale * jnp.einsum(
        "bhqk,kbhd->qbhd", narrow_gradient, key_all, preferred_element_type=jnp.float32
    )
    key_terms = logit_scale * jnp.einsum(
        "bhqk,qbhd->kbhd", narrow_gradient, query_matrix, preferred_element_type=jnp.float32
    )
    value_terms = jnp.einsum(
        "bhqk,qbhd->kbhd", narrow_probabilities, d_out, preferred_element_type=jnp.float32
    )
    d_keys, d_values = (
        lax.psum_scatter(
            key_terms.astype(jnp.bfloat16), "seq", scatter_dimension=0, tiled=True
        ).astype(jnp.float32),
        lax.psum_scatter(
            value_terms.astype(jnp.bfloat16), "seq", scatter_dimension=0, tiled=True
        ).astype(jnp.float32),
    )
    dqkv = (
        jnp.stack([query_gradient, d_keys, d_values])
        .reshape(3, tower_rows, seq_count, local_width)
        .astype(jnp.bfloat16)
    )
    part_w_qkv = jnp.einsum("tbc,itbe->ice", normed_rows, dqkv, preferred_element_type=jnp.float32)
    piece = dqkv
    d_normed = lax.psum_scatter(
        jnp.einsum("itbe,ice->tbc", piece, w_qkv, preferred_element_type=jnp.float32).astype(
            jnp.bfloat16
        ),
        "head",
        scatter_dimension=0,
        tiled=True,
    ).astype(jnp.float32)
    unit_rows = skip_wide * inv_rms
    scaled = d_normed * norm_gain
    d_skip = grad_out.astype(jnp.float32) + inv_rms * (
        scaled - unit_rows * jnp.mean(scaled * unit_rows, axis=-1, keepdims=True)
    )
    d_act = jnp.repeat(d_skip, 2, axis=0) * 0.5
    d_conv = gelu_pull(d_act)[0].astype(jnp.bfloat16)
    d_pad = padded_2(d_conv, ((("seq", "head"), 0),), 2)
    grad_input = jnp.zeros((fine_rows, seq_count, enc_in.shape[2]), jnp.float32)
    for offset in range(KW):
        grad_input = grad_input + jnp.einsum(
            "tbo,io->tbi",
            d_pad[4 - offset : 4 - offset + fine_rows],
            conv_weight[offset],
            preferred_element_type=jnp.float32,
        )
    grad_w_qkv, grad_w_out = (
        lax.psum(part_w_qkv.astype(jnp.bfloat16), "seq").astype(jnp.float32),
        lax.psum(part_w_out.astype(jnp.bfloat16), "seq").astype(jnp.float32),
    )
    return (mixed, grad_input.astype(jnp.bfloat16), grad_w_qkv, grad_w_out)


def body(enc_in, conv_weight, norm_gain, w_qkv, w_out, grad_out):
    heads = w_qkv.shape[2] // DH
    seqs = enc_in.shape[1]
    fits = heads == 2 and seqs == 4 and seqs * heads == lax.axis_size("seq")
    fits = fits and conv_weight.shape[2] == seqs * w_qkv.shape[2]
    chosen = unit_body if fits else gathered_body
    return chosen(enc_in, conv_weight, norm_gain, w_qkv, w_out, grad_out)


def solution(mesh):
    return jax.shard_map(
        body,
        mesh=mesh,
        in_specs=(
            P(("seq", "head"), None, None),
            P(),
            P(),
            P(None, None, "head"),
            P("head", None),
            P(("seq", "head"), None, None),
        ),
        out_specs=(
            P(("seq", "head"), None, None),
            P(("seq", "head"), None, None),
            P(None, None, "head"),
            P("head", None),
        ),
        check_vma=False,
    )
```

```python
import functools

import jax
import jax.numpy as jnp
from jax import lax
from jax.experimental import pallas as pl
from jax.experimental.pallas import tpu as pltpu
from jax.sharding import PartitionSpec as P

DH = 192
KW = 5
VMEM_LIMIT = 24 * 1024 * 1024
STREAMING_LIMIT = 56 * 1024 * 1024
COST = pl.CostEstimate(flops=1000, bytes_accessed=1000, transcendentals=0)
BF = jnp.bfloat16
F32 = jnp.float32
TOKEN = jax.ShapeDtypeStruct((8, 128), F32)


def params(limit=VMEM_LIMIT):
    return pltpu.CompilerParams(vmem_limit_bytes=limit)


def dot(a, b, contract):
    return lax.dot_general(a, b, (contract, ((), ())), preferred_element_type=F32)


NN = ((1,), (0,))
NT = ((1,), (1,))
TN = ((0,), (0,))


def whole(shape):
    return pl.BlockSpec(shape, lambda *_: (0,) * len(shape))


SCALARS = pl.BlockSpec(memory_space=pltpu.SMEM)


def spare(deps):
    return [pl.BlockSpec(memory_space=pl.ANY)] * len(deps)


def turned_rows(ref, low_ref, high_ref, parity, shift):
    seqs, rows, width = ref.shape[1:]
    own = ref[parity]
    if shift != 1:
        wide = own.astype(F32)
        if shift == 0:
            parts = [low_ref[parity].astype(F32), wide[:, : rows - 1]]
        else:
            parts = [wide[:, 1:], high_ref[parity].astype(F32)]
        own = jnp.concatenate(parts, axis=1).astype(BF)
    return own.reshape(seqs * rows, width)


def conv_kernel(
    at_ref, x_ref, low_ref, high_ref, w_ref, gain_ref, skip_ref, slope_ref, *rest
):
    normed_refs, (lhs, squares, whole_normed) = rest[:-3], rest[-3:]
    step = pl.program_id(0)
    seqs, rows, c_in = x_ref.shape[1:]
    half = seqs * rows
    tile = w_ref.shape[2]

    @pl.when(step == 0)
    def _():
        for parity in range(2):
            for shift in range(3):
                value = turned_rows(x_ref, low_ref, high_ref, parity, shift)
                for out in range(2):
                    tap = 2 * shift + parity - out
                    if 0 <= tap < KW:
                        lhs[out * half : (out + 1) * half, tap * c_in : (tap + 1) * c_in] = value
        squares[...] = jnp.zeros_like(squares)

    conv = dot(lhs[...], w_ref[...].reshape(KW * c_in, tile), NN)
    root = 0.7978845608028654
    total = None
    for parity in range(2):
        x = conv[parity * half : (parity + 1) * half, :]
        square = x * x
        t = jnp.tanh(root * (x + 0.044715 * (square * x)))
        left = 0.5 * (1.0 + t)
        act = x * left
        slope = left + (0.5 * root) * x * (1.0 - t * t) * (1.0 + (3 * 0.044715) * square)
        slope_ref[parity] = slope.reshape(slope_ref.shape[1:])
        total = act if total is None else total + act
    skip = (0.5 * total).astype(BF)
    columns = pl.ds(pl.multiple_of(step * tile, tile), tile)
    skip_ref[:, :, columns] = skip.reshape(seqs, rows, tile)
    wide = skip.astype(F32)
    squares[...] += jnp.sum(wide * wide, axis=-1, keepdims=True)

    @pl.when(step == pl.num_programs(0) - 1)
    def _():
        width = skip_ref.shape[2]
        inv = lax.rsqrt(squares[...] * (1.0 / width) + 1e-06)
        wide = skip_ref[...].reshape(half, width).astype(F32)
        normed = (wide * inv * gain_ref[...]).astype(BF)
        whole_normed[...] = normed.reshape(whole_normed.shape)
        for slot in range(seqs):
            normed_refs[slot][...] = whole_normed[at_ref[0] ^ slot]


def encoder(at, pairs, low, high, conv_weight, norm_gain):
    _, seqs, rows, c_in = pairs.shape
    width = conv_weight.shape[2]
    tile = 256 if width % 256 == 0 else width
    shape = (seqs, rows, width)
    outs = pl.pallas_call(
        conv_kernel,
        grid=(width // tile,),
        in_specs=[
            SCALARS,
            whole(pairs.shape),
            whole(low.shape),
            whole(high.shape),
            pl.BlockSpec((KW, c_in, tile), lambda n: (0, 0, n)),
            whole((1, width)),
        ],
        out_specs=[
            whole(shape),
            pl.BlockSpec((2, seqs, rows, tile), lambda n: (0, 0, 0, n)),
        ]
        + [whole((rows, width))] * seqs,
        out_shape=[
            jax.ShapeDtypeStruct(shape, BF),
            jax.ShapeDtypeStruct((2,) + shape, F32),
        ]
        + [jax.ShapeDtypeStruct((rows, width), BF)] * seqs,
        scratch_shapes=[
            pltpu.VMEM((2 * seqs * rows, KW * c_in), BF),
            pltpu.VMEM((seqs * rows, 1), F32),
            pltpu.VMEM(shape, BF),
        ],
        compiler_params=params(STREAMING_LIMIT),
        cost_estimate=COST,
        name="encoder_forward",
    )(at, pairs, low, high, conv_weight, norm_gain.reshape(1, width))
    return outs[0], outs[1], list(outs[2:])


def d_conv_kernel(at_ref, own_ref, near_ref, far_ref, *refs):
    skip_ref, grad_ref, gain_ref, slope_ref = refs[:4]
    out_ref, first_ref, last_ref = refs[-3:]
    rows = out_ref.shape[2]
    for slot, (ref, place) in enumerate(((own_ref, 0), (near_ref, 0), (far_ref, 0), (far_ref, 1))):
        b = at_ref[0] ^ slot
        wide = skip_ref[b].astype(F32)
        inv = lax.rsqrt(jnp.mean(wide * wide, axis=-1, keepdims=True) + 1e-06)
        unit = wide * inv
        scaled = ref[place].astype(F32) * gain_ref[...]
        d_skip = grad_ref[b].astype(F32) + inv * (
            scaled - unit * jnp.mean(scaled * unit, axis=-1, keepdims=True)
        )
        d_act = 0.5 * d_skip
        for parity in range(2):
            value = slope_ref[parity, b] * d_act
            out_ref[parity, b] = value.astype(BF)
            first_ref[parity, b] = value[:1].astype(BF)
            last_ref[parity, b] = value[rows - 1 :].astype(BF)


def conv_gradient(at, own, near, far, skip, grad, norm_gain, slope, *deps):
    vmem = pl.BlockSpec(memory_space=pltpu.VMEM)
    edge = jax.ShapeDtypeStruct(slope.shape[:2] + (1, slope.shape[3]), BF)
    return pl.pallas_call(
        d_conv_kernel,
        in_specs=[SCALARS] + [vmem] * 7 + spare(deps),
        out_specs=[vmem] * 3,
        out_shape=[jax.ShapeDtypeStruct(slope.shape, BF)] + [edge] * 2,
        compiler_params=params(),
        cost_estimate=COST,
        name="conv_gradient",
    )(at, own, near, far, skip, grad, norm_gain.reshape(1, -1), slope, *deps)


def mixed_body(seqs, at_ref, *refs):
    skip_ref, out_ref = refs[seqs], refs[-1]
    for slot in range(seqs):
        b = at_ref[0] ^ slot
        out_ref[b] = (skip_ref[b].astype(F32) + refs[slot][...].astype(F32)).astype(BF)


def mixed_call(at, terms, skip, *deps):
    seqs = len(terms)
    vmem = pl.BlockSpec(memory_space=pltpu.VMEM)
    return pl.pallas_call(
        functools.partial(mixed_body, seqs),
        in_specs=[SCALARS] + [vmem] * (seqs + 1) + spare(deps),
        out_specs=vmem,
        out_shape=jax.ShapeDtypeStruct(skip.shape, BF),
        compiler_params=params(),
        cost_estimate=COST,
        name="mixed_sum",
    )(at, *terms, skip, *deps)


def marker_kernel(*refs):
    refs[-1][...] = jnp.zeros_like(refs[-1])


def marker(*deps):
    return pl.pallas_call(
        marker_kernel,
        in_specs=spare(deps),
        out_shape=TOKEN,
        compiler_params=params(),
        cost_estimate=COST,
        name="marker",
    )(*deps)


def conv_back_kernel(d_ref, low_ref, high_ref, w_ref, *rest):
    out_ref, turned, acc = rest[-3:]
    step = pl.program_id(0)

    @pl.when(step == 0)
    def _():
        for parity in range(2):
            for shift in range(3):
                turned[parity, shift] = turned_rows(d_ref, low_ref, high_ref, parity, shift).T

    for tap in range(KW):

        @pl.when(step == tap)
        def _():
            places = [KW - 1 - tap, KW - tap]
            rhs = jnp.concatenate([turned[p % 2, p // 2] for p in places], axis=1)
            term = dot(w_ref[0], rhs, NN)
            if tap == 0:
                acc[...] = term
            elif tap < KW - 1:
                acc[...] += term
            else:
                out_ref[...] = (acc[...] + term).T.astype(BF)


def conv_back(d_conv, low, high, conv_weight, *deps):
    _, seqs, rows, width = d_conv.shape
    c_in = conv_weight.shape[1]
    flat = 2 * seqs * rows
    return pl.pallas_call(
        conv_back_kernel,
        grid=(KW,),
        in_specs=[
            whole(d_conv.shape),
            whole(low.shape),
            whole(high.shape),
            pl.BlockSpec((1, c_in, width), lambda k: (k, 0, 0)),
        ]
        + spare(deps),
        out_specs=whole((flat, c_in)),
        out_shape=jax.ShapeDtypeStruct((flat, c_in), BF),
        scratch_shapes=[
            pltpu.VMEM((2, 3, width, seqs * rows), BF),
            pltpu.VMEM((c_in, flat), F32),
        ],
        compiler_params=params(),
        cost_estimate=COST,
        name="encoder_backward",
    )(d_conv, low, high, conv_weight, *deps)


def pack_kernel(w_ref, pack_ref, turned_ref, token_ref):
    token_ref[...] = jnp.zeros_like(token_ref)
    for i in range(3):
        for head in range(pack_ref.shape[0]):
            part = w_ref[i, :, head * DH : (head + 1) * DH]
            columns = slice(i * DH, (i + 1) * DH)
            pack_ref[head, :, columns] = part
            turned_ref[head, columns, :] = part.T


def pack_weights(w_qkv):
    _, width, local = w_qkv.shape
    heads = local // DH
    tile = local
    return pl.pallas_call(
        pack_kernel,
        grid=(width // tile,),
        in_specs=[pl.BlockSpec((3, tile, local), lambda n: (0, n, 0))],
        out_specs=[
            pl.BlockSpec((heads, tile, 3 * DH), lambda n: (0, n, 0)),
            pl.BlockSpec((heads, 3 * DH, tile), lambda n: (0, 0, n)),
            pl.BlockSpec(TOKEN.shape, lambda n: (0, 0)),
        ],
        out_shape=[
            jax.ShapeDtypeStruct((heads, width, 3 * DH), BF),
            jax.ShapeDtypeStruct((heads, 3 * DH, width), BF),
            TOKEN,
        ],
        compiler_params=params(),
        cost_estimate=COST,
        name="pack_weights",
    )(w_qkv)


def product_kernel(head_ref, x_ref, w_ref, *rest, contract):
    del head_ref
    out_ref, token_ref = rest[-2:]
    token_ref[...] = jnp.zeros_like(token_ref)
    value = dot(x_ref[...], w_ref[0], contract).astype(BF)
    out_ref[:, : value.shape[1]] = value
    if value.shape[1] < out_ref.shape[1]:
        out_ref[:, value.shape[1] :] = jnp.zeros_like(out_ref[:, value.shape[1] :])


def head_product(head, x, weight, contract, name, *deps):
    columns = weight.shape[2] if contract == NN else weight.shape[1]
    columns += -columns % 128
    rows, width = x.shape
    return pl.pallas_call(
        functools.partial(product_kernel, contract=contract),
        grid_spec=pltpu.PrefetchScalarGridSpec(
            num_scalar_prefetch=1,
            grid=(1,),
            in_specs=[
                pl.BlockSpec((rows, width), lambda i, head: (0, 0)),
                pl.BlockSpec((1,) + weight.shape[1:], lambda i, head: (head[0], 0, 0)),
            ]
            + spare(deps),
            out_specs=[
                pl.BlockSpec((rows, columns), lambda i, head: (0, 0)),
                pl.BlockSpec(TOKEN.shape, lambda i, head: (0, 0)),
            ],
        ),
        out_shape=[jax.ShapeDtypeStruct((rows, columns), BF), TOKEN],
        compiler_params=params(),
        cost_estimate=COST,
        name=name,
    )(head, x, weight, *deps)


def attention_kernel(qa_ref, qb_ref, da_ref, db_ref, *rest, block):
    oa_ref, ob_ref, k_all, v_all, dk_acc, dv_acc = rest[-6:]
    scale = DH ** (-0.5)
    half = qa_ref.shape[0]
    for place, ref in enumerate((qa_ref, qb_ref)):
        rows = pl.ds(place * half, half)
        k_all[rows, :] = ref[:, DH : 2 * DH]
        v_all[rows, :] = ref[:, 2 * DH : 3 * DH]
    k = k_all[...]
    v = v_all[...]
    for place, (q_ref, d_ref, out_ref) in enumerate(
        ((qa_ref, da_ref, oa_ref), (qb_ref, db_ref, ob_ref))
    ):
        for start in range(0, half, block):
            rows = pl.ds(start, block)
            q = q_ref[rows, 0:DH]
            d_o = d_ref[rows, 0:DH]
            s = dot(q, k, NT) * scale
            e = jnp.exp(s - jnp.max(s, axis=-1, keepdims=True))
            p = e * (1.0 / jnp.sum(e, axis=-1, keepdims=True))
            p_b = p.astype(BF)
            o = dot(p_b, v, NN)
            delta = jnp.sum(d_o.astype(F32) * o, axis=-1, keepdims=True)
            d_p = dot(d_o, v, NT)
            ds = (p * (d_p - delta)).astype(BF)
            dq = scale * dot(ds, k, NN)
            dk = dot(ds, q, TN)
            dv = dot(p_b, d_o, TN)
            if place == 0 and start == 0:
                dk_acc[...] = dk
                dv_acc[...] = dv
            else:
                dk_acc[...] += dk
                dv_acc[...] += dv
            out_ref[rows, 0:DH] = dq.astype(BF)
            out_ref[rows, 3 * DH : 4 * DH] = o.astype(BF)
    for place, out_ref in enumerate((oa_ref, ob_ref)):
        rows = pl.ds(place * half, half)
        out_ref[:, DH : 2 * DH] = (scale * dk_acc[rows, :]).astype(BF)
        out_ref[:, 2 * DH : 3 * DH] = dv_acc[rows, :].astype(BF)


def attention(qkv_a, qkv_b, d_a, d_b, *deps):
    half = qkv_a.shape[0]
    shape = jax.ShapeDtypeStruct((half, 4 * DH), BF)
    return pl.pallas_call(
        functools.partial(attention_kernel, block=min(256, half)),
        in_specs=[pl.BlockSpec(memory_space=pltpu.VMEM)] * 4 + spare(deps),
        out_shape=[shape, shape],
        scratch_shapes=[
            pltpu.VMEM((2 * half, DH), BF),
            pltpu.VMEM((2 * half, DH), BF),
            pltpu.VMEM((2 * half, DH), F32),
            pltpu.VMEM((2 * half, DH), F32),
        ],
        compiler_params=params(),
        cost_estimate=COST,
        name="attention",
    )(qkv_a, qkv_b, d_a, d_b, *deps)


def term_kernel(head_ref, a_ref, b_ref, w_ref, *rest, first, last):
    head = head_ref[0]
    total = dot(a_ref[:, first:last], w_ref[head], NN)
    total += dot(b_ref[:, first:last], w_ref[1 - head], NN)
    rest[-1][...] = total.astype(BF)


def pair_term(head, mine, got, weight, first, last, name, *deps):
    half, full = mine.shape
    heads, depth, width = weight.shape
    tile = 512 if width % 512 == 0 else width
    return pl.pallas_call(
        functools.partial(term_kernel, first=first, last=last),
        grid_spec=pltpu.PrefetchScalarGridSpec(
            num_scalar_prefetch=1,
            grid=(width // tile,),
            in_specs=[
                pl.BlockSpec((half, full), lambda n, at: (0, 0)),
                pl.BlockSpec((half, full), lambda n, at: (0, 0)),
                pl.BlockSpec((heads, depth, tile), lambda n, at: (0, 0, n)),
            ]
            + spare(deps),
            out_specs=pl.BlockSpec((half, tile), lambda n, at: (0, n)),
        ),
        out_shape=jax.ShapeDtypeStruct((half, width), BF),
        compiler_params=params(),
        cost_estimate=COST,
        name=name,
    )(head, mine, got, weight, *deps)


def part_kernel(head_ref, x_ref, w_ref, *rest, last):
    del head_ref
    total = dot(x_ref[:, :last], w_ref[0], NN)
    if len(rest) > 1:
        total += rest[0][...]
    rest[-1][...] = total.astype(rest[-1].dtype)


def term_part(head, x, weight, last, name, *before):
    half, full = x.shape
    _, depth, width = weight.shape
    tile = 512 if width % 512 == 0 else width
    column = pl.BlockSpec((half, tile), lambda n, at: (0, n))
    return pl.pallas_call(
        functools.partial(part_kernel, last=last),
        grid_spec=pltpu.PrefetchScalarGridSpec(
            num_scalar_prefetch=1,
            grid=(width // tile,),
            in_specs=[
                pl.BlockSpec((half, full), lambda n, at: (0, 0)),
                pl.BlockSpec((1, depth, tile), lambda n, at: (at[0], 0, n)),
            ]
            + [column] * len(before),
            out_specs=column,
        ),
        out_shape=jax.ShapeDtypeStruct((half, width), BF if before else F32),
        compiler_params=params(),
        cost_estimate=COST,
        name=name,
    )(head, x, weight, *before)


def weight_kernel(at_ref, xa_ref, xb_ref, ga_ref, gb_ref, ra_ref, rb_ref, *rest):
    del at_ref
    out_refs, turned = rest[:-1], rest[-1]
    step = pl.program_id(0)
    half = ra_ref.shape[0]
    split = 3 * DH

    @pl.when(step == 0)
    def _():
        turned[:, :half] = ra_ref[...].T
        turned[:, half:] = rb_ref[...].T

    a, b = slice(0, half), slice(half, 2 * half)
    qkv = dot(turned[:split, a], xa_ref[...], NN) + dot(turned[:split, b], xb_ref[...], NN)
    out = dot(turned[split:, a], ga_ref[...], NN) + dot(turned[split:, b], gb_ref[...], NN)
    keep_a, send_a, keep_b, send_b = out_refs
    rows = keep_a.shape[1]
    for slot in range(4):

        @pl.when(step == slot)
        def _():
            first = keep_a if slot % 2 == 0 else send_a
            second = keep_b if slot < 2 else send_b
            first[slot // 2] = qkv[:rows].astype(BF)
            second[slot % 2, : split - rows] = qkv[rows:].astype(BF)
            second[slot % 2, split - rows :] = out.astype(BF)


def weight_gradients(at, xa, xb, ga, gb, ra, rb, seqs):
    half, width = xa.shape
    chunk = width // seqs
    full = ra.shape[1]
    column = pl.BlockSpec((half, chunk), lambda r, at: (0, r ^ at[0]))
    rest = pl.BlockSpec((half, full), lambda r, at: (0, 0))
    return pl.pallas_call(
        weight_kernel,
        grid_spec=pltpu.PrefetchScalarGridSpec(
            num_scalar_prefetch=1,
            grid=(seqs,),
            in_specs=[column] * 4 + [rest] * 2,
            out_specs=[pl.BlockSpec((2, full // 2, chunk), lambda r, at: (0, 0, 0))] * 4,
            scratch_shapes=[pltpu.VMEM((full, 2 * half), BF)],
        ),
        out_shape=[jax.ShapeDtypeStruct((2, full // 2, chunk), BF)] * 4,
        compiler_params=params(STREAMING_LIMIT),
        cost_estimate=COST,
        name="weight_gradients",
    )(at, xa, xb, ga, gb, ra, rb)


def turn_kernel(keep_a, got_a, keep_b, got_b, *rest):
    out_a, out_b = rest[-2:]
    for keep, got, out in ((keep_a, got_a, out_a), (keep_b, got_b, out_b)):
        out[...] = (keep[1].astype(F32) + got[1].astype(F32)).astype(BF)


def weight_turn(keep_a, got_a, keep_b, got_b, *deps):
    shape = jax.ShapeDtypeStruct(keep_a.shape[1:], BF)
    return pl.pallas_call(
        turn_kernel,
        in_specs=[pl.BlockSpec(memory_space=pltpu.VMEM)] * 4 + spare(deps),
        out_shape=[shape, shape],
        compiler_params=params(),
        cost_estimate=COST,
        name="weight_turn",
    )(keep_a, got_a, keep_b, got_b, *deps)


def weight_sum_kernel(keep_a, got_a, last_a, keep_b, got_b, last_b, *rest):
    out_refs = rest[-2:]
    split = 3 * DH
    parts = [
        keep[0].astype(F32) + got[0].astype(F32) + last[...].astype(F32)
        for keep, got, last in ((keep_a, got_a, last_a), (keep_b, got_b, last_b))
    ]
    total = jnp.concatenate(parts, axis=0)
    turned = total[:split].T.astype(BF)
    quarter = DH // 2
    for part, out_ref in enumerate(out_refs):
        out_ref[:, :split] = turned[part * DH : (part + 1) * DH]
        first = split + part * quarter
        piece = total[first : first + quarter].astype(BF)
        out_ref[:quarter, split:] = piece[:, :DH]
        out_ref[quarter:, split:] = piece[:, DH:]


def weight_sum(keep_a, got_a, last_a, keep_b, got_b, last_b, *deps):
    _, rows, chunk = keep_a.shape
    return pl.pallas_call(
        weight_sum_kernel,
        in_specs=[pl.BlockSpec(memory_space=pltpu.VMEM)] * 6 + spare(deps),
        out_shape=[jax.ShapeDtypeStruct((chunk // 2, 2 * rows), BF)] * 2,
        compiler_params=params(),
        cost_estimate=COST,
        name="weight_sum",
    )(keep_a, got_a, last_a, keep_b, got_b, last_b, *deps)


def unpack_kernel(at_ref, *refs):
    qkv_ref, out_ref, token_ref = refs[-3:]
    step = pl.program_id(0)
    split = 3 * DH
    quarter = DH // 2
    token_ref[...] = jnp.zeros_like(token_ref)
    for half in range(2):

        @pl.when(step // 2 == half)
        def _():
            mine = refs[half][...].astype(F32)
            other = refs[2 + half][...].astype(F32)
            swapped = at_ref[1] != 0
            low = jnp.where(swapped, other, mine)
            high = jnp.where(swapped, mine, other)
            for i in range(3):
                columns = slice(i * DH, (i + 1) * DH)
                qkv_ref[i] = jnp.concatenate([low[:, columns], high[:, columns]], axis=1)
            for head, value in enumerate((low, high)):
                folded = [value[:quarter, split:], value[quarter:, split:]]
                out_ref[head, 0] = jnp.concatenate(folded, axis=1)


def unpack_weights(at, mine, other, far, before=(), *deps):
    rows, full = mine[0].shape
    half = rows // 2
    width = 4 * rows

    def chunk(t, at):
        if far:
            return at[0] ^ jnp.where(t < 2, t + 2, 2 * t - 3)
        return at[0] ^ jnp.where(t < 2, t, 2 * t - 4)

    specs = [
        pl.BlockSpec((half, full), lambda t, at: (jnp.minimum(t, 1), 0)),
        pl.BlockSpec((half, full), lambda t, at: (jnp.maximum(t - 2, 0), 0)),
    ]
    return pl.pallas_call(
        unpack_kernel,
        grid_spec=pltpu.PrefetchScalarGridSpec(
            num_scalar_prefetch=1,
            grid=(4,),
            in_specs=specs * 2 + spare(tuple(before) + deps),
            out_specs=[
                pl.BlockSpec((3, half, 2 * DH), lambda t, at: (0, 2 * chunk(t, at) + t // 2, 0)),
                pl.BlockSpec(
                    (2, 1, DH // 2, rows), lambda t, at: (0, t // 2, 0, chunk(t, at))
                ),
                pl.BlockSpec(TOKEN.shape, lambda t, at: (0, 0)),
            ],
        ),
        out_shape=[
            jax.ShapeDtypeStruct((3, width, 2 * DH), F32),
            jax.ShapeDtypeStruct((2, 2, DH // 2, width), F32),
            TOKEN,
        ],
        input_output_aliases={5 + i: i for i in range(len(before))},
        compiler_params=params(),
        cost_estimate=COST,
        name="weight_outputs_far" if far else "weight_outputs_near",
    )(at, *mine, *other, *before, *deps)


def neighbour_edges(first, last):
    axes = ("seq", "head")
    count = lax.axis_size(axes)
    forward = [(i, i + 1) for i in range(count - 1)]
    backward = [(target, source) for source, target in forward]
    return lax.ppermute(last, axes, forward), lax.ppermute(first, axes, backward)


def after(value, *others):
    return lax.optimization_barrier((value,) + others)[0]


def trade_chip(x, bit, heads):
    count = lax.axis_size("seq")
    return lax.ppermute(x, "seq", [(s, s ^ (bit * heads)) for s in range(count)])


def swap_heads(x):
    count = lax.axis_size("seq")
    return lax.ppermute(x, "seq", [(s, s + 1 - 2 * (s % 2)) for s in range(count)])


def unit_body(enc_in, conv_weight, norm_gain, w_qkv, w_out, grad_out):
    rows = enc_in.shape[0] // 2
    seqs = enc_in.shape[1]
    width = conv_weight.shape[2]
    local = w_qkv.shape[2]
    heads = local // DH
    groups = lax.axis_size("head")
    half = groups * seqs * rows
    place = lax.axis_index("seq")
    own_seq = (place // heads).astype(jnp.int32)
    own_head = (place % heads).astype(jnp.int32)
    at = jnp.stack([own_seq, own_head])
    head_mine = own_head.reshape(1)
    head_other = (1 - own_head).reshape(1)

    def to_chips(slots):
        return [x if j == 0 else trade_chip(x, j, heads) for j, x in enumerate(slots)]

    order = (0, 2, 1, 3)

    grad_z = lax.all_gather(grad_out, "head", axis=0, tiled=False)

    pairs = jnp.transpose(enc_in.reshape(rows, 2, seqs, enc_in.shape[2]), (1, 2, 0, 3))
    low, high = neighbour_edges(pairs[:, :, :1, :], pairs[:, :, -1:, :])
    skip, slope, normed = encoder(at, pairs, low, high, conv_weight, norm_gain)
    normed = to_chips(normed)
    normed_slab = jnp.concatenate([normed[j] for j in order], axis=0)
    normed_rows = lax.all_gather(normed_slab, "head", axis=0, tiled=True)

    grad_z = after(grad_z, normed_slab)
    grad_slots = to_chips(
        [lax.dynamic_index_in_dim(grad_z, own_seq ^ j, 2, keepdims=False) for j in range(seqs)]
    )
    grad_rows = jnp.stack([grad_slots[j] for j in order], axis=1).reshape(half, width)
    w_pack, w_turned, packed = pack_weights(after(w_qkv, normed_slab))
    w_rows = w_out.reshape(heads, DH, width)
    d_other, one = head_product(head_other, grad_rows, w_rows, NT, "d_o_other")
    d_got = swap_heads(d_other)
    d_mine, two = head_product(head_mine, grad_rows, w_rows, NT, "d_o_own")
    grad_swapped = swap_heads(grad_rows)
    normed_rows, d_got, d_mine, grad_swapped, w_pack, w_turned, *tokens = (
        lax.optimization_barrier(
            (normed_rows, d_got, d_mine, grad_swapped, w_pack, w_turned, packed, one, two)
        )
    )

    normed_swapped = swap_heads(normed_rows)
    qkv_other, _ = head_product(head_other, normed_rows, w_pack, NN, "qkv_other", *tokens)
    qkv_got = swap_heads(qkv_other)
    qkv_mine, _ = head_product(head_mine, normed_rows, w_pack, NN, "qkv_own")
    result_mine, result_other = attention(qkv_mine, qkv_got, d_mine, d_got, normed_swapped)
    result_got = swap_heads(result_other)

    shape = (groups, seqs, rows, width)
    d_own = term_part(head_mine, result_mine, w_turned, 3 * DH, "d_term_own")
    d_term = term_part(head_other, result_got, w_turned, 3 * DH, "d_term", d_own)
    d_normed = lax.psum_scatter(d_term.reshape(shape), "head", scatter_dimension=0, tiled=False)
    keep_a, send_a, keep_b, send_b = weight_gradients(
        own_seq.reshape(1),
        normed_rows,
        normed_swapped,
        grad_rows,
        grad_swapped,
        result_mine,
        result_other,
        seqs,
    )
    got_a, got_b = trade_chip(send_a, 1, heads), trade_chip(send_b, 2, heads)
    head_term = pair_term(
        head_mine, result_mine, result_got, w_rows, 3 * DH, 4 * DH, "head_term"
    )
    head_sum = lax.psum_scatter(head_term.reshape(shape), "head", scatter_dimension=0, tiled=False)
    turn_a, turn_b = weight_turn(keep_a, got_a, keep_b, got_b, head_term)
    last_a, last_b = trade_chip(turn_a, 2, heads), trade_chip(turn_b, 1, heads)

    d_normed = after(d_normed, turn_a, turn_b)
    leaving = d_normed[2:]
    near = trade_chip(leaving, 1, heads)
    far = trade_chip(jnp.stack([d_normed[1], near[1]]), 2, heads)
    half_a, half_b = weight_sum(keep_a, got_a, last_a, keep_b, got_b, last_b, leaving)
    grad = jnp.transpose(after(grad_out, d_term), (1, 0, 2))
    d_conv, first, last = conv_gradient(
        at, d_normed, near, far, skip, grad, norm_gain, slope, half_a
    )
    low, high = neighbour_edges(first, last)
    low, high, at_hand = lax.optimization_barrier((low, high, marker(conv_weight, first)))

    got_a, got_b = trade_chip(half_a, 1, heads), trade_chip(half_b, 2, heads)
    near_a = jnp.concatenate([half_a, after(got_a, low)], axis=0)
    near_b = jnp.concatenate([half_b, after(got_b, high)], axis=0)
    far_a = trade_chip(near_a, 2, heads)
    far_b = trade_chip(near_b, 1, heads)
    near_other = [swap_heads(near_a), swap_heads(near_b)]
    grad_input = conv_back(d_conv, low, high, conv_weight, at_hand, *near_other)
    *outputs, token = unpack_weights(
        at, [near_a, near_b], near_other, False, (), grad_input
    )

    head_sum = after(head_sum, grad_input, token)
    head_sum = to_chips([head_sum[order.index(j)] for j in range(seqs)])
    far_other = [swap_heads(after(x, *head_sum[1:])) for x in (far_a, far_b)]
    grad_w_qkv, grad_w_out, _ = unpack_weights(at, [far_a, far_b], far_other, True, outputs)
    mixed = mixed_call(at, head_sum, skip, token)
    grad_input = jnp.transpose(grad_input.reshape(2, seqs, rows, -1), (2, 0, 1, 3))
    return (
        jnp.transpose(mixed, (1, 0, 2)),
        grad_input.reshape(enc_in.shape),
        grad_w_qkv,
        grad_w_out.reshape(local, width),
    )


def padded_2(block, sides, width):
    for axis, dim in sides:
        count = lax.axis_size(axis)
        forward = [(i, i + 1) for i in range(count - 1)]
        backward = [(target, source) for source, target in forward]
        low = lax.ppermute(
            lax.slice_in_dim(block, block.shape[dim] - width, None, axis=dim), axis, forward
        )
        high = lax.ppermute(lax.slice_in_dim(block, 0, width, axis=dim), axis, backward)
        block = jnp.concatenate([low, block, high], axis=dim)
    return block


def gathered_body(enc_in, conv_weight, norm_gain, w_qkv, w_out, grad_out):
    fine_rows = enc_in.shape[0]
    slab_rows = fine_rows // 2
    seq_count = enc_in.shape[1]
    out_width = conv_weight.shape[2]
    local_width = w_qkv.shape[2]
    local_heads = local_width // DH
    logit_scale = DH ** (-0.5)
    padded = padded_2(enc_in, ((("seq", "head"), 0),), 2)
    convolved = jnp.zeros((fine_rows, seq_count, out_width), jnp.float32)
    for offset in range(KW):
        convolved = convolved + jnp.einsum(
            "tbi,io->tbo",
            padded[offset : offset + fine_rows],
            conv_weight[offset],
            preferred_element_type=jnp.float32,
        )
    activated, gelu_pull = jax.vjp(jax.nn.gelu, convolved)
    skip = jnp.mean(activated.reshape(slab_rows, 2, seq_count, out_width), axis=1).astype(
        jnp.bfloat16
    )
    skip_wide = skip.astype(jnp.float32)
    inv_rms = lax.rsqrt(jnp.mean(skip_wide * skip_wide, axis=-1, keepdims=True) + 1e-06)
    normed = (skip_wide * inv_rms * norm_gain).astype(jnp.bfloat16)
    normed_rows = lax.all_gather(normed, "head", axis=0, tiled=True)
    grad_rows = lax.all_gather(grad_out, "head", axis=0, tiled=True)
    tower_rows = normed_rows.shape[0]
    qkv = jnp.einsum(
        "tbc,ice->itbe", normed_rows, w_qkv, preferred_element_type=jnp.float32
    ).astype(jnp.bfloat16)
    qkv = qkv.reshape(3, tower_rows, seq_count, local_heads, DH)
    query_matrix, key_matrix, value_matrix = (qkv[0], qkv[1], qkv[2])
    key_all, value_all = (
        lax.all_gather(key_matrix, "seq", axis=0, tiled=True),
        lax.all_gather(value_matrix, "seq", axis=0, tiled=True),
    )
    attention_logits = (
        jnp.einsum("qbhd,kbhd->bhqk", query_matrix, key_all, preferred_element_type=jnp.float32)
        * logit_scale
    )
    row_peak = jnp.max(attention_logits, axis=-1, keepdims=True)
    exponent = jnp.exp(attention_logits - row_peak)
    row_total = jnp.sum(exponent, axis=-1, keepdims=True)
    soft_weights = exponent / row_total
    narrow_probabilities = soft_weights.astype(jnp.bfloat16)
    attention_output = jnp.einsum(
        "bhqk,kbhd->qbhd", narrow_probabilities, value_all, preferred_element_type=jnp.float32
    )
    o_narrow = attention_output.reshape(tower_rows, seq_count, local_width).astype(jnp.bfloat16)
    piece = o_narrow
    head_sum = lax.psum_scatter(
        jnp.einsum("tbe,ec->tbc", piece, w_out, preferred_element_type=jnp.float32).astype(
            jnp.bfloat16
        ),
        "head",
        scatter_dimension=0,
        tiled=True,
    ).astype(jnp.float32)
    mixed = (skip_wide + head_sum).astype(jnp.bfloat16)
    part_w_out = jnp.einsum("tbe,tbc->ec", o_narrow, grad_rows, preferred_element_type=jnp.float32)
    d_out = jnp.einsum("tbc,ec->tbe", grad_rows, w_out, preferred_element_type=jnp.float32).astype(
        jnp.bfloat16
    )
    d_out = d_out.reshape(tower_rows, seq_count, local_heads, DH)
    delta = jnp.sum(d_out.astype(jnp.float32) * attention_output, axis=-1)
    probability_gradient = jnp.einsum(
        "qbhd,kbhd->bhqk", d_out, value_all, preferred_element_type=jnp.float32
    )
    d_scores = soft_weights * (probability_gradient - jnp.transpose(delta, (1, 2, 0))[..., None])
    narrow_gradient = d_scores.astype(jnp.bfloat16)
    query_gradient = logit_scale * jnp.einsum(
        "bhqk,kbhd->qbhd", narrow_gradient, key_all, preferred_element_type=jnp.float32
    )
    key_terms = logit_scale * jnp.einsum(
        "bhqk,qbhd->kbhd", narrow_gradient, query_matrix, preferred_element_type=jnp.float32
    )
    value_terms = jnp.einsum(
        "bhqk,qbhd->kbhd", narrow_probabilities, d_out, preferred_element_type=jnp.float32
    )
    d_keys, d_values = (
        lax.psum_scatter(
            key_terms.astype(jnp.bfloat16), "seq", scatter_dimension=0, tiled=True
        ).astype(jnp.float32),
        lax.psum_scatter(
            value_terms.astype(jnp.bfloat16), "seq", scatter_dimension=0, tiled=True
        ).astype(jnp.float32),
    )
    dqkv = (
        jnp.stack([query_gradient, d_keys, d_values])
        .reshape(3, tower_rows, seq_count, local_width)
        .astype(jnp.bfloat16)
    )
    part_w_qkv = jnp.einsum("tbc,itbe->ice", normed_rows, dqkv, preferred_element_type=jnp.float32)
    piece = dqkv
    d_normed = lax.psum_scatter(
        jnp.einsum("itbe,ice->tbc", piece, w_qkv, preferred_element_type=jnp.float32).astype(
            jnp.bfloat16
        ),
        "head",
        scatter_dimension=0,
        tiled=True,
    ).astype(jnp.float32)
    unit_rows = skip_wide * inv_rms
    scaled = d_normed * norm_gain
    d_skip = grad_out.astype(jnp.float32) + inv_rms * (
        scaled - unit_rows * jnp.mean(scaled * unit_rows, axis=-1, keepdims=True)
    )
    d_act = jnp.repeat(d_skip, 2, axis=0) * 0.5
    d_conv = gelu_pull(d_act)[0].astype(jnp.bfloat16)
    d_pad = padded_2(d_conv, ((("seq", "head"), 0),), 2)
    grad_input = jnp.zeros((fine_rows, seq_count, enc_in.shape[2]), jnp.float32)
    for offset in range(KW):
        grad_input = grad_input + jnp.einsum(
            "tbo,io->tbi",
            d_pad[4 - offset : 4 - offset + fine_rows],
            conv_weight[offset],
            preferred_element_type=jnp.float32,
        )
    grad_w_qkv, grad_w_out = (
        lax.psum(part_w_qkv.astype(jnp.bfloat16), "seq").astype(jnp.float32),
        lax.psum(part_w_out.astype(jnp.bfloat16), "seq").astype(jnp.float32),
    )
    return (mixed, grad_input.astype(jnp.bfloat16), grad_w_qkv, grad_w_out)


def body(enc_in, conv_weight, norm_gain, w_qkv, w_out, grad_out):
    heads = w_qkv.shape[2] // DH
    seqs = enc_in.shape[1]
    fits = heads == 2 and seqs == 4 and seqs * heads == lax.axis_size("seq")
    fits = fits and conv_weight.shape[2] == seqs * w_qkv.shape[2]
    chosen = unit_body if fits else gathered_body
    return chosen(enc_in, conv_weight, norm_gain, w_qkv, w_out, grad_out)


def solution(mesh):
    return jax.shard_map(
        body,
        mesh=mesh,
        in_specs=(
            P(("seq", "head"), None, None),
            P(),
            P(),
            P(None, None, "head"),
            P("head", None),
            P(("seq", "head"), None, None),
        ),
        out_specs=(
            P(("seq", "head"), None, None),
            P(("seq", "head"), None, None),
            P(None, None, "head"),
            P("head", None),
        ),
        check_vma=False,
    )
```

```python
import functools

import jax
import jax.numpy as jnp
from jax import lax
from jax.experimental import pallas as pl
from jax.experimental.pallas import tpu as pltpu
from jax.sharding import PartitionSpec as P

DH = 192
KW = 5
VMEM_LIMIT = 24 * 1024 * 1024
STREAMING_LIMIT = 56 * 1024 * 1024
COST = pl.CostEstimate(flops=1000, bytes_accessed=1000, transcendentals=0)
BF = jnp.bfloat16
F32 = jnp.float32
TOKEN = jax.ShapeDtypeStruct((8, 128), F32)


def params(limit=VMEM_LIMIT):
    return pltpu.CompilerParams(vmem_limit_bytes=limit)


def dot(a, b, contract):
    return lax.dot_general(a, b, (contract, ((), ())), preferred_element_type=F32)


NN = ((1,), (0,))
NT = ((1,), (1,))
TN = ((0,), (0,))


def whole(shape):
    return pl.BlockSpec(shape, lambda *_: (0,) * len(shape))


SCALARS = pl.BlockSpec(memory_space=pltpu.SMEM)


def spare(deps):
    return [pl.BlockSpec(memory_space=pl.ANY)] * len(deps)


def turned_rows(ref, low_ref, high_ref, parity, shift):
    seqs, rows, width = ref.shape[1:]
    own = ref[parity]
    if shift != 1:
        wide = own.astype(F32)
        if shift == 0:
            parts = [low_ref[parity].astype(F32), wide[:, : rows - 1]]
        else:
            parts = [wide[:, 1:], high_ref[parity].astype(F32)]
        own = jnp.concatenate(parts, axis=1).astype(BF)
    return own.reshape(seqs * rows, width)


def conv_kernel(
    at_ref, x_ref, low_ref, high_ref, w_ref, gain_ref, skip_ref, slope_ref, *rest
):
    normed_refs, (lhs, squares, whole_normed) = rest[:-3], rest[-3:]
    step = pl.program_id(0)
    seqs, rows, c_in = x_ref.shape[1:]
    half = seqs * rows
    tile = w_ref.shape[2]

    @pl.when(step == 0)
    def _():
        for parity in range(2):
            for shift in range(3):
                value = turned_rows(x_ref, low_ref, high_ref, parity, shift)
                for out in range(2):
                    tap = 2 * shift + parity - out
                    if 0 <= tap < KW:
                        lhs[out * half : (out + 1) * half, tap * c_in : (tap + 1) * c_in] = value
        squares[...] = jnp.zeros_like(squares)

    conv = dot(lhs[...], w_ref[...].reshape(KW * c_in, tile), NN)
    root = 0.7978845608028654
    total = None
    for parity in range(2):
        x = conv[parity * half : (parity + 1) * half, :]
        square = x * x
        t = jnp.tanh(root * (x + 0.044715 * (square * x)))
        left = 0.5 * (1.0 + t)
        act = x * left
        slope = left + (0.5 * root) * x * (1.0 - t * t) * (1.0 + (3 * 0.044715) * square)
        slope_ref[parity] = slope.reshape(slope_ref.shape[1:])
        total = act if total is None else total + act
    skip = (0.5 * total).astype(BF)
    columns = pl.ds(pl.multiple_of(step * tile, tile), tile)
    skip_ref[:, :, columns] = skip.reshape(seqs, rows, tile)
    wide = skip.astype(F32)
    squares[...] += jnp.sum(wide * wide, axis=-1, keepdims=True)

    @pl.when(step == pl.num_programs(0) - 1)
    def _():
        width = skip_ref.shape[2]
        inv = lax.rsqrt(squares[...] * (1.0 / width) + 1e-06)
        wide = skip_ref[...].reshape(half, width).astype(F32)
        normed = (wide * inv * gain_ref[...]).astype(BF)
        whole_normed[...] = normed.reshape(whole_normed.shape)
        for slot in range(seqs):
            normed_refs[slot][...] = whole_normed[at_ref[0] ^ slot]


def encoder(at, pairs, low, high, conv_weight, norm_gain):
    _, seqs, rows, c_in = pairs.shape
    width = conv_weight.shape[2]
    tile = 256 if width % 256 == 0 else width
    shape = (seqs, rows, width)
    outs = pl.pallas_call(
        conv_kernel,
        grid=(width // tile,),
        in_specs=[
            SCALARS,
            whole(pairs.shape),
            whole(low.shape),
            whole(high.shape),
            pl.BlockSpec((KW, c_in, tile), lambda n: (0, 0, n)),
            whole((1, width)),
        ],
        out_specs=[
            whole(shape),
            pl.BlockSpec((2, seqs, rows, tile), lambda n: (0, 0, 0, n)),
        ]
        + [whole((rows, width))] * seqs,
        out_shape=[
            jax.ShapeDtypeStruct(shape, BF),
            jax.ShapeDtypeStruct((2,) + shape, F32),
        ]
        + [jax.ShapeDtypeStruct((rows, width), BF)] * seqs,
        scratch_shapes=[
            pltpu.VMEM((2 * seqs * rows, KW * c_in), BF),
            pltpu.VMEM((seqs * rows, 1), F32),
            pltpu.VMEM(shape, BF),
        ],
        compiler_params=params(STREAMING_LIMIT),
        cost_estimate=COST,
        name="encoder_forward",
    )(at, pairs, low, high, conv_weight, norm_gain.reshape(1, width))
    return outs[0], outs[1], list(outs[2:])


def d_conv_kernel(at_ref, own_ref, near_ref, far_ref, *refs):
    skip_ref, grad_ref, gain_ref, slope_ref = refs[:4]
    out_ref, first_ref, last_ref = refs[-3:]
    rows = out_ref.shape[2]
    for slot, (ref, place) in enumerate(((own_ref, 0), (near_ref, 0), (far_ref, 0), (far_ref, 1))):
        b = at_ref[0] ^ slot
        wide = skip_ref[b].astype(F32)
        inv = lax.rsqrt(jnp.mean(wide * wide, axis=-1, keepdims=True) + 1e-06)
        unit = wide * inv
        scaled = ref[place].astype(F32) * gain_ref[...]
        d_skip = grad_ref[b].astype(F32) + inv * (
            scaled - unit * jnp.mean(scaled * unit, axis=-1, keepdims=True)
        )
        d_act = 0.5 * d_skip
        for parity in range(2):
            value = slope_ref[parity, b] * d_act
            out_ref[parity, b] = value.astype(BF)
            first_ref[parity, b] = value[:1].astype(BF)
            last_ref[parity, b] = value[rows - 1 :].astype(BF)


def conv_gradient(at, own, near, far, skip, grad, norm_gain, slope, *deps):
    vmem = pl.BlockSpec(memory_space=pltpu.VMEM)
    edge = jax.ShapeDtypeStruct(slope.shape[:2] + (1, slope.shape[3]), BF)
    return pl.pallas_call(
        d_conv_kernel,
        in_specs=[SCALARS] + [vmem] * 7 + spare(deps),
        out_specs=[vmem] * 3,
        out_shape=[jax.ShapeDtypeStruct(slope.shape, BF)] + [edge] * 2,
        compiler_params=params(),
        cost_estimate=COST,
        name="conv_gradient",
    )(at, own, near, far, skip, grad, norm_gain.reshape(1, -1), slope, *deps)


def mixed_body(seqs, at_ref, *refs):
    skip_ref, out_ref = refs[seqs], refs[-1]
    for slot in range(seqs):
        b = at_ref[0] ^ slot
        out_ref[b] = (skip_ref[b].astype(F32) + refs[slot][...].astype(F32)).astype(BF)


def mixed_call(at, terms, skip, *deps):
    seqs = len(terms)
    vmem = pl.BlockSpec(memory_space=pltpu.VMEM)
    return pl.pallas_call(
        functools.partial(mixed_body, seqs),
        in_specs=[SCALARS] + [vmem] * (seqs + 1) + spare(deps),
        out_specs=vmem,
        out_shape=jax.ShapeDtypeStruct(skip.shape, BF),
        compiler_params=params(),
        cost_estimate=COST,
        name="mixed_sum",
    )(at, *terms, skip, *deps)


def marker_kernel(*refs):
    refs[-1][...] = jnp.zeros_like(refs[-1])


def marker(*deps):
    return pl.pallas_call(
        marker_kernel,
        in_specs=spare(deps),
        out_shape=TOKEN,
        compiler_params=params(),
        cost_estimate=COST,
        name="marker",
    )(*deps)


def conv_back_kernel(d_ref, low_ref, high_ref, w_ref, *rest):
    out_ref, turned, acc = rest[-3:]
    step = pl.program_id(0)

    @pl.when(step == 0)
    def _():
        for parity in range(2):
            for shift in range(3):
                turned[parity, shift] = turned_rows(d_ref, low_ref, high_ref, parity, shift).T

    for tap in range(KW):

        @pl.when(step == tap)
        def _():
            places = [KW - 1 - tap, KW - tap]
            rhs = jnp.concatenate([turned[p % 2, p // 2] for p in places], axis=1)
            term = dot(w_ref[0], rhs, NN)
            if tap == 0:
                acc[...] = term
            elif tap < KW - 1:
                acc[...] += term
            else:
                out_ref[...] = (acc[...] + term).T.astype(BF)


def conv_back(d_conv, low, high, conv_weight, *deps):
    _, seqs, rows, width = d_conv.shape
    c_in = conv_weight.shape[1]
    flat = 2 * seqs * rows
    return pl.pallas_call(
        conv_back_kernel,
        grid=(KW,),
        in_specs=[
            whole(d_conv.shape),
            whole(low.shape),
            whole(high.shape),
            pl.BlockSpec((1, c_in, width), lambda k: (k, 0, 0)),
        ]
        + spare(deps),
        out_specs=whole((flat, c_in)),
        out_shape=jax.ShapeDtypeStruct((flat, c_in), BF),
        scratch_shapes=[
            pltpu.VMEM((2, 3, width, seqs * rows), BF),
            pltpu.VMEM((c_in, flat), F32),
        ],
        compiler_params=params(),
        cost_estimate=COST,
        name="encoder_backward",
    )(d_conv, low, high, conv_weight, *deps)


def pack_kernel(w_ref, pack_ref, turned_ref, token_ref):
    token_ref[...] = jnp.zeros_like(token_ref)
    for i in range(3):
        for head in range(pack_ref.shape[0]):
            part = w_ref[i, :, head * DH : (head + 1) * DH]
            columns = slice(i * DH, (i + 1) * DH)
            pack_ref[head, :, columns] = part
            turned_ref[head, columns, :] = part.T


def pack_weights(w_qkv):
    _, width, local = w_qkv.shape
    heads = local // DH
    tile = local
    return pl.pallas_call(
        pack_kernel,
        grid=(width // tile,),
        in_specs=[pl.BlockSpec((3, tile, local), lambda n: (0, n, 0))],
        out_specs=[
            pl.BlockSpec((heads, tile, 3 * DH), lambda n: (0, n, 0)),
            pl.BlockSpec((heads, 3 * DH, tile), lambda n: (0, 0, n)),
            pl.BlockSpec(TOKEN.shape, lambda n: (0, 0)),
        ],
        out_shape=[
            jax.ShapeDtypeStruct((heads, width, 3 * DH), BF),
            jax.ShapeDtypeStruct((heads, 3 * DH, width), BF),
            TOKEN,
        ],
        compiler_params=params(),
        cost_estimate=COST,
        name="pack_weights",
    )(w_qkv)


def product_kernel(head_ref, x_ref, w_ref, *rest, contract):
    del head_ref
    out_ref, token_ref = rest[-2:]
    token_ref[...] = jnp.zeros_like(token_ref)
    value = dot(x_ref[...], w_ref[0], contract).astype(BF)
    out_ref[:, : value.shape[1]] = value
    if value.shape[1] < out_ref.shape[1]:
        out_ref[:, value.shape[1] :] = jnp.zeros_like(out_ref[:, value.shape[1] :])


def head_product(head, x, weight, contract, name, *deps):
    columns = weight.shape[2] if contract == NN else weight.shape[1]
    columns += -columns % 128
    rows, width = x.shape
    return pl.pallas_call(
        functools.partial(product_kernel, contract=contract),
        grid_spec=pltpu.PrefetchScalarGridSpec(
            num_scalar_prefetch=1,
            grid=(1,),
            in_specs=[
                pl.BlockSpec((rows, width), lambda i, head: (0, 0)),
                pl.BlockSpec((1,) + weight.shape[1:], lambda i, head: (head[0], 0, 0)),
            ]
            + spare(deps),
            out_specs=[
                pl.BlockSpec((rows, columns), lambda i, head: (0, 0)),
                pl.BlockSpec(TOKEN.shape, lambda i, head: (0, 0)),
            ],
        ),
        out_shape=[jax.ShapeDtypeStruct((rows, columns), BF), TOKEN],
        compiler_params=params(),
        cost_estimate=COST,
        name=name,
    )(head, x, weight, *deps)


def split_product_kernel(head_ref, xa_ref, xb_ref, w_ref, *rest):
    del head_ref
    out_ref = rest[-1]
    cut = xa_ref.shape[1]
    value = dot(xa_ref[...], w_ref[0, :cut], NN) + dot(xb_ref[...], w_ref[0, cut:], NN)
    out_ref[:, : value.shape[1]] = value.astype(BF)
    out_ref[:, value.shape[1] :] = jnp.zeros_like(out_ref[:, value.shape[1] :])


def split_product(head, xa, xb, weight, name, *deps):
    columns = weight.shape[2]
    columns += -columns % 128
    rows = xa.shape[0]
    return pl.pallas_call(
        split_product_kernel,
        grid_spec=pltpu.PrefetchScalarGridSpec(
            num_scalar_prefetch=1,
            grid=(1,),
            in_specs=[
                pl.BlockSpec(xa.shape, lambda i, head: (0, 0)),
                pl.BlockSpec(xb.shape, lambda i, head: (0, 0)),
                pl.BlockSpec((1,) + weight.shape[1:], lambda i, head: (head[0], 0, 0)),
            ]
            + spare(deps),
            out_specs=pl.BlockSpec((rows, columns), lambda i, head: (0, 0)),
        ),
        out_shape=jax.ShapeDtypeStruct((rows, columns), BF),
        compiler_params=params(),
        cost_estimate=COST,
        name=name,
    )(head, xa, xb, weight, *deps)


def place_kernel(at_ref, *refs):
    del at_ref
    for slot, ref in enumerate(refs[:-1]):

        @pl.when(pl.program_id(0) == slot)
        def _():
            refs[-1][...] = ref[...]


def placed(at, slots, name):
    count = len(slots)
    rows, width = slots[0].shape
    return pl.pallas_call(
        place_kernel,
        grid_spec=pltpu.PrefetchScalarGridSpec(
            num_scalar_prefetch=1,
            grid=(count,),
            in_specs=[pl.BlockSpec((rows, width), lambda q, at: (0, 0))] * count,
            out_specs=pl.BlockSpec((rows, width), lambda q, at: (q ^ at[0], 0)),
        ),
        out_shape=jax.ShapeDtypeStruct((count * rows, width), slots[0].dtype),
        compiler_params=params(),
        cost_estimate=COST,
        name=name,
    )(at, *slots)


def attention_kernel(qa_ref, qb_ref, da_ref, db_ref, *rest, block):
    oa_ref, ob_ref, k_all, v_all, dk_acc, dv_acc = rest[-6:]
    scale = DH ** (-0.5)
    half = qa_ref.shape[0]
    for place, ref in enumerate((qa_ref, qb_ref)):
        rows = pl.ds(place * half, half)
        k_all[rows, :] = ref[:, DH : 2 * DH]
        v_all[rows, :] = ref[:, 2 * DH : 3 * DH]
    k = k_all[...]
    v = v_all[...]
    for place, (q_ref, d_ref, out_ref) in enumerate(
        ((qa_ref, da_ref, oa_ref), (qb_ref, db_ref, ob_ref))
    ):
        for start in range(0, half, block):
            rows = pl.ds(start, block)
            q = q_ref[rows, 0:DH]
            d_o = d_ref[rows, 0:DH]
            s = dot(q, k, NT) * scale
            e = jnp.exp(s - jnp.max(s, axis=-1, keepdims=True))
            p = e * (1.0 / jnp.sum(e, axis=-1, keepdims=True))
            p_b = p.astype(BF)
            o = dot(p_b, v, NN)
            delta = jnp.sum(d_o.astype(F32) * o, axis=-1, keepdims=True)
            d_p = dot(d_o, v, NT)
            ds = (p * (d_p - delta)).astype(BF)
            dq = scale * dot(ds, k, NN)
            dk = dot(ds, q, TN)
            dv = dot(p_b, d_o, TN)
            if place == 0 and start == 0:
                dk_acc[...] = dk
                dv_acc[...] = dv
            else:
                dk_acc[...] += dk
                dv_acc[...] += dv
            out_ref[rows, 0:DH] = dq.astype(BF)
            out_ref[rows, 3 * DH : 4 * DH] = o.astype(BF)
    for place, out_ref in enumerate((oa_ref, ob_ref)):
        rows = pl.ds(place * half, half)
        out_ref[:, DH : 2 * DH] = (scale * dk_acc[rows, :]).astype(BF)
        out_ref[:, 2 * DH : 3 * DH] = dv_acc[rows, :].astype(BF)


def attention(qkv_a, qkv_b, d_a, d_b, *deps):
    half = qkv_a.shape[0]
    shape = jax.ShapeDtypeStruct((half, 4 * DH), BF)
    return pl.pallas_call(
        functools.partial(attention_kernel, block=min(256, half)),
        in_specs=[pl.BlockSpec(memory_space=pltpu.VMEM)] * 4 + spare(deps),
        out_shape=[shape, shape],
        scratch_shapes=[
            pltpu.VMEM((2 * half, DH), BF),
            pltpu.VMEM((2 * half, DH), BF),
            pltpu.VMEM((2 * half, DH), F32),
            pltpu.VMEM((2 * half, DH), F32),
        ],
        compiler_params=params(),
        cost_estimate=COST,
        name="attention",
    )(qkv_a, qkv_b, d_a, d_b, *deps)


def term_kernel(head_ref, a_ref, b_ref, w_ref, *rest, first, last):
    head = head_ref[0]
    total = dot(a_ref[:, first:last], w_ref[head], NN)
    total += dot(b_ref[:, first:last], w_ref[1 - head], NN)
    rest[-1][...] = total.astype(BF)


def pair_term(head, mine, got, weight, first, last, name, *deps):
    half, full = mine.shape
    heads, depth, width = weight.shape
    tile = 512 if width % 512 == 0 else width
    return pl.pallas_call(
        functools.partial(term_kernel, first=first, last=last),
        grid_spec=pltpu.PrefetchScalarGridSpec(
            num_scalar_prefetch=1,
            grid=(width // tile,),
            in_specs=[
                pl.BlockSpec((half, full), lambda n, at: (0, 0)),
                pl.BlockSpec((half, full), lambda n, at: (0, 0)),
                pl.BlockSpec((heads, depth, tile), lambda n, at: (0, 0, n)),
            ]
            + spare(deps),
            out_specs=pl.BlockSpec((half, tile), lambda n, at: (0, n)),
        ),
        out_shape=jax.ShapeDtypeStruct((half, width), BF),
        compiler_params=params(),
        cost_estimate=COST,
        name=name,
    )(head, mine, got, weight, *deps)


def part_kernel(head_ref, x_ref, w_ref, *rest, last):
    del head_ref
    total = dot(x_ref[:, :last], w_ref[0], NN)
    if len(rest) > 1:
        total += rest[0][...]
    rest[-1][...] = total.astype(rest[-1].dtype)


def term_part(head, x, weight, last, name, *before):
    half, full = x.shape
    _, depth, width = weight.shape
    tile = 512 if width % 512 == 0 else width
    column = pl.BlockSpec((half, tile), lambda n, at: (0, n))
    return pl.pallas_call(
        functools.partial(part_kernel, last=last),
        grid_spec=pltpu.PrefetchScalarGridSpec(
            num_scalar_prefetch=1,
            grid=(width // tile,),
            in_specs=[
                pl.BlockSpec((half, full), lambda n, at: (0, 0)),
                pl.BlockSpec((1, depth, tile), lambda n, at: (at[0], 0, n)),
            ]
            + [column] * len(before),
            out_specs=column,
        ),
        out_shape=jax.ShapeDtypeStruct((half, width), BF if before else F32),
        compiler_params=params(),
        cost_estimate=COST,
        name=name,
    )(head, x, weight, *before)


def weight_kernel(
    at_ref, xa_ref, ya_ref, xb_ref, yb_ref, ga_ref, gb_ref, ra_ref, rb_ref, *rest
):
    out_refs, turned = rest[:-1], rest[-1]
    step = pl.program_id(0)
    last = (step ^ at_ref[0]) == pl.num_programs(0) - 1
    xa = jnp.where(last, ya_ref[...], xa_ref[...])
    xb = jnp.where(last, yb_ref[...], xb_ref[...])
    half = ra_ref.shape[0]
    split = 3 * DH

    @pl.when(step == 0)
    def _():
        turned[:, :half] = ra_ref[...].T
        turned[:, half:] = rb_ref[...].T

    a, b = slice(0, half), slice(half, 2 * half)
    qkv = dot(turned[:split, a], xa, NN) + dot(turned[:split, b], xb, NN)
    out = dot(turned[split:, a], ga_ref[...], NN) + dot(turned[split:, b], gb_ref[...], NN)
    keep_a, send_a, keep_b, send_b = out_refs
    rows = keep_a.shape[1]
    for slot in range(4):

        @pl.when(step == slot)
        def _():
            first = keep_a if slot % 2 == 0 else send_a
            second = keep_b if slot < 2 else send_b
            first[slot // 2] = qkv[:rows].astype(BF)
            second[slot % 2, : split - rows] = qkv[rows:].astype(BF)
            second[slot % 2, split - rows :] = out.astype(BF)


def weight_gradients(at, xa, ya, xb, yb, ga, gb, ra, rb, seqs):
    half, width = ga.shape
    chunk = width // seqs
    full = ra.shape[1]
    some = pl.BlockSpec((half, chunk), lambda r, at: (0, jnp.minimum(r ^ at[0], seqs - 2)))
    only = pl.BlockSpec((half, chunk), lambda r, at: (0, 0))
    column = pl.BlockSpec((half, chunk), lambda r, at: (0, r ^ at[0]))
    rest = pl.BlockSpec((half, full), lambda r, at: (0, 0))
    return pl.pallas_call(
        weight_kernel,
        grid_spec=pltpu.PrefetchScalarGridSpec(
            num_scalar_prefetch=1,
            grid=(seqs,),
            in_specs=[some, only] * 2 + [column] * 2 + [rest] * 2,
            out_specs=[pl.BlockSpec((2, full // 2, chunk), lambda r, at: (0, 0, 0))] * 4,
            scratch_shapes=[pltpu.VMEM((full, 2 * half), BF)],
        ),
        out_shape=[jax.ShapeDtypeStruct((2, full // 2, chunk), BF)] * 4,
        compiler_params=params(STREAMING_LIMIT),
        cost_estimate=COST,
        name="weight_gradients",
    )(at, xa, ya, xb, yb, ga, gb, ra, rb)


def turn_kernel(keep_a, got_a, keep_b, got_b, *rest):
    out_a, out_b = rest[-2:]
    for keep, got, out in ((keep_a, got_a, out_a), (keep_b, got_b, out_b)):
        out[...] = (keep[1].astype(F32) + got[1].astype(F32)).astype(BF)


def weight_turn(keep_a, got_a, keep_b, got_b, *deps):
    shape = jax.ShapeDtypeStruct(keep_a.shape[1:], BF)
    return pl.pallas_call(
        turn_kernel,
        in_specs=[pl.BlockSpec(memory_space=pltpu.VMEM)] * 4 + spare(deps),
        out_shape=[shape, shape],
        compiler_params=params(),
        cost_estimate=COST,
        name="weight_turn",
    )(keep_a, got_a, keep_b, got_b, *deps)


def weight_sum_kernel(keep_a, got_a, last_a, keep_b, got_b, last_b, *rest):
    out_refs = rest[-2:]
    split = 3 * DH
    parts = [
        keep[0].astype(F32) + got[0].astype(F32) + last[...].astype(F32)
        for keep, got, last in ((keep_a, got_a, last_a), (keep_b, got_b, last_b))
    ]
    total = jnp.concatenate(parts, axis=0)
    turned = total[:split].T.astype(BF)
    quarter = DH // 2
    for part, out_ref in enumerate(out_refs):
        out_ref[:, :split] = turned[part * DH : (part + 1) * DH]
        first = split + part * quarter
        piece = total[first : first + quarter].astype(BF)
        out_ref[:quarter, split:] = piece[:, :DH]
        out_ref[quarter:, split:] = piece[:, DH:]


def weight_sum(keep_a, got_a, last_a, keep_b, got_b, last_b, *deps):
    _, rows, chunk = keep_a.shape
    return pl.pallas_call(
        weight_sum_kernel,
        in_specs=[pl.BlockSpec(memory_space=pltpu.VMEM)] * 6 + spare(deps),
        out_shape=[jax.ShapeDtypeStruct((chunk // 2, 2 * rows), BF)] * 2,
        compiler_params=params(),
        cost_estimate=COST,
        name="weight_sum",
    )(keep_a, got_a, last_a, keep_b, got_b, last_b, *deps)


def unpack_kernel(at_ref, *refs):
    qkv_ref, out_ref, token_ref = refs[-3:]
    step = pl.program_id(0)
    split = 3 * DH
    quarter = DH // 2
    token_ref[...] = jnp.zeros_like(token_ref)
    for half in range(2):

        @pl.when(step // 2 == half)
        def _():
            mine = refs[half][...].astype(F32)
            other = refs[2 + half][...].astype(F32)
            swapped = at_ref[1] != 0
            low = jnp.where(swapped, other, mine)
            high = jnp.where(swapped, mine, other)
            for i in range(3):
                columns = slice(i * DH, (i + 1) * DH)
                qkv_ref[i] = jnp.concatenate([low[:, columns], high[:, columns]], axis=1)
            for head, value in enumerate((low, high)):
                folded = [value[:quarter, split:], value[quarter:, split:]]
                out_ref[head, 0] = jnp.concatenate(folded, axis=1)


def unpack_weights(at, mine, other, far, before=(), *deps):
    rows, full = mine[0].shape
    half = rows // 2
    width = 4 * rows

    def chunk(t, at):
        if far:
            return at[0] ^ jnp.where(t < 2, t + 2, 2 * t - 3)
        return at[0] ^ jnp.where(t < 2, t, 2 * t - 4)

    specs = [
        pl.BlockSpec((half, full), lambda t, at: (jnp.minimum(t, 1), 0)),
        pl.BlockSpec((half, full), lambda t, at: (jnp.maximum(t - 2, 0), 0)),
    ]
    return pl.pallas_call(
        unpack_kernel,
        grid_spec=pltpu.PrefetchScalarGridSpec(
            num_scalar_prefetch=1,
            grid=(4,),
            in_specs=specs * 2 + spare(tuple(before) + deps),
            out_specs=[
                pl.BlockSpec((3, half, 2 * DH), lambda t, at: (0, 2 * chunk(t, at) + t // 2, 0)),
                pl.BlockSpec(
                    (2, 1, DH // 2, rows), lambda t, at: (0, t // 2, 0, chunk(t, at))
                ),
                pl.BlockSpec(TOKEN.shape, lambda t, at: (0, 0)),
            ],
        ),
        out_shape=[
            jax.ShapeDtypeStruct((3, width, 2 * DH), F32),
            jax.ShapeDtypeStruct((2, 2, DH // 2, width), F32),
            TOKEN,
        ],
        input_output_aliases={5 + i: i for i in range(len(before))},
        compiler_params=params(),
        cost_estimate=COST,
        name="weight_outputs_far" if far else "weight_outputs_near",
    )(at, *mine, *other, *before, *deps)


def neighbour_edges(first, last):
    axes = ("seq", "head")
    count = lax.axis_size(axes)
    forward = [(i, i + 1) for i in range(count - 1)]
    backward = [(target, source) for source, target in forward]
    return lax.ppermute(last, axes, forward), lax.ppermute(first, axes, backward)


def after(value, *others):
    return lax.optimization_barrier((value,) + others)[0]


def trade_chip(x, bit, heads):
    count = lax.axis_size("seq")
    return lax.ppermute(x, "seq", [(s, s ^ (bit * heads)) for s in range(count)])


def trade_z(x, bit):
    count = lax.axis_size("head")
    return lax.ppermute(x, "head", [(z, z ^ bit) for z in range(count)])


def swap_heads(x):
    count = lax.axis_size("seq")
    return lax.ppermute(x, "seq", [(s, s + 1 - 2 * (s % 2)) for s in range(count)])


def unit_body(enc_in, conv_weight, norm_gain, w_qkv, w_out, grad_out):
    rows = enc_in.shape[0] // 2
    seqs = enc_in.shape[1]
    width = conv_weight.shape[2]
    local = w_qkv.shape[2]
    heads = local // DH
    groups = lax.axis_size("head")
    half = groups * seqs * rows
    place = lax.axis_index("seq")
    own_seq = (place // heads).astype(jnp.int32)
    own_head = (place % heads).astype(jnp.int32)
    at = jnp.stack([own_seq, own_head])
    head_mine = own_head.reshape(1)
    head_other = (1 - own_head).reshape(1)

    def to_chips(slots):
        return [x if j == 0 else trade_chip(x, j, heads) for j, x in enumerate(slots)]

    order = (0, 2, 1, 3)

    grad_z = lax.all_gather(grad_out, "head", axis=0, tiled=False)

    pairs = jnp.transpose(enc_in.reshape(rows, 2, seqs, enc_in.shape[2]), (1, 2, 0, 3))
    low, high = neighbour_edges(pairs[:, :, :1, :], pairs[:, :, -1:, :])
    w_pack, w_turned, packed = pack_weights(w_qkv)
    low, high, packed = lax.optimization_barrier((low, high, packed))
    skip, slope, normed = encoder(at, pairs, low, high, conv_weight, norm_gain)
    normed = to_chips(normed)
    edge = width - width // seqs
    slab_a = jnp.concatenate([normed[j][:, :edge] for j in order], axis=0)
    slab_b = jnp.concatenate([normed[j][:, edge:] for j in order], axis=0)
    normed_a = lax.all_gather(slab_a, "head", axis=0, tiled=True)
    slabs_b = [slab_b if q == 0 else trade_z(slab_b, q) for q in range(groups)]
    normed_b = placed(lax.axis_index("head").astype(jnp.int32).reshape(1), slabs_b, "normed_last")

    grad_z = after(grad_z, slab_a, *slabs_b[1:])
    grad_slots = to_chips(
        [lax.dynamic_index_in_dim(grad_z, own_seq ^ j, 2, keepdims=False) for j in range(seqs)]
    )
    grad_rows = jnp.stack([grad_slots[j] for j in order], axis=1).reshape(half, width)
    w_rows = w_out.reshape(heads, DH, width)
    d_other, one = head_product(head_other, grad_rows, w_rows, NT, "d_o_other")
    d_got = swap_heads(d_other)
    d_mine, two = head_product(head_mine, grad_rows, w_rows, NT, "d_o_own")
    grad_swapped = swap_heads(grad_rows)
    normed_a, normed_b, d_got, d_mine, grad_swapped, w_pack, w_turned, *tokens = (
        lax.optimization_barrier(
            (normed_a, normed_b, d_got, d_mine, grad_swapped, w_pack, w_turned, packed, one, two)
        )
    )

    swapped_a, swapped_b = swap_heads(normed_a), swap_heads(normed_b)
    qkv_other = split_product(head_other, normed_a, normed_b, w_pack, "qkv_other", *tokens)
    qkv_got = swap_heads(qkv_other)
    qkv_mine = split_product(head_mine, normed_a, normed_b, w_pack, "qkv_own")
    result_mine, result_other = attention(
        qkv_mine, qkv_got, d_mine, d_got, swapped_a, swapped_b
    )
    result_got = swap_heads(result_other)

    shape = (groups, seqs, rows, width)
    d_own = term_part(head_mine, result_mine, w_turned, 3 * DH, "d_term_own")
    d_term = term_part(head_other, result_got, w_turned, 3 * DH, "d_term", d_own)
    d_normed = lax.psum_scatter(d_term.reshape(shape), "head", scatter_dimension=0, tiled=False)
    keep_a, send_a, keep_b, send_b = weight_gradients(
        own_seq.reshape(1),
        normed_a,
        normed_b,
        swapped_a,
        swapped_b,
        grad_rows,
        grad_swapped,
        result_mine,
        result_other,
        seqs,
    )
    got_a, got_b = trade_chip(send_a, 1, heads), trade_chip(send_b, 2, heads)
    head_term = pair_term(
        head_mine, result_mine, result_got, w_rows, 3 * DH, 4 * DH, "head_term"
    )
    head_sum = lax.psum_scatter(head_term.reshape(shape), "head", scatter_dimension=0, tiled=False)
    turn_a, turn_b = weight_turn(keep_a, got_a, keep_b, got_b, head_term)
    last_a, last_b = trade_chip(turn_a, 2, heads), trade_chip(turn_b, 1, heads)

    d_normed = after(d_normed, turn_a, turn_b)
    leaving = d_normed[2:]
    near = trade_chip(leaving, 1, heads)
    far = trade_chip(jnp.stack([d_normed[1], near[1]]), 2, heads)
    half_a, half_b = weight_sum(keep_a, got_a, last_a, keep_b, got_b, last_b, leaving)
    grad = jnp.transpose(after(grad_out, d_term), (1, 0, 2))
    d_conv, first, last = conv_gradient(
        at, d_normed, near, far, skip, grad, norm_gain, slope, half_a
    )
    low, high = neighbour_edges(first, last)
    low, high, at_hand = lax.optimization_barrier((low, high, marker(conv_weight, first)))

    got_a, got_b = trade_chip(half_a, 1, heads), trade_chip(half_b, 2, heads)
    near_a = jnp.concatenate([half_a, after(got_a, low)], axis=0)
    near_b = jnp.concatenate([half_b, after(got_b, high)], axis=0)
    far_a = trade_chip(near_a, 2, heads)
    far_b = trade_chip(near_b, 1, heads)
    near_other = [swap_heads(near_a), swap_heads(near_b)]
    grad_input = conv_back(d_conv, low, high, conv_weight, at_hand, *near_other)
    *outputs, token = unpack_weights(
        at, [near_a, near_b], near_other, False, (), grad_input
    )

    head_sum = after(head_sum, grad_input)
    head_sum = to_chips([head_sum[order.index(j)] for j in range(seqs)])
    far_other = [swap_heads(after(x, *head_sum[1:])) for x in (far_a, far_b)]
    grad_w_qkv, grad_w_out, _ = unpack_weights(at, [far_a, far_b], far_other, True, outputs)
    mixed = mixed_call(at, head_sum, skip, token)
    grad_input = jnp.transpose(grad_input.reshape(2, seqs, rows, -1), (2, 0, 1, 3))
    return (
        jnp.transpose(mixed, (1, 0, 2)),
        grad_input.reshape(enc_in.shape),
        grad_w_qkv,
        grad_w_out.reshape(local, width),
    )


def padded_2(block, sides, width):
    for axis, dim in sides:
        count = lax.axis_size(axis)
        forward = [(i, i + 1) for i in range(count - 1)]
        backward = [(target, source) for source, target in forward]
        low = lax.ppermute(
            lax.slice_in_dim(block, block.shape[dim] - width, None, axis=dim), axis, forward
        )
        high = lax.ppermute(lax.slice_in_dim(block, 0, width, axis=dim), axis, backward)
        block = jnp.concatenate([low, block, high], axis=dim)
    return block


def gathered_body(enc_in, conv_weight, norm_gain, w_qkv, w_out, grad_out):
    fine_rows = enc_in.shape[0]
    slab_rows = fine_rows // 2
    seq_count = enc_in.shape[1]
    out_width = conv_weight.shape[2]
    local_width = w_qkv.shape[2]
    local_heads = local_width // DH
    logit_scale = DH ** (-0.5)
    padded = padded_2(enc_in, ((("seq", "head"), 0),), 2)
    convolved = jnp.zeros((fine_rows, seq_count, out_width), jnp.float32)
    for offset in range(KW):
        convolved = convolved + jnp.einsum(
            "tbi,io->tbo",
            padded[offset : offset + fine_rows],
            conv_weight[offset],
            preferred_element_type=jnp.float32,
        )
    activated, gelu_pull = jax.vjp(jax.nn.gelu, convolved)
    skip = jnp.mean(activated.reshape(slab_rows, 2, seq_count, out_width), axis=1).astype(
        jnp.bfloat16
    )
    skip_wide = skip.astype(jnp.float32)
    inv_rms = lax.rsqrt(jnp.mean(skip_wide * skip_wide, axis=-1, keepdims=True) + 1e-06)
    normed = (skip_wide * inv_rms * norm_gain).astype(jnp.bfloat16)
    normed_rows = lax.all_gather(normed, "head", axis=0, tiled=True)
    grad_rows = lax.all_gather(grad_out, "head", axis=0, tiled=True)
    tower_rows = normed_rows.shape[0]
    qkv = jnp.einsum(
        "tbc,ice->itbe", normed_rows, w_qkv, preferred_element_type=jnp.float32
    ).astype(jnp.bfloat16)
    qkv = qkv.reshape(3, tower_rows, seq_count, local_heads, DH)
    query_matrix, key_matrix, value_matrix = (qkv[0], qkv[1], qkv[2])
    key_all, value_all = (
        lax.all_gather(key_matrix, "seq", axis=0, tiled=True),
        lax.all_gather(value_matrix, "seq", axis=0, tiled=True),
    )
    attention_logits = (
        jnp.einsum("qbhd,kbhd->bhqk", query_matrix, key_all, preferred_element_type=jnp.float32)
        * logit_scale
    )
    row_peak = jnp.max(attention_logits, axis=-1, keepdims=True)
    exponent = jnp.exp(attention_logits - row_peak)
    row_total = jnp.sum(exponent, axis=-1, keepdims=True)
    soft_weights = exponent / row_total
    narrow_probabilities = soft_weights.astype(jnp.bfloat16)
    attention_output = jnp.einsum(
        "bhqk,kbhd->qbhd", narrow_probabilities, value_all, preferred_element_type=jnp.float32
    )
    o_narrow = attention_output.reshape(tower_rows, seq_count, local_width).astype(jnp.bfloat16)
    piece = o_narrow
    head_sum = lax.psum_scatter(
        jnp.einsum("tbe,ec->tbc", piece, w_out, preferred_element_type=jnp.float32).astype(
            jnp.bfloat16
        ),
        "head",
        scatter_dimension=0,
        tiled=True,
    ).astype(jnp.float32)
    mixed = (skip_wide + head_sum).astype(jnp.bfloat16)
    part_w_out = jnp.einsum("tbe,tbc->ec", o_narrow, grad_rows, preferred_element_type=jnp.float32)
    d_out = jnp.einsum("tbc,ec->tbe", grad_rows, w_out, preferred_element_type=jnp.float32).astype(
        jnp.bfloat16
    )
    d_out = d_out.reshape(tower_rows, seq_count, local_heads, DH)
    delta = jnp.sum(d_out.astype(jnp.float32) * attention_output, axis=-1)
    probability_gradient = jnp.einsum(
        "qbhd,kbhd->bhqk", d_out, value_all, preferred_element_type=jnp.float32
    )
    d_scores = soft_weights * (probability_gradient - jnp.transpose(delta, (1, 2, 0))[..., None])
    narrow_gradient = d_scores.astype(jnp.bfloat16)
    query_gradient = logit_scale * jnp.einsum(
        "bhqk,kbhd->qbhd", narrow_gradient, key_all, preferred_element_type=jnp.float32
    )
    key_terms = logit_scale * jnp.einsum(
        "bhqk,qbhd->kbhd", narrow_gradient, query_matrix, preferred_element_type=jnp.float32
    )
    value_terms = jnp.einsum(
        "bhqk,qbhd->kbhd", narrow_probabilities, d_out, preferred_element_type=jnp.float32
    )
    d_keys, d_values = (
        lax.psum_scatter(
            key_terms.astype(jnp.bfloat16), "seq", scatter_dimension=0, tiled=True
        ).astype(jnp.float32),
        lax.psum_scatter(
            value_terms.astype(jnp.bfloat16), "seq", scatter_dimension=0, tiled=True
        ).astype(jnp.float32),
    )
    dqkv = (
        jnp.stack([query_gradient, d_keys, d_values])
        .reshape(3, tower_rows, seq_count, local_width)
        .astype(jnp.bfloat16)
    )
    part_w_qkv = jnp.einsum("tbc,itbe->ice", normed_rows, dqkv, preferred_element_type=jnp.float32)
    piece = dqkv
    d_normed = lax.psum_scatter(
        jnp.einsum("itbe,ice->tbc", piece, w_qkv, preferred_element_type=jnp.float32).astype(
            jnp.bfloat16
        ),
        "head",
        scatter_dimension=0,
        tiled=True,
    ).astype(jnp.float32)
    unit_rows = skip_wide * inv_rms
    scaled = d_normed * norm_gain
    d_skip = grad_out.astype(jnp.float32) + inv_rms * (
        scaled - unit_rows * jnp.mean(scaled * unit_rows, axis=-1, keepdims=True)
    )
    d_act = jnp.repeat(d_skip, 2, axis=0) * 0.5
    d_conv = gelu_pull(d_act)[0].astype(jnp.bfloat16)
    d_pad = padded_2(d_conv, ((("seq", "head"), 0),), 2)
    grad_input = jnp.zeros((fine_rows, seq_count, enc_in.shape[2]), jnp.float32)
    for offset in range(KW):
        grad_input = grad_input + jnp.einsum(
            "tbo,io->tbi",
            d_pad[4 - offset : 4 - offset + fine_rows],
            conv_weight[offset],
            preferred_element_type=jnp.float32,
        )
    grad_w_qkv, grad_w_out = (
        lax.psum(part_w_qkv.astype(jnp.bfloat16), "seq").astype(jnp.float32),
        lax.psum(part_w_out.astype(jnp.bfloat16), "seq").astype(jnp.float32),
    )
    return (mixed, grad_input.astype(jnp.bfloat16), grad_w_qkv, grad_w_out)


def body(enc_in, conv_weight, norm_gain, w_qkv, w_out, grad_out):
    heads = w_qkv.shape[2] // DH
    seqs = enc_in.shape[1]
    fits = lax.axis_size("head") == 4 and heads == 2 and seqs == 4 and seqs * heads == lax.axis_size("seq")
    fits = fits and conv_weight.shape[2] == seqs * w_qkv.shape[2]
    chosen = unit_body if fits else gathered_body
    return chosen(enc_in, conv_weight, norm_gain, w_qkv, w_out, grad_out)


def solution(mesh):
    return jax.shard_map(
        body,
        mesh=mesh,
        in_specs=(
            P(("seq", "head"), None, None),
            P(),
            P(),
            P(None, None, "head"),
            P("head", None),
            P(("seq", "head"), None, None),
        ),
        out_specs=(
            P(("seq", "head"), None, None),
            P(("seq", "head"), None, None),
            P(None, None, "head"),
            P("head", None),
        ),
        check_vma=False,
    )
```

```python
import functools

import jax
import jax.numpy as jnp
from jax import lax
from jax.experimental import pallas as pl
from jax.experimental.pallas import tpu as pltpu
from jax.sharding import PartitionSpec as P

DH = 192
KW = 5
VMEM_LIMIT = 24 * 1024 * 1024
STREAMING_LIMIT = 56 * 1024 * 1024
COST = pl.CostEstimate(flops=1000, bytes_accessed=1000, transcendentals=0)
BF = jnp.bfloat16
F32 = jnp.float32
TOKEN = jax.ShapeDtypeStruct((8, 128), F32)


def params(limit=VMEM_LIMIT):
    return pltpu.CompilerParams(vmem_limit_bytes=limit)


def dot(a, b, contract):
    return lax.dot_general(a, b, (contract, ((), ())), preferred_element_type=F32)


NN = ((1,), (0,))
NT = ((1,), (1,))
TN = ((0,), (0,))


def whole(shape):
    return pl.BlockSpec(shape, lambda *_: (0,) * len(shape))


SCALARS = pl.BlockSpec(memory_space=pltpu.SMEM)


def spare(deps):
    return [pl.BlockSpec(memory_space=pl.ANY)] * len(deps)


def turned_rows(ref, low_ref, high_ref, parity, shift):
    seqs, rows, width = ref.shape[1:]
    own = ref[parity]
    if shift != 1:
        wide = own.astype(F32)
        if shift == 0:
            parts = [low_ref[parity].astype(F32), wide[:, : rows - 1]]
        else:
            parts = [wide[:, 1:], high_ref[parity].astype(F32)]
        own = jnp.concatenate(parts, axis=1).astype(BF)
    return own.reshape(seqs * rows, width)


def conv_kernel(
    at_ref, x_ref, low_ref, high_ref, w_ref, gain_ref, skip_ref, slope_ref, *rest
):
    normed_refs, (lhs, squares, whole_normed) = rest[:-3], rest[-3:]
    step = pl.program_id(0)
    seqs, rows, c_in = x_ref.shape[1:]
    half = seqs * rows
    tile = w_ref.shape[2]

    @pl.when(step == 0)
    def _():
        for parity in range(2):
            for shift in range(3):
                value = turned_rows(x_ref, low_ref, high_ref, parity, shift)
                for out in range(2):
                    tap = 2 * shift + parity - out
                    if 0 <= tap < KW:
                        lhs[out * half : (out + 1) * half, tap * c_in : (tap + 1) * c_in] = value
        squares[...] = jnp.zeros_like(squares)

    conv = dot(lhs[...], w_ref[...].reshape(KW * c_in, tile), NN)
    root = 0.7978845608028654
    total = None
    for parity in range(2):
        x = conv[parity * half : (parity + 1) * half, :]
        square = x * x
        t = jnp.tanh(root * (x + 0.044715 * (square * x)))
        left = 0.5 * (1.0 + t)
        act = x * left
        slope = left + (0.5 * root) * x * (1.0 - t * t) * (1.0 + (3 * 0.044715) * square)
        slope_ref[parity] = slope.reshape(slope_ref.shape[1:])
        total = act if total is None else total + act
    skip = (0.5 * total).astype(BF)
    columns = pl.ds(pl.multiple_of(step * tile, tile), tile)
    skip_ref[:, :, columns] = skip.reshape(seqs, rows, tile)
    wide = skip.astype(F32)
    squares[...] += jnp.sum(wide * wide, axis=-1, keepdims=True)

    @pl.when(step == pl.num_programs(0) - 1)
    def _():
        width = skip_ref.shape[2]
        inv = lax.rsqrt(squares[...] * (1.0 / width) + 1e-06)
        wide = skip_ref[...].reshape(half, width).astype(F32)
        normed = (wide * inv * gain_ref[...]).astype(BF)
        whole_normed[...] = normed.reshape(whole_normed.shape)
        for slot in range(seqs):
            normed_refs[slot][...] = whole_normed[at_ref[0] ^ slot]


def encoder(at, pairs, low, high, conv_weight, norm_gain):
    _, seqs, rows, c_in = pairs.shape
    width = conv_weight.shape[2]
    tile = 256 if width % 256 == 0 else width
    shape = (seqs, rows, width)
    outs = pl.pallas_call(
        conv_kernel,
        grid=(width // tile,),
        in_specs=[
            SCALARS,
            whole(pairs.shape),
            whole(low.shape),
            whole(high.shape),
            pl.BlockSpec((KW, c_in, tile), lambda n: (0, 0, n)),
            whole((1, width)),
        ],
        out_specs=[
            whole(shape),
            pl.BlockSpec((2, seqs, rows, tile), lambda n: (0, 0, 0, n)),
        ]
        + [whole((rows, width))] * seqs,
        out_shape=[
            jax.ShapeDtypeStruct(shape, BF),
            jax.ShapeDtypeStruct((2,) + shape, F32),
        ]
        + [jax.ShapeDtypeStruct((rows, width), BF)] * seqs,
        scratch_shapes=[
            pltpu.VMEM((2 * seqs * rows, KW * c_in), BF),
            pltpu.VMEM((seqs * rows, 1), F32),
            pltpu.VMEM(shape, BF),
        ],
        compiler_params=params(STREAMING_LIMIT),
        cost_estimate=COST,
        name="encoder_forward",
    )(at, pairs, low, high, conv_weight, norm_gain.reshape(1, width))
    return outs[0], outs[1], list(outs[2:])


def d_conv_kernel(at_ref, own_ref, near_ref, far_ref, *refs):
    skip_ref, grad_ref, gain_ref, slope_ref = refs[:4]
    out_ref, first_ref, last_ref = refs[-3:]
    rows = out_ref.shape[2]
    for slot, (ref, place) in enumerate(((own_ref, 0), (near_ref, 0), (far_ref, 0), (far_ref, 1))):
        b = at_ref[0] ^ slot
        wide = skip_ref[b].astype(F32)
        inv = lax.rsqrt(jnp.mean(wide * wide, axis=-1, keepdims=True) + 1e-06)
        unit = wide * inv
        scaled = ref[place].astype(F32) * gain_ref[...]
        d_skip = grad_ref[b].astype(F32) + inv * (
            scaled - unit * jnp.mean(scaled * unit, axis=-1, keepdims=True)
        )
        d_act = 0.5 * d_skip
        for parity in range(2):
            value = slope_ref[parity, b] * d_act
            out_ref[parity, b] = value.astype(BF)
            first_ref[parity, b] = value[:1].astype(BF)
            last_ref[parity, b] = value[rows - 1 :].astype(BF)


def conv_gradient(at, own, near, far, skip, grad, norm_gain, slope, *deps):
    vmem = pl.BlockSpec(memory_space=pltpu.VMEM)
    edge = jax.ShapeDtypeStruct(slope.shape[:2] + (1, slope.shape[3]), BF)
    return pl.pallas_call(
        d_conv_kernel,
        in_specs=[SCALARS] + [vmem] * 7 + spare(deps),
        out_specs=[vmem] * 3,
        out_shape=[jax.ShapeDtypeStruct(slope.shape, BF)] + [edge] * 2,
        compiler_params=params(),
        cost_estimate=COST,
        name="conv_gradient",
    )(at, own, near, far, skip, grad, norm_gain.reshape(1, -1), slope, *deps)


def mixed_body(seqs, at_ref, *refs):
    skip_ref, out_ref = refs[seqs], refs[-1]
    for slot in range(seqs):
        b = at_ref[0] ^ slot
        out_ref[b] = (skip_ref[b].astype(F32) + refs[slot][...].astype(F32)).astype(BF)


def mixed_call(at, terms, skip, *deps):
    seqs = len(terms)
    vmem = pl.BlockSpec(memory_space=pltpu.VMEM)
    return pl.pallas_call(
        functools.partial(mixed_body, seqs),
        in_specs=[SCALARS] + [vmem] * (seqs + 1) + spare(deps),
        out_specs=vmem,
        out_shape=jax.ShapeDtypeStruct(skip.shape, BF),
        compiler_params=params(),
        cost_estimate=COST,
        name="mixed_sum",
    )(at, *terms, skip, *deps)


def marker_kernel(*refs):
    refs[-1][...] = jnp.zeros_like(refs[-1])


def marker(*deps):
    return pl.pallas_call(
        marker_kernel,
        in_specs=spare(deps),
        out_shape=TOKEN,
        compiler_params=params(),
        cost_estimate=COST,
        name="marker",
    )(*deps)


def conv_back_kernel(d_ref, low_ref, high_ref, w_ref, *rest):
    out_ref, turned, acc = rest[-3:]
    step = pl.program_id(0)

    @pl.when(step == 0)
    def _():
        for parity in range(2):
            for shift in range(3):
                turned[parity, shift] = turned_rows(d_ref, low_ref, high_ref, parity, shift).T

    for tap in range(KW):

        @pl.when(step == tap)
        def _():
            places = [KW - 1 - tap, KW - tap]
            rhs = jnp.concatenate([turned[p % 2, p // 2] for p in places], axis=1)
            term = dot(w_ref[0], rhs, NN)
            if tap == 0:
                acc[...] = term
            elif tap < KW - 1:
                acc[...] += term
            else:
                out_ref[...] = (acc[...] + term).T.astype(BF)


def conv_back(d_conv, low, high, conv_weight, *deps):
    _, seqs, rows, width = d_conv.shape
    c_in = conv_weight.shape[1]
    flat = 2 * seqs * rows
    return pl.pallas_call(
        conv_back_kernel,
        grid=(KW,),
        in_specs=[
            whole(d_conv.shape),
            whole(low.shape),
            whole(high.shape),
            pl.BlockSpec((1, c_in, width), lambda k: (k, 0, 0)),
        ]
        + spare(deps),
        out_specs=whole((flat, c_in)),
        out_shape=jax.ShapeDtypeStruct((flat, c_in), BF),
        scratch_shapes=[
            pltpu.VMEM((2, 3, width, seqs * rows), BF),
            pltpu.VMEM((c_in, flat), F32),
        ],
        compiler_params=params(),
        cost_estimate=COST,
        name="encoder_backward",
    )(d_conv, low, high, conv_weight, *deps)


def pack_kernel(w_ref, pack_ref, turned_ref, token_ref):
    token_ref[...] = jnp.zeros_like(token_ref)
    for i in range(3):
        for head in range(pack_ref.shape[0]):
            part = w_ref[i, :, head * DH : (head + 1) * DH]
            columns = slice(i * DH, (i + 1) * DH)
            pack_ref[head, :, columns] = part
            turned_ref[head, columns, :] = part.T


def pack_weights(w_qkv):
    _, width, local = w_qkv.shape
    heads = local // DH
    tile = local
    return pl.pallas_call(
        pack_kernel,
        grid=(width // tile,),
        in_specs=[pl.BlockSpec((3, tile, local), lambda n: (0, n, 0))],
        out_specs=[
            pl.BlockSpec((heads, tile, 3 * DH), lambda n: (0, n, 0)),
            pl.BlockSpec((heads, 3 * DH, tile), lambda n: (0, 0, n)),
            pl.BlockSpec(TOKEN.shape, lambda n: (0, 0)),
        ],
        out_shape=[
            jax.ShapeDtypeStruct((heads, width, 3 * DH), BF),
            jax.ShapeDtypeStruct((heads, 3 * DH, width), BF),
            TOKEN,
        ],
        compiler_params=params(),
        cost_estimate=COST,
        name="pack_weights",
    )(w_qkv)


def product_kernel(head_ref, x_ref, w_ref, *rest, contract):
    del head_ref
    out_ref, token_ref = rest[-2:]
    token_ref[...] = jnp.zeros_like(token_ref)
    value = dot(x_ref[...], w_ref[0], contract).astype(BF)
    out_ref[:, : value.shape[1]] = value
    if value.shape[1] < out_ref.shape[1]:
        out_ref[:, value.shape[1] :] = jnp.zeros_like(out_ref[:, value.shape[1] :])


def head_product(head, x, weight, contract, name, *deps):
    columns = weight.shape[2] if contract == NN else weight.shape[1]
    columns += -columns % 128
    rows, width = x.shape
    return pl.pallas_call(
        functools.partial(product_kernel, contract=contract),
        grid_spec=pltpu.PrefetchScalarGridSpec(
            num_scalar_prefetch=1,
            grid=(1,),
            in_specs=[
                pl.BlockSpec((rows, width), lambda i, head: (0, 0)),
                pl.BlockSpec((1,) + weight.shape[1:], lambda i, head: (head[0], 0, 0)),
            ]
            + spare(deps),
            out_specs=[
                pl.BlockSpec((rows, columns), lambda i, head: (0, 0)),
                pl.BlockSpec(TOKEN.shape, lambda i, head: (0, 0)),
            ],
        ),
        out_shape=[jax.ShapeDtypeStruct((rows, columns), BF), TOKEN],
        compiler_params=params(),
        cost_estimate=COST,
        name=name,
    )(head, x, weight, *deps)


def split_product_kernel(head_ref, xa_ref, xb_ref, w_ref, *rest):
    del head_ref
    out_ref = rest[-1]
    cut = xa_ref.shape[1]
    value = dot(xa_ref[...], w_ref[0, :cut], NN) + dot(xb_ref[...], w_ref[0, cut:], NN)
    out_ref[:, : value.shape[1]] = value.astype(BF)
    out_ref[:, value.shape[1] :] = jnp.zeros_like(out_ref[:, value.shape[1] :])


def split_product(head, xa, xb, weight, name, *deps):
    columns = weight.shape[2]
    columns += -columns % 128
    rows = xa.shape[0]
    return pl.pallas_call(
        split_product_kernel,
        grid_spec=pltpu.PrefetchScalarGridSpec(
            num_scalar_prefetch=1,
            grid=(1,),
            in_specs=[
                pl.BlockSpec(xa.shape, lambda i, head: (0, 0)),
                pl.BlockSpec(xb.shape, lambda i, head: (0, 0)),
                pl.BlockSpec((1,) + weight.shape[1:], lambda i, head: (head[0], 0, 0)),
            ]
            + spare(deps),
            out_specs=pl.BlockSpec((rows, columns), lambda i, head: (0, 0)),
        ),
        out_shape=jax.ShapeDtypeStruct((rows, columns), BF),
        compiler_params=params(),
        cost_estimate=COST,
        name=name,
    )(head, xa, xb, weight, *deps)


def place_kernel(at_ref, *refs):
    del at_ref
    for slot, ref in enumerate(refs[:-1]):

        @pl.when(pl.program_id(0) == slot)
        def _():
            refs[-1][...] = ref[...]


def placed(at, slots, name):
    count = len(slots)
    rows, width = slots[0].shape
    return pl.pallas_call(
        place_kernel,
        grid_spec=pltpu.PrefetchScalarGridSpec(
            num_scalar_prefetch=1,
            grid=(count,),
            in_specs=[pl.BlockSpec((rows, width), lambda q, at: (0, 0))] * count,
            out_specs=pl.BlockSpec((rows, width), lambda q, at: (q ^ at[0], 0)),
        ),
        out_shape=jax.ShapeDtypeStruct((count * rows, width), slots[0].dtype),
        compiler_params=params(),
        cost_estimate=COST,
        name=name,
    )(at, *slots)


def attention_kernel(qa_ref, qb_ref, da_ref, db_ref, *rest, block):
    oa_ref, ob_ref, k_all, v_all, dk_acc, dv_acc = rest[-6:]
    scale = DH ** (-0.5)
    half = qa_ref.shape[0]
    for place, ref in enumerate((qa_ref, qb_ref)):
        rows = pl.ds(place * half, half)
        k_all[rows, :] = ref[:, DH : 2 * DH]
        v_all[rows, :] = ref[:, 2 * DH : 3 * DH]
    k = k_all[...]
    v = v_all[...]
    for place, (q_ref, d_ref, out_ref) in enumerate(
        ((qa_ref, da_ref, oa_ref), (qb_ref, db_ref, ob_ref))
    ):
        for start in range(0, half, block):
            rows = pl.ds(start, block)
            q = q_ref[rows, 0:DH]
            d_o = d_ref[rows, 0:DH]
            s = dot(q, k, NT) * scale
            e = jnp.exp(s - jnp.max(s, axis=-1, keepdims=True))
            p = e * (1.0 / jnp.sum(e, axis=-1, keepdims=True))
            p_b = p.astype(BF)
            o = dot(p_b, v, NN)
            delta = jnp.sum(d_o.astype(F32) * o, axis=-1, keepdims=True)
            d_p = dot(d_o, v, NT)
            ds = (p * (d_p - delta)).astype(BF)
            dq = scale * dot(ds, k, NN)
            dk = dot(ds, q, TN)
            dv = dot(p_b, d_o, TN)
            if place == 0 and start == 0:
                dk_acc[...] = dk
                dv_acc[...] = dv
            else:
                dk_acc[...] += dk
                dv_acc[...] += dv
            out_ref[rows, 0:DH] = dq.astype(BF)
            out_ref[rows, 3 * DH : 4 * DH] = o.astype(BF)
    for place, out_ref in enumerate((oa_ref, ob_ref)):
        rows = pl.ds(place * half, half)
        out_ref[:, DH : 2 * DH] = (scale * dk_acc[rows, :]).astype(BF)
        out_ref[:, 2 * DH : 3 * DH] = dv_acc[rows, :].astype(BF)


def attention(qkv_a, qkv_b, d_a, d_b, *deps):
    half = qkv_a.shape[0]
    shape = jax.ShapeDtypeStruct((half, 4 * DH), BF)
    return pl.pallas_call(
        functools.partial(attention_kernel, block=min(256, half)),
        in_specs=[pl.BlockSpec(memory_space=pltpu.VMEM)] * 4 + spare(deps),
        out_shape=[shape, shape],
        scratch_shapes=[
            pltpu.VMEM((2 * half, DH), BF),
            pltpu.VMEM((2 * half, DH), BF),
            pltpu.VMEM((2 * half, DH), F32),
            pltpu.VMEM((2 * half, DH), F32),
        ],
        compiler_params=params(),
        cost_estimate=COST,
        name="attention",
    )(qkv_a, qkv_b, d_a, d_b, *deps)


def term_kernel(head_ref, a_ref, b_ref, w_ref, *rest, first, last):
    head = head_ref[0]
    total = dot(a_ref[:, first:last], w_ref[head], NN)
    total += dot(b_ref[:, first:last], w_ref[1 - head], NN)
    rest[-1][...] = total.astype(BF)


def pair_term(head, mine, got, weight, first, last, name, *deps):
    half, full = mine.shape
    heads, depth, width = weight.shape
    tile = 512 if width % 512 == 0 else width
    return pl.pallas_call(
        functools.partial(term_kernel, first=first, last=last),
        grid_spec=pltpu.PrefetchScalarGridSpec(
            num_scalar_prefetch=1,
            grid=(width // tile,),
            in_specs=[
                pl.BlockSpec((half, full), lambda n, at: (0, 0)),
                pl.BlockSpec((half, full), lambda n, at: (0, 0)),
                pl.BlockSpec((heads, depth, tile), lambda n, at: (0, 0, n)),
            ]
            + spare(deps),
            out_specs=pl.BlockSpec((half, tile), lambda n, at: (0, n)),
        ),
        out_shape=jax.ShapeDtypeStruct((half, width), BF),
        compiler_params=params(),
        cost_estimate=COST,
        name=name,
    )(head, mine, got, weight, *deps)


def part_kernel(head_ref, x_ref, w_ref, *rest, last):
    del head_ref
    total = dot(x_ref[:, :last], w_ref[0], NN)
    if len(rest) > 1:
        total += rest[0][...]
    rest[-1][...] = total.astype(rest[-1].dtype)


def term_part(head, x, weight, last, name, *before):
    half, full = x.shape
    _, depth, width = weight.shape
    tile = 512 if width % 512 == 0 else width
    column = pl.BlockSpec((half, tile), lambda n, at: (0, n))
    return pl.pallas_call(
        functools.partial(part_kernel, last=last),
        grid_spec=pltpu.PrefetchScalarGridSpec(
            num_scalar_prefetch=1,
            grid=(width // tile,),
            in_specs=[
                pl.BlockSpec((half, full), lambda n, at: (0, 0)),
                pl.BlockSpec((1, depth, tile), lambda n, at: (at[0], 0, n)),
            ]
            + [column] * len(before),
            out_specs=column,
        ),
        out_shape=jax.ShapeDtypeStruct((half, width), BF if before else F32),
        compiler_params=params(),
        cost_estimate=COST,
        name=name,
    )(head, x, weight, *before)


def weight_kernel(
    at_ref, xa_ref, ya_ref, xb_ref, yb_ref, ga_ref, gb_ref, ra_ref, rb_ref, *rest
):
    out_refs, turned = rest[:-1], rest[-1]
    step = pl.program_id(0)
    last = (step ^ at_ref[0]) == pl.num_programs(0) - 1
    xa = jnp.where(last, ya_ref[...], xa_ref[...])
    xb = jnp.where(last, yb_ref[...], xb_ref[...])
    half = ra_ref.shape[0]
    split = 3 * DH

    @pl.when(step == 0)
    def _():
        turned[:, :half] = ra_ref[...].T
        turned[:, half:] = rb_ref[...].T

    a, b = slice(0, half), slice(half, 2 * half)
    qkv = dot(turned[:split, a], xa, NN) + dot(turned[:split, b], xb, NN)
    out = dot(turned[split:, a], ga_ref[...], NN) + dot(turned[split:, b], gb_ref[...], NN)
    keep_a, send_a, keep_b, send_b = out_refs
    rows = keep_a.shape[1]
    for slot in range(4):

        @pl.when(step == slot)
        def _():
            first = keep_a if slot % 2 == 0 else send_a
            second = keep_b if slot < 2 else send_b
            first[slot // 2] = qkv[:rows].astype(BF)
            second[slot % 2, : split - rows] = qkv[rows:].astype(BF)
            second[slot % 2, split - rows :] = out.astype(BF)


def weight_gradients(at, xa, ya, xb, yb, ga, gb, ra, rb, seqs):
    half, width = ga.shape
    chunk = width // seqs
    full = ra.shape[1]
    some = pl.BlockSpec((half, chunk), lambda r, at: (0, jnp.minimum(r ^ at[0], seqs - 2)))
    only = pl.BlockSpec((half, chunk), lambda r, at: (0, 0))
    column = pl.BlockSpec((half, chunk), lambda r, at: (0, r ^ at[0]))
    rest = pl.BlockSpec((half, full), lambda r, at: (0, 0))
    return pl.pallas_call(
        weight_kernel,
        grid_spec=pltpu.PrefetchScalarGridSpec(
            num_scalar_prefetch=1,
            grid=(seqs,),
            in_specs=[some, only] * 2 + [column] * 2 + [rest] * 2,
            out_specs=[pl.BlockSpec((2, full // 2, chunk), lambda r, at: (0, 0, 0))] * 4,
            scratch_shapes=[pltpu.VMEM((full, 2 * half), BF)],
        ),
        out_shape=[jax.ShapeDtypeStruct((2, full // 2, chunk), BF)] * 4,
        compiler_params=params(STREAMING_LIMIT),
        cost_estimate=COST,
        name="weight_gradients",
    )(at, xa, ya, xb, yb, ga, gb, ra, rb)


def turn_kernel(keep_a, got_a, keep_b, got_b, *rest):
    out_a, out_b = rest[-2:]
    for keep, got, out in ((keep_a, got_a, out_a), (keep_b, got_b, out_b)):
        out[...] = (keep[1].astype(F32) + got[1].astype(F32)).astype(BF)


def weight_turn(keep_a, got_a, keep_b, got_b, *deps):
    shape = jax.ShapeDtypeStruct(keep_a.shape[1:], BF)
    return pl.pallas_call(
        turn_kernel,
        in_specs=[pl.BlockSpec(memory_space=pltpu.VMEM)] * 4 + spare(deps),
        out_shape=[shape, shape],
        compiler_params=params(),
        cost_estimate=COST,
        name="weight_turn",
    )(keep_a, got_a, keep_b, got_b, *deps)


def weight_sum_kernel(keep_a, got_a, last_a, keep_b, got_b, last_b, *rest):
    out_refs = rest[-2:]
    split = 3 * DH
    parts = [
        keep[0].astype(F32) + got[0].astype(F32) + last[...].astype(F32)
        for keep, got, last in ((keep_a, got_a, last_a), (keep_b, got_b, last_b))
    ]
    total = jnp.concatenate(parts, axis=0)
    turned = total[:split].T.astype(BF)
    quarter = DH // 2
    for part, out_ref in enumerate(out_refs):
        out_ref[:, :split] = turned[part * DH : (part + 1) * DH]
        first = split + part * quarter
        piece = total[first : first + quarter].astype(BF)
        out_ref[:quarter, split:] = piece[:, :DH]
        out_ref[quarter:, split:] = piece[:, DH:]


def weight_sum(keep_a, got_a, last_a, keep_b, got_b, last_b, *deps):
    _, rows, chunk = keep_a.shape
    return pl.pallas_call(
        weight_sum_kernel,
        in_specs=[pl.BlockSpec(memory_space=pltpu.VMEM)] * 6 + spare(deps),
        out_shape=[jax.ShapeDtypeStruct((chunk // 2, 2 * rows), BF)] * 2,
        compiler_params=params(),
        cost_estimate=COST,
        name="weight_sum",
    )(keep_a, got_a, last_a, keep_b, got_b, last_b, *deps)


def unpack_kernel(at_ref, *refs):
    qkv_ref, out_ref, token_ref = refs[-3:]
    step = pl.program_id(0)
    split = 3 * DH
    quarter = DH // 2
    token_ref[...] = jnp.zeros_like(token_ref)
    for half in range(2):

        @pl.when(step // 2 == half)
        def _():
            mine = refs[half][...].astype(F32)
            other = refs[2 + half][...].astype(F32)
            swapped = at_ref[1] != 0
            low = jnp.where(swapped, other, mine)
            high = jnp.where(swapped, mine, other)
            for i in range(3):
                columns = slice(i * DH, (i + 1) * DH)
                qkv_ref[i] = jnp.concatenate([low[:, columns], high[:, columns]], axis=1)
            for head, value in enumerate((low, high)):
                folded = [value[:quarter, split:], value[quarter:, split:]]
                out_ref[head, 0] = jnp.concatenate(folded, axis=1)


def unpack_weights(at, mine, other, far, before=(), *deps):
    rows, full = mine[0].shape
    half = rows // 2
    width = 4 * rows

    def chunk(t, at):
        if far:
            return at[0] ^ jnp.where(t < 2, t + 2, 2 * t - 3)
        return at[0] ^ jnp.where(t < 2, t, 2 * t - 4)

    specs = [
        pl.BlockSpec((half, full), lambda t, at: (jnp.minimum(t, 1), 0)),
        pl.BlockSpec((half, full), lambda t, at: (jnp.maximum(t - 2, 0), 0)),
    ]
    return pl.pallas_call(
        unpack_kernel,
        grid_spec=pltpu.PrefetchScalarGridSpec(
            num_scalar_prefetch=1,
            grid=(4,),
            in_specs=specs * 2 + spare(tuple(before) + deps),
            out_specs=[
                pl.BlockSpec((3, half, 2 * DH), lambda t, at: (0, 2 * chunk(t, at) + t // 2, 0)),
                pl.BlockSpec(
                    (2, 1, DH // 2, rows), lambda t, at: (0, t // 2, 0, chunk(t, at))
                ),
                pl.BlockSpec(TOKEN.shape, lambda t, at: (0, 0)),
            ],
        ),
        out_shape=[
            jax.ShapeDtypeStruct((3, width, 2 * DH), F32),
            jax.ShapeDtypeStruct((2, 2, DH // 2, width), F32),
            TOKEN,
        ],
        input_output_aliases={5 + i: i for i in range(len(before))},
        compiler_params=params(),
        cost_estimate=COST,
        name="weight_outputs_far" if far else "weight_outputs_near",
    )(at, *mine, *other, *before, *deps)


def neighbour_edges(first, last):
    axes = ("seq", "head")
    count = lax.axis_size(axes)
    forward = [(i, i + 1) for i in range(count - 1)]
    backward = [(target, source) for source, target in forward]
    return lax.ppermute(last, axes, forward), lax.ppermute(first, axes, backward)


def after(value, *others):
    return lax.optimization_barrier((value,) + others)[0]


def trade_chip(x, bit, heads):
    count = lax.axis_size("seq")
    return lax.ppermute(x, "seq", [(s, s ^ (bit * heads)) for s in range(count)])


def trade_z(x, bit):
    count = lax.axis_size("head")
    return lax.ppermute(x, "head", [(z, z ^ bit) for z in range(count)])


def swap_heads(x):
    count = lax.axis_size("seq")
    return lax.ppermute(x, "seq", [(s, s + 1 - 2 * (s % 2)) for s in range(count)])


def unit_body(enc_in, conv_weight, norm_gain, w_qkv, w_out, grad_out):
    rows = enc_in.shape[0] // 2
    seqs = enc_in.shape[1]
    width = conv_weight.shape[2]
    local = w_qkv.shape[2]
    heads = local // DH
    groups = lax.axis_size("head")
    half = groups * seqs * rows
    place = lax.axis_index("seq")
    own_seq = (place // heads).astype(jnp.int32)
    own_head = (place % heads).astype(jnp.int32)
    at = jnp.stack([own_seq, own_head])
    head_mine = own_head.reshape(1)
    head_other = (1 - own_head).reshape(1)

    def to_chips(slots):
        return [x if j == 0 else trade_chip(x, j, heads) for j, x in enumerate(slots)]

    order = (0, 2, 1, 3)

    grad_z = lax.all_gather(grad_out, "head", axis=0, tiled=False)

    pairs = jnp.transpose(enc_in.reshape(rows, 2, seqs, enc_in.shape[2]), (1, 2, 0, 3))
    low, high = neighbour_edges(pairs[:, :, :1, :], pairs[:, :, -1:, :])
    skip, slope, normed = encoder(at, pairs, low, high, conv_weight, norm_gain)
    normed = to_chips(normed)
    edge = width - width // seqs
    slab_a = jnp.concatenate([normed[j][:, :edge] for j in order], axis=0)
    slab_b = jnp.concatenate([normed[j][:, edge:] for j in order], axis=0)
    normed_a = lax.all_gather(slab_a, "head", axis=0, tiled=True)
    slabs_b = [slab_b if q == 0 else trade_z(slab_b, q) for q in range(groups)]
    normed_b = placed(lax.axis_index("head").astype(jnp.int32).reshape(1), slabs_b, "normed_last")

    grad_z = after(grad_z, slab_a)
    grad_slots = to_chips(
        [lax.dynamic_index_in_dim(grad_z, own_seq ^ j, 2, keepdims=False) for j in range(seqs)]
    )
    grad_rows = jnp.stack([grad_slots[j] for j in order], axis=1).reshape(half, width)
    w_pack, w_turned, packed = pack_weights(after(w_qkv, slab_a))
    w_rows = w_out.reshape(heads, DH, width)
    d_other, one = head_product(head_other, grad_rows, w_rows, NT, "d_o_other")
    d_got = swap_heads(d_other)
    d_mine, two = head_product(head_mine, grad_rows, w_rows, NT, "d_o_own")
    grad_swapped = swap_heads(grad_rows)
    normed_a, normed_b, d_got, d_mine, grad_swapped, w_pack, w_turned, *tokens = (
        lax.optimization_barrier(
            (normed_a, normed_b, d_got, d_mine, grad_swapped, w_pack, w_turned, packed, one, two)
        )
    )

    swapped_a, swapped_b = swap_heads(normed_a), swap_heads(normed_b)
    qkv_other = split_product(head_other, normed_a, normed_b, w_pack, "qkv_other", *tokens)
    qkv_got = swap_heads(qkv_other)
    qkv_mine = split_product(head_mine, normed_a, normed_b, w_pack, "qkv_own")
    result_mine, result_other = attention(
        qkv_mine, qkv_got, d_mine, d_got, swapped_a, swapped_b
    )
    result_got = swap_heads(result_other)

    shape = (groups, seqs, rows, width)
    d_own = term_part(head_mine, result_mine, w_turned, 3 * DH, "d_term_own")
    d_term = term_part(head_other, result_got, w_turned, 3 * DH, "d_term", d_own)
    d_normed = lax.psum_scatter(d_term.reshape(shape), "head", scatter_dimension=0, tiled=False)
    keep_a, send_a, keep_b, send_b = weight_gradients(
        own_seq.reshape(1),
        normed_a,
        normed_b,
        swapped_a,
        swapped_b,
        grad_rows,
        grad_swapped,
        result_mine,
        result_other,
        seqs,
    )
    got_a, got_b = trade_chip(send_a, 1, heads), trade_chip(send_b, 2, heads)
    head_term = pair_term(
        head_mine, result_mine, result_got, w_rows, 3 * DH, 4 * DH, "head_term"
    )
    head_sum = lax.psum_scatter(head_term.reshape(shape), "head", scatter_dimension=0, tiled=False)
    turn_a, turn_b = weight_turn(keep_a, got_a, keep_b, got_b, head_term)
    last_a, last_b = trade_chip(turn_a, 2, heads), trade_chip(turn_b, 1, heads)

    d_normed = after(d_normed, turn_a, turn_b)
    leaving = d_normed[2:]
    near = trade_chip(leaving, 1, heads)
    far = trade_chip(jnp.stack([d_normed[1], near[1]]), 2, heads)
    half_a, half_b = weight_sum(keep_a, got_a, last_a, keep_b, got_b, last_b, leaving)
    grad = jnp.transpose(after(grad_out, d_term), (1, 0, 2))
    d_conv, first, last = conv_gradient(
        at, d_normed, near, far, skip, grad, norm_gain, slope, half_a
    )
    low, high = neighbour_edges(first, last)
    low, high, at_hand = lax.optimization_barrier((low, high, marker(conv_weight, first)))

    got_a, got_b = trade_chip(half_a, 1, heads), trade_chip(half_b, 2, heads)
    near_a = jnp.concatenate([half_a, after(got_a, low)], axis=0)
    near_b = jnp.concatenate([half_b, after(got_b, high)], axis=0)
    far_a = trade_chip(near_a, 2, heads)
    far_b = trade_chip(near_b, 1, heads)
    near_other = [swap_heads(near_a), swap_heads(near_b)]
    grad_input = conv_back(d_conv, low, high, conv_weight, at_hand, *near_other)
    *outputs, token = unpack_weights(
        at, [near_a, near_b], near_other, False, (), grad_input
    )

    head_sum = after(head_sum, grad_input, token)
    head_sum = to_chips([head_sum[order.index(j)] for j in range(seqs)])
    far_other = [swap_heads(after(x, *head_sum[1:])) for x in (far_a, far_b)]
    grad_w_qkv, grad_w_out, _ = unpack_weights(at, [far_a, far_b], far_other, True, outputs)
    mixed = mixed_call(at, head_sum, skip, token)
    grad_input = jnp.transpose(grad_input.reshape(2, seqs, rows, -1), (2, 0, 1, 3))
    return (
        jnp.transpose(mixed, (1, 0, 2)),
        grad_input.reshape(enc_in.shape),
        grad_w_qkv,
        grad_w_out.reshape(local, width),
    )


def padded_2(block, sides, width):
    for axis, dim in sides:
        count = lax.axis_size(axis)
        forward = [(i, i + 1) for i in range(count - 1)]
        backward = [(target, source) for source, target in forward]
        low = lax.ppermute(
            lax.slice_in_dim(block, block.shape[dim] - width, None, axis=dim), axis, forward
        )
        high = lax.ppermute(lax.slice_in_dim(block, 0, width, axis=dim), axis, backward)
        block = jnp.concatenate([low, block, high], axis=dim)
    return block


def gathered_body(enc_in, conv_weight, norm_gain, w_qkv, w_out, grad_out):
    fine_rows = enc_in.shape[0]
    slab_rows = fine_rows // 2
    seq_count = enc_in.shape[1]
    out_width = conv_weight.shape[2]
    local_width = w_qkv.shape[2]
    local_heads = local_width // DH
    logit_scale = DH ** (-0.5)
    padded = padded_2(enc_in, ((("seq", "head"), 0),), 2)
    convolved = jnp.zeros((fine_rows, seq_count, out_width), jnp.float32)
    for offset in range(KW):
        convolved = convolved + jnp.einsum(
            "tbi,io->tbo",
            padded[offset : offset + fine_rows],
            conv_weight[offset],
            preferred_element_type=jnp.float32,
        )
    activated, gelu_pull = jax.vjp(jax.nn.gelu, convolved)
    skip = jnp.mean(activated.reshape(slab_rows, 2, seq_count, out_width), axis=1).astype(
        jnp.bfloat16
    )
    skip_wide = skip.astype(jnp.float32)
    inv_rms = lax.rsqrt(jnp.mean(skip_wide * skip_wide, axis=-1, keepdims=True) + 1e-06)
    normed = (skip_wide * inv_rms * norm_gain).astype(jnp.bfloat16)
    normed_rows = lax.all_gather(normed, "head", axis=0, tiled=True)
    grad_rows = lax.all_gather(grad_out, "head", axis=0, tiled=True)
    tower_rows = normed_rows.shape[0]
    qkv = jnp.einsum(
        "tbc,ice->itbe", normed_rows, w_qkv, preferred_element_type=jnp.float32
    ).astype(jnp.bfloat16)
    qkv = qkv.reshape(3, tower_rows, seq_count, local_heads, DH)
    query_matrix, key_matrix, value_matrix = (qkv[0], qkv[1], qkv[2])
    key_all, value_all = (
        lax.all_gather(key_matrix, "seq", axis=0, tiled=True),
        lax.all_gather(value_matrix, "seq", axis=0, tiled=True),
    )
    attention_logits = (
        jnp.einsum("qbhd,kbhd->bhqk", query_matrix, key_all, preferred_element_type=jnp.float32)
        * logit_scale
    )
    row_peak = jnp.max(attention_logits, axis=-1, keepdims=True)
    exponent = jnp.exp(attention_logits - row_peak)
    row_total = jnp.sum(exponent, axis=-1, keepdims=True)
    soft_weights = exponent / row_total
    narrow_probabilities = soft_weights.astype(jnp.bfloat16)
    attention_output = jnp.einsum(
        "bhqk,kbhd->qbhd", narrow_probabilities, value_all, preferred_element_type=jnp.float32
    )
    o_narrow = attention_output.reshape(tower_rows, seq_count, local_width).astype(jnp.bfloat16)
    piece = o_narrow
    head_sum = lax.psum_scatter(
        jnp.einsum("tbe,ec->tbc", piece, w_out, preferred_element_type=jnp.float32).astype(
            jnp.bfloat16
        ),
        "head",
        scatter_dimension=0,
        tiled=True,
    ).astype(jnp.float32)
    mixed = (skip_wide + head_sum).astype(jnp.bfloat16)
    part_w_out = jnp.einsum("tbe,tbc->ec", o_narrow, grad_rows, preferred_element_type=jnp.float32)
    d_out = jnp.einsum("tbc,ec->tbe", grad_rows, w_out, preferred_element_type=jnp.float32).astype(
        jnp.bfloat16
    )
    d_out = d_out.reshape(tower_rows, seq_count, local_heads, DH)
    delta = jnp.sum(d_out.astype(jnp.float32) * attention_output, axis=-1)
    probability_gradient = jnp.einsum(
        "qbhd,kbhd->bhqk", d_out, value_all, preferred_element_type=jnp.float32
    )
    d_scores = soft_weights * (probability_gradient - jnp.transpose(delta, (1, 2, 0))[..., None])
    narrow_gradient = d_scores.astype(jnp.bfloat16)
    query_gradient = logit_scale * jnp.einsum(
        "bhqk,kbhd->qbhd", narrow_gradient, key_all, preferred_element_type=jnp.float32
    )
    key_terms = logit_scale * jnp.einsum(
        "bhqk,qbhd->kbhd", narrow_gradient, query_matrix, preferred_element_type=jnp.float32
    )
    value_terms = jnp.einsum(
        "bhqk,qbhd->kbhd", narrow_probabilities, d_out, preferred_element_type=jnp.float32
    )
    d_keys, d_values = (
        lax.psum_scatter(
            key_terms.astype(jnp.bfloat16), "seq", scatter_dimension=0, tiled=True
        ).astype(jnp.float32),
        lax.psum_scatter(
            value_terms.astype(jnp.bfloat16), "seq", scatter_dimension=0, tiled=True
        ).astype(jnp.float32),
    )
    dqkv = (
        jnp.stack([query_gradient, d_keys, d_values])
        .reshape(3, tower_rows, seq_count, local_width)
        .astype(jnp.bfloat16)
    )
    part_w_qkv = jnp.einsum("tbc,itbe->ice", normed_rows, dqkv, preferred_element_type=jnp.float32)
    piece = dqkv
    d_normed = lax.psum_scatter(
        jnp.einsum("itbe,ice->tbc", piece, w_qkv, preferred_element_type=jnp.float32).astype(
            jnp.bfloat16
        ),
        "head",
        scatter_dimension=0,
        tiled=True,
    ).astype(jnp.float32)
    unit_rows = skip_wide * inv_rms
    scaled = d_normed * norm_gain
    d_skip = grad_out.astype(jnp.float32) + inv_rms * (
        scaled - unit_rows * jnp.mean(scaled * unit_rows, axis=-1, keepdims=True)
    )
    d_act = jnp.repeat(d_skip, 2, axis=0) * 0.5
    d_conv = gelu_pull(d_act)[0].astype(jnp.bfloat16)
    d_pad = padded_2(d_conv, ((("seq", "head"), 0),), 2)
    grad_input = jnp.zeros((fine_rows, seq_count, enc_in.shape[2]), jnp.float32)
    for offset in range(KW):
        grad_input = grad_input + jnp.einsum(
            "tbo,io->tbi",
            d_pad[4 - offset : 4 - offset + fine_rows],
            conv_weight[offset],
            preferred_element_type=jnp.float32,
        )
    grad_w_qkv, grad_w_out = (
        lax.psum(part_w_qkv.astype(jnp.bfloat16), "seq").astype(jnp.float32),
        lax.psum(part_w_out.astype(jnp.bfloat16), "seq").astype(jnp.float32),
    )
    return (mixed, grad_input.astype(jnp.bfloat16), grad_w_qkv, grad_w_out)


def body(enc_in, conv_weight, norm_gain, w_qkv, w_out, grad_out):
    heads = w_qkv.shape[2] // DH
    seqs = enc_in.shape[1]
    fits = lax.axis_size("head") == 4 and heads == 2 and seqs == 4 and seqs * heads == lax.axis_size("seq")
    fits = fits and conv_weight.shape[2] == seqs * w_qkv.shape[2]
    chosen = unit_body if fits else gathered_body
    return chosen(enc_in, conv_weight, norm_gain, w_qkv, w_out, grad_out)


def solution(mesh):
    return jax.shard_map(
        body,
        mesh=mesh,
        in_specs=(
            P(("seq", "head"), None, None),
            P(),
            P(),
            P(None, None, "head"),
            P("head", None),
            P(("seq", "head"), None, None),
        ),
        out_specs=(
            P(("seq", "head"), None, None),
            P(("seq", "head"), None, None),
            P(None, None, "head"),
            P("head", None),
        ),
        check_vma=False,
    )
```

```python
import functools

import jax
import jax.numpy as jnp
from jax import lax
from jax.experimental import pallas as pl
from jax.experimental.pallas import tpu as pltpu
from jax.sharding import PartitionSpec as P

DH = 192
KW = 5
VMEM_LIMIT = 24 * 1024 * 1024
STREAMING_LIMIT = 56 * 1024 * 1024
COST = pl.CostEstimate(flops=1000, bytes_accessed=1000, transcendentals=0)
BF = jnp.bfloat16
F32 = jnp.float32
TOKEN = jax.ShapeDtypeStruct((8, 128), F32)


def params(limit=VMEM_LIMIT):
    return pltpu.CompilerParams(vmem_limit_bytes=limit)


def dot(a, b, contract):
    return lax.dot_general(a, b, (contract, ((), ())), preferred_element_type=F32)


NN = ((1,), (0,))
NT = ((1,), (1,))
TN = ((0,), (0,))


def whole(shape):
    return pl.BlockSpec(shape, lambda *_: (0,) * len(shape))


SCALARS = pl.BlockSpec(memory_space=pltpu.SMEM)


def spare(deps):
    return [pl.BlockSpec(memory_space=pl.ANY)] * len(deps)


def turned_rows(ref, low_ref, high_ref, parity, shift):
    seqs, rows, width = ref.shape[1:]
    own = ref[parity]
    if shift != 1:
        wide = own.astype(F32)
        if shift == 0:
            parts = [low_ref[parity].astype(F32), wide[:, : rows - 1]]
        else:
            parts = [wide[:, 1:], high_ref[parity].astype(F32)]
        own = jnp.concatenate(parts, axis=1).astype(BF)
    return own.reshape(seqs * rows, width)


def conv_kernel(
    at_ref, x_ref, low_ref, high_ref, w_ref, gain_ref, skip_ref, slope_ref, *rest
):
    normed_refs, (lhs, squares, whole_normed) = rest[:-3], rest[-3:]
    step = pl.program_id(0)
    seqs, rows, c_in = x_ref.shape[1:]
    half = seqs * rows
    tile = w_ref.shape[2]

    @pl.when(step == 0)
    def _():
        for parity in range(2):
            for shift in range(3):
                value = turned_rows(x_ref, low_ref, high_ref, parity, shift)
                for out in range(2):
                    tap = 2 * shift + parity - out
                    if 0 <= tap < KW:
                        lhs[out * half : (out + 1) * half, tap * c_in : (tap + 1) * c_in] = value
        squares[...] = jnp.zeros_like(squares)

    conv = dot(lhs[...], w_ref[...].reshape(KW * c_in, tile), NN)
    root = 0.7978845608028654
    total = None
    for parity in range(2):
        x = conv[parity * half : (parity + 1) * half, :]
        square = x * x
        t = jnp.tanh(root * (x + 0.044715 * (square * x)))
        left = 0.5 * (1.0 + t)
        act = x * left
        slope = left + (0.5 * root) * x * (1.0 - t * t) * (1.0 + (3 * 0.044715) * square)
        slope_ref[parity] = slope.reshape(slope_ref.shape[1:])
        total = act if total is None else total + act
    skip = (0.5 * total).astype(BF)
    columns = pl.ds(pl.multiple_of(step * tile, tile), tile)
    skip_ref[:, :, columns] = skip.reshape(seqs, rows, tile)
    wide = skip.astype(F32)
    squares[...] += jnp.sum(wide * wide, axis=-1, keepdims=True)

    @pl.when(step == pl.num_programs(0) - 1)
    def _():
        width = skip_ref.shape[2]
        inv = lax.rsqrt(squares[...] * (1.0 / width) + 1e-06)
        wide = skip_ref[...].reshape(half, width).astype(F32)
        normed = (wide * inv * gain_ref[...]).astype(BF)
        whole_normed[...] = normed.reshape(whole_normed.shape)
        for slot in range(seqs):
            normed_refs[slot][...] = whole_normed[at_ref[0] ^ slot]


def encoder(at, pairs, low, high, conv_weight, norm_gain):
    _, seqs, rows, c_in = pairs.shape
    width = conv_weight.shape[2]
    tile = 256 if width % 256 == 0 else width
    shape = (seqs, rows, width)
    outs = pl.pallas_call(
        conv_kernel,
        grid=(width // tile,),
        in_specs=[
            SCALARS,
            whole(pairs.shape),
            whole(low.shape),
            whole(high.shape),
            pl.BlockSpec((KW, c_in, tile), lambda n: (0, 0, n)),
            whole((1, width)),
        ],
        out_specs=[
            whole(shape),
            pl.BlockSpec((2, seqs, rows, tile), lambda n: (0, 0, 0, n)),
        ]
        + [whole((rows, width))] * seqs,
        out_shape=[
            jax.ShapeDtypeStruct(shape, BF),
            jax.ShapeDtypeStruct((2,) + shape, F32),
        ]
        + [jax.ShapeDtypeStruct((rows, width), BF)] * seqs,
        scratch_shapes=[
            pltpu.VMEM((2 * seqs * rows, KW * c_in), BF),
            pltpu.VMEM((seqs * rows, 1), F32),
            pltpu.VMEM(shape, BF),
        ],
        compiler_params=params(STREAMING_LIMIT),
        cost_estimate=COST,
        name="encoder_forward",
    )(at, pairs, low, high, conv_weight, norm_gain.reshape(1, width))
    return outs[0], outs[1], list(outs[2:])


def d_conv_kernel(at_ref, own_ref, near_ref, far_ref, *refs):
    skip_ref, grad_ref, gain_ref, slope_ref = refs[:4]
    out_ref, first_ref, last_ref = refs[-3:]
    rows = out_ref.shape[2]
    for slot, (ref, place) in enumerate(((own_ref, 0), (near_ref, 0), (far_ref, 0), (far_ref, 1))):
        b = at_ref[0] ^ slot
        wide = skip_ref[b].astype(F32)
        inv = lax.rsqrt(jnp.mean(wide * wide, axis=-1, keepdims=True) + 1e-06)
        unit = wide * inv
        scaled = ref[place].astype(F32) * gain_ref[...]
        d_skip = grad_ref[b].astype(F32) + inv * (
            scaled - unit * jnp.mean(scaled * unit, axis=-1, keepdims=True)
        )
        d_act = 0.5 * d_skip
        for parity in range(2):
            value = slope_ref[parity, b] * d_act
            out_ref[parity, b] = value.astype(BF)
            first_ref[parity, b] = value[:1].astype(BF)
            last_ref[parity, b] = value[rows - 1 :].astype(BF)


def conv_gradient(at, own, near, far, skip, grad, norm_gain, slope, *deps):
    vmem = pl.BlockSpec(memory_space=pltpu.VMEM)
    edge = jax.ShapeDtypeStruct(slope.shape[:2] + (1, slope.shape[3]), BF)
    return pl.pallas_call(
        d_conv_kernel,
        in_specs=[SCALARS] + [vmem] * 7 + spare(deps),
        out_specs=[vmem] * 3,
        out_shape=[jax.ShapeDtypeStruct(slope.shape, BF)] + [edge] * 2,
        compiler_params=params(),
        cost_estimate=COST,
        name="conv_gradient",
    )(at, own, near, far, skip, grad, norm_gain.reshape(1, -1), slope, *deps)


def mixed_body(seqs, at_ref, *refs):
    skip_ref, out_ref = refs[seqs], refs[-1]
    for slot in range(seqs):
        b = at_ref[0] ^ slot
        out_ref[b] = (skip_ref[b].astype(F32) + refs[slot][...].astype(F32)).astype(BF)


def mixed_call(at, terms, skip, *deps):
    seqs = len(terms)
    vmem = pl.BlockSpec(memory_space=pltpu.VMEM)
    return pl.pallas_call(
        functools.partial(mixed_body, seqs),
        in_specs=[SCALARS] + [vmem] * (seqs + 1) + spare(deps),
        out_specs=vmem,
        out_shape=jax.ShapeDtypeStruct(skip.shape, BF),
        compiler_params=params(),
        cost_estimate=COST,
        name="mixed_sum",
    )(at, *terms, skip, *deps)


def marker_kernel(*refs):
    refs[-1][...] = jnp.zeros_like(refs[-1])


def marker(*deps):
    return pl.pallas_call(
        marker_kernel,
        in_specs=spare(deps),
        out_shape=TOKEN,
        compiler_params=params(),
        cost_estimate=COST,
        name="marker",
    )(*deps)


def conv_back_kernel(d_ref, low_ref, high_ref, w_ref, *rest):
    out_ref, turned, acc = rest[-3:]
    step = pl.program_id(0)

    @pl.when(step == 0)
    def _():
        for parity in range(2):
            for shift in range(3):
                turned[parity, shift] = turned_rows(d_ref, low_ref, high_ref, parity, shift).T

    for tap in range(KW):

        @pl.when(step == tap)
        def _():
            places = [KW - 1 - tap, KW - tap]
            rhs = jnp.concatenate([turned[p % 2, p // 2] for p in places], axis=1)
            term = dot(w_ref[0], rhs, NN)
            if tap == 0:
                acc[...] = term
            elif tap < KW - 1:
                acc[...] += term
            else:
                out_ref[...] = (acc[...] + term).T.astype(BF)


def conv_back(d_conv, low, high, conv_weight, *deps):
    _, seqs, rows, width = d_conv.shape
    c_in = conv_weight.shape[1]
    flat = 2 * seqs * rows
    return pl.pallas_call(
        conv_back_kernel,
        grid=(KW,),
        in_specs=[
            whole(d_conv.shape),
            whole(low.shape),
            whole(high.shape),
            pl.BlockSpec((1, c_in, width), lambda k: (k, 0, 0)),
        ]
        + spare(deps),
        out_specs=whole((flat, c_in)),
        out_shape=jax.ShapeDtypeStruct((flat, c_in), BF),
        scratch_shapes=[
            pltpu.VMEM((2, 3, width, seqs * rows), BF),
            pltpu.VMEM((c_in, flat), F32),
        ],
        compiler_params=params(),
        cost_estimate=COST,
        name="encoder_backward",
    )(d_conv, low, high, conv_weight, *deps)


def pack_kernel(w_ref, pack_ref, turned_ref, token_ref):
    token_ref[...] = jnp.zeros_like(token_ref)
    for i in range(3):
        for head in range(pack_ref.shape[0]):
            part = w_ref[i, :, head * DH : (head + 1) * DH]
            columns = slice(i * DH, (i + 1) * DH)
            pack_ref[head, :, columns] = part
            turned_ref[head, columns, :] = part.T


def pack_weights(w_qkv):
    _, width, local = w_qkv.shape
    heads = local // DH
    tile = local
    return pl.pallas_call(
        pack_kernel,
        grid=(width // tile,),
        in_specs=[pl.BlockSpec((3, tile, local), lambda n: (0, n, 0))],
        out_specs=[
            pl.BlockSpec((heads, tile, 3 * DH), lambda n: (0, n, 0)),
            pl.BlockSpec((heads, 3 * DH, tile), lambda n: (0, 0, n)),
            pl.BlockSpec(TOKEN.shape, lambda n: (0, 0)),
        ],
        out_shape=[
            jax.ShapeDtypeStruct((heads, width, 3 * DH), BF),
            jax.ShapeDtypeStruct((heads, 3 * DH, width), BF),
            TOKEN,
        ],
        compiler_params=params(),
        cost_estimate=COST,
        name="pack_weights",
    )(w_qkv)


def product_kernel(head_ref, x_ref, w_ref, *rest, contract):
    del head_ref
    out_ref, token_ref = rest[-2:]
    token_ref[...] = jnp.zeros_like(token_ref)
    value = dot(x_ref[...], w_ref[0], contract).astype(BF)
    out_ref[:, : value.shape[1]] = value
    if value.shape[1] < out_ref.shape[1]:
        out_ref[:, value.shape[1] :] = jnp.zeros_like(out_ref[:, value.shape[1] :])


def head_product(head, x, weight, contract, name, *deps):
    columns = weight.shape[2] if contract == NN else weight.shape[1]
    columns += -columns % 128
    rows, width = x.shape
    return pl.pallas_call(
        functools.partial(product_kernel, contract=contract),
        grid_spec=pltpu.PrefetchScalarGridSpec(
            num_scalar_prefetch=1,
            grid=(1,),
            in_specs=[
                pl.BlockSpec((rows, width), lambda i, head: (0, 0)),
                pl.BlockSpec((1,) + weight.shape[1:], lambda i, head: (head[0], 0, 0)),
            ]
            + spare(deps),
            out_specs=[
                pl.BlockSpec((rows, columns), lambda i, head: (0, 0)),
                pl.BlockSpec(TOKEN.shape, lambda i, head: (0, 0)),
            ],
        ),
        out_shape=[jax.ShapeDtypeStruct((rows, columns), BF), TOKEN],
        compiler_params=params(),
        cost_estimate=COST,
        name=name,
    )(head, x, weight, *deps)


def split_product_kernel(head_ref, xa_ref, xb_ref, w_ref, *rest):
    del head_ref
    out_ref = rest[-1]
    cut = xa_ref.shape[1]
    value = dot(xa_ref[...], w_ref[0, :cut], NN) + dot(xb_ref[...], w_ref[0, cut:], NN)
    out_ref[:, : value.shape[1]] = value.astype(BF)
    out_ref[:, value.shape[1] :] = jnp.zeros_like(out_ref[:, value.shape[1] :])


def split_product(head, xa, xb, weight, name, *deps):
    columns = weight.shape[2]
    columns += -columns % 128
    rows = xa.shape[0]
    return pl.pallas_call(
        split_product_kernel,
        grid_spec=pltpu.PrefetchScalarGridSpec(
            num_scalar_prefetch=1,
            grid=(1,),
            in_specs=[
                pl.BlockSpec(xa.shape, lambda i, head: (0, 0)),
                pl.BlockSpec(xb.shape, lambda i, head: (0, 0)),
                pl.BlockSpec((1,) + weight.shape[1:], lambda i, head: (head[0], 0, 0)),
            ]
            + spare(deps),
            out_specs=pl.BlockSpec((rows, columns), lambda i, head: (0, 0)),
        ),
        out_shape=jax.ShapeDtypeStruct((rows, columns), BF),
        compiler_params=params(),
        cost_estimate=COST,
        name=name,
    )(head, xa, xb, weight, *deps)


def place_kernel(at_ref, *refs):
    del at_ref
    for slot, ref in enumerate(refs[:-1]):

        @pl.when(pl.program_id(0) == slot)
        def _():
            refs[-1][...] = ref[...]


def placed(at, slots, name):
    count = len(slots)
    rows, width = slots[0].shape
    return pl.pallas_call(
        place_kernel,
        grid_spec=pltpu.PrefetchScalarGridSpec(
            num_scalar_prefetch=1,
            grid=(count,),
            in_specs=[pl.BlockSpec((rows, width), lambda q, at: (0, 0))] * count,
            out_specs=pl.BlockSpec((rows, width), lambda q, at: (q ^ at[0], 0)),
        ),
        out_shape=jax.ShapeDtypeStruct((count * rows, width), slots[0].dtype),
        compiler_params=params(),
        cost_estimate=COST,
        name=name,
    )(at, *slots)


def attention_kernel(qa_ref, qb_ref, da_ref, db_ref, *rest, block):
    oa_ref, ob_ref, k_all, v_all, dk_acc, dv_acc = rest[-6:]
    scale = DH ** (-0.5)
    half = qa_ref.shape[0]
    for place, ref in enumerate((qa_ref, qb_ref)):
        rows = pl.ds(place * half, half)
        k_all[rows, :] = ref[:, DH : 2 * DH]
        v_all[rows, :] = ref[:, 2 * DH : 3 * DH]
    k = k_all[...]
    v = v_all[...]
    for place, (q_ref, d_ref, out_ref) in enumerate(
        ((qa_ref, da_ref, oa_ref), (qb_ref, db_ref, ob_ref))
    ):
        for start in range(0, half, block):
            rows = pl.ds(start, block)
            q = q_ref[rows, 0:DH]
            d_o = d_ref[rows, 0:DH]
            s = dot(q, k, NT) * scale
            e = jnp.exp(s - jnp.max(s, axis=-1, keepdims=True))
            p = e * (1.0 / jnp.sum(e, axis=-1, keepdims=True))
            p_b = p.astype(BF)
            o = dot(p_b, v, NN)
            delta = jnp.sum(d_o.astype(F32) * o, axis=-1, keepdims=True)
            d_p = dot(d_o, v, NT)
            ds = (p * (d_p - delta)).astype(BF)
            dq = scale * dot(ds, k, NN)
            dk = dot(ds, q, TN)
            dv = dot(p_b, d_o, TN)
            if place == 0 and start == 0:
                dk_acc[...] = dk
                dv_acc[...] = dv
            else:
                dk_acc[...] += dk
                dv_acc[...] += dv
            out_ref[rows, 0:DH] = dq.astype(BF)
            out_ref[rows, 3 * DH : 4 * DH] = o.astype(BF)
    for place, out_ref in enumerate((oa_ref, ob_ref)):
        rows = pl.ds(place * half, half)
        out_ref[:, DH : 2 * DH] = (scale * dk_acc[rows, :]).astype(BF)
        out_ref[:, 2 * DH : 3 * DH] = dv_acc[rows, :].astype(BF)


def attention(qkv_a, qkv_b, d_a, d_b, *deps):
    half = qkv_a.shape[0]
    shape = jax.ShapeDtypeStruct((half, 4 * DH), BF)
    return pl.pallas_call(
        functools.partial(attention_kernel, block=min(256, half)),
        in_specs=[pl.BlockSpec(memory_space=pltpu.VMEM)] * 4 + spare(deps),
        out_shape=[shape, shape],
        scratch_shapes=[
            pltpu.VMEM((2 * half, DH), BF),
            pltpu.VMEM((2 * half, DH), BF),
            pltpu.VMEM((2 * half, DH), F32),
            pltpu.VMEM((2 * half, DH), F32),
        ],
        compiler_params=params(),
        cost_estimate=COST,
        name="attention",
    )(qkv_a, qkv_b, d_a, d_b, *deps)


def term_kernel(head_ref, a_ref, b_ref, w_ref, *rest, first, last):
    head = head_ref[0]
    total = dot(a_ref[:, first:last], w_ref[head], NN)
    total += dot(b_ref[:, first:last], w_ref[1 - head], NN)
    rest[-1][...] = total.astype(BF)


def pair_term(head, mine, got, weight, first, last, name, *deps):
    half, full = mine.shape
    heads, depth, width = weight.shape
    tile = 512 if width % 512 == 0 else width
    return pl.pallas_call(
        functools.partial(term_kernel, first=first, last=last),
        grid_spec=pltpu.PrefetchScalarGridSpec(
            num_scalar_prefetch=1,
            grid=(width // tile,),
            in_specs=[
                pl.BlockSpec((half, full), lambda n, at: (0, 0)),
                pl.BlockSpec((half, full), lambda n, at: (0, 0)),
                pl.BlockSpec((heads, depth, tile), lambda n, at: (0, 0, n)),
            ]
            + spare(deps),
            out_specs=pl.BlockSpec((half, tile), lambda n, at: (0, n)),
        ),
        out_shape=jax.ShapeDtypeStruct((half, width), BF),
        compiler_params=params(),
        cost_estimate=COST,
        name=name,
    )(head, mine, got, weight, *deps)


def part_kernel(head_ref, x_ref, w_ref, *rest, last):
    del head_ref
    total = dot(x_ref[:, :last], w_ref[0], NN)
    if len(rest) > 1:
        total += rest[0][...]
    rest[-1][...] = total.astype(rest[-1].dtype)


def term_part(head, x, weight, last, name, *before):
    half, full = x.shape
    _, depth, width = weight.shape
    tile = 512 if width % 512 == 0 else width
    column = pl.BlockSpec((half, tile), lambda n, at: (0, n))
    return pl.pallas_call(
        functools.partial(part_kernel, last=last),
        grid_spec=pltpu.PrefetchScalarGridSpec(
            num_scalar_prefetch=1,
            grid=(width // tile,),
            in_specs=[
                pl.BlockSpec((half, full), lambda n, at: (0, 0)),
                pl.BlockSpec((1, depth, tile), lambda n, at: (at[0], 0, n)),
            ]
            + [column] * len(before),
            out_specs=column,
        ),
        out_shape=jax.ShapeDtypeStruct((half, width), BF if before else F32),
        compiler_params=params(),
        cost_estimate=COST,
        name=name,
    )(head, x, weight, *before)


def weight_kernel(
    at_ref, xa_ref, ya_ref, xb_ref, yb_ref, ga_ref, gb_ref, ra_ref, rb_ref, *rest
):
    out_refs, turned = rest[:-1], rest[-1]
    step = pl.program_id(0)
    last = (step ^ at_ref[0]) == pl.num_programs(0) - 1
    xa = jnp.where(last, ya_ref[...], xa_ref[...])
    xb = jnp.where(last, yb_ref[...], xb_ref[...])
    half = ra_ref.shape[0]
    split = 3 * DH

    @pl.when(step == 0)
    def _():
        turned[:, :half] = ra_ref[...].T
        turned[:, half:] = rb_ref[...].T

    a, b = slice(0, half), slice(half, 2 * half)
    qkv = dot(turned[:split, a], xa, NN) + dot(turned[:split, b], xb, NN)
    out = dot(turned[split:, a], ga_ref[...], NN) + dot(turned[split:, b], gb_ref[...], NN)
    keep_a, send_a, keep_b, send_b = out_refs
    rows = keep_a.shape[1]
    for slot in range(4):

        @pl.when(step == slot)
        def _():
            first = keep_a if slot % 2 == 0 else send_a
            second = keep_b if slot < 2 else send_b
            first[slot // 2] = qkv[:rows].astype(BF)
            second[slot % 2, : split - rows] = qkv[rows:].astype(BF)
            second[slot % 2, split - rows :] = out.astype(BF)


def weight_gradients(at, xa, ya, xb, yb, ga, gb, ra, rb, seqs):
    half, width = ga.shape
    chunk = width // seqs
    full = ra.shape[1]
    some = pl.BlockSpec((half, chunk), lambda r, at: (0, jnp.minimum(r ^ at[0], seqs - 2)))
    only = pl.BlockSpec((half, chunk), lambda r, at: (0, 0))
    column = pl.BlockSpec((half, chunk), lambda r, at: (0, r ^ at[0]))
    rest = pl.BlockSpec((half, full), lambda r, at: (0, 0))
    return pl.pallas_call(
        weight_kernel,
        grid_spec=pltpu.PrefetchScalarGridSpec(
            num_scalar_prefetch=1,
            grid=(seqs,),
            in_specs=[some, only] * 2 + [column] * 2 + [rest] * 2,
            out_specs=[pl.BlockSpec((2, full // 2, chunk), lambda r, at: (0, 0, 0))] * 4,
            scratch_shapes=[pltpu.VMEM((full, 2 * half), BF)],
        ),
        out_shape=[jax.ShapeDtypeStruct((2, full // 2, chunk), BF)] * 4,
        compiler_params=params(STREAMING_LIMIT),
        cost_estimate=COST,
        name="weight_gradients",
    )(at, xa, ya, xb, yb, ga, gb, ra, rb)


def turn_kernel(keep_a, got_a, keep_b, got_b, *rest):
    out_a, out_b = rest[-2:]
    for keep, got, out in ((keep_a, got_a, out_a), (keep_b, got_b, out_b)):
        out[...] = (keep[1].astype(F32) + got[1].astype(F32)).astype(BF)


def weight_turn(keep_a, got_a, keep_b, got_b, *deps):
    shape = jax.ShapeDtypeStruct(keep_a.shape[1:], BF)
    return pl.pallas_call(
        turn_kernel,
        in_specs=[pl.BlockSpec(memory_space=pltpu.VMEM)] * 4 + spare(deps),
        out_shape=[shape, shape],
        compiler_params=params(),
        cost_estimate=COST,
        name="weight_turn",
    )(keep_a, got_a, keep_b, got_b, *deps)


def weight_sum_kernel(keep_a, got_a, last_a, keep_b, got_b, last_b, *rest):
    out_refs = rest[-2:]
    split = 3 * DH
    parts = [
        keep[0].astype(F32) + got[0].astype(F32) + last[...].astype(F32)
        for keep, got, last in ((keep_a, got_a, last_a), (keep_b, got_b, last_b))
    ]
    total = jnp.concatenate(parts, axis=0)
    turned = total[:split].T.astype(BF)
    quarter = DH // 2
    for part, out_ref in enumerate(out_refs):
        out_ref[:, :split] = turned[part * DH : (part + 1) * DH]
        first = split + part * quarter
        piece = total[first : first + quarter].astype(BF)
        out_ref[:quarter, split:] = piece[:, :DH]
        out_ref[quarter:, split:] = piece[:, DH:]


def weight_sum(keep_a, got_a, last_a, keep_b, got_b, last_b, *deps):
    _, rows, chunk = keep_a.shape
    return pl.pallas_call(
        weight_sum_kernel,
        in_specs=[pl.BlockSpec(memory_space=pltpu.VMEM)] * 6 + spare(deps),
        out_shape=[jax.ShapeDtypeStruct((chunk // 2, 2 * rows), BF)] * 2,
        compiler_params=params(),
        cost_estimate=COST,
        name="weight_sum",
    )(keep_a, got_a, last_a, keep_b, got_b, last_b, *deps)


def unpack_kernel(at_ref, *refs):
    qkv_ref, out_ref, token_ref = refs[-3:]
    step = pl.program_id(0)
    split = 3 * DH
    quarter = DH // 2
    token_ref[...] = jnp.zeros_like(token_ref)
    for half in range(2):

        @pl.when(step // 2 == half)
        def _():
            mine = refs[half][...].astype(F32)
            other = refs[2 + half][...].astype(F32)
            swapped = at_ref[1] != 0
            low = jnp.where(swapped, other, mine)
            high = jnp.where(swapped, mine, other)
            for i in range(3):
                columns = slice(i * DH, (i + 1) * DH)
                qkv_ref[i] = jnp.concatenate([low[:, columns], high[:, columns]], axis=1)
            for head, value in enumerate((low, high)):
                folded = [value[:quarter, split:], value[quarter:, split:]]
                out_ref[head, 0] = jnp.concatenate(folded, axis=1)


def unpack_weights(at, mine, other, far, before=(), *deps):
    rows, full = mine[0].shape
    half = rows // 2
    width = 4 * rows

    def chunk(t, at):
        if far:
            return at[0] ^ jnp.where(t < 2, t + 2, 2 * t - 3)
        return at[0] ^ jnp.where(t < 2, t, 2 * t - 4)

    specs = [
        pl.BlockSpec((half, full), lambda t, at: (jnp.minimum(t, 1), 0)),
        pl.BlockSpec((half, full), lambda t, at: (jnp.maximum(t - 2, 0), 0)),
    ]
    return pl.pallas_call(
        unpack_kernel,
        grid_spec=pltpu.PrefetchScalarGridSpec(
            num_scalar_prefetch=1,
            grid=(4,),
            in_specs=specs * 2 + spare(tuple(before) + deps),
            out_specs=[
                pl.BlockSpec((3, half, 2 * DH), lambda t, at: (0, 2 * chunk(t, at) + t // 2, 0)),
                pl.BlockSpec(
                    (2, 1, DH // 2, rows), lambda t, at: (0, t // 2, 0, chunk(t, at))
                ),
                pl.BlockSpec(TOKEN.shape, lambda t, at: (0, 0)),
            ],
        ),
        out_shape=[
            jax.ShapeDtypeStruct((3, width, 2 * DH), F32),
            jax.ShapeDtypeStruct((2, 2, DH // 2, width), F32),
            TOKEN,
        ],
        input_output_aliases={5 + i: i for i in range(len(before))},
        compiler_params=params(),
        cost_estimate=COST,
        name="weight_outputs_far" if far else "weight_outputs_near",
    )(at, *mine, *other, *before, *deps)


def neighbour_edges(first, last):
    axes = ("seq", "head")
    count = lax.axis_size(axes)
    forward = [(i, i + 1) for i in range(count - 1)]
    backward = [(target, source) for source, target in forward]
    return lax.ppermute(last, axes, forward), lax.ppermute(first, axes, backward)


def after(value, *others):
    return lax.optimization_barrier((value,) + others)[0]


def trade_chip(x, bit, heads):
    count = lax.axis_size("seq")
    return lax.ppermute(x, "seq", [(s, s ^ (bit * heads)) for s in range(count)])


def trade_z(x, bit):
    count = lax.axis_size("head")
    return lax.ppermute(x, "head", [(z, z ^ bit) for z in range(count)])


def swap_heads(x):
    count = lax.axis_size("seq")
    return lax.ppermute(x, "seq", [(s, s + 1 - 2 * (s % 2)) for s in range(count)])


def unit_body(enc_in, conv_weight, norm_gain, w_qkv, w_out, grad_out):
    rows = enc_in.shape[0] // 2
    seqs = enc_in.shape[1]
    width = conv_weight.shape[2]
    local = w_qkv.shape[2]
    heads = local // DH
    groups = lax.axis_size("head")
    half = groups * seqs * rows
    place = lax.axis_index("seq")
    own_seq = (place // heads).astype(jnp.int32)
    own_head = (place % heads).astype(jnp.int32)
    at = jnp.stack([own_seq, own_head])
    head_mine = own_head.reshape(1)
    head_other = (1 - own_head).reshape(1)

    def to_chips(slots):
        return [x if j == 0 else trade_chip(x, j, heads) for j, x in enumerate(slots)]

    order = (0, 2, 1, 3)

    grad_z = lax.all_gather(grad_out, "head", axis=0, tiled=False)

    pairs = jnp.transpose(enc_in.reshape(rows, 2, seqs, enc_in.shape[2]), (1, 2, 0, 3))
    low, high = neighbour_edges(pairs[:, :, :1, :], pairs[:, :, -1:, :])
    skip, slope, normed = encoder(at, pairs, low, high, conv_weight, norm_gain)
    normed = to_chips(normed)
    edge = width - width // seqs
    slab_a = jnp.concatenate([normed[j][:, :edge] for j in order], axis=0)
    slab_b = jnp.concatenate([normed[j][:, edge:] for j in order], axis=0)
    normed_a = lax.all_gather(slab_a, "head", axis=0, tiled=True)
    slabs_b = [slab_b if q == 0 else trade_z(slab_b, q) for q in range(groups)]
    normed_b = placed(lax.axis_index("head").astype(jnp.int32).reshape(1), slabs_b, "normed_last")

    grad_z = after(grad_z, slab_a)
    grad_slots = to_chips(
        [lax.dynamic_index_in_dim(grad_z, own_seq ^ j, 2, keepdims=False) for j in range(seqs)]
    )
    w_pack, w_turned, packed = pack_weights(after(w_qkv, slab_a))
    *grad_slots, packed, normed_b = lax.optimization_barrier((*grad_slots, packed, normed_b))
    grad_rows = jnp.stack([grad_slots[j] for j in order], axis=1).reshape(half, width)
    w_rows = w_out.reshape(heads, DH, width)
    d_other, one = head_product(head_other, grad_rows, w_rows, NT, "d_o_other")
    d_got = swap_heads(d_other)
    d_mine, two = head_product(head_mine, grad_rows, w_rows, NT, "d_o_own")
    grad_swapped = swap_heads(grad_rows)
    normed_a, normed_b, d_got, d_mine, grad_swapped, w_pack, w_turned, *tokens = (
        lax.optimization_barrier(
            (normed_a, normed_b, d_got, d_mine, grad_swapped, w_pack, w_turned, packed, one, two)
        )
    )

    swapped_a, swapped_b = swap_heads(normed_a), swap_heads(normed_b)
    qkv_other = split_product(head_other, normed_a, normed_b, w_pack, "qkv_other", *tokens)
    qkv_got = swap_heads(qkv_other)
    qkv_mine = split_product(head_mine, normed_a, normed_b, w_pack, "qkv_own")
    result_mine, result_other = attention(
        qkv_mine, qkv_got, d_mine, d_got, swapped_a, swapped_b
    )
    result_got = swap_heads(result_other)

    shape = (groups, seqs, rows, width)
    d_own = term_part(head_mine, result_mine, w_turned, 3 * DH, "d_term_own")
    d_term = term_part(head_other, result_got, w_turned, 3 * DH, "d_term", d_own)
    d_normed = lax.psum_scatter(d_term.reshape(shape), "head", scatter_dimension=0, tiled=False)
    keep_a, send_a, keep_b, send_b = weight_gradients(
        own_seq.reshape(1),
        normed_a,
        normed_b,
        swapped_a,
        swapped_b,
        grad_rows,
        grad_swapped,
        result_mine,
        result_other,
        seqs,
    )
    got_a, got_b = trade_chip(send_a, 1, heads), trade_chip(send_b, 2, heads)
    head_term = pair_term(
        head_mine, result_mine, result_got, w_rows, 3 * DH, 4 * DH, "head_term"
    )
    head_sum = lax.psum_scatter(head_term.reshape(shape), "head", scatter_dimension=0, tiled=False)
    turn_a, turn_b = weight_turn(keep_a, got_a, keep_b, got_b, head_term)
    last_a, last_b = trade_chip(turn_a, 2, heads), trade_chip(turn_b, 1, heads)

    d_normed = after(d_normed, turn_a, turn_b)
    leaving = d_normed[2:]
    near = trade_chip(leaving, 1, heads)
    far = trade_chip(jnp.stack([d_normed[1], near[1]]), 2, heads)
    half_a, half_b = weight_sum(keep_a, got_a, last_a, keep_b, got_b, last_b, leaving)
    grad = jnp.transpose(after(grad_out, d_term), (1, 0, 2))
    d_conv, first, last = conv_gradient(
        at, d_normed, near, far, skip, grad, norm_gain, slope, half_a
    )
    low, high = neighbour_edges(first, last)
    low, high, at_hand = lax.optimization_barrier((low, high, marker(conv_weight, first)))

    got_a, got_b = trade_chip(half_a, 1, heads), trade_chip(half_b, 2, heads)
    near_a = jnp.concatenate([half_a, after(got_a, low)], axis=0)
    near_b = jnp.concatenate([half_b, after(got_b, high)], axis=0)
    far_a = trade_chip(near_a, 2, heads)
    far_b = trade_chip(near_b, 1, heads)
    near_other = [swap_heads(near_a), swap_heads(near_b)]
    grad_input = conv_back(d_conv, low, high, conv_weight, at_hand, *near_other)
    *outputs, token = unpack_weights(
        at, [near_a, near_b], near_other, False, (), grad_input
    )

    head_sum = after(head_sum, grad_input, token)
    head_sum = to_chips([head_sum[order.index(j)] for j in range(seqs)])
    far_other = [swap_heads(after(x, *head_sum[1:])) for x in (far_a, far_b)]
    grad_w_qkv, grad_w_out, _ = unpack_weights(at, [far_a, far_b], far_other, True, outputs)
    mixed = mixed_call(at, head_sum, skip, token)
    grad_input = jnp.transpose(grad_input.reshape(2, seqs, rows, -1), (2, 0, 1, 3))
    return (
        jnp.transpose(mixed, (1, 0, 2)),
        grad_input.reshape(enc_in.shape),
        grad_w_qkv,
        grad_w_out.reshape(local, width),
    )


def padded_2(block, sides, width):
    for axis, dim in sides:
        count = lax.axis_size(axis)
        forward = [(i, i + 1) for i in range(count - 1)]
        backward = [(target, source) for source, target in forward]
        low = lax.ppermute(
            lax.slice_in_dim(block, block.shape[dim] - width, None, axis=dim), axis, forward
        )
        high = lax.ppermute(lax.slice_in_dim(block, 0, width, axis=dim), axis, backward)
        block = jnp.concatenate([low, block, high], axis=dim)
    return block


def gathered_body(enc_in, conv_weight, norm_gain, w_qkv, w_out, grad_out):
    fine_rows = enc_in.shape[0]
    slab_rows = fine_rows // 2
    seq_count = enc_in.shape[1]
    out_width = conv_weight.shape[2]
    local_width = w_qkv.shape[2]
    local_heads = local_width // DH
    logit_scale = DH ** (-0.5)
    padded = padded_2(enc_in, ((("seq", "head"), 0),), 2)
    convolved = jnp.zeros((fine_rows, seq_count, out_width), jnp.float32)
    for offset in range(KW):
        convolved = convolved + jnp.einsum(
            "tbi,io->tbo",
            padded[offset : offset + fine_rows],
            conv_weight[offset],
            preferred_element_type=jnp.float32,
        )
    activated, gelu_pull = jax.vjp(jax.nn.gelu, convolved)
    skip = jnp.mean(activated.reshape(slab_rows, 2, seq_count, out_width), axis=1).astype(
        jnp.bfloat16
    )
    skip_wide = skip.astype(jnp.float32)
    inv_rms = lax.rsqrt(jnp.mean(skip_wide * skip_wide, axis=-1, keepdims=True) + 1e-06)
    normed = (skip_wide * inv_rms * norm_gain).astype(jnp.bfloat16)
    normed_rows = lax.all_gather(normed, "head", axis=0, tiled=True)
    grad_rows = lax.all_gather(grad_out, "head", axis=0, tiled=True)
    tower_rows = normed_rows.shape[0]
    qkv = jnp.einsum(
        "tbc,ice->itbe", normed_rows, w_qkv, preferred_element_type=jnp.float32
    ).astype(jnp.bfloat16)
    qkv = qkv.reshape(3, tower_rows, seq_count, local_heads, DH)
    query_matrix, key_matrix, value_matrix = (qkv[0], qkv[1], qkv[2])
    key_all, value_all = (
        lax.all_gather(key_matrix, "seq", axis=0, tiled=True),
        lax.all_gather(value_matrix, "seq", axis=0, tiled=True),
    )
    attention_logits = (
        jnp.einsum("qbhd,kbhd->bhqk", query_matrix, key_all, preferred_element_type=jnp.float32)
        * logit_scale
    )
    row_peak = jnp.max(attention_logits, axis=-1, keepdims=True)
    exponent = jnp.exp(attention_logits - row_peak)
    row_total = jnp.sum(exponent, axis=-1, keepdims=True)
    soft_weights = exponent / row_total
    narrow_probabilities = soft_weights.astype(jnp.bfloat16)
    attention_output = jnp.einsum(
        "bhqk,kbhd->qbhd", narrow_probabilities, value_all, preferred_element_type=jnp.float32
    )
    o_narrow = attention_output.reshape(tower_rows, seq_count, local_width).astype(jnp.bfloat16)
    piece = o_narrow
    head_sum = lax.psum_scatter(
        jnp.einsum("tbe,ec->tbc", piece, w_out, preferred_element_type=jnp.float32).astype(
            jnp.bfloat16
        ),
        "head",
        scatter_dimension=0,
        tiled=True,
    ).astype(jnp.float32)
    mixed = (skip_wide + head_sum).astype(jnp.bfloat16)
    part_w_out = jnp.einsum("tbe,tbc->ec", o_narrow, grad_rows, preferred_element_type=jnp.float32)
    d_out = jnp.einsum("tbc,ec->tbe", grad_rows, w_out, preferred_element_type=jnp.float32).astype(
        jnp.bfloat16
    )
    d_out = d_out.reshape(tower_rows, seq_count, local_heads, DH)
    delta = jnp.sum(d_out.astype(jnp.float32) * attention_output, axis=-1)
    probability_gradient = jnp.einsum(
        "qbhd,kbhd->bhqk", d_out, value_all, preferred_element_type=jnp.float32
    )
    d_scores = soft_weights * (probability_gradient - jnp.transpose(delta, (1, 2, 0))[..., None])
    narrow_gradient = d_scores.astype(jnp.bfloat16)
    query_gradient = logit_scale * jnp.einsum(
        "bhqk,kbhd->qbhd", narrow_gradient, key_all, preferred_element_type=jnp.float32
    )
    key_terms = logit_scale * jnp.einsum(
        "bhqk,qbhd->kbhd", narrow_gradient, query_matrix, preferred_element_type=jnp.float32
    )
    value_terms = jnp.einsum(
        "bhqk,qbhd->kbhd", narrow_probabilities, d_out, preferred_element_type=jnp.float32
    )
    d_keys, d_values = (
        lax.psum_scatter(
            key_terms.astype(jnp.bfloat16), "seq", scatter_dimension=0, tiled=True
        ).astype(jnp.float32),
        lax.psum_scatter(
            value_terms.astype(jnp.bfloat16), "seq", scatter_dimension=0, tiled=True
        ).astype(jnp.float32),
    )
    dqkv = (
        jnp.stack([query_gradient, d_keys, d_values])
        .reshape(3, tower_rows, seq_count, local_width)
        .astype(jnp.bfloat16)
    )
    part_w_qkv = jnp.einsum("tbc,itbe->ice", normed_rows, dqkv, preferred_element_type=jnp.float32)
    piece = dqkv
    d_normed = lax.psum_scatter(
        jnp.einsum("itbe,ice->tbc", piece, w_qkv, preferred_element_type=jnp.float32).astype(
            jnp.bfloat16
        ),
        "head",
        scatter_dimension=0,
        tiled=True,
    ).astype(jnp.float32)
    unit_rows = skip_wide * inv_rms
    scaled = d_normed * norm_gain
    d_skip = grad_out.astype(jnp.float32) + inv_rms * (
        scaled - unit_rows * jnp.mean(scaled * unit_rows, axis=-1, keepdims=True)
    )
    d_act = jnp.repeat(d_skip, 2, axis=0) * 0.5
    d_conv = gelu_pull(d_act)[0].astype(jnp.bfloat16)
    d_pad = padded_2(d_conv, ((("seq", "head"), 0),), 2)
    grad_input = jnp.zeros((fine_rows, seq_count, enc_in.shape[2]), jnp.float32)
    for offset in range(KW):
        grad_input = grad_input + jnp.einsum(
            "tbo,io->tbi",
            d_pad[4 - offset : 4 - offset + fine_rows],
            conv_weight[offset],
            preferred_element_type=jnp.float32,
        )
    grad_w_qkv, grad_w_out = (
        lax.psum(part_w_qkv.astype(jnp.bfloat16), "seq").astype(jnp.float32),
        lax.psum(part_w_out.astype(jnp.bfloat16), "seq").astype(jnp.float32),
    )
    return (mixed, grad_input.astype(jnp.bfloat16), grad_w_qkv, grad_w_out)


def body(enc_in, conv_weight, norm_gain, w_qkv, w_out, grad_out):
    heads = w_qkv.shape[2] // DH
    seqs = enc_in.shape[1]
    fits = lax.axis_size("head") == 4 and heads == 2 and seqs == 4 and seqs * heads == lax.axis_size("seq")
    fits = fits and conv_weight.shape[2] == seqs * w_qkv.shape[2]
    chosen = unit_body if fits else gathered_body
    return chosen(enc_in, conv_weight, norm_gain, w_qkv, w_out, grad_out)


def solution(mesh):
    return jax.shard_map(
        body,
        mesh=mesh,
        in_specs=(
            P(("seq", "head"), None, None),
            P(),
            P(),
            P(None, None, "head"),
            P("head", None),
            P(("seq", "head"), None, None),
        ),
        out_specs=(
            P(("seq", "head"), None, None),
            P(("seq", "head"), None, None),
            P(None, None, "head"),
            P("head", None),
        ),
        check_vma=False,
    )
```

```python
import functools

import jax
import jax.numpy as jnp
from jax import lax
from jax.experimental import pallas as pl
from jax.experimental.pallas import tpu as pltpu
from jax.sharding import PartitionSpec as P

DH = 192
KW = 5
VMEM_LIMIT = 24 * 1024 * 1024
STREAMING_LIMIT = 56 * 1024 * 1024
COST = pl.CostEstimate(flops=1000, bytes_accessed=1000, transcendentals=0)
BF = jnp.bfloat16
F32 = jnp.float32
TOKEN = jax.ShapeDtypeStruct((8, 128), F32)


def params(limit=VMEM_LIMIT):
    return pltpu.CompilerParams(vmem_limit_bytes=limit)


def dot(a, b, contract):
    return lax.dot_general(a, b, (contract, ((), ())), preferred_element_type=F32)


NN = ((1,), (0,))
NT = ((1,), (1,))
TN = ((0,), (0,))


def whole(shape):
    return pl.BlockSpec(shape, lambda *_: (0,) * len(shape))


SCALARS = pl.BlockSpec(memory_space=pltpu.SMEM)


def spare(deps):
    return [pl.BlockSpec(memory_space=pl.ANY)] * len(deps)


def turned_rows(ref, low_ref, high_ref, parity, shift):
    seqs, rows, width = ref.shape[1:]
    own = ref[parity]
    if shift != 1:
        wide = own.astype(F32)
        if shift == 0:
            parts = [low_ref[parity].astype(F32), wide[:, : rows - 1]]
        else:
            parts = [wide[:, 1:], high_ref[parity].astype(F32)]
        own = jnp.concatenate(parts, axis=1).astype(BF)
    return own.reshape(seqs * rows, width)


def conv_kernel(
    at_ref, x_ref, low_ref, high_ref, w_ref, gain_ref, skip_ref, slope_ref, *rest
):
    normed_refs, (lhs, squares, whole_normed) = rest[:-3], rest[-3:]
    step = pl.program_id(0)
    seqs, rows, c_in = x_ref.shape[1:]
    half = seqs * rows
    tile = w_ref.shape[2]

    @pl.when(step == 0)
    def _():
        for parity in range(2):
            for shift in range(3):
                value = turned_rows(x_ref, low_ref, high_ref, parity, shift)
                for out in range(2):
                    tap = 2 * shift + parity - out
                    if 0 <= tap < KW:
                        lhs[out * half : (out + 1) * half, tap * c_in : (tap + 1) * c_in] = value
        squares[...] = jnp.zeros_like(squares)

    conv = dot(lhs[...], w_ref[...].reshape(KW * c_in, tile), NN)
    root = 0.7978845608028654
    total = None
    for parity in range(2):
        x = conv[parity * half : (parity + 1) * half, :]
        square = x * x
        t = jnp.tanh(root * (x + 0.044715 * (square * x)))
        left = 0.5 * (1.0 + t)
        act = x * left
        slope = left + (0.5 * root) * x * (1.0 - t * t) * (1.0 + (3 * 0.044715) * square)
        slope_ref[parity] = slope.reshape(slope_ref.shape[1:])
        total = act if total is None else total + act
    skip = (0.5 * total).astype(BF)
    columns = pl.ds(pl.multiple_of(step * tile, tile), tile)
    skip_ref[:, :, columns] = skip.reshape(seqs, rows, tile)
    wide = skip.astype(F32)
    squares[...] += jnp.sum(wide * wide, axis=-1, keepdims=True)

    @pl.when(step == pl.num_programs(0) - 1)
    def _():
        width = skip_ref.shape[2]
        inv = lax.rsqrt(squares[...] * (1.0 / width) + 1e-06)
        wide = skip_ref[...].reshape(half, width).astype(F32)
        normed = (wide * inv * gain_ref[...]).astype(BF)
        whole_normed[...] = normed.reshape(whole_normed.shape)
        for slot in range(seqs):
            normed_refs[slot][...] = whole_normed[at_ref[0] ^ slot]


def encoder(at, pairs, low, high, conv_weight, norm_gain):
    _, seqs, rows, c_in = pairs.shape
    width = conv_weight.shape[2]
    tile = 256 if width % 256 == 0 else width
    shape = (seqs, rows, width)
    outs = pl.pallas_call(
        conv_kernel,
        grid=(width // tile,),
        in_specs=[
            SCALARS,
            whole(pairs.shape),
            whole(low.shape),
            whole(high.shape),
            pl.BlockSpec((KW, c_in, tile), lambda n: (0, 0, n)),
            whole((1, width)),
        ],
        out_specs=[
            whole(shape),
            pl.BlockSpec((2, seqs, rows, tile), lambda n: (0, 0, 0, n)),
        ]
        + [whole((rows, width))] * seqs,
        out_shape=[
            jax.ShapeDtypeStruct(shape, BF),
            jax.ShapeDtypeStruct((2,) + shape, F32),
        ]
        + [jax.ShapeDtypeStruct((rows, width), BF)] * seqs,
        scratch_shapes=[
            pltpu.VMEM((2 * seqs * rows, KW * c_in), BF),
            pltpu.VMEM((seqs * rows, 1), F32),
            pltpu.VMEM(shape, BF),
        ],
        compiler_params=params(STREAMING_LIMIT),
        cost_estimate=COST,
        name="encoder_forward",
    )(at, pairs, low, high, conv_weight, norm_gain.reshape(1, width))
    return outs[0], outs[1], list(outs[2:])


def d_conv_kernel(at_ref, own_ref, near_ref, far_ref, *refs):
    skip_ref, grad_ref, gain_ref, slope_ref = refs[:4]
    out_ref, first_ref, last_ref = refs[-3:]
    rows = out_ref.shape[2]
    for slot, (ref, place) in enumerate(((own_ref, 0), (near_ref, 0), (far_ref, 0), (far_ref, 1))):
        b = at_ref[0] ^ slot
        wide = skip_ref[b].astype(F32)
        inv = lax.rsqrt(jnp.mean(wide * wide, axis=-1, keepdims=True) + 1e-06)
        unit = wide * inv
        scaled = ref[place].astype(F32) * gain_ref[...]
        d_skip = grad_ref[b].astype(F32) + inv * (
            scaled - unit * jnp.mean(scaled * unit, axis=-1, keepdims=True)
        )
        d_act = 0.5 * d_skip
        for parity in range(2):
            value = slope_ref[parity, b] * d_act
            out_ref[parity, b] = value.astype(BF)
            first_ref[parity, b] = value[:1].astype(BF)
            last_ref[parity, b] = value[rows - 1 :].astype(BF)


def conv_gradient(at, own, near, far, skip, grad, norm_gain, slope, *deps):
    vmem = pl.BlockSpec(memory_space=pltpu.VMEM)
    edge = jax.ShapeDtypeStruct(slope.shape[:2] + (1, slope.shape[3]), BF)
    return pl.pallas_call(
        d_conv_kernel,
        in_specs=[SCALARS] + [vmem] * 7 + spare(deps),
        out_specs=[vmem] * 3,
        out_shape=[jax.ShapeDtypeStruct(slope.shape, BF)] + [edge] * 2,
        compiler_params=params(),
        cost_estimate=COST,
        name="conv_gradient",
    )(at, own, near, far, skip, grad, norm_gain.reshape(1, -1), slope, *deps)


def mixed_body(seqs, at_ref, *refs):
    skip_ref, out_ref = refs[seqs], refs[-1]
    for slot in range(seqs):
        b = at_ref[0] ^ slot
        out_ref[b] = (skip_ref[b].astype(F32) + refs[slot][...].astype(F32)).astype(BF)


def mixed_call(at, terms, skip, *deps):
    seqs = len(terms)
    vmem = pl.BlockSpec(memory_space=pltpu.VMEM)
    return pl.pallas_call(
        functools.partial(mixed_body, seqs),
        in_specs=[SCALARS] + [vmem] * (seqs + 1) + spare(deps),
        out_specs=vmem,
        out_shape=jax.ShapeDtypeStruct(skip.shape, BF),
        compiler_params=params(),
        cost_estimate=COST,
        name="mixed_sum",
    )(at, *terms, skip, *deps)


def marker_kernel(*refs):
    refs[-1][...] = jnp.zeros_like(refs[-1])


def marker(*deps):
    return pl.pallas_call(
        marker_kernel,
        in_specs=spare(deps),
        out_shape=TOKEN,
        compiler_params=params(),
        cost_estimate=COST,
        name="marker",
    )(*deps)


def conv_back_kernel(d_ref, low_ref, high_ref, w_ref, *rest):
    out_ref, turned, acc = rest[-3:]
    step = pl.program_id(0)

    @pl.when(step == 0)
    def _():
        for parity in range(2):
            for shift in range(3):
                turned[parity, shift] = turned_rows(d_ref, low_ref, high_ref, parity, shift).T

    for tap in range(KW):

        @pl.when(step == tap)
        def _():
            places = [KW - 1 - tap, KW - tap]
            rhs = jnp.concatenate([turned[p % 2, p // 2] for p in places], axis=1)
            term = dot(w_ref[0], rhs, NN)
            if tap == 0:
                acc[...] = term
            elif tap < KW - 1:
                acc[...] += term
            else:
                out_ref[...] = (acc[...] + term).T.astype(BF)


def conv_back(d_conv, low, high, conv_weight, *deps):
    _, seqs, rows, width = d_conv.shape
    c_in = conv_weight.shape[1]
    flat = 2 * seqs * rows
    return pl.pallas_call(
        conv_back_kernel,
        grid=(KW,),
        in_specs=[
            whole(d_conv.shape),
            whole(low.shape),
            whole(high.shape),
            pl.BlockSpec((1, c_in, width), lambda k: (k, 0, 0)),
        ]
        + spare(deps),
        out_specs=whole((flat, c_in)),
        out_shape=jax.ShapeDtypeStruct((flat, c_in), BF),
        scratch_shapes=[
            pltpu.VMEM((2, 3, width, seqs * rows), BF),
            pltpu.VMEM((c_in, flat), F32),
        ],
        compiler_params=params(),
        cost_estimate=COST,
        name="encoder_backward",
    )(d_conv, low, high, conv_weight, *deps)


def pack_kernel(at_ref, w_ref, own_ref, other_ref, own_turned, other_turned, token_ref):
    token_ref[...] = jnp.zeros_like(token_ref)
    first_head = at_ref[1] == 0
    for i in range(3):
        low, high = w_ref[i, :, :DH], w_ref[i, :, DH:]
        columns = slice(i * DH, (i + 1) * DH)
        own = jnp.where(first_head, low, high)
        other = jnp.where(first_head, high, low)
        own_ref[:, columns] = own
        other_ref[:, columns] = other
        own_turned[columns, :] = own.T
        other_turned[columns, :] = other.T


def pack_weights(at, w_qkv):
    _, width, local = w_qkv.shape
    tile = local
    plain = pl.BlockSpec((tile, 3 * DH), lambda n: (n, 0))
    turned = pl.BlockSpec((3 * DH, tile), lambda n: (0, n))
    return pl.pallas_call(
        pack_kernel,
        grid=(width // tile,),
        in_specs=[SCALARS, pl.BlockSpec((3, tile, local), lambda n: (0, n, 0))],
        out_specs=[plain, plain, turned, turned, pl.BlockSpec(TOKEN.shape, lambda n: (0, 0))],
        out_shape=[jax.ShapeDtypeStruct((width, 3 * DH), BF)] * 2
        + [jax.ShapeDtypeStruct((3 * DH, width), BF)] * 2
        + [TOKEN],
        compiler_params=params(),
        cost_estimate=COST,
        name="pack_weights",
    )(at, w_qkv)


def product_kernel(head_ref, x_ref, w_ref, *rest, contract):
    del head_ref
    out_ref, token_ref = rest[-2:]
    token_ref[...] = jnp.zeros_like(token_ref)
    value = dot(x_ref[...], w_ref[0], contract).astype(BF)
    out_ref[:, : value.shape[1]] = value
    if value.shape[1] < out_ref.shape[1]:
        out_ref[:, value.shape[1] :] = jnp.zeros_like(out_ref[:, value.shape[1] :])


def head_product(head, x, weight, contract, name, *deps):
    columns = weight.shape[2] if contract == NN else weight.shape[1]
    columns += -columns % 128
    rows, width = x.shape
    return pl.pallas_call(
        functools.partial(product_kernel, contract=contract),
        grid_spec=pltpu.PrefetchScalarGridSpec(
            num_scalar_prefetch=1,
            grid=(1,),
            in_specs=[
                pl.BlockSpec((rows, width), lambda i, head: (0, 0)),
                pl.BlockSpec((1,) + weight.shape[1:], lambda i, head: (head[0], 0, 0)),
            ]
            + spare(deps),
            out_specs=[
                pl.BlockSpec((rows, columns), lambda i, head: (0, 0)),
                pl.BlockSpec(TOKEN.shape, lambda i, head: (0, 0)),
            ],
        ),
        out_shape=[jax.ShapeDtypeStruct((rows, columns), BF), TOKEN],
        compiler_params=params(),
        cost_estimate=COST,
        name=name,
    )(head, x, weight, *deps)


def attention_kernel(qa_ref, qb_ref, da_ref, db_ref, *rest, block):
    oa_ref, ob_ref, k_all, v_all, dk_acc, dv_acc = rest[-6:]
    scale = DH ** (-0.5)
    half = qa_ref.shape[0]
    for place, ref in enumerate((qa_ref, qb_ref)):
        rows = pl.ds(place * half, half)
        k_all[rows, :] = ref[:, DH : 2 * DH]
        v_all[rows, :] = ref[:, 2 * DH : 3 * DH]
    k = k_all[...]
    v = v_all[...]
    for place, (q_ref, d_ref, out_ref) in enumerate(
        ((qa_ref, da_ref, oa_ref), (qb_ref, db_ref, ob_ref))
    ):
        for start in range(0, half, block):
            rows = pl.ds(start, block)
            q = q_ref[rows, 0:DH]
            d_o = d_ref[rows, 0:DH]
            s = dot(q, k, NT) * scale
            e = jnp.exp(s - jnp.max(s, axis=-1, keepdims=True))
            p = e * (1.0 / jnp.sum(e, axis=-1, keepdims=True))
            p_b = p.astype(BF)
            o = dot(p_b, v, NN)
            delta = jnp.sum(d_o.astype(F32) * o, axis=-1, keepdims=True)
            d_p = dot(d_o, v, NT)
            ds = (p * (d_p - delta)).astype(BF)
            dq = scale * dot(ds, k, NN)
            dk = dot(ds, q, TN)
            dv = dot(p_b, d_o, TN)
            if place == 0 and start == 0:
                dk_acc[...] = dk
                dv_acc[...] = dv
            else:
                dk_acc[...] += dk
                dv_acc[...] += dv
            out_ref[rows, 0:DH] = dq.astype(BF)
            out_ref[rows, 3 * DH : 4 * DH] = o.astype(BF)
    for place, out_ref in enumerate((oa_ref, ob_ref)):
        rows = pl.ds(place * half, half)
        out_ref[:, DH : 2 * DH] = (scale * dk_acc[rows, :]).astype(BF)
        out_ref[:, 2 * DH : 3 * DH] = dv_acc[rows, :].astype(BF)


def attention(qkv_a, qkv_b, d_a, d_b, *deps):
    half = qkv_a.shape[0]
    shape = jax.ShapeDtypeStruct((half, 4 * DH), BF)
    return pl.pallas_call(
        functools.partial(attention_kernel, block=min(256, half)),
        in_specs=[pl.BlockSpec(memory_space=pltpu.VMEM)] * 4 + spare(deps),
        out_shape=[shape, shape],
        scratch_shapes=[
            pltpu.VMEM((2 * half, DH), BF),
            pltpu.VMEM((2 * half, DH), BF),
            pltpu.VMEM((2 * half, DH), F32),
            pltpu.VMEM((2 * half, DH), F32),
        ],
        compiler_params=params(),
        cost_estimate=COST,
        name="attention",
    )(qkv_a, qkv_b, d_a, d_b, *deps)


def term_kernel(head_ref, a_ref, b_ref, w_ref, *rest, first, last):
    head = head_ref[0]
    total = dot(a_ref[:, first:last], w_ref[head], NN)
    total += dot(b_ref[:, first:last], w_ref[1 - head], NN)
    rest[-1][...] = total.astype(BF)


def pair_term(head, mine, got, weight, first, last, name, *deps):
    half, full = mine.shape
    heads, depth, width = weight.shape
    tile = 512 if width % 512 == 0 else width
    return pl.pallas_call(
        functools.partial(term_kernel, first=first, last=last),
        grid_spec=pltpu.PrefetchScalarGridSpec(
            num_scalar_prefetch=1,
            grid=(width // tile,),
            in_specs=[
                pl.BlockSpec((half, full), lambda n, at: (0, 0)),
                pl.BlockSpec((half, full), lambda n, at: (0, 0)),
                pl.BlockSpec((heads, depth, tile), lambda n, at: (0, 0, n)),
            ]
            + spare(deps),
            out_specs=pl.BlockSpec((half, tile), lambda n, at: (0, n)),
        ),
        out_shape=jax.ShapeDtypeStruct((half, width), BF),
        compiler_params=params(),
        cost_estimate=COST,
        name=name,
    )(head, mine, got, weight, *deps)


def part_kernel(head_ref, x_ref, w_ref, *rest, last):
    del head_ref
    total = dot(x_ref[:, :last], w_ref[0], NN)
    if len(rest) > 1:
        total += rest[0][...]
    rest[-1][...] = total.astype(rest[-1].dtype)


def term_part(head, x, weight, last, name, *before):
    half, full = x.shape
    _, depth, width = weight.shape
    tile = 512 if width % 512 == 0 else width
    column = pl.BlockSpec((half, tile), lambda n, at: (0, n))
    return pl.pallas_call(
        functools.partial(part_kernel, last=last),
        grid_spec=pltpu.PrefetchScalarGridSpec(
            num_scalar_prefetch=1,
            grid=(width // tile,),
            in_specs=[
                pl.BlockSpec((half, full), lambda n, at: (0, 0)),
                pl.BlockSpec((1, depth, tile), lambda n, at: (at[0], 0, n)),
            ]
            + [column] * len(before),
            out_specs=column,
        ),
        out_shape=jax.ShapeDtypeStruct((half, width), BF if before else F32),
        compiler_params=params(),
        cost_estimate=COST,
        name=name,
    )(head, x, weight, *before)


def weight_kernel(at_ref, xa_ref, xb_ref, ga_ref, gb_ref, ra_ref, rb_ref, *rest):
    del at_ref
    out_refs, turned = rest[:-1], rest[-1]
    step = pl.program_id(0)
    half = ra_ref.shape[0]
    split = 3 * DH

    @pl.when(step == 0)
    def _():
        turned[:, :half] = ra_ref[...].T
        turned[:, half:] = rb_ref[...].T

    a, b = slice(0, half), slice(half, 2 * half)
    qkv = dot(turned[:split, a], xa_ref[...], NN) + dot(turned[:split, b], xb_ref[...], NN)
    out = dot(turned[split:, a], ga_ref[...], NN) + dot(turned[split:, b], gb_ref[...], NN)
    keep_a, send_a, keep_b, send_b = out_refs
    rows = keep_a.shape[1]
    for slot in range(4):

        @pl.when(step == slot)
        def _():
            first = keep_a if slot % 2 == 0 else send_a
            second = keep_b if slot < 2 else send_b
            first[slot // 2] = qkv[:rows].astype(BF)
            second[slot % 2, : split - rows] = qkv[rows:].astype(BF)
            second[slot % 2, split - rows :] = out.astype(BF)


def weight_gradients(at, xa, xb, ga, gb, ra, rb, seqs):
    half, width = xa.shape
    chunk = width // seqs
    full = ra.shape[1]
    column = pl.BlockSpec((half, chunk), lambda r, at: (0, r ^ at[0]))
    rest = pl.BlockSpec((half, full), lambda r, at: (0, 0))
    return pl.pallas_call(
        weight_kernel,
        grid_spec=pltpu.PrefetchScalarGridSpec(
            num_scalar_prefetch=1,
            grid=(seqs,),
            in_specs=[column] * 4 + [rest] * 2,
            out_specs=[pl.BlockSpec((2, full // 2, chunk), lambda r, at: (0, 0, 0))] * 4,
            scratch_shapes=[pltpu.VMEM((full, 2 * half), BF)],
        ),
        out_shape=[jax.ShapeDtypeStruct((2, full // 2, chunk), BF)] * 4,
        compiler_params=params(STREAMING_LIMIT),
        cost_estimate=COST,
        name="weight_gradients",
    )(at, xa, xb, ga, gb, ra, rb)


def turn_kernel(keep_a, got_a, keep_b, got_b, *rest):
    out_a, out_b = rest[-2:]
    for keep, got, out in ((keep_a, got_a, out_a), (keep_b, got_b, out_b)):
        out[...] = (keep[1].astype(F32) + got[1].astype(F32)).astype(BF)


def weight_turn(keep_a, got_a, keep_b, got_b, *deps):
    shape = jax.ShapeDtypeStruct(keep_a.shape[1:], BF)
    return pl.pallas_call(
        turn_kernel,
        in_specs=[pl.BlockSpec(memory_space=pltpu.VMEM)] * 4 + spare(deps),
        out_shape=[shape, shape],
        compiler_params=params(),
        cost_estimate=COST,
        name="weight_turn",
    )(keep_a, got_a, keep_b, got_b, *deps)


def weight_sum_kernel(keep_a, got_a, last_a, keep_b, got_b, last_b, *rest):
    out_refs = rest[-2:]
    split = 3 * DH
    parts = [
        keep[0].astype(F32) + got[0].astype(F32) + last[...].astype(F32)
        for keep, got, last in ((keep_a, got_a, last_a), (keep_b, got_b, last_b))
    ]
    total = jnp.concatenate(parts, axis=0)
    turned = total[:split].T.astype(BF)
    quarter = DH // 2
    for part, out_ref in enumerate(out_refs):
        out_ref[:, :split] = turned[part * DH : (part + 1) * DH]
        first = split + part * quarter
        piece = total[first : first + quarter].astype(BF)
        out_ref[:quarter, split:] = piece[:, :DH]
        out_ref[quarter:, split:] = piece[:, DH:]


def weight_sum(keep_a, got_a, last_a, keep_b, got_b, last_b, *deps):
    _, rows, chunk = keep_a.shape
    return pl.pallas_call(
        weight_sum_kernel,
        in_specs=[pl.BlockSpec(memory_space=pltpu.VMEM)] * 6 + spare(deps),
        out_shape=[jax.ShapeDtypeStruct((chunk // 2, 2 * rows), BF)] * 2,
        compiler_params=params(),
        cost_estimate=COST,
        name="weight_sum",
    )(keep_a, got_a, last_a, keep_b, got_b, last_b, *deps)


def unpack_kernel(at_ref, *refs):
    qkv_ref, out_ref, token_ref = refs[-3:]
    step = pl.program_id(0)
    split = 3 * DH
    quarter = DH // 2
    token_ref[...] = jnp.zeros_like(token_ref)
    for half in range(2):

        @pl.when(step // 2 == half)
        def _():
            mine = refs[half][...].astype(F32)
            other = refs[2 + half][...].astype(F32)
            swapped = at_ref[1] != 0
            low = jnp.where(swapped, other, mine)
            high = jnp.where(swapped, mine, other)
            for i in range(3):
                columns = slice(i * DH, (i + 1) * DH)
                qkv_ref[i] = jnp.concatenate([low[:, columns], high[:, columns]], axis=1)
            for head, value in enumerate((low, high)):
                folded = [value[:quarter, split:], value[quarter:, split:]]
                out_ref[head, 0] = jnp.concatenate(folded, axis=1)


def unpack_weights(at, mine, other, far, before=(), *deps):
    rows, full = mine[0].shape
    half = rows // 2
    width = 4 * rows

    def chunk(t, at):
        if far:
            return at[0] ^ jnp.where(t < 2, t + 2, 2 * t - 3)
        return at[0] ^ jnp.where(t < 2, t, 2 * t - 4)

    specs = [
        pl.BlockSpec((half, full), lambda t, at: (jnp.minimum(t, 1), 0)),
        pl.BlockSpec((half, full), lambda t, at: (jnp.maximum(t - 2, 0), 0)),
    ]
    return pl.pallas_call(
        unpack_kernel,
        grid_spec=pltpu.PrefetchScalarGridSpec(
            num_scalar_prefetch=1,
            grid=(4,),
            in_specs=specs * 2 + spare(tuple(before) + deps),
            out_specs=[
                pl.BlockSpec((3, half, 2 * DH), lambda t, at: (0, 2 * chunk(t, at) + t // 2, 0)),
                pl.BlockSpec(
                    (2, 1, DH // 2, rows), lambda t, at: (0, t // 2, 0, chunk(t, at))
                ),
                pl.BlockSpec(TOKEN.shape, lambda t, at: (0, 0)),
            ],
        ),
        out_shape=[
            jax.ShapeDtypeStruct((3, width, 2 * DH), F32),
            jax.ShapeDtypeStruct((2, 2, DH // 2, width), F32),
            TOKEN,
        ],
        input_output_aliases={5 + i: i for i in range(len(before))},
        compiler_params=params(),
        cost_estimate=COST,
        name="weight_outputs_far" if far else "weight_outputs_near",
    )(at, *mine, *other, *before, *deps)


def neighbour_edges(first, last):
    axes = ("seq", "head")
    count = lax.axis_size(axes)
    forward = [(i, i + 1) for i in range(count - 1)]
    backward = [(target, source) for source, target in forward]
    return lax.ppermute(last, axes, forward), lax.ppermute(first, axes, backward)


def after(value, *others):
    return lax.optimization_barrier((value,) + others)[0]


def trade_chip(x, bit, heads):
    count = lax.axis_size("seq")
    return lax.ppermute(x, "seq", [(s, s ^ (bit * heads)) for s in range(count)])


def swap_heads(x):
    count = lax.axis_size("seq")
    return lax.ppermute(x, "seq", [(s, s + 1 - 2 * (s % 2)) for s in range(count)])


def unit_body(enc_in, conv_weight, norm_gain, w_qkv, w_out, grad_out):
    rows = enc_in.shape[0] // 2
    seqs = enc_in.shape[1]
    width = conv_weight.shape[2]
    local = w_qkv.shape[2]
    heads = local // DH
    groups = lax.axis_size("head")
    half = groups * seqs * rows
    place = lax.axis_index("seq")
    own_seq = (place // heads).astype(jnp.int32)
    own_head = (place % heads).astype(jnp.int32)
    at = jnp.stack([own_seq, own_head])
    head_mine = own_head.reshape(1)
    head_other = (1 - own_head).reshape(1)

    def to_chips(slots):
        return [x if j == 0 else trade_chip(x, j, heads) for j, x in enumerate(slots)]

    order = (0, 2, 1, 3)

    grad_z = lax.all_gather(grad_out, "head", axis=0, tiled=False)

    pairs = jnp.transpose(enc_in.reshape(rows, 2, seqs, enc_in.shape[2]), (1, 2, 0, 3))
    low, high = neighbour_edges(pairs[:, :, :1, :], pairs[:, :, -1:, :])
    skip, slope, normed = encoder(at, pairs, low, high, conv_weight, norm_gain)
    normed = to_chips(normed)
    normed_slab = jnp.concatenate([normed[j] for j in order], axis=0)
    normed_rows = lax.all_gather(normed_slab, "head", axis=0, tiled=True)

    grad_z = after(grad_z, normed_slab)
    grad_slots = to_chips(
        [lax.dynamic_index_in_dim(grad_z, own_seq ^ j, 2, keepdims=False) for j in range(seqs)]
    )
    grad_rows = jnp.stack([grad_slots[j] for j in order], axis=1).reshape(half, width)
    *weights, packed = pack_weights(at, after(w_qkv, normed_slab))
    w_rows = w_out.reshape(heads, DH, width)
    d_other, one = head_product(head_other, grad_rows, w_rows, NT, "d_o_other")
    d_got = swap_heads(d_other)
    d_mine, two = head_product(head_mine, grad_rows, w_rows, NT, "d_o_own")
    grad_swapped = swap_heads(grad_rows)
    normed_rows, d_got, d_mine, grad_swapped, *weights = lax.optimization_barrier(
        (normed_rows, d_got, d_mine, grad_swapped, *weights, packed, one, two)
    )
    w_own, w_other, turned_own, turned_other = [w[None] for w in weights[:4]]
    tokens = weights[4:]
    sole = jnp.zeros((1,), jnp.int32)

    normed_swapped = swap_heads(normed_rows)
    qkv_other, _ = head_product(sole, normed_rows, w_other, NN, "qkv_other", *tokens)
    qkv_got = swap_heads(qkv_other)
    qkv_mine, _ = head_product(sole, normed_rows, w_own, NN, "qkv_own")
    result_mine, result_other = attention(qkv_mine, qkv_got, d_mine, d_got, normed_swapped)
    result_got = swap_heads(result_other)

    shape = (groups, seqs, rows, width)
    d_own = term_part(sole, result_mine, turned_own, 3 * DH, "d_term_own")
    d_term = term_part(sole, result_got, turned_other, 3 * DH, "d_term", d_own)
    d_normed = lax.psum_scatter(d_term.reshape(shape), "head", scatter_dimension=0, tiled=False)
    keep_a, send_a, keep_b, send_b = weight_gradients(
        own_seq.reshape(1),
        normed_rows,
        normed_swapped,
        grad_rows,
        grad_swapped,
        result_mine,
        result_other,
        seqs,
    )
    got_a, got_b = trade_chip(send_a, 1, heads), trade_chip(send_b, 2, heads)
    head_term = pair_term(
        head_mine, result_mine, result_got, w_rows, 3 * DH, 4 * DH, "head_term"
    )
    head_sum = lax.psum_scatter(head_term.reshape(shape), "head", scatter_dimension=0, tiled=False)
    turn_a, turn_b = weight_turn(keep_a, got_a, keep_b, got_b, head_term)
    last_a, last_b = trade_chip(turn_a, 2, heads), trade_chip(turn_b, 1, heads)

    d_normed = after(d_normed, turn_a, turn_b)
    leaving = d_normed[2:]
    near = trade_chip(leaving, 1, heads)
    far = trade_chip(jnp.stack([d_normed[1], near[1]]), 2, heads)
    half_a, half_b = weight_sum(keep_a, got_a, last_a, keep_b, got_b, last_b, leaving)
    grad = jnp.transpose(after(grad_out, d_term), (1, 0, 2))
    d_conv, first, last = conv_gradient(
        at, d_normed, near, far, skip, grad, norm_gain, slope, half_a
    )
    low, high = neighbour_edges(first, last)
    low, high, at_hand = lax.optimization_barrier((low, high, marker(conv_weight, first)))

    got_a, got_b = trade_chip(half_a, 1, heads), trade_chip(half_b, 2, heads)
    near_a = jnp.concatenate([half_a, after(got_a, low)], axis=0)
    near_b = jnp.concatenate([half_b, after(got_b, high)], axis=0)
    far_a = trade_chip(near_a, 2, heads)
    far_b = trade_chip(near_b, 1, heads)
    near_other = [swap_heads(near_a), swap_heads(near_b)]
    grad_input = conv_back(d_conv, low, high, conv_weight, at_hand, *near_other)
    *outputs, token = unpack_weights(
        at, [near_a, near_b], near_other, False, (), grad_input
    )

    head_sum = after(head_sum, grad_input, token)
    head_sum = to_chips([head_sum[order.index(j)] for j in range(seqs)])
    far_other = [swap_heads(after(x, *head_sum[1:])) for x in (far_a, far_b)]
    grad_w_qkv, grad_w_out, _ = unpack_weights(at, [far_a, far_b], far_other, True, outputs)
    mixed = mixed_call(at, head_sum, skip, token)
    grad_input = jnp.transpose(grad_input.reshape(2, seqs, rows, -1), (2, 0, 1, 3))
    return (
        jnp.transpose(mixed, (1, 0, 2)),
        grad_input.reshape(enc_in.shape),
        grad_w_qkv,
        grad_w_out.reshape(local, width),
    )


def padded_2(block, sides, width):
    for axis, dim in sides:
        count = lax.axis_size(axis)
        forward = [(i, i + 1) for i in range(count - 1)]
        backward = [(target, source) for source, target in forward]
        low = lax.ppermute(
            lax.slice_in_dim(block, block.shape[dim] - width, None, axis=dim), axis, forward
        )
        high = lax.ppermute(lax.slice_in_dim(block, 0, width, axis=dim), axis, backward)
        block = jnp.concatenate([low, block, high], axis=dim)
    return block


def gathered_body(enc_in, conv_weight, norm_gain, w_qkv, w_out, grad_out):
    fine_rows = enc_in.shape[0]
    slab_rows = fine_rows // 2
    seq_count = enc_in.shape[1]
    out_width = conv_weight.shape[2]
    local_width = w_qkv.shape[2]
    local_heads = local_width // DH
    logit_scale = DH ** (-0.5)
    padded = padded_2(enc_in, ((("seq", "head"), 0),), 2)
    convolved = jnp.zeros((fine_rows, seq_count, out_width), jnp.float32)
    for offset in range(KW):
        convolved = convolved + jnp.einsum(
            "tbi,io->tbo",
            padded[offset : offset + fine_rows],
            conv_weight[offset],
            preferred_element_type=jnp.float32,
        )
    activated, gelu_pull = jax.vjp(jax.nn.gelu, convolved)
    skip = jnp.mean(activated.reshape(slab_rows, 2, seq_count, out_width), axis=1).astype(
        jnp.bfloat16
    )
    skip_wide = skip.astype(jnp.float32)
    inv_rms = lax.rsqrt(jnp.mean(skip_wide * skip_wide, axis=-1, keepdims=True) + 1e-06)
    normed = (skip_wide * inv_rms * norm_gain).astype(jnp.bfloat16)
    normed_rows = lax.all_gather(normed, "head", axis=0, tiled=True)
    grad_rows = lax.all_gather(grad_out, "head", axis=0, tiled=True)
    tower_rows = normed_rows.shape[0]
    qkv = jnp.einsum(
        "tbc,ice->itbe", normed_rows, w_qkv, preferred_element_type=jnp.float32
    ).astype(jnp.bfloat16)
    qkv = qkv.reshape(3, tower_rows, seq_count, local_heads, DH)
    query_matrix, key_matrix, value_matrix = (qkv[0], qkv[1], qkv[2])
    key_all, value_all = (
        lax.all_gather(key_matrix, "seq", axis=0, tiled=True),
        lax.all_gather(value_matrix, "seq", axis=0, tiled=True),
    )
    attention_logits = (
        jnp.einsum("qbhd,kbhd->bhqk", query_matrix, key_all, preferred_element_type=jnp.float32)
        * logit_scale
    )
    row_peak = jnp.max(attention_logits, axis=-1, keepdims=True)
    exponent = jnp.exp(attention_logits - row_peak)
    row_total = jnp.sum(exponent, axis=-1, keepdims=True)
    soft_weights = exponent / row_total
    narrow_probabilities = soft_weights.astype(jnp.bfloat16)
    attention_output = jnp.einsum(
        "bhqk,kbhd->qbhd", narrow_probabilities, value_all, preferred_element_type=jnp.float32
    )
    o_narrow = attention_output.reshape(tower_rows, seq_count, local_width).astype(jnp.bfloat16)
    piece = o_narrow
    head_sum = lax.psum_scatter(
        jnp.einsum("tbe,ec->tbc", piece, w_out, preferred_element_type=jnp.float32).astype(
            jnp.bfloat16
        ),
        "head",
        scatter_dimension=0,
        tiled=True,
    ).astype(jnp.float32)
    mixed = (skip_wide + head_sum).astype(jnp.bfloat16)
    part_w_out = jnp.einsum("tbe,tbc->ec", o_narrow, grad_rows, preferred_element_type=jnp.float32)
    d_out = jnp.einsum("tbc,ec->tbe", grad_rows, w_out, preferred_element_type=jnp.float32).astype(
        jnp.bfloat16
    )
    d_out = d_out.reshape(tower_rows, seq_count, local_heads, DH)
    delta = jnp.sum(d_out.astype(jnp.float32) * attention_output, axis=-1)
    probability_gradient = jnp.einsum(
        "qbhd,kbhd->bhqk", d_out, value_all, preferred_element_type=jnp.float32
    )
    d_scores = soft_weights * (probability_gradient - jnp.transpose(delta, (1, 2, 0))[..., None])
    narrow_gradient = d_scores.astype(jnp.bfloat16)
    query_gradient = logit_scale * jnp.einsum(
        "bhqk,kbhd->qbhd", narrow_gradient, key_all, preferred_element_type=jnp.float32
    )
    key_terms = logit_scale * jnp.einsum(
        "bhqk,qbhd->kbhd", narrow_gradient, query_matrix, preferred_element_type=jnp.float32
    )
    value_terms = jnp.einsum(
        "bhqk,qbhd->kbhd", narrow_probabilities, d_out, preferred_element_type=jnp.float32
    )
    d_keys, d_values = (
        lax.psum_scatter(
            key_terms.astype(jnp.bfloat16), "seq", scatter_dimension=0, tiled=True
        ).astype(jnp.float32),
        lax.psum_scatter(
            value_terms.astype(jnp.bfloat16), "seq", scatter_dimension=0, tiled=True
        ).astype(jnp.float32),
    )
    dqkv = (
        jnp.stack([query_gradient, d_keys, d_values])
        .reshape(3, tower_rows, seq_count, local_width)
        .astype(jnp.bfloat16)
    )
    part_w_qkv = jnp.einsum("tbc,itbe->ice", normed_rows, dqkv, preferred_element_type=jnp.float32)
    piece = dqkv
    d_normed = lax.psum_scatter(
        jnp.einsum("itbe,ice->tbc", piece, w_qkv, preferred_element_type=jnp.float32).astype(
            jnp.bfloat16
        ),
        "head",
        scatter_dimension=0,
        tiled=True,
    ).astype(jnp.float32)
    unit_rows = skip_wide * inv_rms
    scaled = d_normed * norm_gain
    d_skip = grad_out.astype(jnp.float32) + inv_rms * (
        scaled - unit_rows * jnp.mean(scaled * unit_rows, axis=-1, keepdims=True)
    )
    d_act = jnp.repeat(d_skip, 2, axis=0) * 0.5
    d_conv = gelu_pull(d_act)[0].astype(jnp.bfloat16)
    d_pad = padded_2(d_conv, ((("seq", "head"), 0),), 2)
    grad_input = jnp.zeros((fine_rows, seq_count, enc_in.shape[2]), jnp.float32)
    for offset in range(KW):
        grad_input = grad_input + jnp.einsum(
            "tbo,io->tbi",
            d_pad[4 - offset : 4 - offset + fine_rows],
            conv_weight[offset],
            preferred_element_type=jnp.float32,
        )
    grad_w_qkv, grad_w_out = (
        lax.psum(part_w_qkv.astype(jnp.bfloat16), "seq").astype(jnp.float32),
        lax.psum(part_w_out.astype(jnp.bfloat16), "seq").astype(jnp.float32),
    )
    return (mixed, grad_input.astype(jnp.bfloat16), grad_w_qkv, grad_w_out)


def body(enc_in, conv_weight, norm_gain, w_qkv, w_out, grad_out):
    heads = w_qkv.shape[2] // DH
    seqs = enc_in.shape[1]
    fits = heads == 2 and seqs == 4 and seqs * heads == lax.axis_size("seq")
    fits = fits and conv_weight.shape[2] == seqs * w_qkv.shape[2]
    chosen = unit_body if fits else gathered_body
    return chosen(enc_in, conv_weight, norm_gain, w_qkv, w_out, grad_out)


def solution(mesh):
    return jax.shard_map(
        body,
        mesh=mesh,
        in_specs=(
            P(("seq", "head"), None, None),
            P(),
            P(),
            P(None, None, "head"),
            P("head", None),
            P(("seq", "head"), None, None),
        ),
        out_specs=(
            P(("seq", "head"), None, None),
            P(("seq", "head"), None, None),
            P(None, None, "head"),
            P("head", None),
        ),
        check_vma=False,
    )
```

```python
import functools

import jax
import jax.numpy as jnp
from jax import lax
from jax.experimental import pallas as pl
from jax.experimental.pallas import tpu as pltpu
from jax.sharding import PartitionSpec as P

DH = 192
KW = 5
VMEM_LIMIT = 24 * 1024 * 1024
STREAMING_LIMIT = 56 * 1024 * 1024
COST = pl.CostEstimate(flops=1000, bytes_accessed=1000, transcendentals=0)
BF = jnp.bfloat16
F32 = jnp.float32
TOKEN = jax.ShapeDtypeStruct((8, 128), F32)


def params(limit=VMEM_LIMIT):
    return pltpu.CompilerParams(vmem_limit_bytes=limit)


def dot(a, b, contract):
    return lax.dot_general(a, b, (contract, ((), ())), preferred_element_type=F32)


NN = ((1,), (0,))
NT = ((1,), (1,))
TN = ((0,), (0,))


def whole(shape):
    return pl.BlockSpec(shape, lambda *_: (0,) * len(shape))


SCALARS = pl.BlockSpec(memory_space=pltpu.SMEM)


def spare(deps):
    return [pl.BlockSpec(memory_space=pl.ANY)] * len(deps)


def turned_rows(ref, low_ref, high_ref, parity, shift):
    seqs, rows, width = ref.shape[1:]
    own = ref[parity]
    if shift != 1:
        wide = own.astype(F32)
        if shift == 0:
            parts = [low_ref[parity].astype(F32), wide[:, : rows - 1]]
        else:
            parts = [wide[:, 1:], high_ref[parity].astype(F32)]
        own = jnp.concatenate(parts, axis=1).astype(BF)
    return own.reshape(seqs * rows, width)


def conv_kernel(
    at_ref, x_ref, low_ref, high_ref, w_ref, gain_ref, skip_ref, slope_ref, *rest
):
    normed_refs, (lhs, squares, whole_normed) = rest[:-3], rest[-3:]
    step = pl.program_id(0)
    seqs, rows, c_in = x_ref.shape[1:]
    half = seqs * rows
    tile = w_ref.shape[2]

    @pl.when(step == 0)
    def _():
        for parity in range(2):
            for shift in range(3):
                value = turned_rows(x_ref, low_ref, high_ref, parity, shift)
                for out in range(2):
                    tap = 2 * shift + parity - out
                    if 0 <= tap < KW:
                        lhs[out * half : (out + 1) * half, tap * c_in : (tap + 1) * c_in] = value
        squares[...] = jnp.zeros_like(squares)

    conv = dot(lhs[...], w_ref[...].reshape(KW * c_in, tile), NN)
    root = 0.7978845608028654
    total = None
    for parity in range(2):
        x = conv[parity * half : (parity + 1) * half, :]
        square = x * x
        t = jnp.tanh(root * (x + 0.044715 * (square * x)))
        left = 0.5 * (1.0 + t)
        act = x * left
        slope = left + (0.5 * root) * x * (1.0 - t * t) * (1.0 + (3 * 0.044715) * square)
        slope_ref[parity] = slope.reshape(slope_ref.shape[1:])
        total = act if total is None else total + act
    skip = (0.5 * total).astype(BF)
    columns = pl.ds(pl.multiple_of(step * tile, tile), tile)
    skip_ref[:, :, columns] = skip.reshape(seqs, rows, tile)
    wide = skip.astype(F32)
    squares[...] += jnp.sum(wide * wide, axis=-1, keepdims=True)

    @pl.when(step == pl.num_programs(0) - 1)
    def _():
        width = skip_ref.shape[2]
        inv = lax.rsqrt(squares[...] * (1.0 / width) + 1e-06)
        wide = skip_ref[...].reshape(half, width).astype(F32)
        normed = (wide * inv * gain_ref[...]).astype(BF)
        whole_normed[...] = normed.reshape(whole_normed.shape)
        for slot in range(seqs):
            normed_refs[slot][...] = whole_normed[at_ref[0] ^ slot]


def encoder(at, pairs, low, high, conv_weight, norm_gain):
    _, seqs, rows, c_in = pairs.shape
    width = conv_weight.shape[2]
    tile = 256 if width % 256 == 0 else width
    shape = (seqs, rows, width)
    outs = pl.pallas_call(
        conv_kernel,
        grid=(width // tile,),
        in_specs=[
            SCALARS,
            whole(pairs.shape),
            whole(low.shape),
            whole(high.shape),
            pl.BlockSpec((KW, c_in, tile), lambda n: (0, 0, n)),
            whole((1, width)),
        ],
        out_specs=[
            whole(shape),
            pl.BlockSpec((2, seqs, rows, tile), lambda n: (0, 0, 0, n)),
        ]
        + [whole((rows, width))] * seqs,
        out_shape=[
            jax.ShapeDtypeStruct(shape, BF),
            jax.ShapeDtypeStruct((2,) + shape, F32),
        ]
        + [jax.ShapeDtypeStruct((rows, width), BF)] * seqs,
        scratch_shapes=[
            pltpu.VMEM((2 * seqs * rows, KW * c_in), BF),
            pltpu.VMEM((seqs * rows, 1), F32),
            pltpu.VMEM(shape, BF),
        ],
        compiler_params=params(STREAMING_LIMIT),
        cost_estimate=COST,
        name="encoder_forward",
    )(at, pairs, low, high, conv_weight, norm_gain.reshape(1, width))
    return outs[0], outs[1], list(outs[2:])


def d_conv_kernel(at_ref, own_ref, near_ref, far_ref, *refs):
    skip_ref, grad_ref, gain_ref, slope_ref = refs[:4]
    out_ref, first_ref, last_ref = refs[-3:]
    rows = out_ref.shape[2]
    for slot, (ref, place) in enumerate(((own_ref, 0), (near_ref, 0), (far_ref, 0), (far_ref, 1))):
        b = at_ref[0] ^ slot
        wide = skip_ref[b].astype(F32)
        inv = lax.rsqrt(jnp.mean(wide * wide, axis=-1, keepdims=True) + 1e-06)
        unit = wide * inv
        scaled = ref[place].astype(F32) * gain_ref[...]
        d_skip = grad_ref[b].astype(F32) + inv * (
            scaled - unit * jnp.mean(scaled * unit, axis=-1, keepdims=True)
        )
        d_act = 0.5 * d_skip
        for parity in range(2):
            value = slope_ref[parity, b] * d_act
            out_ref[parity, b] = value.astype(BF)
            first_ref[parity, b] = value[:1].astype(BF)
            last_ref[parity, b] = value[rows - 1 :].astype(BF)


def conv_gradient(at, own, near, far, skip, grad, norm_gain, slope, *deps):
    vmem = pl.BlockSpec(memory_space=pltpu.VMEM)
    edge = jax.ShapeDtypeStruct(slope.shape[:2] + (1, slope.shape[3]), BF)
    return pl.pallas_call(
        d_conv_kernel,
        in_specs=[SCALARS] + [vmem] * 7 + spare(deps),
        out_specs=[vmem] * 3,
        out_shape=[jax.ShapeDtypeStruct(slope.shape, BF)] + [edge] * 2,
        compiler_params=params(),
        cost_estimate=COST,
        name="conv_gradient",
    )(at, own, near, far, skip, grad, norm_gain.reshape(1, -1), slope, *deps)


def mixed_body(seqs, at_ref, *refs):
    skip_ref, out_ref = refs[seqs], refs[-1]
    for slot in range(seqs):
        b = at_ref[0] ^ slot
        out_ref[b] = (skip_ref[b].astype(F32) + refs[slot][...].astype(F32)).astype(BF)


def mixed_call(at, terms, skip, *deps):
    seqs = len(terms)
    vmem = pl.BlockSpec(memory_space=pltpu.VMEM)
    return pl.pallas_call(
        functools.partial(mixed_body, seqs),
        in_specs=[SCALARS] + [vmem] * (seqs + 1) + spare(deps),
        out_specs=vmem,
        out_shape=jax.ShapeDtypeStruct(skip.shape, BF),
        compiler_params=params(),
        cost_estimate=COST,
        name="mixed_sum",
    )(at, *terms, skip, *deps)


def marker_kernel(*refs):
    refs[-1][...] = jnp.zeros_like(refs[-1])


def marker(*deps):
    return pl.pallas_call(
        marker_kernel,
        in_specs=spare(deps),
        out_shape=TOKEN,
        compiler_params=params(),
        cost_estimate=COST,
        name="marker",
    )(*deps)


def conv_back_kernel(d_ref, low_ref, high_ref, w_ref, *rest):
    out_ref, turned, acc = rest[-3:]
    step = pl.program_id(0)

    @pl.when(step == 0)
    def _():
        for parity in range(2):
            for shift in range(3):
                turned[parity, shift] = turned_rows(d_ref, low_ref, high_ref, parity, shift).T

    for tap in range(KW):

        @pl.when(step == tap)
        def _():
            places = [KW - 1 - tap, KW - tap]
            rhs = jnp.concatenate([turned[p % 2, p // 2] for p in places], axis=1)
            term = dot(w_ref[0], rhs, NN)
            if tap == 0:
                acc[...] = term
            elif tap < KW - 1:
                acc[...] += term
            else:
                out_ref[...] = (acc[...] + term).T.astype(BF)


def conv_back(d_conv, low, high, conv_weight, *deps):
    _, seqs, rows, width = d_conv.shape
    c_in = conv_weight.shape[1]
    flat = 2 * seqs * rows
    return pl.pallas_call(
        conv_back_kernel,
        grid=(KW,),
        in_specs=[
            whole(d_conv.shape),
            whole(low.shape),
            whole(high.shape),
            pl.BlockSpec((1, c_in, width), lambda k: (k, 0, 0)),
        ]
        + spare(deps),
        out_specs=whole((flat, c_in)),
        out_shape=jax.ShapeDtypeStruct((flat, c_in), BF),
        scratch_shapes=[
            pltpu.VMEM((2, 3, width, seqs * rows), BF),
            pltpu.VMEM((c_in, flat), F32),
        ],
        compiler_params=params(),
        cost_estimate=COST,
        name="encoder_backward",
    )(d_conv, low, high, conv_weight, *deps)


def pack_kernel(at_ref, w_ref, own_ref, other_ref, own_turned, other_turned, token_ref):
    token_ref[...] = jnp.zeros_like(token_ref)
    first_head = at_ref[1] == 0
    for i in range(3):
        low, high = w_ref[i, :, :DH], w_ref[i, :, DH:]
        columns = slice(i * DH, (i + 1) * DH)
        own = jnp.where(first_head, low, high)
        other = jnp.where(first_head, high, low)
        own_ref[:, columns] = own
        other_ref[:, columns] = other
        own_turned[columns, :] = own.T
        other_turned[columns, :] = other.T


def pack_weights(at, w_qkv):
    _, width, local = w_qkv.shape
    tile = local
    plain = pl.BlockSpec((tile, 3 * DH), lambda n: (n, 0))
    turned = pl.BlockSpec((3 * DH, tile), lambda n: (0, n))
    return pl.pallas_call(
        pack_kernel,
        grid=(width // tile,),
        in_specs=[SCALARS, pl.BlockSpec((3, tile, local), lambda n: (0, n, 0))],
        out_specs=[plain, plain, turned, turned, pl.BlockSpec(TOKEN.shape, lambda n: (0, 0))],
        out_shape=[jax.ShapeDtypeStruct((width, 3 * DH), BF)] * 2
        + [jax.ShapeDtypeStruct((3 * DH, width), BF)] * 2
        + [TOKEN],
        compiler_params=params(),
        cost_estimate=COST,
        name="pack_weights",
    )(at, w_qkv)


def product_kernel(head_ref, x_ref, w_ref, *rest, contract):
    del head_ref
    out_ref, token_ref = rest[-2:]
    token_ref[...] = jnp.zeros_like(token_ref)
    value = dot(x_ref[...], w_ref[0], contract).astype(BF)
    out_ref[:, : value.shape[1]] = value
    if value.shape[1] < out_ref.shape[1]:
        out_ref[:, value.shape[1] :] = jnp.zeros_like(out_ref[:, value.shape[1] :])


def head_product(head, x, weight, contract, name, *deps):
    columns = weight.shape[2] if contract == NN else weight.shape[1]
    columns += -columns % 128
    rows, width = x.shape
    return pl.pallas_call(
        functools.partial(product_kernel, contract=contract),
        grid_spec=pltpu.PrefetchScalarGridSpec(
            num_scalar_prefetch=1,
            grid=(1,),
            in_specs=[
                pl.BlockSpec((rows, width), lambda i, head: (0, 0)),
                pl.BlockSpec((1,) + weight.shape[1:], lambda i, head: (head[0], 0, 0)),
            ]
            + spare(deps),
            out_specs=[
                pl.BlockSpec((rows, columns), lambda i, head: (0, 0)),
                pl.BlockSpec(TOKEN.shape, lambda i, head: (0, 0)),
            ],
        ),
        out_shape=[jax.ShapeDtypeStruct((rows, columns), BF), TOKEN],
        compiler_params=params(),
        cost_estimate=COST,
        name=name,
    )(head, x, weight, *deps)


def place_kernel(at_ref, *refs):
    del at_ref
    for slot, ref in enumerate(refs[:-1]):

        @pl.when(pl.program_id(0) == slot)
        def _():
            refs[-1][0] = ref[...]


def placed(at, slots, name):
    count = len(slots)
    shape = slots[0].shape
    return pl.pallas_call(
        place_kernel,
        grid_spec=pltpu.PrefetchScalarGridSpec(
            num_scalar_prefetch=1,
            grid=(count,),
            in_specs=[pl.BlockSpec(shape, lambda q, at: (0, 0, 0))] * count,
            out_specs=pl.BlockSpec((1,) + shape, lambda q, at: (q ^ at[0], 0, 0, 0)),
        ),
        out_shape=jax.ShapeDtypeStruct((count,) + shape, slots[0].dtype),
        compiler_params=params(),
        cost_estimate=COST,
        name=name,
    )(at, *slots)


def attention_kernel(qa_ref, qb_ref, da_ref, db_ref, *rest, block):
    oa_ref, ob_ref, k_all, v_all, dk_acc, dv_acc = rest[-6:]
    scale = DH ** (-0.5)
    half = qa_ref.shape[0]
    for place, ref in enumerate((qa_ref, qb_ref)):
        rows = pl.ds(place * half, half)
        k_all[rows, :] = ref[:, DH : 2 * DH]
        v_all[rows, :] = ref[:, 2 * DH : 3 * DH]
    k = k_all[...]
    v = v_all[...]
    for place, (q_ref, d_ref, out_ref) in enumerate(
        ((qa_ref, da_ref, oa_ref), (qb_ref, db_ref, ob_ref))
    ):
        for start in range(0, half, block):
            rows = pl.ds(start, block)
            q = q_ref[rows, 0:DH]
            d_o = d_ref[rows, 0:DH]
            s = dot(q, k, NT) * scale
            e = jnp.exp(s - jnp.max(s, axis=-1, keepdims=True))
            p = e * (1.0 / jnp.sum(e, axis=-1, keepdims=True))
            p_b = p.astype(BF)
            o = dot(p_b, v, NN)
            delta = jnp.sum(d_o.astype(F32) * o, axis=-1, keepdims=True)
            d_p = dot(d_o, v, NT)
            ds = (p * (d_p - delta)).astype(BF)
            dq = scale * dot(ds, k, NN)
            dk = dot(ds, q, TN)
            dv = dot(p_b, d_o, TN)
            if place == 0 and start == 0:
                dk_acc[...] = dk
                dv_acc[...] = dv
            else:
                dk_acc[...] += dk
                dv_acc[...] += dv
            out_ref[rows, 0:DH] = dq.astype(BF)
            out_ref[rows, 3 * DH : 4 * DH] = o.astype(BF)
    for place, out_ref in enumerate((oa_ref, ob_ref)):
        rows = pl.ds(place * half, half)
        out_ref[:, DH : 2 * DH] = (scale * dk_acc[rows, :]).astype(BF)
        out_ref[:, 2 * DH : 3 * DH] = dv_acc[rows, :].astype(BF)


def attention(qkv_a, qkv_b, d_a, d_b, *deps):
    half = qkv_a.shape[0]
    shape = jax.ShapeDtypeStruct((half, 4 * DH), BF)
    return pl.pallas_call(
        functools.partial(attention_kernel, block=min(256, half)),
        in_specs=[pl.BlockSpec(memory_space=pltpu.VMEM)] * 4 + spare(deps),
        out_shape=[shape, shape],
        scratch_shapes=[
            pltpu.VMEM((2 * half, DH), BF),
            pltpu.VMEM((2 * half, DH), BF),
            pltpu.VMEM((2 * half, DH), F32),
            pltpu.VMEM((2 * half, DH), F32),
        ],
        compiler_params=params(),
        cost_estimate=COST,
        name="attention",
    )(qkv_a, qkv_b, d_a, d_b, *deps)


def term_kernel(head_ref, a_ref, b_ref, w_ref, *rest, first, last):
    head = head_ref[0]
    total = dot(a_ref[:, first:last], w_ref[head], NN)
    total += dot(b_ref[:, first:last], w_ref[1 - head], NN)
    rest[-1][...] = total.astype(BF)


def pair_term(head, mine, got, weight, first, last, name, *deps):
    half, full = mine.shape
    heads, depth, width = weight.shape
    tile = 512 if width % 512 == 0 else width
    return pl.pallas_call(
        functools.partial(term_kernel, first=first, last=last),
        grid_spec=pltpu.PrefetchScalarGridSpec(
            num_scalar_prefetch=1,
            grid=(width // tile,),
            in_specs=[
                pl.BlockSpec((half, full), lambda n, at: (0, 0)),
                pl.BlockSpec((half, full), lambda n, at: (0, 0)),
                pl.BlockSpec((heads, depth, tile), lambda n, at: (0, 0, n)),
            ]
            + spare(deps),
            out_specs=pl.BlockSpec((half, tile), lambda n, at: (0, n)),
        ),
        out_shape=jax.ShapeDtypeStruct((half, width), BF),
        compiler_params=params(),
        cost_estimate=COST,
        name=name,
    )(head, mine, got, weight, *deps)


def part_kernel(head_ref, x_ref, w_ref, *rest, last):
    del head_ref
    total = dot(x_ref[:, :last], w_ref[0], NN)
    if len(rest) > 1:
        total += rest[0][...]
    rest[-1][...] = total.astype(rest[-1].dtype)


def term_part(head, x, weight, last, name, *before):
    half, full = x.shape
    _, depth, width = weight.shape
    tile = 512 if width % 512 == 0 else width
    column = pl.BlockSpec((half, tile), lambda n, at: (0, n))
    return pl.pallas_call(
        functools.partial(part_kernel, last=last),
        grid_spec=pltpu.PrefetchScalarGridSpec(
            num_scalar_prefetch=1,
            grid=(width // tile,),
            in_specs=[
                pl.BlockSpec((half, full), lambda n, at: (0, 0)),
                pl.BlockSpec((1, depth, tile), lambda n, at: (at[0], 0, n)),
            ]
            + [column] * len(before),
            out_specs=column,
        ),
        out_shape=jax.ShapeDtypeStruct((half, width), BF if before else F32),
        compiler_params=params(),
        cost_estimate=COST,
        name=name,
    )(head, x, weight, *before)


def weight_kernel(at_ref, xa_ref, xb_ref, ga_ref, gb_ref, ra_ref, rb_ref, *rest):
    del at_ref
    out_refs, turned = rest[:-1], rest[-1]
    step = pl.program_id(0)
    half = ra_ref.shape[0]
    split = 3 * DH

    @pl.when(step == 0)
    def _():
        turned[:, :half] = ra_ref[...].T
        turned[:, half:] = rb_ref[...].T

    a, b = slice(0, half), slice(half, 2 * half)
    qkv = dot(turned[:split, a], xa_ref[...], NN) + dot(turned[:split, b], xb_ref[...], NN)
    out = dot(turned[split:, a], ga_ref[...], NN) + dot(turned[split:, b], gb_ref[...], NN)
    keep_a, send_a, keep_b, send_b = out_refs
    rows = keep_a.shape[1]
    for slot in range(4):

        @pl.when(step == slot)
        def _():
            first = keep_a if slot % 2 == 0 else send_a
            second = keep_b if slot < 2 else send_b
            first[slot // 2] = qkv[:rows].astype(BF)
            second[slot % 2, : split - rows] = qkv[rows:].astype(BF)
            second[slot % 2, split - rows :] = out.astype(BF)


def weight_gradients(at, xa, xb, ga, gb, ra, rb, seqs):
    half, width = xa.shape
    chunk = width // seqs
    full = ra.shape[1]
    column = pl.BlockSpec((half, chunk), lambda r, at: (0, r ^ at[0]))
    rest = pl.BlockSpec((half, full), lambda r, at: (0, 0))
    return pl.pallas_call(
        weight_kernel,
        grid_spec=pltpu.PrefetchScalarGridSpec(
            num_scalar_prefetch=1,
            grid=(seqs,),
            in_specs=[column] * 4 + [rest] * 2,
            out_specs=[pl.BlockSpec((2, full // 2, chunk), lambda r, at: (0, 0, 0))] * 4,
            scratch_shapes=[pltpu.VMEM((full, 2 * half), BF)],
        ),
        out_shape=[jax.ShapeDtypeStruct((2, full // 2, chunk), BF)] * 4,
        compiler_params=params(STREAMING_LIMIT),
        cost_estimate=COST,
        name="weight_gradients",
    )(at, xa, xb, ga, gb, ra, rb)


def turn_kernel(keep_a, got_a, keep_b, got_b, *rest):
    out_a, out_b = rest[-2:]
    for keep, got, out in ((keep_a, got_a, out_a), (keep_b, got_b, out_b)):
        out[...] = (keep[1].astype(F32) + got[1].astype(F32)).astype(BF)


def weight_turn(keep_a, got_a, keep_b, got_b, *deps):
    shape = jax.ShapeDtypeStruct(keep_a.shape[1:], BF)
    return pl.pallas_call(
        turn_kernel,
        in_specs=[pl.BlockSpec(memory_space=pltpu.VMEM)] * 4 + spare(deps),
        out_shape=[shape, shape],
        compiler_params=params(),
        cost_estimate=COST,
        name="weight_turn",
    )(keep_a, got_a, keep_b, got_b, *deps)


def weight_sum_kernel(keep_a, got_a, last_a, keep_b, got_b, last_b, *rest):
    out_refs = rest[-2:]
    split = 3 * DH
    parts = [
        keep[0].astype(F32) + got[0].astype(F32) + last[...].astype(F32)
        for keep, got, last in ((keep_a, got_a, last_a), (keep_b, got_b, last_b))
    ]
    total = jnp.concatenate(parts, axis=0)
    turned = total[:split].T.astype(BF)
    quarter = DH // 2
    for part, out_ref in enumerate(out_refs):
        out_ref[:, :split] = turned[part * DH : (part + 1) * DH]
        first = split + part * quarter
        piece = total[first : first + quarter].astype(BF)
        out_ref[:quarter, split:] = piece[:, :DH]
        out_ref[quarter:, split:] = piece[:, DH:]


def weight_sum(keep_a, got_a, last_a, keep_b, got_b, last_b, *deps):
    _, rows, chunk = keep_a.shape
    return pl.pallas_call(
        weight_sum_kernel,
        in_specs=[pl.BlockSpec(memory_space=pltpu.VMEM)] * 6 + spare(deps),
        out_shape=[jax.ShapeDtypeStruct((chunk // 2, 2 * rows), BF)] * 2,
        compiler_params=params(),
        cost_estimate=COST,
        name="weight_sum",
    )(keep_a, got_a, last_a, keep_b, got_b, last_b, *deps)


def unpack_kernel(at_ref, *refs):
    qkv_ref, out_ref, token_ref = refs[-3:]
    step = pl.program_id(0)
    split = 3 * DH
    quarter = DH // 2
    token_ref[...] = jnp.zeros_like(token_ref)
    for half in range(2):

        @pl.when(step // 2 == half)
        def _():
            mine = refs[half][...].astype(F32)
            other = refs[2 + half][...].astype(F32)
            swapped = at_ref[1] != 0
            low = jnp.where(swapped, other, mine)
            high = jnp.where(swapped, mine, other)
            for i in range(3):
                columns = slice(i * DH, (i + 1) * DH)
                qkv_ref[i] = jnp.concatenate([low[:, columns], high[:, columns]], axis=1)
            for head, value in enumerate((low, high)):
                folded = [value[:quarter, split:], value[quarter:, split:]]
                out_ref[head, 0] = jnp.concatenate(folded, axis=1)


def unpack_weights(at, mine, other, far, before=(), *deps):
    rows, full = mine[0].shape
    half = rows // 2
    width = 4 * rows

    def chunk(t, at):
        if far:
            return at[0] ^ jnp.where(t < 2, t + 2, 2 * t - 3)
        return at[0] ^ jnp.where(t < 2, t, 2 * t - 4)

    specs = [
        pl.BlockSpec((half, full), lambda t, at: (jnp.minimum(t, 1), 0)),
        pl.BlockSpec((half, full), lambda t, at: (jnp.maximum(t - 2, 0), 0)),
    ]
    return pl.pallas_call(
        unpack_kernel,
        grid_spec=pltpu.PrefetchScalarGridSpec(
            num_scalar_prefetch=1,
            grid=(4,),
            in_specs=specs * 2 + spare(tuple(before) + deps),
            out_specs=[
                pl.BlockSpec((3, half, 2 * DH), lambda t, at: (0, 2 * chunk(t, at) + t // 2, 0)),
                pl.BlockSpec(
                    (2, 1, DH // 2, rows), lambda t, at: (0, t // 2, 0, chunk(t, at))
                ),
                pl.BlockSpec(TOKEN.shape, lambda t, at: (0, 0)),
            ],
        ),
        out_shape=[
            jax.ShapeDtypeStruct((3, width, 2 * DH), F32),
            jax.ShapeDtypeStruct((2, 2, DH // 2, width), F32),
            TOKEN,
        ],
        input_output_aliases={5 + i: i for i in range(len(before))},
        compiler_params=params(),
        cost_estimate=COST,
        name="weight_outputs_far" if far else "weight_outputs_near",
    )(at, *mine, *other, *before, *deps)


def neighbour_edges(first, last):
    axes = ("seq", "head")
    count = lax.axis_size(axes)
    forward = [(i, i + 1) for i in range(count - 1)]
    backward = [(target, source) for source, target in forward]
    return lax.ppermute(last, axes, forward), lax.ppermute(first, axes, backward)


def after(value, *others):
    return lax.optimization_barrier((value,) + others)[0]


def trade_chip(x, bit, heads):
    count = lax.axis_size("seq")
    return lax.ppermute(x, "seq", [(s, s ^ (bit * heads)) for s in range(count)])


def trade_z(x, bit):
    count = lax.axis_size("head")
    return lax.ppermute(x, "head", [(z, z ^ bit) for z in range(count)])


def swap_heads(x):
    count = lax.axis_size("seq")
    return lax.ppermute(x, "seq", [(s, s + 1 - 2 * (s % 2)) for s in range(count)])


def unit_body(enc_in, conv_weight, norm_gain, w_qkv, w_out, grad_out):
    rows = enc_in.shape[0] // 2
    seqs = enc_in.shape[1]
    width = conv_weight.shape[2]
    local = w_qkv.shape[2]
    heads = local // DH
    groups = lax.axis_size("head")
    half = groups * seqs * rows
    place = lax.axis_index("seq")
    own_seq = (place // heads).astype(jnp.int32)
    own_head = (place % heads).astype(jnp.int32)
    at = jnp.stack([own_seq, own_head])
    head_mine = own_head.reshape(1)
    head_other = (1 - own_head).reshape(1)

    def to_chips(slots):
        return [x if j == 0 else trade_chip(x, j, heads) for j, x in enumerate(slots)]

    order = (0, 2, 1, 3)

    edge = width - width // seqs
    grad_z = lax.all_gather(grad_out[:, :, :edge], "head", axis=0, tiled=False)

    pairs = jnp.transpose(enc_in.reshape(rows, 2, seqs, enc_in.shape[2]), (1, 2, 0, 3))
    ends = (pairs[:, :, :1, :], pairs[:, :, -1:, :])
    own_part, *ends = lax.optimization_barrier((grad_out[:, :, edge:], *ends))
    parts = [trade_z(own_part, q) for q in range(1, groups)]
    low, high = neighbour_edges(*ends)
    low, high, *parts = lax.optimization_barrier((low, high, *parts))
    skip, slope, normed = encoder(at, pairs, low, high, conv_weight, norm_gain)
    normed = to_chips(normed)
    normed_slab = jnp.concatenate([normed[j] for j in order], axis=0)
    normed_rows = lax.all_gather(normed_slab, "head", axis=0, tiled=True)

    grad_z = after(grad_z, normed_slab)
    own_z = lax.axis_index("head").astype(jnp.int32).reshape(1)
    grad_z = jnp.concatenate([grad_z, placed(own_z, [own_part, *parts], "grad_last")], axis=3)
    grad_slots = to_chips(
        [lax.dynamic_index_in_dim(grad_z, own_seq ^ j, 2, keepdims=False) for j in range(seqs)]
    )
    *weights, packed = pack_weights(at, after(w_qkv, normed_slab))
    *grad_slots, packed = lax.optimization_barrier((*grad_slots, packed))
    grad_rows = jnp.stack([grad_slots[j] for j in order], axis=1).reshape(half, width)
    w_rows = w_out.reshape(heads, DH, width)
    d_other, one = head_product(head_other, grad_rows, w_rows, NT, "d_o_other")
    d_got = swap_heads(d_other)
    d_mine, two = head_product(head_mine, grad_rows, w_rows, NT, "d_o_own")
    grad_swapped = swap_heads(grad_rows)
    normed_rows, d_got, d_mine, grad_swapped, *weights = lax.optimization_barrier(
        (normed_rows, d_got, d_mine, grad_swapped, *weights, packed, one, two)
    )
    w_own, w_other, turned_own, turned_other = [w[None] for w in weights[:4]]
    tokens = weights[4:]
    sole = jnp.zeros((1,), jnp.int32)

    normed_swapped = swap_heads(normed_rows)
    qkv_other, _ = head_product(sole, normed_rows, w_other, NN, "qkv_other", *tokens)
    qkv_got = swap_heads(qkv_other)
    qkv_mine, _ = head_product(sole, normed_rows, w_own, NN, "qkv_own")
    result_mine, result_other = attention(qkv_mine, qkv_got, d_mine, d_got, normed_swapped)
    result_got = swap_heads(result_other)

    shape = (groups, seqs, rows, width)
    d_own = term_part(sole, result_mine, turned_own, 3 * DH, "d_term_own")
    d_term = term_part(sole, result_got, turned_other, 3 * DH, "d_term", d_own)
    d_normed = lax.psum_scatter(d_term.reshape(shape), "head", scatter_dimension=0, tiled=False)
    keep_a, send_a, keep_b, send_b = weight_gradients(
        own_seq.reshape(1),
        normed_rows,
        normed_swapped,
        grad_rows,
        grad_swapped,
        result_mine,
        result_other,
        seqs,
    )
    got_a, got_b = trade_chip(send_a, 1, heads), trade_chip(send_b, 2, heads)
    head_term = pair_term(
        head_mine, result_mine, result_got, w_rows, 3 * DH, 4 * DH, "head_term"
    )
    head_sum = lax.psum_scatter(head_term.reshape(shape), "head", scatter_dimension=0, tiled=False)
    turn_a, turn_b = weight_turn(keep_a, got_a, keep_b, got_b, head_term)
    last_a, last_b = trade_chip(turn_a, 2, heads), trade_chip(turn_b, 1, heads)

    d_normed = after(d_normed, turn_a, turn_b)
    leaving = d_normed[2:]
    near = trade_chip(leaving, 1, heads)
    far = trade_chip(jnp.stack([d_normed[1], near[1]]), 2, heads)
    half_a, half_b = weight_sum(keep_a, got_a, last_a, keep_b, got_b, last_b, leaving)
    grad = jnp.transpose(after(grad_out, d_term), (1, 0, 2))
    d_conv, first, last = conv_gradient(
        at, d_normed, near, far, skip, grad, norm_gain, slope, half_a
    )
    low, high = neighbour_edges(first, last)
    low, high, at_hand = lax.optimization_barrier((low, high, marker(conv_weight, first)))

    got_a, got_b = trade_chip(half_a, 1, heads), trade_chip(half_b, 2, heads)
    near_a = jnp.concatenate([half_a, after(got_a, low)], axis=0)
    near_b = jnp.concatenate([half_b, after(got_b, high)], axis=0)
    far_a = trade_chip(near_a, 2, heads)
    far_b = trade_chip(near_b, 1, heads)
    near_other = [swap_heads(near_a), swap_heads(near_b)]
    grad_input = conv_back(d_conv, low, high, conv_weight, at_hand, *near_other)
    *outputs, token = unpack_weights(
        at, [near_a, near_b], near_other, False, (), grad_input
    )

    head_sum = after(head_sum, grad_input, token)
    head_sum = to_chips([head_sum[order.index(j)] for j in range(seqs)])
    far_other = [swap_heads(after(x, *head_sum[1:])) for x in (far_a, far_b)]
    grad_w_qkv, grad_w_out, _ = unpack_weights(at, [far_a, far_b], far_other, True, outputs)
    mixed = mixed_call(at, head_sum, skip, token)
    grad_input = jnp.transpose(grad_input.reshape(2, seqs, rows, -1), (2, 0, 1, 3))
    return (
        jnp.transpose(mixed, (1, 0, 2)),
        grad_input.reshape(enc_in.shape),
        grad_w_qkv,
        grad_w_out.reshape(local, width),
    )


def padded_2(block, sides, width):
    for axis, dim in sides:
        count = lax.axis_size(axis)
        forward = [(i, i + 1) for i in range(count - 1)]
        backward = [(target, source) for source, target in forward]
        low = lax.ppermute(
            lax.slice_in_dim(block, block.shape[dim] - width, None, axis=dim), axis, forward
        )
        high = lax.ppermute(lax.slice_in_dim(block, 0, width, axis=dim), axis, backward)
        block = jnp.concatenate([low, block, high], axis=dim)
    return block


def gathered_body(enc_in, conv_weight, norm_gain, w_qkv, w_out, grad_out):
    fine_rows = enc_in.shape[0]
    slab_rows = fine_rows // 2
    seq_count = enc_in.shape[1]
    out_width = conv_weight.shape[2]
    local_width = w_qkv.shape[2]
    local_heads = local_width // DH
    logit_scale = DH ** (-0.5)
    padded = padded_2(enc_in, ((("seq", "head"), 0),), 2)
    convolved = jnp.zeros((fine_rows, seq_count, out_width), jnp.float32)
    for offset in range(KW):
        convolved = convolved + jnp.einsum(
            "tbi,io->tbo",
            padded[offset : offset + fine_rows],
            conv_weight[offset],
            preferred_element_type=jnp.float32,
        )
    activated, gelu_pull = jax.vjp(jax.nn.gelu, convolved)
    skip = jnp.mean(activated.reshape(slab_rows, 2, seq_count, out_width), axis=1).astype(
        jnp.bfloat16
    )
    skip_wide = skip.astype(jnp.float32)
    inv_rms = lax.rsqrt(jnp.mean(skip_wide * skip_wide, axis=-1, keepdims=True) + 1e-06)
    normed = (skip_wide * inv_rms * norm_gain).astype(jnp.bfloat16)
    normed_rows = lax.all_gather(normed, "head", axis=0, tiled=True)
    grad_rows = lax.all_gather(grad_out, "head", axis=0, tiled=True)
    tower_rows = normed_rows.shape[0]
    qkv = jnp.einsum(
        "tbc,ice->itbe", normed_rows, w_qkv, preferred_element_type=jnp.float32
    ).astype(jnp.bfloat16)
    qkv = qkv.reshape(3, tower_rows, seq_count, local_heads, DH)
    query_matrix, key_matrix, value_matrix = (qkv[0], qkv[1], qkv[2])
    key_all, value_all = (
        lax.all_gather(key_matrix, "seq", axis=0, tiled=True),
        lax.all_gather(value_matrix, "seq", axis=0, tiled=True),
    )
    attention_logits = (
        jnp.einsum("qbhd,kbhd->bhqk", query_matrix, key_all, preferred_element_type=jnp.float32)
        * logit_scale
    )
    row_peak = jnp.max(attention_logits, axis=-1, keepdims=True)
    exponent = jnp.exp(attention_logits - row_peak)
    row_total = jnp.sum(exponent, axis=-1, keepdims=True)
    soft_weights = exponent / row_total
    narrow_probabilities = soft_weights.astype(jnp.bfloat16)
    attention_output = jnp.einsum(
        "bhqk,kbhd->qbhd", narrow_probabilities, value_all, preferred_element_type=jnp.float32
    )
    o_narrow = attention_output.reshape(tower_rows, seq_count, local_width).astype(jnp.bfloat16)
    piece = o_narrow
    head_sum = lax.psum_scatter(
        jnp.einsum("tbe,ec->tbc", piece, w_out, preferred_element_type=jnp.float32).astype(
            jnp.bfloat16
        ),
        "head",
        scatter_dimension=0,
        tiled=True,
    ).astype(jnp.float32)
    mixed = (skip_wide + head_sum).astype(jnp.bfloat16)
    part_w_out = jnp.einsum("tbe,tbc->ec", o_narrow, grad_rows, preferred_element_type=jnp.float32)
    d_out = jnp.einsum("tbc,ec->tbe", grad_rows, w_out, preferred_element_type=jnp.float32).astype(
        jnp.bfloat16
    )
    d_out = d_out.reshape(tower_rows, seq_count, local_heads, DH)
    delta = jnp.sum(d_out.astype(jnp.float32) * attention_output, axis=-1)
    probability_gradient = jnp.einsum(
        "qbhd,kbhd->bhqk", d_out, value_all, preferred_element_type=jnp.float32
    )
    d_scores = soft_weights * (probability_gradient - jnp.transpose(delta, (1, 2, 0))[..., None])
    narrow_gradient = d_scores.astype(jnp.bfloat16)
    query_gradient = logit_scale * jnp.einsum(
        "bhqk,kbhd->qbhd", narrow_gradient, key_all, preferred_element_type=jnp.float32
    )
    key_terms = logit_scale * jnp.einsum(
        "bhqk,qbhd->kbhd", narrow_gradient, query_matrix, preferred_element_type=jnp.float32
    )
    value_terms = jnp.einsum(
        "bhqk,qbhd->kbhd", narrow_probabilities, d_out, preferred_element_type=jnp.float32
    )
    d_keys, d_values = (
        lax.psum_scatter(
            key_terms.astype(jnp.bfloat16), "seq", scatter_dimension=0, tiled=True
        ).astype(jnp.float32),
        lax.psum_scatter(
            value_terms.astype(jnp.bfloat16), "seq", scatter_dimension=0, tiled=True
        ).astype(jnp.float32),
    )
    dqkv = (
        jnp.stack([query_gradient, d_keys, d_values])
        .reshape(3, tower_rows, seq_count, local_width)
        .astype(jnp.bfloat16)
    )
    part_w_qkv = jnp.einsum("tbc,itbe->ice", normed_rows, dqkv, preferred_element_type=jnp.float32)
    piece = dqkv
    d_normed = lax.psum_scatter(
        jnp.einsum("itbe,ice->tbc", piece, w_qkv, preferred_element_type=jnp.float32).astype(
            jnp.bfloat16
        ),
        "head",
        scatter_dimension=0,
        tiled=True,
    ).astype(jnp.float32)
    unit_rows = skip_wide * inv_rms
    scaled = d_normed * norm_gain
    d_skip = grad_out.astype(jnp.float32) + inv_rms * (
        scaled - unit_rows * jnp.mean(scaled * unit_rows, axis=-1, keepdims=True)
    )
    d_act = jnp.repeat(d_skip, 2, axis=0) * 0.5
    d_conv = gelu_pull(d_act)[0].astype(jnp.bfloat16)
    d_pad = padded_2(d_conv, ((("seq", "head"), 0),), 2)
    grad_input = jnp.zeros((fine_rows, seq_count, enc_in.shape[2]), jnp.float32)
    for offset in range(KW):
        grad_input = grad_input + jnp.einsum(
            "tbo,io->tbi",
            d_pad[4 - offset : 4 - offset + fine_rows],
            conv_weight[offset],
            preferred_element_type=jnp.float32,
        )
    grad_w_qkv, grad_w_out = (
        lax.psum(part_w_qkv.astype(jnp.bfloat16), "seq").astype(jnp.float32),
        lax.psum(part_w_out.astype(jnp.bfloat16), "seq").astype(jnp.float32),
    )
    return (mixed, grad_input.astype(jnp.bfloat16), grad_w_qkv, grad_w_out)


def body(enc_in, conv_weight, norm_gain, w_qkv, w_out, grad_out):
    heads = w_qkv.shape[2] // DH
    seqs = enc_in.shape[1]
    fits = lax.axis_size("head") == 4 and heads == 2 and seqs == 4 and seqs * heads == lax.axis_size("seq")
    fits = fits and conv_weight.shape[2] == seqs * w_qkv.shape[2]
    chosen = unit_body if fits else gathered_body
    return chosen(enc_in, conv_weight, norm_gain, w_qkv, w_out, grad_out)


def solution(mesh):
    return jax.shard_map(
        body,
        mesh=mesh,
        in_specs=(
            P(("seq", "head"), None, None),
            P(),
            P(),
            P(None, None, "head"),
            P("head", None),
            P(("seq", "head"), None, None),
        ),
        out_specs=(
            P(("seq", "head"), None, None),
            P(("seq", "head"), None, None),
            P(None, None, "head"),
            P("head", None),
        ),
        check_vma=False,
    )
```

```python
import functools

import jax
import jax.numpy as jnp
from jax import lax
from jax.experimental import pallas as pl
from jax.experimental.pallas import tpu as pltpu
from jax.sharding import PartitionSpec as P

DH = 192
KW = 5
VMEM_LIMIT = 24 * 1024 * 1024
STREAMING_LIMIT = 56 * 1024 * 1024
COST = pl.CostEstimate(flops=1000, bytes_accessed=1000, transcendentals=0)
BF = jnp.bfloat16
F32 = jnp.float32
TOKEN = jax.ShapeDtypeStruct((8, 128), F32)


def params(limit=VMEM_LIMIT):
    return pltpu.CompilerParams(vmem_limit_bytes=limit)


def dot(a, b, contract):
    return lax.dot_general(a, b, (contract, ((), ())), preferred_element_type=F32)


NN = ((1,), (0,))
NT = ((1,), (1,))
TN = ((0,), (0,))


def whole(shape):
    return pl.BlockSpec(shape, lambda *_: (0,) * len(shape))


SCALARS = pl.BlockSpec(memory_space=pltpu.SMEM)


def spare(deps):
    return [pl.BlockSpec(memory_space=pl.ANY)] * len(deps)


def turned_rows(ref, low_ref, high_ref, parity, shift):
    seqs, rows, width = ref.shape[1:]
    own = ref[parity]
    if shift != 1:
        wide = own.astype(F32)
        if shift == 0:
            parts = [low_ref[parity].astype(F32), wide[:, : rows - 1]]
        else:
            parts = [wide[:, 1:], high_ref[parity].astype(F32)]
        own = jnp.concatenate(parts, axis=1).astype(BF)
    return own.reshape(seqs * rows, width)


def conv_kernel(
    at_ref, x_ref, low_ref, high_ref, w_ref, gain_ref, skip_ref, slope_ref, *rest
):
    normed_refs, (lhs, squares, whole_normed) = rest[:-3], rest[-3:]
    step = pl.program_id(0)
    seqs, rows, c_in = x_ref.shape[1:]
    half = seqs * rows
    tile = w_ref.shape[2]

    @pl.when(step == 0)
    def _():
        for parity in range(2):
            for shift in range(3):
                value = turned_rows(x_ref, low_ref, high_ref, parity, shift)
                for out in range(2):
                    tap = 2 * shift + parity - out
                    if 0 <= tap < KW:
                        lhs[out * half : (out + 1) * half, tap * c_in : (tap + 1) * c_in] = value
        squares[...] = jnp.zeros_like(squares)

    conv = dot(lhs[...], w_ref[...].reshape(KW * c_in, tile), NN)
    root = 0.7978845608028654
    total = None
    for parity in range(2):
        x = conv[parity * half : (parity + 1) * half, :]
        square = x * x
        t = jnp.tanh(root * (x + 0.044715 * (square * x)))
        left = 0.5 * (1.0 + t)
        act = x * left
        slope = left + (0.5 * root) * x * (1.0 - t * t) * (1.0 + (3 * 0.044715) * square)
        slope_ref[parity] = slope.reshape(slope_ref.shape[1:])
        total = act if total is None else total + act
    skip = (0.5 * total).astype(BF)
    columns = pl.ds(pl.multiple_of(step * tile, tile), tile)
    skip_ref[:, :, columns] = skip.reshape(seqs, rows, tile)
    wide = skip.astype(F32)
    squares[...] += jnp.sum(wide * wide, axis=-1, keepdims=True)

    @pl.when(step == pl.num_programs(0) - 1)
    def _():
        width = skip_ref.shape[2]
        inv = lax.rsqrt(squares[...] * (1.0 / width) + 1e-06)
        wide = skip_ref[...].reshape(half, width).astype(F32)
        normed = (wide * inv * gain_ref[...]).astype(BF)
        whole_normed[...] = normed.reshape(whole_normed.shape)
        for slot in range(seqs):
            normed_refs[slot][...] = whole_normed[at_ref[0] ^ slot]


def encoder(at, pairs, low, high, conv_weight, norm_gain):
    _, seqs, rows, c_in = pairs.shape
    width = conv_weight.shape[2]
    tile = 256 if width % 256 == 0 else width
    shape = (seqs, rows, width)
    outs = pl.pallas_call(
        conv_kernel,
        grid=(width // tile,),
        in_specs=[
            SCALARS,
            whole(pairs.shape),
            whole(low.shape),
            whole(high.shape),
            pl.BlockSpec((KW, c_in, tile), lambda n: (0, 0, n)),
            whole((1, width)),
        ],
        out_specs=[
            whole(shape),
            pl.BlockSpec((2, seqs, rows, tile), lambda n: (0, 0, 0, n)),
        ]
        + [whole((rows, width))] * seqs,
        out_shape=[
            jax.ShapeDtypeStruct(shape, BF),
            jax.ShapeDtypeStruct((2,) + shape, F32),
        ]
        + [jax.ShapeDtypeStruct((rows, width), BF)] * seqs,
        scratch_shapes=[
            pltpu.VMEM((2 * seqs * rows, KW * c_in), BF),
            pltpu.VMEM((seqs * rows, 1), F32),
            pltpu.VMEM(shape, BF),
        ],
        compiler_params=params(STREAMING_LIMIT),
        cost_estimate=COST,
        name="encoder_forward",
    )(at, pairs, low, high, conv_weight, norm_gain.reshape(1, width))
    return outs[0], outs[1], list(outs[2:])


def d_conv_kernel(at_ref, own_ref, near_ref, far_ref, *refs):
    skip_ref, grad_ref, gain_ref, slope_ref = refs[:4]
    out_ref, first_ref, last_ref = refs[-3:]
    rows = out_ref.shape[2]
    for slot, (ref, place) in enumerate(((own_ref, 0), (near_ref, 0), (far_ref, 0), (far_ref, 1))):
        b = at_ref[0] ^ slot
        wide = skip_ref[b].astype(F32)
        inv = lax.rsqrt(jnp.mean(wide * wide, axis=-1, keepdims=True) + 1e-06)
        unit = wide * inv
        scaled = ref[place].astype(F32) * gain_ref[...]
        d_skip = grad_ref[b].astype(F32) + inv * (
            scaled - unit * jnp.mean(scaled * unit, axis=-1, keepdims=True)
        )
        d_act = 0.5 * d_skip
        for parity in range(2):
            value = slope_ref[parity, b] * d_act
            out_ref[parity, b] = value.astype(BF)
            first_ref[parity, b] = value[:1].astype(BF)
            last_ref[parity, b] = value[rows - 1 :].astype(BF)


def conv_gradient(at, own, near, far, skip, grad, norm_gain, slope, *deps):
    vmem = pl.BlockSpec(memory_space=pltpu.VMEM)
    edge = jax.ShapeDtypeStruct(slope.shape[:2] + (1, slope.shape[3]), BF)
    return pl.pallas_call(
        d_conv_kernel,
        in_specs=[SCALARS] + [vmem] * 7 + spare(deps),
        out_specs=[vmem] * 3,
        out_shape=[jax.ShapeDtypeStruct(slope.shape, BF)] + [edge] * 2,
        compiler_params=params(),
        cost_estimate=COST,
        name="conv_gradient",
    )(at, own, near, far, skip, grad, norm_gain.reshape(1, -1), slope, *deps)


def mixed_body(seqs, at_ref, *refs):
    skip_ref, out_ref = refs[seqs], refs[-1]
    for slot in range(seqs):
        b = at_ref[0] ^ slot
        out_ref[b] = (skip_ref[b].astype(F32) + refs[slot][...].astype(F32)).astype(BF)


def mixed_call(at, terms, skip, *deps):
    seqs = len(terms)
    vmem = pl.BlockSpec(memory_space=pltpu.VMEM)
    return pl.pallas_call(
        functools.partial(mixed_body, seqs),
        in_specs=[SCALARS] + [vmem] * (seqs + 1) + spare(deps),
        out_specs=vmem,
        out_shape=jax.ShapeDtypeStruct(skip.shape, BF),
        compiler_params=params(),
        cost_estimate=COST,
        name="mixed_sum",
    )(at, *terms, skip, *deps)


def marker_kernel(*refs):
    refs[-1][...] = jnp.zeros_like(refs[-1])


def marker(*deps):
    return pl.pallas_call(
        marker_kernel,
        in_specs=spare(deps),
        out_shape=TOKEN,
        compiler_params=params(),
        cost_estimate=COST,
        name="marker",
    )(*deps)


def conv_back_kernel(d_ref, low_ref, high_ref, w_ref, *rest):
    out_ref, turned, acc = rest[-3:]
    step = pl.program_id(0)

    @pl.when(step == 0)
    def _():
        for parity in range(2):
            for shift in range(3):
                turned[parity, shift] = turned_rows(d_ref, low_ref, high_ref, parity, shift).T

    for tap in range(KW):

        @pl.when(step == tap)
        def _():
            places = [KW - 1 - tap, KW - tap]
            rhs = jnp.concatenate([turned[p % 2, p // 2] for p in places], axis=1)
            term = dot(w_ref[0], rhs, NN)
            if tap == 0:
                acc[...] = term
            elif tap < KW - 1:
                acc[...] += term
            else:
                out_ref[...] = (acc[...] + term).T.astype(BF)


def conv_back(d_conv, low, high, conv_weight, *deps):
    _, seqs, rows, width = d_conv.shape
    c_in = conv_weight.shape[1]
    flat = 2 * seqs * rows
    return pl.pallas_call(
        conv_back_kernel,
        grid=(KW,),
        in_specs=[
            whole(d_conv.shape),
            whole(low.shape),
            whole(high.shape),
            pl.BlockSpec((1, c_in, width), lambda k: (k, 0, 0)),
        ]
        + spare(deps),
        out_specs=whole((flat, c_in)),
        out_shape=jax.ShapeDtypeStruct((flat, c_in), BF),
        scratch_shapes=[
            pltpu.VMEM((2, 3, width, seqs * rows), BF),
            pltpu.VMEM((c_in, flat), F32),
        ],
        compiler_params=params(),
        cost_estimate=COST,
        name="encoder_backward",
    )(d_conv, low, high, conv_weight, *deps)


def pack_kernel(at_ref, w_ref, own_ref, other_ref, own_turned, other_turned, token_ref):
    token_ref[...] = jnp.zeros_like(token_ref)
    first_head = at_ref[1] == 0
    for i in range(3):
        low, high = w_ref[i, :, :DH], w_ref[i, :, DH:]
        columns = slice(i * DH, (i + 1) * DH)
        own = jnp.where(first_head, low, high)
        other = jnp.where(first_head, high, low)
        own_ref[:, columns] = own
        other_ref[:, columns] = other
        own_turned[columns, :] = own.T
        other_turned[columns, :] = other.T


def pack_weights(at, w_qkv):
    _, width, local = w_qkv.shape
    tile = local
    plain = pl.BlockSpec((tile, 3 * DH), lambda n: (n, 0))
    turned = pl.BlockSpec((3 * DH, tile), lambda n: (0, n))
    return pl.pallas_call(
        pack_kernel,
        grid=(width // tile,),
        in_specs=[SCALARS, pl.BlockSpec((3, tile, local), lambda n: (0, n, 0))],
        out_specs=[plain, plain, turned, turned, pl.BlockSpec(TOKEN.shape, lambda n: (0, 0))],
        out_shape=[jax.ShapeDtypeStruct((width, 3 * DH), BF)] * 2
        + [jax.ShapeDtypeStruct((3 * DH, width), BF)] * 2
        + [TOKEN],
        compiler_params=params(),
        cost_estimate=COST,
        name="pack_weights",
    )(at, w_qkv)


def product_kernel(head_ref, x_ref, w_ref, *rest, contract):
    del head_ref
    out_ref, token_ref = rest[-2:]
    token_ref[...] = jnp.zeros_like(token_ref)
    value = dot(x_ref[...], w_ref[0], contract).astype(BF)
    out_ref[:, : value.shape[1]] = value
    if value.shape[1] < out_ref.shape[1]:
        out_ref[:, value.shape[1] :] = jnp.zeros_like(out_ref[:, value.shape[1] :])


def head_product(head, x, weight, contract, name, *deps):
    columns = weight.shape[2] if contract == NN else weight.shape[1]
    columns += -columns % 128
    rows, width = x.shape
    return pl.pallas_call(
        functools.partial(product_kernel, contract=contract),
        grid_spec=pltpu.PrefetchScalarGridSpec(
            num_scalar_prefetch=1,
            grid=(1,),
            in_specs=[
                pl.BlockSpec((rows, width), lambda i, head: (0, 0)),
                pl.BlockSpec((1,) + weight.shape[1:], lambda i, head: (head[0], 0, 0)),
            ]
            + spare(deps),
            out_specs=[
                pl.BlockSpec((rows, columns), lambda i, head: (0, 0)),
                pl.BlockSpec(TOKEN.shape, lambda i, head: (0, 0)),
            ],
        ),
        out_shape=[jax.ShapeDtypeStruct((rows, columns), BF), TOKEN],
        compiler_params=params(),
        cost_estimate=COST,
        name=name,
    )(head, x, weight, *deps)


def place_kernel(at_ref, *refs):
    del at_ref
    for slot, ref in enumerate(refs[:-1]):

        @pl.when(pl.program_id(0) == slot)
        def _():
            refs[-1][0] = ref[...]


def placed(at, slots, name):
    count = len(slots)
    shape = slots[0].shape
    return pl.pallas_call(
        place_kernel,
        grid_spec=pltpu.PrefetchScalarGridSpec(
            num_scalar_prefetch=1,
            grid=(count,),
            in_specs=[pl.BlockSpec(shape, lambda q, at: (0, 0, 0))] * count,
            out_specs=pl.BlockSpec((1,) + shape, lambda q, at: (q ^ at[0], 0, 0, 0)),
        ),
        out_shape=jax.ShapeDtypeStruct((count,) + shape, slots[0].dtype),
        compiler_params=params(),
        cost_estimate=COST,
        name=name,
    )(at, *slots)


def attention_kernel(qa_ref, qb_ref, da_ref, db_ref, *rest, block):
    oa_ref, ob_ref, k_all, v_all, dk_acc, dv_acc = rest[-6:]
    scale = DH ** (-0.5)
    half = qa_ref.shape[0]
    for place, ref in enumerate((qa_ref, qb_ref)):
        rows = pl.ds(place * half, half)
        k_all[rows, :] = ref[:, DH : 2 * DH]
        v_all[rows, :] = ref[:, 2 * DH : 3 * DH]
    k = k_all[...]
    v = v_all[...]
    for place, (q_ref, d_ref, out_ref) in enumerate(
        ((qa_ref, da_ref, oa_ref), (qb_ref, db_ref, ob_ref))
    ):
        for start in range(0, half, block):
            rows = pl.ds(start, block)
            q = q_ref[rows, 0:DH]
            d_o = d_ref[rows, 0:DH]
            s = dot(q, k, NT) * scale
            e = jnp.exp(s - jnp.max(s, axis=-1, keepdims=True))
            p = e * (1.0 / jnp.sum(e, axis=-1, keepdims=True))
            p_b = p.astype(BF)
            o = dot(p_b, v, NN)
            delta = jnp.sum(d_o.astype(F32) * o, axis=-1, keepdims=True)
            d_p = dot(d_o, v, NT)
            ds = (p * (d_p - delta)).astype(BF)
            dq = scale * dot(ds, k, NN)
            dk = dot(ds, q, TN)
            dv = dot(p_b, d_o, TN)
            if place == 0 and start == 0:
                dk_acc[...] = dk
                dv_acc[...] = dv
            else:
                dk_acc[...] += dk
                dv_acc[...] += dv
            out_ref[rows, 0:DH] = dq.astype(BF)
            out_ref[rows, 3 * DH : 4 * DH] = o.astype(BF)
    for place, out_ref in enumerate((oa_ref, ob_ref)):
        rows = pl.ds(place * half, half)
        out_ref[:, DH : 2 * DH] = (scale * dk_acc[rows, :]).astype(BF)
        out_ref[:, 2 * DH : 3 * DH] = dv_acc[rows, :].astype(BF)


def attention(qkv_a, qkv_b, d_a, d_b, *deps):
    half = qkv_a.shape[0]
    shape = jax.ShapeDtypeStruct((half, 4 * DH), BF)
    return pl.pallas_call(
        functools.partial(attention_kernel, block=min(256, half)),
        in_specs=[pl.BlockSpec(memory_space=pltpu.VMEM)] * 4 + spare(deps),
        out_shape=[shape, shape],
        scratch_shapes=[
            pltpu.VMEM((2 * half, DH), BF),
            pltpu.VMEM((2 * half, DH), BF),
            pltpu.VMEM((2 * half, DH), F32),
            pltpu.VMEM((2 * half, DH), F32),
        ],
        compiler_params=params(),
        cost_estimate=COST,
        name="attention",
    )(qkv_a, qkv_b, d_a, d_b, *deps)


def term_kernel(head_ref, a_ref, b_ref, w_ref, *rest, first, last):
    head = head_ref[0]
    total = dot(a_ref[:, first:last], w_ref[head], NN)
    total += dot(b_ref[:, first:last], w_ref[1 - head], NN)
    rest[-1][...] = total.astype(BF)


def pair_term(head, mine, got, weight, first, last, name, *deps):
    half, full = mine.shape
    heads, depth, width = weight.shape
    tile = 512 if width % 512 == 0 else width
    return pl.pallas_call(
        functools.partial(term_kernel, first=first, last=last),
        grid_spec=pltpu.PrefetchScalarGridSpec(
            num_scalar_prefetch=1,
            grid=(width // tile,),
            in_specs=[
                pl.BlockSpec((half, full), lambda n, at: (0, 0)),
                pl.BlockSpec((half, full), lambda n, at: (0, 0)),
                pl.BlockSpec((heads, depth, tile), lambda n, at: (0, 0, n)),
            ]
            + spare(deps),
            out_specs=pl.BlockSpec((half, tile), lambda n, at: (0, n)),
        ),
        out_shape=jax.ShapeDtypeStruct((half, width), BF),
        compiler_params=params(),
        cost_estimate=COST,
        name=name,
    )(head, mine, got, weight, *deps)


def part_kernel(head_ref, x_ref, w_ref, *rest, last):
    del head_ref
    total = dot(x_ref[:, :last], w_ref[0], NN)
    if len(rest) > 1:
        total += rest[0][...]
    rest[-1][...] = total.astype(rest[-1].dtype)


def term_part(head, x, weight, last, name, *before):
    half, full = x.shape
    _, depth, width = weight.shape
    tile = 512 if width % 512 == 0 else width
    column = pl.BlockSpec((half, tile), lambda n, at: (0, n))
    return pl.pallas_call(
        functools.partial(part_kernel, last=last),
        grid_spec=pltpu.PrefetchScalarGridSpec(
            num_scalar_prefetch=1,
            grid=(width // tile,),
            in_specs=[
                pl.BlockSpec((half, full), lambda n, at: (0, 0)),
                pl.BlockSpec((1, depth, tile), lambda n, at: (at[0], 0, n)),
            ]
            + [column] * len(before),
            out_specs=column,
        ),
        out_shape=jax.ShapeDtypeStruct((half, width), BF if before else F32),
        compiler_params=params(),
        cost_estimate=COST,
        name=name,
    )(head, x, weight, *before)


def weight_kernel(at_ref, xa_ref, xb_ref, ga_ref, gb_ref, ra_ref, rb_ref, *rest):
    del at_ref
    out_refs, turned = rest[:-1], rest[-1]
    step = pl.program_id(0)
    half = ra_ref.shape[0]
    split = 3 * DH

    @pl.when(step == 0)
    def _():
        turned[:, :half] = ra_ref[...].T
        turned[:, half:] = rb_ref[...].T

    a, b = slice(0, half), slice(half, 2 * half)
    qkv = dot(turned[:split, a], xa_ref[...], NN) + dot(turned[:split, b], xb_ref[...], NN)
    out = dot(turned[split:, a], ga_ref[...], NN) + dot(turned[split:, b], gb_ref[...], NN)
    keep_a, send_a, keep_b, send_b = out_refs
    rows = keep_a.shape[1]
    for slot in range(4):

        @pl.when(step == slot)
        def _():
            first = keep_a if slot % 2 == 0 else send_a
            second = keep_b if slot < 2 else send_b
            first[slot // 2] = qkv[:rows].astype(BF)
            second[slot % 2, : split - rows] = qkv[rows:].astype(BF)
            second[slot % 2, split - rows :] = out.astype(BF)


def weight_gradients(at, xa, xb, ga, gb, ra, rb, seqs):
    half, width = xa.shape
    chunk = width // seqs
    full = ra.shape[1]
    column = pl.BlockSpec((half, chunk), lambda r, at: (0, r ^ at[0]))
    rest = pl.BlockSpec((half, full), lambda r, at: (0, 0))
    return pl.pallas_call(
        weight_kernel,
        grid_spec=pltpu.PrefetchScalarGridSpec(
            num_scalar_prefetch=1,
            grid=(seqs,),
            in_specs=[column] * 4 + [rest] * 2,
            out_specs=[pl.BlockSpec((2, full // 2, chunk), lambda r, at: (0, 0, 0))] * 4,
            scratch_shapes=[pltpu.VMEM((full, 2 * half), BF)],
        ),
        out_shape=[jax.ShapeDtypeStruct((2, full // 2, chunk), BF)] * 4,
        compiler_params=params(STREAMING_LIMIT),
        cost_estimate=COST,
        name="weight_gradients",
    )(at, xa, xb, ga, gb, ra, rb)


def turn_kernel(keep_a, got_a, keep_b, got_b, *rest):
    out_a, out_b = rest[-2:]
    for keep, got, out in ((keep_a, got_a, out_a), (keep_b, got_b, out_b)):
        out[...] = (keep[1].astype(F32) + got[1].astype(F32)).astype(BF)


def weight_turn(keep_a, got_a, keep_b, got_b, *deps):
    shape = jax.ShapeDtypeStruct(keep_a.shape[1:], BF)
    return pl.pallas_call(
        turn_kernel,
        in_specs=[pl.BlockSpec(memory_space=pltpu.VMEM)] * 4 + spare(deps),
        out_shape=[shape, shape],
        compiler_params=params(),
        cost_estimate=COST,
        name="weight_turn",
    )(keep_a, got_a, keep_b, got_b, *deps)


def weight_sum_kernel(keep_a, got_a, last_a, keep_b, got_b, last_b, *rest):
    out_refs = rest[-2:]
    split = 3 * DH
    parts = [
        keep[0].astype(F32) + got[0].astype(F32) + last[...].astype(F32)
        for keep, got, last in ((keep_a, got_a, last_a), (keep_b, got_b, last_b))
    ]
    total = jnp.concatenate(parts, axis=0)
    turned = total[:split].T.astype(BF)
    quarter = DH // 2
    for part, out_ref in enumerate(out_refs):
        out_ref[:, :split] = turned[part * DH : (part + 1) * DH]
        first = split + part * quarter
        piece = total[first : first + quarter].astype(BF)
        out_ref[:quarter, split:] = piece[:, :DH]
        out_ref[quarter:, split:] = piece[:, DH:]


def weight_sum(keep_a, got_a, last_a, keep_b, got_b, last_b, *deps):
    _, rows, chunk = keep_a.shape
    return pl.pallas_call(
        weight_sum_kernel,
        in_specs=[pl.BlockSpec(memory_space=pltpu.VMEM)] * 6 + spare(deps),
        out_shape=[jax.ShapeDtypeStruct((chunk // 2, 2 * rows), BF)] * 2,
        compiler_params=params(),
        cost_estimate=COST,
        name="weight_sum",
    )(keep_a, got_a, last_a, keep_b, got_b, last_b, *deps)


def unpack_kernel(at_ref, *refs):
    qkv_ref, out_ref, token_ref = refs[-3:]
    step = pl.program_id(0)
    split = 3 * DH
    quarter = DH // 2
    token_ref[...] = jnp.zeros_like(token_ref)
    for half in range(2):

        @pl.when(step // 2 == half)
        def _():
            mine = refs[half][...].astype(F32)
            other = refs[2 + half][...].astype(F32)
            swapped = at_ref[1] != 0
            low = jnp.where(swapped, other, mine)
            high = jnp.where(swapped, mine, other)
            for i in range(3):
                columns = slice(i * DH, (i + 1) * DH)
                qkv_ref[i] = jnp.concatenate([low[:, columns], high[:, columns]], axis=1)
            for head, value in enumerate((low, high)):
                folded = [value[:quarter, split:], value[quarter:, split:]]
                out_ref[head, 0] = jnp.concatenate(folded, axis=1)


def unpack_weights(at, mine, other, far, before=(), *deps):
    rows, full = mine[0].shape
    half = rows // 2
    width = 4 * rows

    def chunk(t, at):
        if far:
            return at[0] ^ jnp.where(t < 2, t + 2, 2 * t - 3)
        return at[0] ^ jnp.where(t < 2, t, 2 * t - 4)

    specs = [
        pl.BlockSpec((half, full), lambda t, at: (jnp.minimum(t, 1), 0)),
        pl.BlockSpec((half, full), lambda t, at: (jnp.maximum(t - 2, 0), 0)),
    ]
    return pl.pallas_call(
        unpack_kernel,
        grid_spec=pltpu.PrefetchScalarGridSpec(
            num_scalar_prefetch=1,
            grid=(4,),
            in_specs=specs * 2 + spare(tuple(before) + deps),
            out_specs=[
                pl.BlockSpec((3, half, 2 * DH), lambda t, at: (0, 2 * chunk(t, at) + t // 2, 0)),
                pl.BlockSpec(
                    (2, 1, DH // 2, rows), lambda t, at: (0, t // 2, 0, chunk(t, at))
                ),
                pl.BlockSpec(TOKEN.shape, lambda t, at: (0, 0)),
            ],
        ),
        out_shape=[
            jax.ShapeDtypeStruct((3, width, 2 * DH), F32),
            jax.ShapeDtypeStruct((2, 2, DH // 2, width), F32),
            TOKEN,
        ],
        input_output_aliases={5 + i: i for i in range(len(before))},
        compiler_params=params(),
        cost_estimate=COST,
        name="weight_outputs_far" if far else "weight_outputs_near",
    )(at, *mine, *other, *before, *deps)


def neighbour_edges(first, last):
    axes = ("seq", "head")
    count = lax.axis_size(axes)
    forward = [(i, i + 1) for i in range(count - 1)]
    backward = [(target, source) for source, target in forward]
    return lax.ppermute(last, axes, forward), lax.ppermute(first, axes, backward)


def after(value, *others):
    return lax.optimization_barrier((value,) + others)[0]


def trade_chip(x, bit, heads):
    count = lax.axis_size("seq")
    return lax.ppermute(x, "seq", [(s, s ^ (bit * heads)) for s in range(count)])


def trade_z(x, bit):
    count = lax.axis_size("head")
    return lax.ppermute(x, "head", [(z, z ^ bit) for z in range(count)])


def swap_heads(x):
    count = lax.axis_size("seq")
    return lax.ppermute(x, "seq", [(s, s + 1 - 2 * (s % 2)) for s in range(count)])


def unit_body(enc_in, conv_weight, norm_gain, w_qkv, w_out, grad_out):
    rows = enc_in.shape[0] // 2
    seqs = enc_in.shape[1]
    width = conv_weight.shape[2]
    local = w_qkv.shape[2]
    heads = local // DH
    groups = lax.axis_size("head")
    half = groups * seqs * rows
    place = lax.axis_index("seq")
    own_seq = (place // heads).astype(jnp.int32)
    own_head = (place % heads).astype(jnp.int32)
    at = jnp.stack([own_seq, own_head])
    head_mine = own_head.reshape(1)
    head_other = (1 - own_head).reshape(1)

    def to_chips(slots):
        return [x if j == 0 else trade_chip(x, j, heads) for j, x in enumerate(slots)]

    order = (0, 2, 1, 3)

    edge = width - width // seqs
    grad_z = lax.all_gather(grad_out[:, :, :edge], "head", axis=0, tiled=False)

    pairs = jnp.transpose(enc_in.reshape(rows, 2, seqs, enc_in.shape[2]), (1, 2, 0, 3))
    low, high = neighbour_edges(pairs[:, :, :1, :], pairs[:, :, -1:, :])
    own_part = grad_out[:, :, edge:]
    parts = [trade_z(own_part, q) for q in range(1, groups)]
    skip, slope, normed = encoder(at, pairs, low, high, conv_weight, norm_gain)
    normed = to_chips(normed)
    normed_slab = jnp.concatenate([normed[j] for j in order], axis=0)
    normed_slab, *parts = lax.optimization_barrier((normed_slab, *parts))
    normed_rows = lax.all_gather(normed_slab, "head", axis=0, tiled=True)

    grad_z = after(grad_z, normed_slab)
    own_z = lax.axis_index("head").astype(jnp.int32).reshape(1)
    grad_z = jnp.concatenate([grad_z, placed(own_z, [own_part, *parts], "grad_last")], axis=3)
    grad_slots = to_chips(
        [lax.dynamic_index_in_dim(grad_z, own_seq ^ j, 2, keepdims=False) for j in range(seqs)]
    )
    *weights, packed = pack_weights(at, after(w_qkv, normed_slab))
    *grad_slots, packed = lax.optimization_barrier((*grad_slots, packed))
    grad_rows = jnp.stack([grad_slots[j] for j in order], axis=1).reshape(half, width)
    w_rows = w_out.reshape(heads, DH, width)
    d_other, one = head_product(head_other, grad_rows, w_rows, NT, "d_o_other")
    d_got = swap_heads(d_other)
    d_mine, two = head_product(head_mine, grad_rows, w_rows, NT, "d_o_own")
    grad_swapped = swap_heads(grad_rows)
    normed_rows, d_got, d_mine, grad_swapped, *weights = lax.optimization_barrier(
        (normed_rows, d_got, d_mine, grad_swapped, *weights, packed, one, two)
    )
    w_own, w_other, turned_own, turned_other = [w[None] for w in weights[:4]]
    tokens = weights[4:]
    sole = jnp.zeros((1,), jnp.int32)

    normed_swapped = swap_heads(normed_rows)
    qkv_other, _ = head_product(sole, normed_rows, w_other, NN, "qkv_other", *tokens)
    qkv_got = swap_heads(qkv_other)
    qkv_mine, _ = head_product(sole, normed_rows, w_own, NN, "qkv_own")
    result_mine, result_other = attention(qkv_mine, qkv_got, d_mine, d_got, normed_swapped)
    result_got = swap_heads(result_other)

    shape = (groups, seqs, rows, width)
    d_own = term_part(sole, result_mine, turned_own, 3 * DH, "d_term_own")
    d_term = term_part(sole, result_got, turned_other, 3 * DH, "d_term", d_own)
    d_normed = lax.psum_scatter(d_term.reshape(shape), "head", scatter_dimension=0, tiled=False)
    keep_a, send_a, keep_b, send_b = weight_gradients(
        own_seq.reshape(1),
        normed_rows,
        normed_swapped,
        grad_rows,
        grad_swapped,
        result_mine,
        result_other,
        seqs,
    )
    got_a, got_b = trade_chip(send_a, 1, heads), trade_chip(send_b, 2, heads)
    head_term = pair_term(
        head_mine, result_mine, result_got, w_rows, 3 * DH, 4 * DH, "head_term"
    )
    head_sum = lax.psum_scatter(head_term.reshape(shape), "head", scatter_dimension=0, tiled=False)
    turn_a, turn_b = weight_turn(keep_a, got_a, keep_b, got_b, head_term)
    last_a, last_b = trade_chip(turn_a, 2, heads), trade_chip(turn_b, 1, heads)

    d_normed = after(d_normed, turn_a, turn_b)
    leaving = d_normed[2:]
    near = trade_chip(leaving, 1, heads)
    far = trade_chip(jnp.stack([d_normed[1], near[1]]), 2, heads)
    half_a, half_b = weight_sum(keep_a, got_a, last_a, keep_b, got_b, last_b, leaving)
    grad = jnp.transpose(after(grad_out, d_term), (1, 0, 2))
    d_conv, first, last = conv_gradient(
        at, d_normed, near, far, skip, grad, norm_gain, slope, half_a
    )
    low, high = neighbour_edges(first, last)
    low, high, at_hand = lax.optimization_barrier((low, high, marker(conv_weight, first)))

    got_a, got_b = trade_chip(half_a, 1, heads), trade_chip(half_b, 2, heads)
    near_a = jnp.concatenate([half_a, after(got_a, low)], axis=0)
    near_b = jnp.concatenate([half_b, after(got_b, high)], axis=0)
    far_a = trade_chip(near_a, 2, heads)
    far_b = trade_chip(near_b, 1, heads)
    near_other = [swap_heads(near_a), swap_heads(near_b)]
    grad_input = conv_back(d_conv, low, high, conv_weight, at_hand, *near_other)
    *outputs, token = unpack_weights(
        at, [near_a, near_b], near_other, False, (), grad_input
    )

    head_sum = after(head_sum, grad_input, token)
    head_sum = to_chips([head_sum[order.index(j)] for j in range(seqs)])
    far_other = [swap_heads(after(x, *head_sum[1:])) for x in (far_a, far_b)]
    grad_w_qkv, grad_w_out, _ = unpack_weights(at, [far_a, far_b], far_other, True, outputs)
    mixed = mixed_call(at, head_sum, skip, token)
    grad_input = jnp.transpose(grad_input.reshape(2, seqs, rows, -1), (2, 0, 1, 3))
    return (
        jnp.transpose(mixed, (1, 0, 2)),
        grad_input.reshape(enc_in.shape),
        grad_w_qkv,
        grad_w_out.reshape(local, width),
    )


def padded_2(block, sides, width):
    for axis, dim in sides:
        count = lax.axis_size(axis)
        forward = [(i, i + 1) for i in range(count - 1)]
        backward = [(target, source) for source, target in forward]
        low = lax.ppermute(
            lax.slice_in_dim(block, block.shape[dim] - width, None, axis=dim), axis, forward
        )
        high = lax.ppermute(lax.slice_in_dim(block, 0, width, axis=dim), axis, backward)
        block = jnp.concatenate([low, block, high], axis=dim)
    return block


def gathered_body(enc_in, conv_weight, norm_gain, w_qkv, w_out, grad_out):
    fine_rows = enc_in.shape[0]
    slab_rows = fine_rows // 2
    seq_count = enc_in.shape[1]
    out_width = conv_weight.shape[2]
    local_width = w_qkv.shape[2]
    local_heads = local_width // DH
    logit_scale = DH ** (-0.5)
    padded = padded_2(enc_in, ((("seq", "head"), 0),), 2)
    convolved = jnp.zeros((fine_rows, seq_count, out_width), jnp.float32)
    for offset in range(KW):
        convolved = convolved + jnp.einsum(
            "tbi,io->tbo",
            padded[offset : offset + fine_rows],
            conv_weight[offset],
            preferred_element_type=jnp.float32,
        )
    activated, gelu_pull = jax.vjp(jax.nn.gelu, convolved)
    skip = jnp.mean(activated.reshape(slab_rows, 2, seq_count, out_width), axis=1).astype(
        jnp.bfloat16
    )
    skip_wide = skip.astype(jnp.float32)
    inv_rms = lax.rsqrt(jnp.mean(skip_wide * skip_wide, axis=-1, keepdims=True) + 1e-06)
    normed = (skip_wide * inv_rms * norm_gain).astype(jnp.bfloat16)
    normed_rows = lax.all_gather(normed, "head", axis=0, tiled=True)
    grad_rows = lax.all_gather(grad_out, "head", axis=0, tiled=True)
    tower_rows = normed_rows.shape[0]
    qkv = jnp.einsum(
        "tbc,ice->itbe", normed_rows, w_qkv, preferred_element_type=jnp.float32
    ).astype(jnp.bfloat16)
    qkv = qkv.reshape(3, tower_rows, seq_count, local_heads, DH)
    query_matrix, key_matrix, value_matrix = (qkv[0], qkv[1], qkv[2])
    key_all, value_all = (
        lax.all_gather(key_matrix, "seq", axis=0, tiled=True),
        lax.all_gather(value_matrix, "seq", axis=0, tiled=True),
    )
    attention_logits = (
        jnp.einsum("qbhd,kbhd->bhqk", query_matrix, key_all, preferred_element_type=jnp.float32)
        * logit_scale
    )
    row_peak = jnp.max(attention_logits, axis=-1, keepdims=True)
    exponent = jnp.exp(attention_logits - row_peak)
    row_total = jnp.sum(exponent, axis=-1, keepdims=True)
    soft_weights = exponent / row_total
    narrow_probabilities = soft_weights.astype(jnp.bfloat16)
    attention_output = jnp.einsum(
        "bhqk,kbhd->qbhd", narrow_probabilities, value_all, preferred_element_type=jnp.float32
    )
    o_narrow = attention_output.reshape(tower_rows, seq_count, local_width).astype(jnp.bfloat16)
    piece = o_narrow
    head_sum = lax.psum_scatter(
        jnp.einsum("tbe,ec->tbc", piece, w_out, preferred_element_type=jnp.float32).astype(
            jnp.bfloat16
        ),
        "head",
        scatter_dimension=0,
        tiled=True,
    ).astype(jnp.float32)
    mixed = (skip_wide + head_sum).astype(jnp.bfloat16)
    part_w_out = jnp.einsum("tbe,tbc->ec", o_narrow, grad_rows, preferred_element_type=jnp.float32)
    d_out = jnp.einsum("tbc,ec->tbe", grad_rows, w_out, preferred_element_type=jnp.float32).astype(
        jnp.bfloat16
    )
    d_out = d_out.reshape(tower_rows, seq_count, local_heads, DH)
    delta = jnp.sum(d_out.astype(jnp.float32) * attention_output, axis=-1)
    probability_gradient = jnp.einsum(
        "qbhd,kbhd->bhqk", d_out, value_all, preferred_element_type=jnp.float32
    )
    d_scores = soft_weights * (probability_gradient - jnp.transpose(delta, (1, 2, 0))[..., None])
    narrow_gradient = d_scores.astype(jnp.bfloat16)
    query_gradient = logit_scale * jnp.einsum(
        "bhqk,kbhd->qbhd", narrow_gradient, key_all, preferred_element_type=jnp.float32
    )
    key_terms = logit_scale * jnp.einsum(
        "bhqk,qbhd->kbhd", narrow_gradient, query_matrix, preferred_element_type=jnp.float32
    )
    value_terms = jnp.einsum(
        "bhqk,qbhd->kbhd", narrow_probabilities, d_out, preferred_element_type=jnp.float32
    )
    d_keys, d_values = (
        lax.psum_scatter(
            key_terms.astype(jnp.bfloat16), "seq", scatter_dimension=0, tiled=True
        ).astype(jnp.float32),
        lax.psum_scatter(
            value_terms.astype(jnp.bfloat16), "seq", scatter_dimension=0, tiled=True
        ).astype(jnp.float32),
    )
    dqkv = (
        jnp.stack([query_gradient, d_keys, d_values])
        .reshape(3, tower_rows, seq_count, local_width)
        .astype(jnp.bfloat16)
    )
    part_w_qkv = jnp.einsum("tbc,itbe->ice", normed_rows, dqkv, preferred_element_type=jnp.float32)
    piece = dqkv
    d_normed = lax.psum_scatter(
        jnp.einsum("itbe,ice->tbc", piece, w_qkv, preferred_element_type=jnp.float32).astype(
            jnp.bfloat16
        ),
        "head",
        scatter_dimension=0,
        tiled=True,
    ).astype(jnp.float32)
    unit_rows = skip_wide * inv_rms
    scaled = d_normed * norm_gain
    d_skip = grad_out.astype(jnp.float32) + inv_rms * (
        scaled - unit_rows * jnp.mean(scaled * unit_rows, axis=-1, keepdims=True)
    )
    d_act = jnp.repeat(d_skip, 2, axis=0) * 0.5
    d_conv = gelu_pull(d_act)[0].astype(jnp.bfloat16)
    d_pad = padded_2(d_conv, ((("seq", "head"), 0),), 2)
    grad_input = jnp.zeros((fine_rows, seq_count, enc_in.shape[2]), jnp.float32)
    for offset in range(KW):
        grad_input = grad_input + jnp.einsum(
            "tbo,io->tbi",
            d_pad[4 - offset : 4 - offset + fine_rows],
            conv_weight[offset],
            preferred_element_type=jnp.float32,
        )
    grad_w_qkv, grad_w_out = (
        lax.psum(part_w_qkv.astype(jnp.bfloat16), "seq").astype(jnp.float32),
        lax.psum(part_w_out.astype(jnp.bfloat16), "seq").astype(jnp.float32),
    )
    return (mixed, grad_input.astype(jnp.bfloat16), grad_w_qkv, grad_w_out)


def body(enc_in, conv_weight, norm_gain, w_qkv, w_out, grad_out):
    heads = w_qkv.shape[2] // DH
    seqs = enc_in.shape[1]
    fits = lax.axis_size("head") == 4 and heads == 2 and seqs == 4 and seqs * heads == lax.axis_size("seq")
    fits = fits and conv_weight.shape[2] == seqs * w_qkv.shape[2]
    chosen = unit_body if fits else gathered_body
    return chosen(enc_in, conv_weight, norm_gain, w_qkv, w_out, grad_out)


def solution(mesh):
    return jax.shard_map(
        body,
        mesh=mesh,
        in_specs=(
            P(("seq", "head"), None, None),
            P(),
            P(),
            P(None, None, "head"),
            P("head", None),
            P(("seq", "head"), None, None),
        ),
        out_specs=(
            P(("seq", "head"), None, None),
            P(("seq", "head"), None, None),
            P(None, None, "head"),
            P("head", None),
        ),
        check_vma=False,
    )
```

```python
import functools

import jax
import jax.numpy as jnp
from jax import lax
from jax.experimental import pallas as pl
from jax.experimental.pallas import tpu as pltpu
from jax.sharding import PartitionSpec as P

DH = 192
KW = 5
VMEM_LIMIT = 24 * 1024 * 1024
STREAMING_LIMIT = 56 * 1024 * 1024
COST = pl.CostEstimate(flops=1000, bytes_accessed=1000, transcendentals=0)
BF = jnp.bfloat16
F32 = jnp.float32
TOKEN = jax.ShapeDtypeStruct((8, 128), F32)


def params(limit=VMEM_LIMIT):
    return pltpu.CompilerParams(vmem_limit_bytes=limit)


def dot(a, b, contract):
    return lax.dot_general(a, b, (contract, ((), ())), preferred_element_type=F32)


NN = ((1,), (0,))
NT = ((1,), (1,))
TN = ((0,), (0,))


def whole(shape):
    return pl.BlockSpec(shape, lambda *_: (0,) * len(shape))


SCALARS = pl.BlockSpec(memory_space=pltpu.SMEM)


def spare(deps):
    return [pl.BlockSpec(memory_space=pl.ANY)] * len(deps)


def turned_rows(ref, low_ref, high_ref, parity, shift):
    seqs, rows, width = ref.shape[1:]
    own = ref[parity]
    if shift != 1:
        wide = own.astype(F32)
        if shift == 0:
            parts = [low_ref[parity].astype(F32), wide[:, : rows - 1]]
        else:
            parts = [wide[:, 1:], high_ref[parity].astype(F32)]
        own = jnp.concatenate(parts, axis=1).astype(BF)
    return own.reshape(seqs * rows, width)


def conv_kernel(
    at_ref, x_ref, low_ref, high_ref, w_ref, gain_ref, skip_ref, slope_ref, *rest
):
    normed_refs, (lhs, squares, whole_normed) = rest[:-3], rest[-3:]
    step = pl.program_id(0)
    seqs, rows, c_in = x_ref.shape[1:]
    half = seqs * rows
    tile = w_ref.shape[2]

    @pl.when(step == 0)
    def _():
        for parity in range(2):
            for shift in range(3):
                value = turned_rows(x_ref, low_ref, high_ref, parity, shift)
                for out in range(2):
                    tap = 2 * shift + parity - out
                    if 0 <= tap < KW:
                        lhs[out * half : (out + 1) * half, tap * c_in : (tap + 1) * c_in] = value
        squares[...] = jnp.zeros_like(squares)

    conv = dot(lhs[...], w_ref[...].reshape(KW * c_in, tile), NN)
    root = 0.7978845608028654
    total = None
    for parity in range(2):
        x = conv[parity * half : (parity + 1) * half, :]
        square = x * x
        t = jnp.tanh(root * (x + 0.044715 * (square * x)))
        left = 0.5 * (1.0 + t)
        act = x * left
        slope = left + (0.5 * root) * x * (1.0 - t * t) * (1.0 + (3 * 0.044715) * square)
        slope_ref[parity] = slope.reshape(slope_ref.shape[1:])
        total = act if total is None else total + act
    skip = (0.5 * total).astype(BF)
    columns = pl.ds(pl.multiple_of(step * tile, tile), tile)
    skip_ref[:, :, columns] = skip.reshape(seqs, rows, tile)
    wide = skip.astype(F32)
    squares[...] += jnp.sum(wide * wide, axis=-1, keepdims=True)

    @pl.when(step == pl.num_programs(0) - 1)
    def _():
        width = skip_ref.shape[2]
        inv = lax.rsqrt(squares[...] * (1.0 / width) + 1e-06)
        wide = skip_ref[...].reshape(half, width).astype(F32)
        normed = (wide * inv * gain_ref[...]).astype(BF)
        whole_normed[...] = normed.reshape(whole_normed.shape)
        for slot in range(seqs):
            normed_refs[slot][...] = whole_normed[at_ref[0] ^ slot]


def encoder(at, pairs, low, high, conv_weight, norm_gain):
    _, seqs, rows, c_in = pairs.shape
    width = conv_weight.shape[2]
    tile = 256 if width % 256 == 0 else width
    shape = (seqs, rows, width)
    outs = pl.pallas_call(
        conv_kernel,
        grid=(width // tile,),
        in_specs=[
            SCALARS,
            whole(pairs.shape),
            whole(low.shape),
            whole(high.shape),
            pl.BlockSpec((KW, c_in, tile), lambda n: (0, 0, n)),
            whole((1, width)),
        ],
        out_specs=[
            whole(shape),
            pl.BlockSpec((2, seqs, rows, tile), lambda n: (0, 0, 0, n)),
        ]
        + [whole((rows, width))] * seqs,
        out_shape=[
            jax.ShapeDtypeStruct(shape, BF),
            jax.ShapeDtypeStruct((2,) + shape, F32),
        ]
        + [jax.ShapeDtypeStruct((rows, width), BF)] * seqs,
        scratch_shapes=[
            pltpu.VMEM((2 * seqs * rows, KW * c_in), BF),
            pltpu.VMEM((seqs * rows, 1), F32),
            pltpu.VMEM(shape, BF),
        ],
        compiler_params=params(STREAMING_LIMIT),
        cost_estimate=COST,
        name="encoder_forward",
    )(at, pairs, low, high, conv_weight, norm_gain.reshape(1, width))
    return outs[0], outs[1], list(outs[2:])


def d_conv_kernel(at_ref, own_ref, near_ref, far_ref, *refs):
    skip_ref, grad_ref, gain_ref, slope_ref = refs[:4]
    out_ref, first_ref, last_ref = refs[-3:]
    rows = out_ref.shape[2]
    for slot, (ref, place) in enumerate(((own_ref, 0), (near_ref, 0), (far_ref, 0), (far_ref, 1))):
        b = at_ref[0] ^ slot
        wide = skip_ref[b].astype(F32)
        inv = lax.rsqrt(jnp.mean(wide * wide, axis=-1, keepdims=True) + 1e-06)
        unit = wide * inv
        scaled = ref[place].astype(F32) * gain_ref[...]
        d_skip = grad_ref[b].astype(F32) + inv * (
            scaled - unit * jnp.mean(scaled * unit, axis=-1, keepdims=True)
        )
        d_act = 0.5 * d_skip
        for parity in range(2):
            value = slope_ref[parity, b] * d_act
            out_ref[parity, b] = value.astype(BF)
            first_ref[parity, b] = value[:1].astype(BF)
            last_ref[parity, b] = value[rows - 1 :].astype(BF)


def conv_gradient(at, own, near, far, skip, grad, norm_gain, slope, *deps):
    vmem = pl.BlockSpec(memory_space=pltpu.VMEM)
    edge = jax.ShapeDtypeStruct(slope.shape[:2] + (1, slope.shape[3]), BF)
    return pl.pallas_call(
        d_conv_kernel,
        in_specs=[SCALARS] + [vmem] * 7 + spare(deps),
        out_specs=[vmem] * 3,
        out_shape=[jax.ShapeDtypeStruct(slope.shape, BF)] + [edge] * 2,
        compiler_params=params(),
        cost_estimate=COST,
        name="conv_gradient",
    )(at, own, near, far, skip, grad, norm_gain.reshape(1, -1), slope, *deps)


def mixed_body(seqs, at_ref, *refs):
    skip_ref, out_ref = refs[seqs], refs[-1]
    for slot in range(seqs):
        b = at_ref[0] ^ slot
        out_ref[b] = (skip_ref[b].astype(F32) + refs[slot][...].astype(F32)).astype(BF)


def mixed_call(at, terms, skip, *deps):
    seqs = len(terms)
    vmem = pl.BlockSpec(memory_space=pltpu.VMEM)
    return pl.pallas_call(
        functools.partial(mixed_body, seqs),
        in_specs=[SCALARS] + [vmem] * (seqs + 1) + spare(deps),
        out_specs=vmem,
        out_shape=jax.ShapeDtypeStruct(skip.shape, BF),
        compiler_params=params(),
        cost_estimate=COST,
        name="mixed_sum",
    )(at, *terms, skip, *deps)


def marker_kernel(*refs):
    refs[-1][...] = jnp.zeros_like(refs[-1])


def marker(*deps):
    return pl.pallas_call(
        marker_kernel,
        in_specs=spare(deps),
        out_shape=TOKEN,
        compiler_params=params(),
        cost_estimate=COST,
        name="marker",
    )(*deps)


def conv_back_kernel(d_ref, low_ref, high_ref, w_ref, *rest):
    out_ref, turned, acc = rest[-3:]
    step = pl.program_id(0)

    @pl.when(step == 0)
    def _():
        for parity in range(2):
            for shift in range(3):
                turned[parity, shift] = turned_rows(d_ref, low_ref, high_ref, parity, shift).T

    for tap in range(KW):

        @pl.when(step == tap)
        def _():
            places = [KW - 1 - tap, KW - tap]
            rhs = jnp.concatenate([turned[p % 2, p // 2] for p in places], axis=1)
            term = dot(w_ref[0], rhs, NN)
            if tap == 0:
                acc[...] = term
            elif tap < KW - 1:
                acc[...] += term
            else:
                out_ref[...] = (acc[...] + term).T.astype(BF)


def conv_back(d_conv, low, high, conv_weight, *deps):
    _, seqs, rows, width = d_conv.shape
    c_in = conv_weight.shape[1]
    flat = 2 * seqs * rows
    return pl.pallas_call(
        conv_back_kernel,
        grid=(KW,),
        in_specs=[
            whole(d_conv.shape),
            whole(low.shape),
            whole(high.shape),
            pl.BlockSpec((1, c_in, width), lambda k: (k, 0, 0)),
        ]
        + spare(deps),
        out_specs=whole((flat, c_in)),
        out_shape=jax.ShapeDtypeStruct((flat, c_in), BF),
        scratch_shapes=[
            pltpu.VMEM((2, 3, width, seqs * rows), BF),
            pltpu.VMEM((c_in, flat), F32),
        ],
        compiler_params=params(),
        cost_estimate=COST,
        name="encoder_backward",
    )(d_conv, low, high, conv_weight, *deps)


def pack_kernel(at_ref, w_ref, own_ref, other_ref, own_turned, other_turned, token_ref):
    token_ref[...] = jnp.zeros_like(token_ref)
    first_head = at_ref[1] == 0
    for i in range(3):
        low, high = w_ref[i, :, :DH], w_ref[i, :, DH:]
        columns = slice(i * DH, (i + 1) * DH)
        own = jnp.where(first_head, low, high)
        other = jnp.where(first_head, high, low)
        own_ref[:, columns] = own
        other_ref[:, columns] = other
        own_turned[columns, :] = own.T
        other_turned[columns, :] = other.T


def pack_weights(at, w_qkv):
    _, width, local = w_qkv.shape
    tile = local
    plain = pl.BlockSpec((tile, 3 * DH), lambda n: (n, 0))
    turned = pl.BlockSpec((3 * DH, tile), lambda n: (0, n))
    return pl.pallas_call(
        pack_kernel,
        grid=(width // tile,),
        in_specs=[SCALARS, pl.BlockSpec((3, tile, local), lambda n: (0, n, 0))],
        out_specs=[plain, plain, turned, turned, pl.BlockSpec(TOKEN.shape, lambda n: (0, 0))],
        out_shape=[jax.ShapeDtypeStruct((width, 3 * DH), BF)] * 2
        + [jax.ShapeDtypeStruct((3 * DH, width), BF)] * 2
        + [TOKEN],
        compiler_params=params(),
        cost_estimate=COST,
        name="pack_weights",
    )(at, w_qkv)


def product_kernel(head_ref, x_ref, w_ref, *rest, contract):
    del head_ref
    out_ref, token_ref = rest[-2:]
    token_ref[...] = jnp.zeros_like(token_ref)
    value = dot(x_ref[...], w_ref[0], contract).astype(BF)
    out_ref[:, : value.shape[1]] = value
    if value.shape[1] < out_ref.shape[1]:
        out_ref[:, value.shape[1] :] = jnp.zeros_like(out_ref[:, value.shape[1] :])


def head_product(head, x, weight, contract, name, *deps):
    columns = weight.shape[2] if contract == NN else weight.shape[1]
    columns += -columns % 128
    rows, width = x.shape
    return pl.pallas_call(
        functools.partial(product_kernel, contract=contract),
        grid_spec=pltpu.PrefetchScalarGridSpec(
            num_scalar_prefetch=1,
            grid=(1,),
            in_specs=[
                pl.BlockSpec((rows, width), lambda i, head: (0, 0)),
                pl.BlockSpec((1,) + weight.shape[1:], lambda i, head: (head[0], 0, 0)),
            ]
            + spare(deps),
            out_specs=[
                pl.BlockSpec((rows, columns), lambda i, head: (0, 0)),
                pl.BlockSpec(TOKEN.shape, lambda i, head: (0, 0)),
            ],
        ),
        out_shape=[jax.ShapeDtypeStruct((rows, columns), BF), TOKEN],
        compiler_params=params(),
        cost_estimate=COST,
        name=name,
    )(head, x, weight, *deps)


def place_kernel(at_ref, *refs):
    del at_ref
    for slot, ref in enumerate(refs[:-1]):

        @pl.when(pl.program_id(0) == slot)
        def _():
            refs[-1][0] = ref[...]


def placed(at, slots, name):
    count = len(slots)
    shape = slots[0].shape
    return pl.pallas_call(
        place_kernel,
        grid_spec=pltpu.PrefetchScalarGridSpec(
            num_scalar_prefetch=1,
            grid=(count,),
            in_specs=[pl.BlockSpec(shape, lambda q, at: (0, 0, 0))] * count,
            out_specs=pl.BlockSpec((1,) + shape, lambda q, at: (q ^ at[0], 0, 0, 0)),
        ),
        out_shape=jax.ShapeDtypeStruct((count,) + shape, slots[0].dtype),
        compiler_params=params(),
        cost_estimate=COST,
        name=name,
    )(at, *slots)


def attention_kernel(qa_ref, qb_ref, da_ref, db_ref, *rest, block):
    oa_ref, ob_ref, k_all, v_all, dk_acc, dv_acc = rest[-6:]
    scale = DH ** (-0.5)
    half = qa_ref.shape[0]
    for place, ref in enumerate((qa_ref, qb_ref)):
        rows = pl.ds(place * half, half)
        k_all[rows, :] = ref[:, DH : 2 * DH]
        v_all[rows, :] = ref[:, 2 * DH : 3 * DH]
    k = k_all[...]
    v = v_all[...]
    for place, (q_ref, d_ref, out_ref) in enumerate(
        ((qa_ref, da_ref, oa_ref), (qb_ref, db_ref, ob_ref))
    ):
        for start in range(0, half, block):
            rows = pl.ds(start, block)
            q = q_ref[rows, 0:DH]
            d_o = d_ref[rows, 0:DH]
            s = dot(q, k, NT) * scale
            e = jnp.exp(s - jnp.max(s, axis=-1, keepdims=True))
            p = e * (1.0 / jnp.sum(e, axis=-1, keepdims=True))
            p_b = p.astype(BF)
            o = dot(p_b, v, NN)
            delta = jnp.sum(d_o.astype(F32) * o, axis=-1, keepdims=True)
            d_p = dot(d_o, v, NT)
            ds = (p * (d_p - delta)).astype(BF)
            dq = scale * dot(ds, k, NN)
            dk = dot(ds, q, TN)
            dv = dot(p_b, d_o, TN)
            if place == 0 and start == 0:
                dk_acc[...] = dk
                dv_acc[...] = dv
            else:
                dk_acc[...] += dk
                dv_acc[...] += dv
            out_ref[rows, 0:DH] = dq.astype(BF)
            out_ref[rows, 3 * DH : 4 * DH] = o.astype(BF)
    for place, out_ref in enumerate((oa_ref, ob_ref)):
        rows = pl.ds(place * half, half)
        out_ref[:, DH : 2 * DH] = (scale * dk_acc[rows, :]).astype(BF)
        out_ref[:, 2 * DH : 3 * DH] = dv_acc[rows, :].astype(BF)


def attention(qkv_a, qkv_b, d_a, d_b, *deps):
    half = qkv_a.shape[0]
    shape = jax.ShapeDtypeStruct((half, 4 * DH), BF)
    return pl.pallas_call(
        functools.partial(attention_kernel, block=min(256, half)),
        in_specs=[pl.BlockSpec(memory_space=pltpu.VMEM)] * 4 + spare(deps),
        out_shape=[shape, shape],
        scratch_shapes=[
            pltpu.VMEM((2 * half, DH), BF),
            pltpu.VMEM((2 * half, DH), BF),
            pltpu.VMEM((2 * half, DH), F32),
            pltpu.VMEM((2 * half, DH), F32),
        ],
        compiler_params=params(),
        cost_estimate=COST,
        name="attention",
    )(qkv_a, qkv_b, d_a, d_b, *deps)


def term_kernel(head_ref, a_ref, b_ref, w_ref, *rest, first, last):
    head = head_ref[0]
    total = dot(a_ref[:, first:last], w_ref[head], NN)
    total += dot(b_ref[:, first:last], w_ref[1 - head], NN)
    rest[-1][...] = total.astype(BF)


def pair_term(head, mine, got, weight, first, last, name, *deps):
    half, full = mine.shape
    heads, depth, width = weight.shape
    tile = 512 if width % 512 == 0 else width
    return pl.pallas_call(
        functools.partial(term_kernel, first=first, last=last),
        grid_spec=pltpu.PrefetchScalarGridSpec(
            num_scalar_prefetch=1,
            grid=(width // tile,),
            in_specs=[
                pl.BlockSpec((half, full), lambda n, at: (0, 0)),
                pl.BlockSpec((half, full), lambda n, at: (0, 0)),
                pl.BlockSpec((heads, depth, tile), lambda n, at: (0, 0, n)),
            ]
            + spare(deps),
            out_specs=pl.BlockSpec((half, tile), lambda n, at: (0, n)),
        ),
        out_shape=jax.ShapeDtypeStruct((half, width), BF),
        compiler_params=params(),
        cost_estimate=COST,
        name=name,
    )(head, mine, got, weight, *deps)


def part_kernel(head_ref, x_ref, w_ref, *rest, last):
    del head_ref
    total = dot(x_ref[:, :last], w_ref[0], NN)
    if len(rest) > 1:
        total += rest[0][...]
    rest[-1][...] = total.astype(rest[-1].dtype)


def term_part(head, x, weight, last, name, *before):
    half, full = x.shape
    _, depth, width = weight.shape
    tile = 512 if width % 512 == 0 else width
    column = pl.BlockSpec((half, tile), lambda n, at: (0, n))
    return pl.pallas_call(
        functools.partial(part_kernel, last=last),
        grid_spec=pltpu.PrefetchScalarGridSpec(
            num_scalar_prefetch=1,
            grid=(width // tile,),
            in_specs=[
                pl.BlockSpec((half, full), lambda n, at: (0, 0)),
                pl.BlockSpec((1, depth, tile), lambda n, at: (at[0], 0, n)),
            ]
            + [column] * len(before),
            out_specs=column,
        ),
        out_shape=jax.ShapeDtypeStruct((half, width), BF if before else F32),
        compiler_params=params(),
        cost_estimate=COST,
        name=name,
    )(head, x, weight, *before)


def weight_kernel(at_ref, xa_ref, xb_ref, ga_ref, gb_ref, ra_ref, rb_ref, *rest):
    del at_ref
    out_refs, turned = rest[:-1], rest[-1]
    step = pl.program_id(0)
    half = ra_ref.shape[0]
    split = 3 * DH

    @pl.when(step == 0)
    def _():
        turned[:, :half] = ra_ref[...].T
        turned[:, half:] = rb_ref[...].T

    a, b = slice(0, half), slice(half, 2 * half)
    qkv = dot(turned[:split, a], xa_ref[...], NN) + dot(turned[:split, b], xb_ref[...], NN)
    out = dot(turned[split:, a], ga_ref[...], NN) + dot(turned[split:, b], gb_ref[...], NN)
    keep_a, send_a, keep_b, send_b = out_refs
    rows = keep_a.shape[1]
    for slot in range(4):

        @pl.when(step == slot)
        def _():
            first = keep_a if slot % 2 == 0 else send_a
            second = keep_b if slot < 2 else send_b
            first[slot // 2] = qkv[:rows].astype(BF)
            second[slot % 2, : split - rows] = qkv[rows:].astype(BF)
            second[slot % 2, split - rows :] = out.astype(BF)


def weight_gradients(at, xa, xb, ga, gb, ra, rb, seqs):
    half, width = xa.shape
    chunk = width // seqs
    full = ra.shape[1]
    column = pl.BlockSpec((half, chunk), lambda r, at: (0, r ^ at[0]))
    rest = pl.BlockSpec((half, full), lambda r, at: (0, 0))
    return pl.pallas_call(
        weight_kernel,
        grid_spec=pltpu.PrefetchScalarGridSpec(
            num_scalar_prefetch=1,
            grid=(seqs,),
            in_specs=[column] * 4 + [rest] * 2,
            out_specs=[pl.BlockSpec((2, full // 2, chunk), lambda r, at: (0, 0, 0))] * 4,
            scratch_shapes=[pltpu.VMEM((full, 2 * half), BF)],
        ),
        out_shape=[jax.ShapeDtypeStruct((2, full // 2, chunk), BF)] * 4,
        compiler_params=params(STREAMING_LIMIT),
        cost_estimate=COST,
        name="weight_gradients",
    )(at, xa, xb, ga, gb, ra, rb)


def turn_kernel(keep_a, got_a, keep_b, got_b, *rest):
    out_a, out_b = rest[-2:]
    for keep, got, out in ((keep_a, got_a, out_a), (keep_b, got_b, out_b)):
        out[...] = (keep[1].astype(F32) + got[1].astype(F32)).astype(BF)


def weight_turn(keep_a, got_a, keep_b, got_b, *deps):
    shape = jax.ShapeDtypeStruct(keep_a.shape[1:], BF)
    return pl.pallas_call(
        turn_kernel,
        in_specs=[pl.BlockSpec(memory_space=pltpu.VMEM)] * 4 + spare(deps),
        out_shape=[shape, shape],
        compiler_params=params(),
        cost_estimate=COST,
        name="weight_turn",
    )(keep_a, got_a, keep_b, got_b, *deps)


def weight_sum_kernel(keep_a, got_a, last_a, keep_b, got_b, last_b, *rest):
    out_refs = rest[-2:]
    split = 3 * DH
    parts = [
        keep[0].astype(F32) + got[0].astype(F32) + last[...].astype(F32)
        for keep, got, last in ((keep_a, got_a, last_a), (keep_b, got_b, last_b))
    ]
    total = jnp.concatenate(parts, axis=0)
    turned = total[:split].T.astype(BF)
    quarter = DH // 2
    for part, out_ref in enumerate(out_refs):
        out_ref[:, :split] = turned[part * DH : (part + 1) * DH]
        first = split + part * quarter
        piece = total[first : first + quarter].astype(BF)
        out_ref[:quarter, split:] = piece[:, :DH]
        out_ref[quarter:, split:] = piece[:, DH:]


def weight_sum(keep_a, got_a, last_a, keep_b, got_b, last_b, *deps):
    _, rows, chunk = keep_a.shape
    return pl.pallas_call(
        weight_sum_kernel,
        in_specs=[pl.BlockSpec(memory_space=pltpu.VMEM)] * 6 + spare(deps),
        out_shape=[jax.ShapeDtypeStruct((chunk // 2, 2 * rows), BF)] * 2,
        compiler_params=params(),
        cost_estimate=COST,
        name="weight_sum",
    )(keep_a, got_a, last_a, keep_b, got_b, last_b, *deps)


def unpack_kernel(at_ref, *refs):
    qkv_ref, out_ref, token_ref = refs[-3:]
    step = pl.program_id(0)
    split = 3 * DH
    quarter = DH // 2
    token_ref[...] = jnp.zeros_like(token_ref)
    for half in range(2):

        @pl.when(step // 2 == half)
        def _():
            mine = refs[half][...].astype(F32)
            other = refs[2 + half][...].astype(F32)
            swapped = at_ref[1] != 0
            low = jnp.where(swapped, other, mine)
            high = jnp.where(swapped, mine, other)
            for i in range(3):
                columns = slice(i * DH, (i + 1) * DH)
                qkv_ref[i] = jnp.concatenate([low[:, columns], high[:, columns]], axis=1)
            for head, value in enumerate((low, high)):
                folded = [value[:quarter, split:], value[quarter:, split:]]
                out_ref[head, 0] = jnp.concatenate(folded, axis=1)


def unpack_weights(at, mine, other, far, before=(), *deps):
    rows, full = mine[0].shape
    half = rows // 2
    width = 4 * rows

    def chunk(t, at):
        if far:
            return at[0] ^ jnp.where(t < 2, t + 2, 2 * t - 3)
        return at[0] ^ jnp.where(t < 2, t, 2 * t - 4)

    specs = [
        pl.BlockSpec((half, full), lambda t, at: (jnp.minimum(t, 1), 0)),
        pl.BlockSpec((half, full), lambda t, at: (jnp.maximum(t - 2, 0), 0)),
    ]
    return pl.pallas_call(
        unpack_kernel,
        grid_spec=pltpu.PrefetchScalarGridSpec(
            num_scalar_prefetch=1,
            grid=(4,),
            in_specs=specs * 2 + spare(tuple(before) + deps),
            out_specs=[
                pl.BlockSpec((3, half, 2 * DH), lambda t, at: (0, 2 * chunk(t, at) + t // 2, 0)),
                pl.BlockSpec(
                    (2, 1, DH // 2, rows), lambda t, at: (0, t // 2, 0, chunk(t, at))
                ),
                pl.BlockSpec(TOKEN.shape, lambda t, at: (0, 0)),
            ],
        ),
        out_shape=[
            jax.ShapeDtypeStruct((3, width, 2 * DH), F32),
            jax.ShapeDtypeStruct((2, 2, DH // 2, width), F32),
            TOKEN,
        ],
        input_output_aliases={5 + i: i for i in range(len(before))},
        compiler_params=params(),
        cost_estimate=COST,
        name="weight_outputs_far" if far else "weight_outputs_near",
    )(at, *mine, *other, *before, *deps)


def neighbour_edges(first, last):
    axes = ("seq", "head")
    count = lax.axis_size(axes)
    forward = [(i, i + 1) for i in range(count - 1)]
    backward = [(target, source) for source, target in forward]
    return lax.ppermute(last, axes, forward), lax.ppermute(first, axes, backward)


def after(value, *others):
    return lax.optimization_barrier((value,) + others)[0]


def trade_chip(x, bit, heads):
    count = lax.axis_size("seq")
    return lax.ppermute(x, "seq", [(s, s ^ (bit * heads)) for s in range(count)])


def trade_z(x, bit):
    count = lax.axis_size("head")
    return lax.ppermute(x, "head", [(z, z ^ bit) for z in range(count)])


def swap_heads(x):
    count = lax.axis_size("seq")
    return lax.ppermute(x, "seq", [(s, s + 1 - 2 * (s % 2)) for s in range(count)])


def unit_body(enc_in, conv_weight, norm_gain, w_qkv, w_out, grad_out):
    rows = enc_in.shape[0] // 2
    seqs = enc_in.shape[1]
    width = conv_weight.shape[2]
    local = w_qkv.shape[2]
    heads = local // DH
    groups = lax.axis_size("head")
    half = groups * seqs * rows
    place = lax.axis_index("seq")
    own_seq = (place // heads).astype(jnp.int32)
    own_head = (place % heads).astype(jnp.int32)
    at = jnp.stack([own_seq, own_head])
    head_mine = own_head.reshape(1)
    head_other = (1 - own_head).reshape(1)

    def to_chips(slots):
        return [x if j == 0 else trade_chip(x, j, heads) for j, x in enumerate(slots)]

    order = (0, 2, 1, 3)

    edge = width - width // seqs
    grad_z = lax.all_gather(grad_out[:, :, :edge], "head", axis=0, tiled=False)

    pairs = jnp.transpose(enc_in.reshape(rows, 2, seqs, enc_in.shape[2]), (1, 2, 0, 3))
    low, high = neighbour_edges(pairs[:, :, :1, :], pairs[:, :, -1:, :])
    own_part = grad_out[:, :, edge:]
    parts = [trade_z(own_part, q) for q in range(1, groups)]
    skip, slope, normed = encoder(at, pairs, low, high, conv_weight, norm_gain)
    normed = to_chips(normed)
    normed_slab = jnp.concatenate([normed[j] for j in order], axis=0)
    normed_rows = lax.all_gather(normed_slab, "head", axis=0, tiled=True)

    grad_z = after(grad_z, normed_slab)
    own_z = lax.axis_index("head").astype(jnp.int32).reshape(1)
    grad_z = jnp.concatenate([grad_z, placed(own_z, [own_part, *parts], "grad_last")], axis=3)
    grad_slots = to_chips(
        [lax.dynamic_index_in_dim(grad_z, own_seq ^ j, 2, keepdims=False) for j in range(seqs)]
    )
    *weights, packed = pack_weights(at, after(w_qkv, normed_slab))
    *grad_slots, packed = lax.optimization_barrier((*grad_slots, packed))
    grad_rows = jnp.stack([grad_slots[j] for j in order], axis=1).reshape(half, width)
    w_rows = w_out.reshape(heads, DH, width)
    d_other, one = head_product(head_other, grad_rows, w_rows, NT, "d_o_other")
    d_got = swap_heads(d_other)
    d_mine, two = head_product(head_mine, grad_rows, w_rows, NT, "d_o_own")
    grad_swapped = swap_heads(grad_rows)
    normed_rows, d_got, d_mine, grad_swapped, *weights = lax.optimization_barrier(
        (normed_rows, d_got, d_mine, grad_swapped, *weights, packed, one, two)
    )
    w_own, w_other, turned_own, turned_other = [w[None] for w in weights[:4]]
    tokens = weights[4:]
    sole = jnp.zeros((1,), jnp.int32)

    normed_swapped = swap_heads(normed_rows)
    qkv_other, _ = head_product(sole, normed_rows, w_other, NN, "qkv_other", *tokens)
    qkv_got = swap_heads(qkv_other)
    qkv_mine, _ = head_product(sole, normed_rows, w_own, NN, "qkv_own")
    result_mine, result_other = attention(qkv_mine, qkv_got, d_mine, d_got, normed_swapped)
    result_got = swap_heads(result_other)

    shape = (groups, seqs, rows, width)
    d_own = term_part(sole, result_mine, turned_own, 3 * DH, "d_term_own")
    d_term = term_part(sole, result_got, turned_other, 3 * DH, "d_term", d_own)
    d_normed = lax.psum_scatter(d_term.reshape(shape), "head", scatter_dimension=0, tiled=False)
    keep_a, send_a, keep_b, send_b = weight_gradients(
        own_seq.reshape(1),
        normed_rows,
        normed_swapped,
        grad_rows,
        grad_swapped,
        result_mine,
        result_other,
        seqs,
    )
    got_a, got_b = trade_chip(send_a, 1, heads), trade_chip(send_b, 2, heads)
    head_term = pair_term(
        head_mine, result_mine, result_got, w_rows, 3 * DH, 4 * DH, "head_term"
    )
    head_sum = lax.psum_scatter(head_term.reshape(shape), "head", scatter_dimension=0, tiled=False)
    turn_a, turn_b = weight_turn(keep_a, got_a, keep_b, got_b, head_term)
    last_a, last_b = trade_chip(turn_a, 2, heads), trade_chip(turn_b, 1, heads)

    d_normed = after(d_normed, turn_a, turn_b)
    leaving = d_normed[2:]
    near = trade_chip(leaving, 1, heads)
    far = trade_chip(jnp.stack([d_normed[1], near[1]]), 2, heads)
    half_a, half_b = weight_sum(keep_a, got_a, last_a, keep_b, got_b, last_b, leaving)
    grad = jnp.transpose(after(grad_out, d_term), (1, 0, 2))
    d_conv, first, last = conv_gradient(
        at, d_normed, near, far, skip, grad, norm_gain, slope, half_a
    )
    low, high = neighbour_edges(first, last)
    low, high, at_hand = lax.optimization_barrier((low, high, marker(conv_weight, first)))

    got_a, got_b = trade_chip(half_a, 1, heads), trade_chip(half_b, 2, heads)
    near_a = jnp.concatenate([half_a, after(got_a, low)], axis=0)
    near_b = jnp.concatenate([half_b, after(got_b, high)], axis=0)
    far_a = trade_chip(near_a, 2, heads)
    far_b = trade_chip(near_b, 1, heads)
    near_other = [swap_heads(near_a), swap_heads(near_b)]
    grad_input = conv_back(d_conv, low, high, conv_weight, at_hand, *near_other)
    *outputs, token = unpack_weights(
        at, [near_a, near_b], near_other, False, (), grad_input
    )

    head_sum = after(head_sum, grad_input, token)
    head_sum = to_chips([head_sum[order.index(j)] for j in range(seqs)])
    far_other = [swap_heads(after(x, *head_sum[1:])) for x in (far_a, far_b)]
    grad_w_qkv, grad_w_out, _ = unpack_weights(at, [far_a, far_b], far_other, True, outputs)
    mixed = mixed_call(at, head_sum, skip, token)
    grad_input = jnp.transpose(grad_input.reshape(2, seqs, rows, -1), (2, 0, 1, 3))
    return (
        jnp.transpose(mixed, (1, 0, 2)),
        grad_input.reshape(enc_in.shape),
        grad_w_qkv,
        grad_w_out.reshape(local, width),
    )


def padded_2(block, sides, width):
    for axis, dim in sides:
        count = lax.axis_size(axis)
        forward = [(i, i + 1) for i in range(count - 1)]
        backward = [(target, source) for source, target in forward]
        low = lax.ppermute(
            lax.slice_in_dim(block, block.shape[dim] - width, None, axis=dim), axis, forward
        )
        high = lax.ppermute(lax.slice_in_dim(block, 0, width, axis=dim), axis, backward)
        block = jnp.concatenate([low, block, high], axis=dim)
    return block


def gathered_body(enc_in, conv_weight, norm_gain, w_qkv, w_out, grad_out):
    fine_rows = enc_in.shape[0]
    slab_rows = fine_rows // 2
    seq_count = enc_in.shape[1]
    out_width = conv_weight.shape[2]
    local_width = w_qkv.shape[2]
    local_heads = local_width // DH
    logit_scale = DH ** (-0.5)
    padded = padded_2(enc_in, ((("seq", "head"), 0),), 2)
    convolved = jnp.zeros((fine_rows, seq_count, out_width), jnp.float32)
    for offset in range(KW):
        convolved = convolved + jnp.einsum(
            "tbi,io->tbo",
            padded[offset : offset + fine_rows],
            conv_weight[offset],
            preferred_element_type=jnp.float32,
        )
    activated, gelu_pull = jax.vjp(jax.nn.gelu, convolved)
    skip = jnp.mean(activated.reshape(slab_rows, 2, seq_count, out_width), axis=1).astype(
        jnp.bfloat16
    )
    skip_wide = skip.astype(jnp.float32)
    inv_rms = lax.rsqrt(jnp.mean(skip_wide * skip_wide, axis=-1, keepdims=True) + 1e-06)
    normed = (skip_wide * inv_rms * norm_gain).astype(jnp.bfloat16)
    normed_rows = lax.all_gather(normed, "head", axis=0, tiled=True)
    grad_rows = lax.all_gather(grad_out, "head", axis=0, tiled=True)
    tower_rows = normed_rows.shape[0]
    qkv = jnp.einsum(
        "tbc,ice->itbe", normed_rows, w_qkv, preferred_element_type=jnp.float32
    ).astype(jnp.bfloat16)
    qkv = qkv.reshape(3, tower_rows, seq_count, local_heads, DH)
    query_matrix, key_matrix, value_matrix = (qkv[0], qkv[1], qkv[2])
    key_all, value_all = (
        lax.all_gather(key_matrix, "seq", axis=0, tiled=True),
        lax.all_gather(value_matrix, "seq", axis=0, tiled=True),
    )
    attention_logits = (
        jnp.einsum("qbhd,kbhd->bhqk", query_matrix, key_all, preferred_element_type=jnp.float32)
        * logit_scale
    )
    row_peak = jnp.max(attention_logits, axis=-1, keepdims=True)
    exponent = jnp.exp(attention_logits - row_peak)
    row_total = jnp.sum(exponent, axis=-1, keepdims=True)
    soft_weights = exponent / row_total
    narrow_probabilities = soft_weights.astype(jnp.bfloat16)
    attention_output = jnp.einsum(
        "bhqk,kbhd->qbhd", narrow_probabilities, value_all, preferred_element_type=jnp.float32
    )
    o_narrow = attention_output.reshape(tower_rows, seq_count, local_width).astype(jnp.bfloat16)
    piece = o_narrow
    head_sum = lax.psum_scatter(
        jnp.einsum("tbe,ec->tbc", piece, w_out, preferred_element_type=jnp.float32).astype(
            jnp.bfloat16
        ),
        "head",
        scatter_dimension=0,
        tiled=True,
    ).astype(jnp.float32)
    mixed = (skip_wide + head_sum).astype(jnp.bfloat16)
    part_w_out = jnp.einsum("tbe,tbc->ec", o_narrow, grad_rows, preferred_element_type=jnp.float32)
    d_out = jnp.einsum("tbc,ec->tbe", grad_rows, w_out, preferred_element_type=jnp.float32).astype(
        jnp.bfloat16
    )
    d_out = d_out.reshape(tower_rows, seq_count, local_heads, DH)
    delta = jnp.sum(d_out.astype(jnp.float32) * attention_output, axis=-1)
    probability_gradient = jnp.einsum(
        "qbhd,kbhd->bhqk", d_out, value_all, preferred_element_type=jnp.float32
    )
    d_scores = soft_weights * (probability_gradient - jnp.transpose(delta, (1, 2, 0))[..., None])
    narrow_gradient = d_scores.astype(jnp.bfloat16)
    query_gradient = logit_scale * jnp.einsum(
        "bhqk,kbhd->qbhd", narrow_gradient, key_all, preferred_element_type=jnp.float32
    )
    key_terms = logit_scale * jnp.einsum(
        "bhqk,qbhd->kbhd", narrow_gradient, query_matrix, preferred_element_type=jnp.float32
    )
    value_terms = jnp.einsum(
        "bhqk,qbhd->kbhd", narrow_probabilities, d_out, preferred_element_type=jnp.float32
    )
    d_keys, d_values = (
        lax.psum_scatter(
            key_terms.astype(jnp.bfloat16), "seq", scatter_dimension=0, tiled=True
        ).astype(jnp.float32),
        lax.psum_scatter(
            value_terms.astype(jnp.bfloat16), "seq", scatter_dimension=0, tiled=True
        ).astype(jnp.float32),
    )
    dqkv = (
        jnp.stack([query_gradient, d_keys, d_values])
        .reshape(3, tower_rows, seq_count, local_width)
        .astype(jnp.bfloat16)
    )
    part_w_qkv = jnp.einsum("tbc,itbe->ice", normed_rows, dqkv, preferred_element_type=jnp.float32)
    piece = dqkv
    d_normed = lax.psum_scatter(
        jnp.einsum("itbe,ice->tbc", piece, w_qkv, preferred_element_type=jnp.float32).astype(
            jnp.bfloat16
        ),
        "head",
        scatter_dimension=0,
        tiled=True,
    ).astype(jnp.float32)
    unit_rows = skip_wide * inv_rms
    scaled = d_normed * norm_gain
    d_skip = grad_out.astype(jnp.float32) + inv_rms * (
        scaled - unit_rows * jnp.mean(scaled * unit_rows, axis=-1, keepdims=True)
    )
    d_act = jnp.repeat(d_skip, 2, axis=0) * 0.5
    d_conv = gelu_pull(d_act)[0].astype(jnp.bfloat16)
    d_pad = padded_2(d_conv, ((("seq", "head"), 0),), 2)
    grad_input = jnp.zeros((fine_rows, seq_count, enc_in.shape[2]), jnp.float32)
    for offset in range(KW):
        grad_input = grad_input + jnp.einsum(
            "tbo,io->tbi",
            d_pad[4 - offset : 4 - offset + fine_rows],
            conv_weight[offset],
            preferred_element_type=jnp.float32,
        )
    grad_w_qkv, grad_w_out = (
        lax.psum(part_w_qkv.astype(jnp.bfloat16), "seq").astype(jnp.float32),
        lax.psum(part_w_out.astype(jnp.bfloat16), "seq").astype(jnp.float32),
    )
    return (mixed, grad_input.astype(jnp.bfloat16), grad_w_qkv, grad_w_out)


def body(enc_in, conv_weight, norm_gain, w_qkv, w_out, grad_out):
    heads = w_qkv.shape[2] // DH
    seqs = enc_in.shape[1]
    fits = lax.axis_size("head") == 4 and heads == 2 and seqs == 4 and seqs * heads == lax.axis_size("seq")
    fits = fits and conv_weight.shape[2] == seqs * w_qkv.shape[2]
    chosen = unit_body if fits else gathered_body
    return chosen(enc_in, conv_weight, norm_gain, w_qkv, w_out, grad_out)


def solution(mesh):
    return jax.shard_map(
        body,
        mesh=mesh,
        in_specs=(
            P(("seq", "head"), None, None),
            P(),
            P(),
            P(None, None, "head"),
            P("head", None),
            P(("seq", "head"), None, None),
        ),
        out_specs=(
            P(("seq", "head"), None, None),
            P(("seq", "head"), None, None),
            P(None, None, "head"),
            P("head", None),
        ),
        check_vma=False,
    )
```
